32 devices in a mesh: groups: 2 (over y), tensor: 4 (over z), context: 4 (over x, core).
Axes of the slice: x: 2, y: 2, z: 4, core: 2. Of those that a mesh axis runs over, the one named last changes fastest.
Arguments:
- queries: bfloat16 [4096, 1024], P(('groups', 'context'), 'tensor'), parts along dimension 0, may hold values from -200 to 200
- span_kv: bfloat16 [4096, 1, 256], P(('groups', 'context')), parts along dimension 0, may hold values from -6 to 6
- cache: bfloat16 [2, 4096, 256], P('groups', 'context'), parts along dimension 0, may hold values from -6 to 6
- lengths: int32 [8], P(('groups', 'context')), parts along dimension 0, may hold values from 1 to 1024, 3072 in all
- offset: int32 [2], P('groups'), parts along dimension 0, may hold values from 4096 to 20479
- out_weight: bfloat16 [1024, 8192], P('tensor'), may hold values from -0.25 to 0.25
- residual: bfloat16 [4096, 8192], P(('groups', 'context'), 'tensor'), parts along dimension 0, may hold values from -40 to 40
- gain: float32 [8192], replicated, may hold values from 0.1 to 1.9
Outputs:
- hidden: bfloat16 [4096, 8192], P(('groups', 'context'), 'tensor'), parts along dimension 0
- normed: bfloat16 [4096, 8192], P(('groups', 'context')), parts along dimension 0
The draws below stay inside these ranges and needn't reach their ends.
There are 2 independent parts, one for each index of `groups`. The reference program is written for one: setup_inputs(seed, part) draws one part's arguments, and reference() takes and returns one part's arrays. A program takes and returns all parts, laid end to end along the dimension named above; an argument that names none is the same for every part. Nothing has to cross between parts.
All inputs are finite; a program needn't handle non-finite values. Where the reference program divides by a largest or mean magnitude, that divisor is 1e-20 or more. No bound on the sum of `lengths` on one device may be relied on, other than what follows from the above.
Results may differ from the reference program's by a relative error of at most 0.0095.
Values may be sent and summed in bfloat16 or wider, within the bound.
No kernel may reach another device: no remote copies, remote signals or barrier semaphores. Data moves between devices by JAX's collectives and lax.ppermute only.
A program may use at most 128 MiB of HBM per device.

```python
import math
import jax
import jax.numpy as jnp
import numpy as np
from jax import lax

D = 8192
HD = 128
HQ_DEV = 2
GROUP = 8
HB = 128
CACHE_DEV = 1024
HEADS = 8
KVH = 1
TOKENS = 2048
CACHED = 4096
N_TENSOR = 4
N_CONTEXT = 4


def draw_span_kv(key, part):
    key = jax.random.fold_in(key, 3)
    value_part = jnp.clip(jax.random.normal(jax.random.fold_in(key, 1), (TOKENS, KVH, HD), jnp.float32), -6.0, 6.0)
    key_part = jnp.clip(jax.random.normal(jax.random.fold_in(key, 5), (TOKENS, KVH, HD), jnp.float32), -6.0, 6.0)
    return jnp.concatenate([key_part, value_part], axis=-1).astype(jnp.bfloat16)


def draw_queries(key, part):
    key = jax.random.fold_in(key, 13)
    base_rows = 2.5 * jnp.clip(jax.random.normal(key, (TOKENS, KVH, GROUP, HD), jnp.float32), -6.0, 6.0)
    return base_rows.reshape(TOKENS, KVH * GROUP * HD).astype(jnp.bfloat16)


def draw_residual(key, part):
    key = jax.random.fold_in(key, 17)
    column_draw = jax.random.uniform(jax.random.fold_in(key, 1), (D,), jnp.float32)
    row_draw = jax.random.uniform(jax.random.fold_in(key, 2), (TOKENS,), jnp.float32)
    ramp = jnp.power(3.0, jnp.arange(D, dtype=jnp.float32) / D)
    entries = jnp.clip(jax.random.normal(key, (TOKENS, D), jnp.float32), -6.0, 6.0)
    row_scale = jnp.power(10.0, 0.25 * row_draw)
    column_scale = 0.2 * ramp * jnp.power(10.0, 0.5 * column_draw)
    return (entries * column_scale[None, :] * row_scale[:, None]).astype(jnp.bfloat16)


def block_levels(key, shape, shards, smallest, largest):
    factor_of, own = 1.0, jax.random.fold_in(key, 6)
    for dim, blocks in shards:
        draws = jnp.exp(jax.random.uniform(jax.random.fold_in(own, dim), (blocks,), jnp.float32, smallest / len(shards), largest / len(shards)))
        factor_of = factor_of * jnp.repeat(draws, shape[dim] // blocks).reshape([-1 if axis == dim else 1 for axis in range(len(shape))])
    return factor_of


def length_profile(number_of, total, reach, slope):
    weights = [(1 << 20) // math.isqrt(rank ** slope) + 1 for rank in range(2, number_of + 1)]
    spare, given = total - reach - (number_of - 1), [1] * (number_of - 1)
    while spare > 0:
        free = [i for i in range(number_of - 1) if given[i] < reach]
        mass, remaining = sum([weights[i] for i in free]), spare
        for i in free:
            addition = min(reach - given[i], max(1, remaining * weights[i] // mass), spare)
            given[i] = given[i] + addition
            spare = spare - addition
    return np.array([reach] + given)


def ragged(stream_key, number_of, total, limit, skew):
    if number_of == 2:
        one = jax.random.randint(stream_key, (), max(1, total - limit), min(limit, total - 1) + 1)
        return jnp.stack([one, total - one])
    sizes = jnp.asarray(length_profile(number_of, total, limit, skew), jnp.int32)
    pairs = (number_of - 1) // 2
    giver, taker = sizes[1:1 + 2 * pairs:2], sizes[2:2 + 2 * pairs:2]
    margin = jnp.minimum(giver - 1, limit - taker)
    passed = jax.random.randint(jax.random.fold_in(stream_key, 1), (pairs,), 0, 1 << 20) % (margin + 1)
    sizes = sizes.at[1:1 + 2 * pairs:2].set(giver - passed).at[2:2 + 2 * pairs:2].set(taker + passed)
    return sizes[jax.random.permutation(jax.random.fold_in(stream_key, 2), number_of)]


def normal_values(rng, dims, scale, most, split=(), held_as=jnp.bfloat16):
    values = scale * jax.random.normal(rng, dims, jnp.float32)
    if split:
        values = values * block_levels(rng, dims, split, -0.22, 0.18)
    return jnp.clip(values, -most, most).astype(held_as)


def setup_inputs(seed: int = 0, part: int = 0) -> dict:
    splits = jax.random.split(jax.random.key(seed), 9)
    own_keys = jax.random.split(jax.random.fold_in(splits[8], part), 9)
    return {
        "queries": draw_queries(jax.random.fold_in(jax.random.fold_in(splits[8], part), 71), part),
        "span_kv": draw_span_kv(jax.random.fold_in(jax.random.fold_in(splits[8], part), 71), part),
        "cache": normal_values(own_keys[2], (KVH, CACHED, 2 * HD), 1.0, 6.0, ((1, 4),)),
        "lengths": ragged(own_keys[3], N_CONTEXT, CACHED * 3 // 4, CACHE_DEV, 1).astype(jnp.int32),
        "offset": jax.random.randint(own_keys[4], (1,), CACHED, CACHED + 8 * TOKENS).astype(jnp.int32),
        "out_weight": normal_values(splits[5], (HEADS * HD, D), (2 * HQ_DEV * HD) ** -0.5, 0.25, ((0, 4),)),
        "residual": draw_residual(jax.random.fold_in(jax.random.fold_in(splits[8], part), 71), part),
        "gain": jnp.clip(1.0 + 0.18 * jax.random.normal(splits[7], (D,), jnp.float32), 0.1, 1.9),
    }


NEG = -1e+30
EPS_NORM = 1e-05
EPS_SCALE = 1e-06

def frequencies(head_width):
    counter = jnp.arange(head_width // 2, dtype=jnp.float32)
    base_freq = jnp.exp(-(2.0 * counter / head_width) * math.log(500000.0))
    wavelength = 2.0 * math.pi / base_freq
    smoothing = (8192.0 / wavelength - 1.0) / 3.0
    blended = (1.0 - smoothing) * base_freq / 8.0 + smoothing * base_freq
    return jnp.where(wavelength < 2048.0, base_freq, jnp.where(wavelength > 8192.0, base_freq / 8.0, blended))

def rotate(vectors, positions):
    head_width = vectors.shape[-1]
    angles = positions.astype(jnp.float32)[:, None] * frequencies(head_width)[None, :]
    cosine = jnp.cos(angles)[:, None, :]
    sine = jnp.sin(angles)[:, None, :]
    lower = vectors[..., :head_width // 2]
    upper = vectors[..., head_width // 2:]
    return jnp.concatenate([lower * cosine - upper * sine, upper * cosine + lower * sine], axis=-1)

def hadamard(length):
    counter = jnp.arange(length, dtype=jnp.int32)
    parity = jnp.zeros((length, length), jnp.int32)
    for shift_by in range(length.bit_length() - 1):
        digits = jnp.bitwise_and(jnp.right_shift(counter, shift_by), 1)
        parity = parity + digits[:, None] * digits[None, :]
    return (1 - 2 * jnp.bitwise_and(parity, 1)).astype(jnp.float32) / math.sqrt(length)

def reference(queries, span_kv, cache, lengths, offset, out_weight, residual, gain):
    scale_factor = 1.0 / math.sqrt(HD)
    positions = offset[0] + jnp.arange(TOKENS, dtype=jnp.int32)
    query_heads = queries.astype(jnp.float32).reshape(TOKENS, HEADS, HD)
    query_turned = rotate(query_heads, positions).astype(jnp.bfloat16).reshape(TOKENS, KVH, GROUP, HD)
    key_turned = rotate(span_kv[:, :, :HD].astype(jnp.float32), positions).astype(jnp.bfloat16)
    span_values = span_kv[:, :, HD:]
    slot_ids = jnp.arange(CACHED, dtype=jnp.int32)
    owners = slot_ids // CACHE_DEV
    live = slot_ids % CACHE_DEV < lengths[owners]
    token_ids = jnp.arange(TOKENS, dtype=jnp.int32)
    causal = token_ids[:, None] >= token_ids[None, :]
    allowed = jnp.concatenate([jnp.broadcast_to(live[None, :], (TOKENS * GROUP, CACHED)), jnp.repeat(causal, GROUP, axis=0)], axis=1)

    def one_head(group):
        head_queries, head_keys, head_values, cache_block = group
        query_rows = head_queries.reshape(TOKENS * GROUP, HD)
        keys_all = jnp.concatenate([cache_block[:, :HD], head_keys], axis=0)
        values_all = jnp.concatenate([cache_block[:, HD:], head_values], axis=0)
        scores = jnp.dot(query_rows, keys_all.T, preferred_element_type=jnp.float32) * scale_factor
        scores = jnp.where(allowed, scores, NEG)
        peak = lax.optimization_barrier(jnp.max(scores, axis=1))
        weights = jnp.where(allowed, jnp.exp(scores - peak[:, None]), 0.0)
        totals = lax.optimization_barrier(jnp.sum(weights, axis=1))
        mixed = jnp.dot(weights.astype(jnp.bfloat16), values_all, preferred_element_type=jnp.float32) / totals[:, None]
        return mixed.astype(jnp.bfloat16).reshape(TOKENS, GROUP * HD)
    per_head = lax.map(one_head, (jnp.transpose(query_turned, (1, 0, 2, 3)), jnp.transpose(key_turned, (1, 0, 2)), jnp.transpose(span_values, (1, 0, 2)), cache))
    attention = jnp.transpose(per_head, (1, 0, 2)).reshape(TOKENS, HEADS * HD)
    table = hadamard(HB)
    attention_groups = jnp.transpose(attention.reshape(TOKENS, N_TENSOR, HQ_DEV * HD), (1, 0, 2))
    weight_groups = out_weight.reshape(N_TENSOR, HQ_DEV * HD, D)

    def add_group(accum, pieces):
        attention_piece, weight_piece = pieces
        partial_value = jnp.dot(attention_piece, weight_piece, preferred_element_type=jnp.float32)
        turned = jnp.einsum('tbk,kj->tbj', partial_value.reshape(TOKENS, D // HB, HB), table, precision=lax.Precision.HIGHEST)
        block_scale = (lax.optimization_barrier(jnp.max(jnp.abs(turned), axis=-1)) + EPS_SCALE).astype(jnp.bfloat16)
        coded = (turned / block_scale.astype(jnp.float32)[..., None]).astype(jnp.bfloat16)
        restored = block_scale.astype(jnp.float32)[..., None] * coded.astype(jnp.float32)
        return (accum + restored.reshape(TOKENS, D), None)
    summed, unused = lax.scan(add_group, jnp.zeros((TOKENS, D), jnp.float32), (attention_groups, weight_groups))
    back = jnp.einsum('tbk,kj->tbj', summed.reshape(TOKENS, D // HB, HB), table, precision=lax.Precision.HIGHEST).reshape(TOKENS, D)
    hidden = (residual.astype(jnp.float32) + back).astype(jnp.bfloat16)
    hidden_f = hidden.astype(jnp.float32)
    inverse = lax.rsqrt(lax.optimization_barrier(jnp.mean(hidden_f * hidden_f, axis=1)) + EPS_NORM)
    normed = (hidden_f * inverse[:, None] * gain[None, :]).astype(jnp.bfloat16)
    return (hidden, normed)
```

```python
import functools
import math

import jax
import jax.numpy as jnp
from jax import lax
from jax.experimental import pallas as pl
from jax.experimental.pallas import tpu as pltpu
from jax.sharding import PartitionSpec as P

GROUP = 8
HD = 128
NEG = -1e30
EPS_NORM = 1e-05
VMEM_BYTES = 48 * 1024 * 1024
CHUNK = 128
KEY_BLOCK = 512


def frequencies(head_width):
    counter = jnp.arange(head_width // 2, dtype=jnp.float32)
    base_freq = jnp.exp(-(2.0 * counter / head_width) * math.log(500000.0))
    wavelength = 2.0 * math.pi / base_freq
    smoothing = (8192.0 / wavelength - 1.0) / 3.0
    blended = (1.0 - smoothing) * base_freq / 8.0 + smoothing * base_freq
    return jnp.where(
        wavelength < 2048.0, base_freq, jnp.where(wavelength > 8192.0, base_freq / 8.0, blended)
    )


def pieces_of(value, axis, count, me):
    if count & (count - 1) == 0:
        held = {0: value}
        bit = count // 2
        while bit:
            pairs = [(i, i ^ bit) for i in range(count)]
            for mask in sorted(held):
                held[mask | bit] = lax.ppermute(held[mask], axis, pairs)
            bit //= 2
        return [held[mask] for mask in range(count)], [me ^ mask for mask in range(count)]
    blocks, owners = [value], [me]
    for shift in range(1, count):
        pairs = [(i, (i + shift) % count) for i in range(count)]
        blocks.append(lax.ppermute(value, axis, pairs))
        owners.append((me + count - shift) % count)
    return blocks, owners


def rotate_kernel(q_ref, kv_ref, cos_ref, sin_ref, q_out, kv_out):
    cosine, sine = cos_ref[...], sin_ref[...]

    def turn(block):
        block = block.astype(jnp.float32)
        return (block * cosine + pltpu.roll(block, HD // 2, 1) * sine).astype(jnp.bfloat16)

    for head in range(q_ref.shape[1] // HD):
        cols = slice(head * HD, (head + 1) * HD)
        q_out[:, cols] = turn(q_ref[:, cols])
    kv_out[:, :HD] = turn(kv_ref[:, :HD])
    kv_out[:, HD:] = kv_ref[:, HD:]


def rotate_all(queries, span_pairs, cosine, sine):
    rows = queries.shape[0]
    block = min(rows, 256)
    spec = lambda width: pl.BlockSpec((block, width), lambda i: (i, 0))
    return pl.pallas_call(
        rotate_kernel,
        grid=(rows // block,),
        out_shape=(
            jax.ShapeDtypeStruct(queries.shape, jnp.bfloat16),
            jax.ShapeDtypeStruct(span_pairs.shape, jnp.bfloat16),
        ),
        in_specs=[spec(queries.shape[1]), spec(2 * HD), spec(HD), spec(HD)],
        out_specs=(spec(queries.shape[1]), spec(2 * HD)),
        name="rotate",
    )(queries, span_pairs, cosine, sine)


def attend_kernel(count, first, info, q_ref, *refs):
    caches, spans = refs[:count], refs[count : 2 * count]
    out_ref, s_ref = refs[2 * count], refs[2 * count + 1]
    rows = q_ref.shape[0]
    heads = q_ref.shape[1] // HD
    chunk = pl.program_id(0) + first
    mine = info[0]
    q = jnp.concatenate([q_ref[:, h * HD : (h + 1) * HD] for h in range(heads)], axis=0)
    exponent = math.log2(math.e) / math.sqrt(HD)

    blocks = []
    peak = jnp.full((heads * rows, HD), NEG, jnp.float32)
    column = 0
    for kind, group in (("cache", caches), ("span", spans)):
        for number, ref in enumerate(group):
            width = min(KEY_BLOCK, ref.shape[0])
            for begin in range(0, ref.shape[0], width):
                scores = lax.dot_general(
                    q,
                    ref[begin : begin + width, :HD],
                    (((1,), (1,)), ((), ())),
                    preferred_element_type=jnp.float32,
                )
                if kind == "cache":
                    slot = lax.broadcasted_iota(jnp.int32, (1, width), 1) + begin
                    live = slot < info[1 + count + number]
                    scores = scores + jnp.where(live, 0.0, NEG)
                elif number == 0:
                    key = lax.broadcasted_iota(jnp.int32, (rows, width), 1) + begin
                    row = lax.broadcasted_iota(jnp.int32, (rows, width), 0) + chunk * rows
                    bias = jnp.where(key <= row, 0.0, NEG)
                    scores = scores + jnp.concatenate([bias] * heads, axis=0)
                else:
                    scores = scores + jnp.where(info[1 + number] < mine, 0.0, NEG)
                s_ref[:, column : column + width] = scores
                for lane in range(0, width, HD):
                    peak = jnp.maximum(peak, scores[:, lane : lane + HD])
                blocks.append((ref, begin, column, width))
                column += width
    top = jnp.max(peak, axis=1, keepdims=True)
    total = jnp.zeros((heads * rows, HD), jnp.float32)
    mixed = jnp.zeros((heads * rows, HD), jnp.float32)
    for ref, begin, column, width in blocks:
        weights = jnp.exp2((s_ref[:, column : column + width] - top) * exponent)
        for lane in range(0, width, HD):
            total = total + weights[:, lane : lane + HD]
        mixed = mixed + jnp.dot(
            weights.astype(jnp.bfloat16),
            ref[begin : begin + width, HD:],
            preferred_element_type=jnp.float32,
        )
    result = (mixed / jnp.sum(total, axis=1, keepdims=True)).astype(jnp.bfloat16)
    for h in range(heads):
        out_ref[:, h * HD : (h + 1) * HD] = result[h * rows : (h + 1) * rows]


def attend(info, queries, caches, spans, first, chunks, rows):
    count = len(caches)
    width = queries.shape[1]
    heads = width // HD
    keys = sum(a.shape[0] for a in caches) + sum(a.shape[0] for a in spans)
    whole = lambda a: pl.BlockSpec(a.shape, lambda i, info: (0, 0))
    return pl.pallas_call(
        functools.partial(attend_kernel, count, first),
        grid_spec=pltpu.PrefetchScalarGridSpec(
            num_scalar_prefetch=1,
            grid=(chunks,),
            in_specs=[pl.BlockSpec((rows, width), lambda i, info: (i + first, 0))]
            + [whole(a) for a in caches]
            + [whole(a) for a in spans],
            out_specs=pl.BlockSpec((rows, width), lambda i, info: (i, 0)),
            scratch_shapes=[pltpu.VMEM((heads * rows, keys), jnp.float32)],
        ),
        out_shape=jax.ShapeDtypeStruct((chunks * rows, width), jnp.bfloat16),
        compiler_params=pltpu.CompilerParams(vmem_limit_bytes=VMEM_BYTES),
        cost_estimate=pl.CostEstimate(
            flops=4 * chunks * rows * heads * keys * HD,
            bytes_accessed=keys * 4 * HD,
            transcendentals=chunks * rows * heads * keys,
        ),
        name="attend",
    )(info, queries, *caches, *spans)


def cut_kernel(count, info, w_ref, *refs):
    outs, sems = refs[:count], refs[count]
    part, slab = outs[0].shape
    copies = []
    for number, out in enumerate(outs):
        start = pl.multiple_of(info[1 + number] * slab, slab)
        copies.append(
            pltpu.make_async_copy(
                w_ref.at[pl.ds(pl.multiple_of(info[0] * part, part), part), pl.ds(start, slab)],
                out,
                sems.at[number],
            )
        )
    for copy in copies:
        copy.start()
    for copy in copies:
        copy.wait()


def cut(info, out_weight, part, slab, count):
    anywhere = pl.BlockSpec(memory_space=pl.ANY)
    return pl.pallas_call(
        functools.partial(cut_kernel, count),
        grid_spec=pltpu.PrefetchScalarGridSpec(
            num_scalar_prefetch=1,
            grid=(),
            in_specs=[anywhere],
            out_specs=[anywhere] * count,
            scratch_shapes=[pltpu.SemaphoreType.DMA((count,))],
        ),
        out_shape=[jax.ShapeDtypeStruct((part, slab), out_weight.dtype)] * count,
        name="cut",
    )(info, out_weight)


def project_kernel(count, info, a_ref, w_ref, r_ref, h_ref):
    total = r_ref[...].astype(jnp.float32)
    depth = a_ref.shape[2]
    for number in range(count):
        weight = w_ref[:, number].reshape(depth, w_ref.shape[3])
        total = total + jnp.dot(
            a_ref[info[number]], weight, preferred_element_type=jnp.float32
        )
    h_ref[...] = total.astype(jnp.bfloat16)


def project(order, attention, weights, residual, place, chunk, rows):
    count, depth = attention.shape[0], attention.shape[2]
    slab = residual.shape[1]
    tile = min(slab, 512)
    shares, part = weights.shape[0], weights.shape[2]
    return pl.pallas_call(
        functools.partial(project_kernel, count),
        grid_spec=pltpu.PrefetchScalarGridSpec(
            num_scalar_prefetch=1,
            grid=(slab // tile,),
            in_specs=[
                pl.BlockSpec((count, rows, depth), lambda j, info: (0, place, 0)),
                pl.BlockSpec((shares, count, part, tile), lambda j, info: (0, 0, 0, j)),
                pl.BlockSpec((rows, tile), lambda j, info: (chunk, j)),
            ],
            out_specs=pl.BlockSpec((rows, tile), lambda j, info: (0, j)),
        ),
        out_shape=jax.ShapeDtypeStruct((rows, slab), jnp.bfloat16),
        compiler_params=pltpu.CompilerParams(vmem_limit_bytes=VMEM_BYTES),
        cost_estimate=pl.CostEstimate(
            flops=2 * rows * count * depth * slab,
            bytes_accessed=2 * count * depth * slab,
            transcendentals=0,
        ),
        name="project",
    )(order, attention, weights, residual)


def norm_kernel(h_ref, g_ref, *refs):
    out_ref = refs[-1]
    count, rows, slab = h_ref.shape
    squares = jnp.zeros((rows, 1), jnp.float32)
    for number in range(count):
        block = h_ref[number].astype(jnp.float32)
        squares = squares + jnp.sum(block * block, axis=1, keepdims=True)
    inverse = lax.rsqrt(squares / (count * slab) + EPS_NORM)
    for number in range(count):
        cols = slice(number * slab, (number + 1) * slab)
        block = h_ref[number].astype(jnp.float32)
        out_ref[:, cols] = (block * inverse * g_ref[:, cols]).astype(jnp.bfloat16)


def norm_into(buffer, gathered, gain, chunk, total_rows):
    count, rows, slab = gathered.shape
    width = count * slab
    step = min(rows, 32)
    steps = rows // step
    in_specs = [
        pl.BlockSpec((count, step, slab), lambda i: (0, i, 0)),
        pl.BlockSpec((1, width), lambda i: (0, 0)),
    ]
    args = [gathered, gain.reshape(1, width)]
    aliases = {}
    if buffer is not None:
        in_specs.append(pl.BlockSpec(memory_space=pl.ANY))
        args.append(buffer)
        aliases = {2: 0}
    return pl.pallas_call(
        norm_kernel,
        grid=(steps,),
        in_specs=in_specs,
        out_specs=pl.BlockSpec((step, width), lambda i: (chunk * steps + i, 0)),
        out_shape=jax.ShapeDtypeStruct((total_rows, width), jnp.bfloat16),
        input_output_aliases=aliases,
        compiler_params=pltpu.CompilerParams(vmem_limit_bytes=VMEM_BYTES),
        cost_estimate=pl.CostEstimate(
            flops=6 * rows * width, bytes_accessed=4 * rows * width, transcendentals=0
        ),
        name="norm",
    )(*args)


def per_device(queries, span_kv, cache, lengths, offset, out_weight, residual, gain):
    rows = queries.shape[0]
    heads = queries.shape[1] // HD
    depth, model_width = out_weight.shape
    slab = residual.shape[1]
    context_count = lax.axis_size("context")
    tensor_count = lax.axis_size("tensor")
    context_index = lax.axis_index("context")
    tensor_index = lax.axis_index("tensor")
    kv_index = tensor_index * heads // GROUP
    shares = lax.axis_size("groups") * context_count
    share = lax.axis_index("groups") * context_count + context_index

    part = depth // shares
    targets = [(tensor_index + d) % tensor_count for d in range(tensor_count)]
    cuts = cut(
        jnp.stack([share] + targets).astype(jnp.int32), out_weight, part, slab, tensor_count
    )
    mine = [cuts[0]]
    for shift in range(1, tensor_count):
        pairs = [(i, (i + shift) % tensor_count) for i in range(tensor_count)]
        mine.append(lax.ppermute(cuts[shift], "tensor", pairs))
    order = jnp.stack(
        [(tensor_index + tensor_count - d) % tensor_count for d in range(tensor_count)]
    ).astype(jnp.int32)
    weights = lax.all_gather(jnp.stack(mine), ("groups", "context"), axis=0, tiled=False)

    cache_local = lax.dynamic_index_in_dim(cache, kv_index, 0, keepdims=False)
    caches, owners = pieces_of(cache_local, "context", context_count, context_index)
    length_pieces, _ = pieces_of(lengths, "context", context_count, context_index)
    span_local = lax.dynamic_index_in_dim(span_kv, kv_index, 1, keepdims=False)
    positions = offset[0] + context_index * rows + jnp.arange(rows, dtype=jnp.int32)
    angles = positions.astype(jnp.float32)[:, None] * frequencies(HD)[None, :]
    cosine, sine = jnp.cos(angles), jnp.sin(angles)
    q_turned, span_turned = rotate_all(
        queries,
        span_local,
        jnp.concatenate([cosine, cosine], axis=1),
        jnp.concatenate([-sine, sine], axis=1),
    )
    spans, _ = pieces_of(span_turned, "context", context_count, context_index)
    info = jnp.concatenate(
        [jnp.stack([context_index] + owners).astype(jnp.int32)] + length_pieces
    )

    chunk = min(CHUNK, rows)
    chunks = rows // chunk
    gathered = [
        lax.all_gather(
            attend(info, q_turned, caches, spans, 0, 1, chunk), "tensor", axis=0, tiled=False
        )
    ]
    if chunks > 1:
        gathered.append(
            lax.all_gather(
                attend(info, q_turned, caches, spans, 1, chunks - 1, chunk),
                "tensor",
                axis=0,
                tiled=False,
            )
        )

    hidden_parts = []
    normed = None
    for number in range(chunks):
        source = gathered[0] if number == 0 else gathered[1]
        place = 0 if number == 0 else number - 1
        part_hidden = project(order, source, weights, residual, place, number, chunk)
        hidden_parts.append(part_hidden)
    for number in range(chunks):
        whole = lax.all_gather(hidden_parts[number], "tensor", axis=0, tiled=False)
        normed = norm_into(normed, whole, gain, number, rows)
    return (jnp.concatenate(hidden_parts, axis=0), normed)


def solution(mesh):
    in_specs = (
        P(("groups", "context"), "tensor"),
        P(("groups", "context"), None, None),
        P("groups", "context", None),
        P(("groups", "context")),
        P("groups"),
        P("tensor", None),
        P(("groups", "context"), "tensor"),
        P(),
    )
    out_specs = (P(("groups", "context"), "tensor"), P(("groups", "context"), None))
    return jax.shard_map(
        per_device, mesh=mesh, in_specs=in_specs, out_specs=out_specs, check_vma=False
    )
```

```python
import functools
import math

import jax
import jax.numpy as jnp
from jax import lax
from jax.experimental import pallas as pl
from jax.experimental.pallas import tpu as pltpu
from jax.sharding import PartitionSpec as P

GROUP = 8
HD = 128
NEG = -1e30
EPS_NORM = 1e-05
VMEM_BYTES = 48 * 1024 * 1024
CHUNK = 128
KEY_BLOCK = 512
TAIL = 16
DIGIT = 32
PARAMS = pltpu.CompilerParams(vmem_limit_bytes=VMEM_BYTES)
ANYWHERE = pl.BlockSpec(memory_space=pl.ANY)


def frequencies(head_width):
    counter = jnp.arange(head_width // 2, dtype=jnp.float32)
    base_freq = jnp.exp(-(2.0 * counter / head_width) * math.log(500000.0))
    wavelength = 2.0 * math.pi / base_freq
    smoothing = (8192.0 / wavelength - 1.0) / 3.0
    blended = (1.0 - smoothing) * base_freq / 8.0 + smoothing * base_freq
    return jnp.where(
        wavelength < 2048.0, base_freq, jnp.where(wavelength > 8192.0, base_freq / 8.0, blended)
    )


def pieces_of(value, axis, count):
    if count & (count - 1) == 0:
        held = {0: value}
        bit = count // 2
        while bit:
            pairs = [(i, i ^ bit) for i in range(count)]
            for mask in sorted(held):
                held[mask | bit] = lax.ppermute(held[mask], axis, pairs)
            bit //= 2
        return [held[mask] for mask in range(count)]
    blocks = [value]
    for shift in range(1, count):
        pairs = [(i, (i + shift) % count) for i in range(count)]
        blocks.append(lax.ppermute(value, axis, pairs))
    return blocks


def owners_of(count, me):
    if count & (count - 1) == 0:
        return [me ^ mask for mask in range(count)]
    return [(me + count - shift) % count for shift in range(count)]


def line_gather(value, count):
    if count != 4:
        return [lax.all_gather(value, "tensor", axis=0, tiled=False)]
    up = lax.ppermute(value, "tensor", [(0, 1), (1, 2), (2, 3)])
    down = lax.ppermute(value, "tensor", [(1, 0), (2, 1), (3, 2)])
    far = lax.ppermute(value, "tensor", [(0, 2), (1, 3), (2, 0), (3, 1)])
    last = lax.ppermute(far, "tensor", [(1, 0), (2, 3)])
    return [value, up, down, far, last]


class Table:
    def __init__(self, contexts, count):
        self.contexts, self.count = contexts, count
        self.owner = 1
        self.place = 1 + contexts
        self.low = self.place + count
        self.high = self.low + 1
        self.share = self.low + 2


def line_read(table, info, refs, d, cols=slice(None)):
    if len(refs) == 1:
        return refs[0][info[table.place + d], :, cols].astype(jnp.float32)
    if d == 0:
        return refs[0][:, cols].astype(jnp.float32)
    if d == 2:
        return refs[3][:, cols].astype(jnp.float32)
    near = refs[1 if d == 1 else 2][:, cols].astype(jnp.float32)
    other = refs[4][:, cols].astype(jnp.float32)
    at_end = info[table.low if d == 1 else table.high]
    return jnp.where(at_end == 1, other, near)


def line_spec(blocks, rows, index):
    if len(blocks) == 1:
        count, _, width = blocks[0].shape
        return [pl.BlockSpec((count, rows, width), lambda i, info: (0, index(i), 0))]
    width = blocks[0].shape[1]
    return [pl.BlockSpec((rows, width), lambda i, info: (index(i), 0)) for _ in blocks]


def call(kernel, name, info, args, in_specs, out_specs, out_shape, grid=(1,), aliases=None,
         scratch=(), flops=0, transcendentals=0):
    size = sum(math.prod(a.shape) * a.dtype.itemsize for a in args)
    return pl.pallas_call(
        kernel,
        grid_spec=pltpu.PrefetchScalarGridSpec(
            num_scalar_prefetch=1,
            grid=grid,
            in_specs=in_specs,
            out_specs=out_specs,
            scratch_shapes=list(scratch),
        ),
        out_shape=out_shape,
        input_output_aliases=aliases or {},
        compiler_params=PARAMS,
        cost_estimate=pl.CostEstimate(
            flops=flops, bytes_accessed=size, transcendentals=transcendentals
        ),
        name=name,
    )(info, *args)


def whole(a):
    zeros = (0,) * len(a.shape)
    return pl.BlockSpec(tuple(a.shape), lambda i, info: zeros)


def cut_kernel(table, slab, keep, info, w_ref, *outs):
    for d, out in enumerate(outs):
        target = lax.rem(info[table.place] + d, table.count)
        start = pl.multiple_of(target * slab, slab)
        out[:, :keep] = w_ref[:, pl.ds(start, keep)]
        for j in range(table.count if keep < slab else 0):
            raw = slab - keep
            out[:, keep + j * raw : keep + (j + 1) * raw] = w_ref[
                :, j * slab + keep : (j + 1) * slab
            ]


def cut(table, info, out_weight, part, slab, keep):
    width = keep + table.count * (slab - keep)
    shape = jax.ShapeDtypeStruct((part, width), out_weight.dtype)
    return call(
        functools.partial(cut_kernel, table, slab, keep),
        "cut",
        info,
        [out_weight],
        [pl.BlockSpec((part, out_weight.shape[1]), lambda i, info: (info[table.share], 0))],
        [whole(shape)] * table.count,
        [shape] * table.count,
    )


def stack_kernel(count, begin, info, *refs):
    parts, outs = refs[:count], refs[-1]
    for number, part in enumerate(parts):
        outs[number] = part[:, begin : begin + outs.shape[2]]


def stack_raw_kernel(count, begin, raw, info, *refs):
    stack_kernel(count, begin, info, *refs[:count], refs[-2])
    refs[-1][...] = refs[count][...]


def stack(info, parts, begin, width, after=None, residual=None, raw=0):
    count, part = len(parts), parts[0].shape[0]
    shape = jax.ShapeDtypeStruct((count, part, width), parts[0].dtype)
    specs = [whole(p) for p in parts]
    if residual is not None:
        rows, slab = residual.shape
        out = jax.ShapeDtypeStruct((rows, raw), residual.dtype)
        return call(
            functools.partial(stack_raw_kernel, count, begin, raw),
            "stack",
            info,
            [*parts, residual],
            specs + [pl.BlockSpec((rows, raw), lambda i, info: (0, slab // raw - 1))],
            [whole(shape), whole(out)],
            [shape, out],
        )
    extra = [] if after is None else [after]
    return call(
        functools.partial(stack_kernel, count, begin),
        "stack",
        info,
        [*parts, *extra],
        specs + [ANYWHERE] * len(extra),
        whole(shape),
        shape,
    )


def rotate_kernel(info, q_ref, kv_ref, cos_ref, sin_ref, length_ref, q_out, kv_out):
    cosine, sine = cos_ref[...], sin_ref[...]
    rows = q_ref.shape[0]

    def turn(block):
        block = block.astype(jnp.float32)
        return (block * cosine + pltpu.roll(block, HD // 2, 1) * sine).astype(jnp.bfloat16)

    kv_out[:rows, :HD] = turn(kv_ref[:, :HD])
    kv_out[:rows, HD:] = kv_ref[:, HD:]
    length = length_ref[0]
    upper = lax.div(length, DIGIT)
    lower = length - upper * DIGIT
    kv_out[rows:, :HD] = jnp.full((TAIL, HD), upper.astype(jnp.float32)).astype(jnp.bfloat16)
    kv_out[rows:, HD:] = jnp.full((TAIL, HD), lower.astype(jnp.float32)).astype(jnp.bfloat16)
    for head in range(q_ref.shape[1] // HD):
        cols = slice(head * HD, (head + 1) * HD)
        q_out[:, cols] = turn(q_ref[:, cols])


def rotate_all(info, queries, span_pairs, cosine, sine, lengths):
    rows = queries.shape[0]
    pairs = jax.ShapeDtypeStruct((rows + TAIL, 2 * HD), jnp.bfloat16)
    turned = jax.ShapeDtypeStruct(queries.shape, jnp.bfloat16)
    return call(
        rotate_kernel,
        "rotate",
        info,
        [queries, span_pairs, cosine, sine, lengths],
        [whole(a) for a in (queries, span_pairs, cosine, sine)]
        + [pl.BlockSpec(memory_space=pltpu.SMEM)],
        [whole(turned), whole(pairs)],
        [turned, pairs],
    )


def attend_kernel(table, info, q_ref, *refs):
    count = table.contexts
    caches, spans = refs[:count], refs[count : 2 * count]
    out_ref, s_ref = refs[2 * count], refs[2 * count + 1]
    rows = q_ref.shape[0]
    heads = q_ref.shape[1] // HD
    chunk = pl.program_id(0)
    mine = info[0]
    q = jnp.concatenate([q_ref[:, h * HD : (h + 1) * HD] for h in range(heads)], axis=0)
    exponent = math.log2(math.e) / math.sqrt(HD)

    blocks = []
    peak = jnp.full((heads * rows, HD), NEG, jnp.float32)
    column = 0
    for kind, group in (("cache", caches), ("span", spans)):
        for number, ref in enumerate(group):
            keys = ref.shape[0] if kind == "cache" else ref.shape[0] - TAIL
            width = min(KEY_BLOCK, keys)
            tail = spans[number]
            tail_row = tail.shape[0] - TAIL
            length = tail[tail_row : tail_row + 1, :HD].astype(jnp.float32) * DIGIT + tail[
                tail_row : tail_row + 1, HD:
            ].astype(jnp.float32)
            length = jnp.concatenate([length] * (width // HD), axis=1)
            for begin in range(0, keys, width):
                scores = lax.dot_general(
                    q,
                    ref[begin : begin + width, :HD],
                    (((1,), (1,)), ((), ())),
                    preferred_element_type=jnp.float32,
                )
                if kind == "cache":
                    slot = lax.broadcasted_iota(jnp.int32, (1, width), 1) + begin
                    live = slot.astype(jnp.float32) < length
                    scores = scores + jnp.where(live, 0.0, NEG)
                elif number == 0:
                    key = lax.broadcasted_iota(jnp.int32, (rows, width), 1) + begin
                    row = lax.broadcasted_iota(jnp.int32, (rows, width), 0) + chunk * rows
                    bias = jnp.where(key <= row, 0.0, NEG)
                    scores = scores + jnp.concatenate([bias] * heads, axis=0)
                else:
                    scores = scores + jnp.where(info[table.owner + number] < mine, 0.0, NEG)
                s_ref[:, column : column + width] = scores
                for lane in range(0, width, HD):
                    peak = jnp.maximum(peak, scores[:, lane : lane + HD])
                blocks.append((ref, begin, column, width))
                column += width
    top = jnp.max(peak, axis=1, keepdims=True)
    total = jnp.zeros((heads * rows, HD), jnp.float32)
    mixed = jnp.zeros((heads * rows, HD), jnp.float32)
    for ref, begin, column, width in blocks:
        weights = jnp.exp2((s_ref[:, column : column + width] - top) * exponent)
        for lane in range(0, width, HD):
            total = total + weights[:, lane : lane + HD]
        mixed = mixed + jnp.dot(
            weights.astype(jnp.bfloat16),
            ref[begin : begin + width, HD:],
            preferred_element_type=jnp.float32,
        )
    result = (mixed / jnp.sum(total, axis=1, keepdims=True)).astype(jnp.bfloat16)
    for h in range(heads):
        out_ref[:, h * HD : (h + 1) * HD] = result[h * rows : (h + 1) * rows]


def attend(table, info, queries, caches, spans, rows):
    all_rows, width = queries.shape
    heads = width // HD
    keys = sum(a.shape[0] for a in caches) + sum(a.shape[0] - TAIL for a in spans)
    chunk_spec = pl.BlockSpec((rows, width), lambda i, info: (i, 0))
    return call(
        functools.partial(attend_kernel, table),
        "attend",
        info,
        [queries, *caches, *spans],
        [chunk_spec] + [whole(a) for a in caches] + [whole(a) for a in spans],
        chunk_spec,
        jax.ShapeDtypeStruct((all_rows, width), jnp.bfloat16),
        grid=(all_rows // rows,),
        scratch=[pltpu.VMEM((heads * rows, keys), jnp.float32)],
        flops=4 * all_rows * heads * keys * HD,
        transcendentals=all_rows * heads * keys,
    )


def project_kernel(table, lines, keep, info, *refs):
    count = table.count
    attention = refs[:lines]
    w_ref, r_ref = refs[lines], refs[lines + 1]
    parts, h_ref = refs[lines + 2 : -1], refs[-1]
    total = r_ref[:, :keep].astype(jnp.float32)
    for d in range(count):
        block = line_read(table, info, attention, d).astype(jnp.bfloat16)
        weight = w_ref[:, d].reshape(block.shape[1], keep)
        total = total + jnp.dot(block, weight, preferred_element_type=jnp.float32)
    result = total.astype(jnp.bfloat16)
    h_ref[:, :keep] = result
    for number, part in enumerate(parts):

        @pl.when(pl.program_id(0) == number)
        def _():
            part[...] = result


def project(table, info, attention, weights, residual, rows):
    all_rows, slab = residual.shape
    keep = weights.shape[3]
    chunks = all_rows // rows
    part = jax.ShapeDtypeStruct((rows, keep), jnp.bfloat16)
    hidden = jax.ShapeDtypeStruct(residual.shape, jnp.bfloat16)
    row_spec = pl.BlockSpec((rows, slab), lambda i, info: (i, 0))
    return call(
        functools.partial(project_kernel, table, len(attention), keep),
        "project",
        info,
        [*attention, weights, residual],
        line_spec(attention, rows, lambda i: i) + [whole(weights), row_spec],
        [whole(part)] * chunks + [row_spec],
        [part] * chunks + [hidden],
        grid=(chunks,),
        flops=2 * all_rows * math.prod(weights.shape),
    )


def project_raw_kernel(table, lines, raw_lines, info, *refs):
    count = table.count
    attention, residuals = refs[:lines], refs[lines : lines + raw_lines]
    w_ref = refs[lines + raw_lines]
    raw_ref, h_ref = refs[-2:]
    raw = h_ref.shape[1]
    blocks = [
        line_read(table, info, attention, d).astype(jnp.bfloat16) for d in range(count)
    ]
    for slab in range(count):
        start = pl.multiple_of(info[table.place + slab] * raw, raw)
        total = line_read(table, info, residuals, slab)
        for d in range(count):
            weight = w_ref[:, d, :, pl.ds(start, raw)].reshape(blocks[d].shape[1], raw)
            total = total + jnp.dot(blocks[d], weight, preferred_element_type=jnp.float32)
        result = total.astype(jnp.bfloat16)
        raw_ref[:, slab * raw : (slab + 1) * raw] = result
        if slab == 0:
            h_ref[...] = result


def project_raw(table, info, attention, residuals, weights, hidden, raw, rows):
    all_rows, slab = hidden.shape
    args = [*attention, *residuals, weights, hidden]
    out = jax.ShapeDtypeStruct((all_rows, table.count * raw), jnp.bfloat16)
    return call(
        functools.partial(project_raw_kernel, table, len(attention), len(residuals)),
        "project_raw",
        info,
        args,
        line_spec(attention, rows, lambda i: i)
        + line_spec(residuals, rows, lambda i: i)
        + [whole(weights), ANYWHERE],
        [
            pl.BlockSpec((rows, table.count * raw), lambda i, info: (i, 0)),
            pl.BlockSpec((rows, raw), lambda i, info: (i, slab // raw - 1)),
        ],
        [out, jax.ShapeDtypeStruct(hidden.shape, jnp.bfloat16)],
        grid=(all_rows // rows,),
        aliases={len(args): 1},
        flops=2 * all_rows * math.prod(weights.shape),
    )


def norm_kernel(table, lines, keep, slab, info, g_ref, *refs):
    count = table.count
    blocks, out_ref = refs[:lines], refs[-1]
    raw = slab - keep
    values = []
    squares = jnp.zeros((out_ref.shape[0], 1), jnp.float32)

    def read(d):
        found = [(0, keep, line_read(table, info, blocks, d))]
        if raw:
            cols = slice(d * raw, (d + 1) * raw)
            found.append((keep, raw, refs[lines][:, cols].astype(jnp.float32)))
        return found

    for d in range(count):
        for _, _, value in read(d):
            squares = squares + jnp.sum(value * value, axis=1, keepdims=True)
    inverse = lax.rsqrt(squares / (count * slab) + EPS_NORM)
    for d in range(count):
        for offset, width, value in read(d):
            start = pl.multiple_of(info[table.place + d] * slab + offset, HD)
            cols = pl.ds(start, width)
            out_ref[:, cols] = (value * inverse * g_ref[:, cols]).astype(jnp.bfloat16)


def norm_into(table, info, buffer, blocks, raw_hidden, gain, chunk, rows, keep, slab, total_rows):
    width = table.count * slab
    step = min(rows, 32)
    steps = rows // step
    args = [gain.reshape(1, width), *blocks]
    in_specs = [pl.BlockSpec((1, width), lambda i, info: (0, 0))]
    in_specs += line_spec(blocks, step, lambda i: i)
    if raw_hidden is not None:
        args.append(raw_hidden)
        in_specs.append(
            pl.BlockSpec((step, raw_hidden.shape[1]), lambda i, info: (chunk * steps + i, 0))
        )
    aliases = {}
    if buffer is not None:
        args.append(buffer)
        in_specs.append(ANYWHERE)
        aliases = {len(args): 0}
    return call(
        functools.partial(norm_kernel, table, len(blocks), keep, slab),
        "norm",
        info,
        args,
        in_specs,
        pl.BlockSpec((step, width), lambda i, info: (chunk * steps + i, 0)),
        jax.ShapeDtypeStruct((total_rows, width), jnp.bfloat16),
        grid=(steps,),
        aliases=aliases,
        flops=6 * rows * width,
    )


def per_device(queries, span_kv, cache, lengths, offset, out_weight, residual, gain):
    rows = queries.shape[0]
    heads = queries.shape[1] // HD
    depth = out_weight.shape[0]
    slab = residual.shape[1]
    contexts = lax.axis_size("context")
    count = lax.axis_size("tensor")
    context_index = lax.axis_index("context")
    tensor_index = lax.axis_index("tensor")
    kv_index = tensor_index * heads // GROUP
    shares = lax.axis_size("groups") * contexts
    share = lax.axis_index("groups") * contexts + context_index
    raw = slab // 4 if slab % 512 == 0 else 0
    keep = slab - raw
    chunk = min(CHUNK, rows)
    chunks = rows // chunk

    table = Table(contexts, count)
    steering = [context_index, *owners_of(contexts, context_index)]
    steering += [lax.rem(tensor_index + (count - d), count) for d in range(count)]
    steering += [tensor_index == 0, tensor_index == count - 1, share]
    info = jnp.stack([jnp.asarray(v).astype(jnp.int32) for v in steering])

    cache_local = lax.dynamic_index_in_dim(cache, kv_index, 0, keepdims=False)
    caches = pieces_of(cache_local, "context", contexts)
    span_local = lax.dynamic_index_in_dim(span_kv, kv_index, 1, keepdims=False)
    positions = offset[0] + context_index * rows + jnp.arange(rows, dtype=jnp.int32)
    both = jnp.concatenate([frequencies(HD)] * 2)
    angles = positions.astype(jnp.float32)[:, None] * both[None, :]
    sign = jnp.where(jnp.arange(HD) < HD // 2, -1.0, 1.0)
    q_turned, span_turned = rotate_all(
        info, queries, span_local, jnp.cos(angles), jnp.sin(angles) * sign[None, :], lengths
    )
    spans = pieces_of(span_turned, "context", contexts)

    cuts = cut(table, info, out_weight, depth // shares, slab, keep)
    parts = [cuts[0]]
    for shift in range(1, count):
        pairs = [(i, (i + shift) % count) for i in range(count)]
        parts.append(lax.ppermute(cuts[shift], "tensor", pairs))
    plane = ("groups", "context")
    if raw:
        own_weights, residual_raw = stack(info, parts, 0, keep, residual=residual, raw=raw)
        residuals = line_gather(residual_raw, count)
    else:
        own_weights = stack(info, parts, 0, keep)
    own_weights = lax.all_gather(own_weights, plane, axis=0, tiled=False)

    mixed = attend(table, info, q_turned, caches, spans, chunk)
    attention = line_gather(mixed, count)

    *hidden_parts, hidden = project(table, info, attention, own_weights, residual, chunk)
    raw_hidden = None
    if raw:
        raw_weights = stack(info, parts, keep, count * raw, after=mixed)
        raw_weights = lax.all_gather(raw_weights, plane, axis=0, tiled=False)
        raw_hidden, hidden = project_raw(
            table, info, attention, residuals, raw_weights, hidden, raw, chunk
        )
    normed = None
    for number in range(chunks):
        blocks = line_gather(hidden_parts[number], count)
        normed = norm_into(
            table, info, normed, blocks, raw_hidden, gain, number, chunk, keep, slab, rows
        )
    return (hidden, normed)


def solution(mesh):
    in_specs = (
        P(("groups", "context"), "tensor"),
        P(("groups", "context"), None, None),
        P("groups", "context", None),
        P(("groups", "context")),
        P("groups"),
        P("tensor", None),
        P(("groups", "context"), "tensor"),
        P(),
    )
    out_specs = (P(("groups", "context"), "tensor"), P(("groups", "context"), None))
    return jax.shard_map(
        per_device, mesh=mesh, in_specs=in_specs, out_specs=out_specs, check_vma=False
    )
```

```python
import functools
import math

import jax
import jax.numpy as jnp
from jax import lax
from jax.experimental import pallas as pl
from jax.experimental.pallas import tpu as pltpu
from jax.sharding import PartitionSpec as P

GROUP = 8
HD = 128
NEG = -1e30
EPS_NORM = 1e-05
MIB = 1024 * 1024
CHUNK = 128
KEY_BLOCK = 512
ATTEND_FLOPS = 16
TAIL = 16
DIGIT = 32
ANYWHERE = pl.BlockSpec(memory_space=pl.ANY)


def frequencies(head_width):
    counter = jnp.arange(head_width // 2, dtype=jnp.float32)
    base_freq = jnp.exp(-(2.0 * counter / head_width) * math.log(500000.0))
    wavelength = 2.0 * math.pi / base_freq
    smoothing = (8192.0 / wavelength - 1.0) / 3.0
    blended = (1.0 - smoothing) * base_freq / 8.0 + smoothing * base_freq
    return jnp.where(
        wavelength < 2048.0, base_freq, jnp.where(wavelength > 8192.0, base_freq / 8.0, blended)
    )


def pieces_of(value, axis, count, between=lambda block: block):
    if count & (count - 1) == 0:
        held = {0: value}
        bit = count // 2
        while bit:
            pairs = [(i, i ^ bit) for i in range(count)]
            for mask in sorted(held):
                held[mask | bit] = lax.ppermute(held[mask], axis, pairs)
            if bit == count // 2:
                held[bit] = between(held[bit])
            bit //= 2
        return [held[mask] for mask in range(count)]
    blocks = [value]
    for shift in range(1, count):
        pairs = [(i, (i + shift) % count) for i in range(count)]
        blocks.append(lax.ppermute(value, axis, pairs))
    return blocks


def owners_of(count, me):
    if count & (count - 1) == 0:
        return [me ^ mask for mask in range(count)]
    return [(me + count - shift) % count for shift in range(count)]


def plane_gather(value, groups, contexts):
    count = groups * contexts
    if count & (count - 1):
        gathered = lax.all_gather(value, ("groups", "context"), axis=0, tiled=False)
        return [gathered[number] for number in range(count)]
    held = {0: value}
    bits = [1 << b for b in range(contexts.bit_length() - 2, 0, -1)]
    bits += [contexts << b for b in range(groups.bit_length() - 1)]
    bits += [1] if contexts > 1 else []
    for bit in bits:
        axis, flip, size = ("context", bit, contexts)
        if bit >= contexts:
            axis, flip, size = ("groups", bit // contexts, groups)
        pairs = [(i, i ^ flip) for i in range(size)]
        for mask in sorted(held):
            held[mask | bit] = lax.ppermute(held[mask], axis, pairs)
    return [held[mask] for mask in range(count)]


def plane_owners(count, me):
    if count & (count - 1):
        return list(range(count))
    return [me ^ mask for mask in range(count)]


def line_gather(value, count):
    if count != 4:
        return [lax.all_gather(value, "tensor", axis=0, tiled=False)]
    up = lax.ppermute(value, "tensor", [(0, 1), (1, 2), (2, 3)])
    down = lax.ppermute(value, "tensor", [(1, 0), (2, 1), (3, 2)])
    far = lax.ppermute(value, "tensor", [(0, 2), (1, 3), (2, 0), (3, 1)])
    last = lax.ppermute(far, "tensor", [(1, 0), (2, 3)])
    return [value, up, down, far, last]


class Table:
    def __init__(self, contexts, count):
        self.contexts, self.count = contexts, count
        self.owner = 1
        self.place = 1 + contexts
        self.low = self.place + count
        self.high = self.low + 1
        self.share = self.low + 2
        self.rows = self.low + 3


def line_read(table, info, refs, d, cols=slice(None)):
    if len(refs) == 1:
        return refs[0][info[table.place + d], :, cols].astype(jnp.float32)
    if d == 0:
        return refs[0][:, cols].astype(jnp.float32)
    if d == 2:
        return refs[3][:, cols].astype(jnp.float32)
    near = refs[1 if d == 1 else 2][:, cols].astype(jnp.float32)
    other = refs[4][:, cols].astype(jnp.float32)
    at_end = info[table.low if d == 1 else table.high]
    return jnp.where(at_end == 1, other, near)


def line_spec(blocks, rows, index):
    if len(blocks) == 1:
        count, _, width = blocks[0].shape
        return [pl.BlockSpec((count, rows, width), lambda i, info: (0, index(i), 0))]
    width = blocks[0].shape[1]
    return [pl.BlockSpec((rows, width), lambda i, info: (index(i), 0)) for _ in blocks]


def call(kernel, name, info, args, in_specs, out_specs, out_shape, grid=(1,), aliases=None,
         scratch=(), flops=1, vmem=16):
    return pl.pallas_call(
        kernel,
        grid_spec=pltpu.PrefetchScalarGridSpec(
            num_scalar_prefetch=1,
            grid=grid,
            in_specs=in_specs,
            out_specs=out_specs,
            scratch_shapes=list(scratch),
        ),
        out_shape=out_shape,
        input_output_aliases=aliases or {},
        compiler_params=pltpu.CompilerParams(vmem_limit_bytes=vmem * MIB),
        cost_estimate=pl.CostEstimate(flops=flops, bytes_accessed=1, transcendentals=0),
        name=name,
    )(info, *args)


def whole(a):
    zeros = (0,) * len(a.shape)
    return pl.BlockSpec(tuple(a.shape), lambda i, info: zeros)


def prepare_kernel(info, q_ref, kv_ref, cache_ref, cos_ref, sin_ref, length_ref, *refs):
    q_out, kv_out = refs[1:3] if len(refs) > 2 else refs
    if len(refs) > 2:
        rows_early = refs[3].shape[0]
        refs[3][...] = refs[0][:rows_early]
        refs[4][...] = refs[0][rows_early:]
    cosine, sine = cos_ref[...], sin_ref[...]
    slots, rows = cache_ref.shape[0], q_ref.shape[0]
    span, tail = slice(slots, slots + rows), slice(slots + rows, slots + rows + TAIL)

    def turn(block):
        block = block.astype(jnp.float32)
        return (block * cosine + pltpu.roll(block, HD // 2, 1) * sine).astype(jnp.bfloat16)

    kv_out[:slots] = cache_ref[...]
    kv_out[span, :HD] = turn(kv_ref[:, :HD])
    kv_out[span, HD:] = kv_ref[:, HD:]
    length = length_ref[0]
    upper = lax.div(length, DIGIT)
    lower = length - upper * DIGIT
    kv_out[tail, :HD] = jnp.full((TAIL, HD), upper.astype(jnp.float32)).astype(jnp.bfloat16)
    kv_out[tail, HD:] = jnp.full((TAIL, HD), lower.astype(jnp.float32)).astype(jnp.bfloat16)
    for head in range(q_ref.shape[1] // HD):
        cols = slice(head * HD, (head + 1) * HD)
        q_out[:, cols] = turn(q_ref[:, cols])


def cut_kernel(table, slab, keep, info, w_ref, *outs):
    raw = slab - keep
    for d in range(table.count):
        target = lax.rem(info[table.place] + d, table.count)
        outs[d][...] = w_ref[:, pl.ds(pl.multiple_of(target * slab, slab), keep)]
    for j in range(table.count if raw else 0):
        outs[-1][:, j * raw : (j + 1) * raw] = w_ref[:, j * slab + keep : (j + 1) * slab]


def cut(table, info, out_weight, part, slab, keep):
    shapes = [jax.ShapeDtypeStruct((part, keep), out_weight.dtype)] * table.count
    if keep < slab:
        shapes.append(
            jax.ShapeDtypeStruct((part, table.count * (slab - keep)), out_weight.dtype)
        )
    return call(
        functools.partial(cut_kernel, table, slab, keep),
        "cut",
        info,
        [out_weight],
        [pl.BlockSpec((part, out_weight.shape[1]), lambda i, info: (info[table.share], 0))],
        [whole(shape) for shape in shapes],
        shapes,
    )


def prepare(info, queries, span_pairs, cache, cosine, sine, lengths, residual, raw, rows_early):
    rows, slab = residual.shape
    shapes = [
        jax.ShapeDtypeStruct(queries.shape, jnp.bfloat16),
        jax.ShapeDtypeStruct((cache.shape[0] + rows + TAIL, 2 * HD), jnp.bfloat16),
    ]
    args = [queries, span_pairs, cache, cosine, sine, lengths]
    in_specs = [whole(a) for a in args[:-1]] + [pl.BlockSpec(memory_space=pltpu.SMEM)]
    if raw:
        shapes.append(jax.ShapeDtypeStruct((rows_early, raw), residual.dtype))
        shapes.append(jax.ShapeDtypeStruct((rows - rows_early, raw), residual.dtype))
        args.append(residual)
        in_specs.append(pl.BlockSpec((rows, raw), lambda i, info: (0, slab // raw - 1)))
    return call(
        prepare_kernel,
        "prepare",
        info,
        args,
        in_specs,
        [whole(shape) for shape in shapes],
        shapes,
        vmem=58,
    )


def stack_kernel(count, info, *refs):
    for number, part in enumerate(refs[:count]):
        refs[-1][number] = part[...]


def stack(info, parts, after):
    shape = jax.ShapeDtypeStruct((len(parts), *parts[0].shape), parts[0].dtype)
    return call(
        functools.partial(stack_kernel, len(parts)),
        "stack",
        info,
        [*parts, *after],
        [whole(p) for p in parts] + [ANYWHERE] * len(after),
        whole(shape),
        shape,
    )


def gate_kernel(info, *refs):
    pass


def gate(info, value, after):
    return call(
        gate_kernel,
        "gate",
        info,
        [value, *after],
        [ANYWHERE] * (1 + len(after)),
        ANYWHERE,
        jax.ShapeDtypeStruct(value.shape, value.dtype),
        aliases={1: 0},
    )


def attend_kernel(table, slots, info, q_ref, *refs):
    count = table.contexts
    pieces, out_ref, s_ref = refs[:count], refs[-2], refs[-1]
    rows = q_ref.shape[0]
    heads = q_ref.shape[1] // HD
    chunk = pl.program_id(0)
    mine = info[0]
    q = jnp.concatenate([q_ref[:, h * HD : (h + 1) * HD] for h in range(heads)], axis=0)
    exponent = math.log2(math.e) / math.sqrt(HD)

    blocks = []
    peak = jnp.full((heads * rows, HD), NEG, jnp.float32)
    column = 0
    for kind in ("cache", "span"):
        for number, ref in enumerate(pieces):
            tail = ref.shape[0] - TAIL
            first, last = (0, slots) if kind == "cache" else (slots, tail)
            width = min(KEY_BLOCK, last - first)
            length = ref[tail : tail + 1, :HD].astype(jnp.float32) * DIGIT + ref[
                tail : tail + 1, HD:
            ].astype(jnp.float32)
            length = jnp.concatenate([length] * (width // HD), axis=1)
            for begin in range(first, last, width):
                scores = lax.dot_general(
                    q,
                    ref[begin : begin + width, :HD],
                    (((1,), (1,)), ((), ())),
                    preferred_element_type=jnp.float32,
                )
                if kind == "cache":
                    slot = lax.broadcasted_iota(jnp.int32, (1, width), 1) + begin
                    live = slot.astype(jnp.float32) < length
                    scores = scores + jnp.where(live, 0.0, NEG)
                elif number == 0:
                    key = lax.broadcasted_iota(jnp.int32, (rows, width), 1) + (begin - first)
                    row = lax.broadcasted_iota(jnp.int32, (rows, width), 0) + chunk * rows
                    bias = jnp.where(key <= row, 0.0, NEG)
                    scores = scores + jnp.concatenate([bias] * heads, axis=0)
                else:
                    scores = scores + jnp.where(info[table.owner + number] < mine, 0.0, NEG)
                s_ref[:, column : column + width] = scores
                for lane in range(0, width, HD):
                    peak = jnp.maximum(peak, scores[:, lane : lane + HD])
                blocks.append((ref, begin, column, width))
                column += width
    top = jnp.max(peak, axis=1, keepdims=True)
    total = jnp.zeros((heads * rows, HD), jnp.float32)
    mixed = jnp.zeros((heads * rows, HD), jnp.float32)
    for ref, begin, column, width in blocks:
        weights = jnp.exp2((s_ref[:, column : column + width] - top) * exponent)
        for lane in range(0, width, HD):
            total = total + weights[:, lane : lane + HD]
        mixed = mixed + jnp.dot(
            weights.astype(jnp.bfloat16),
            ref[begin : begin + width, HD:],
            preferred_element_type=jnp.float32,
        )
    result = (mixed / jnp.sum(total, axis=1, keepdims=True)).astype(jnp.bfloat16)
    for h in range(heads):
        out_ref[:, h * HD : (h + 1) * HD] = result[h * rows : (h + 1) * rows]


def attend(table, info, queries, pieces, slots, rows):
    all_rows, width = queries.shape
    heads = width // HD
    keys = sum(a.shape[0] - TAIL for a in pieces)
    chunk_spec = pl.BlockSpec((rows, width), lambda i, info: (i, 0))
    return call(
        functools.partial(attend_kernel, table, slots),
        "attend",
        info,
        [queries, *pieces],
        [chunk_spec] + [whole(a) for a in pieces],
        chunk_spec,
        jax.ShapeDtypeStruct((all_rows, width), jnp.bfloat16),
        grid=(all_rows // rows,),
        scratch=[pltpu.VMEM((heads * rows, keys), jnp.float32)],
        flops=ATTEND_FLOPS * all_rows * heads * keys * HD,
        vmem=28,
    )


def project_kernel(table, lines, shares, keep, info, *refs):
    count = table.count
    attention, pieces = refs[:lines], refs[lines : lines + shares]
    r_ref = refs[lines + shares]
    parts, h_ref, w_ref = refs[lines + shares + 1 : -2], refs[-2], refs[-1]
    part_rows = pieces[0].shape[1]

    @pl.when(pl.program_id(0) == 0)
    def _():
        for number, piece in enumerate(pieces):
            start = pl.multiple_of(info[table.rows + number] * part_rows, part_rows)
            for d in range(count):
                w_ref[d, pl.ds(start, part_rows)] = piece[d]

    total = r_ref[:, :keep].astype(jnp.float32)
    for d in range(count):
        block = line_read(table, info, attention, d).astype(jnp.bfloat16)
        total = total + jnp.dot(block, w_ref[d], preferred_element_type=jnp.float32)
    result = total.astype(jnp.bfloat16)
    h_ref[:, :keep] = result
    for number, part in enumerate(parts):

        @pl.when(pl.program_id(0) == number)
        def _():
            part[...] = result


def project(table, info, attention, pieces, residual, rows):
    all_rows, slab = residual.shape
    count, part_rows, keep = pieces[0].shape
    depth = len(pieces) * part_rows
    chunks = all_rows // rows
    part = jax.ShapeDtypeStruct((rows, keep), jnp.bfloat16)
    hidden = jax.ShapeDtypeStruct(residual.shape, jnp.bfloat16)
    row_spec = pl.BlockSpec((rows, slab), lambda i, info: (i, 0))
    return call(
        functools.partial(project_kernel, table, len(attention), len(pieces), keep),
        "project",
        info,
        [*attention, *pieces, residual],
        line_spec(attention, rows, lambda i: i) + [whole(p) for p in pieces] + [row_spec],
        [whole(part)] * chunks + [row_spec],
        [part] * chunks + [hidden],
        grid=(chunks,),
        scratch=[pltpu.VMEM((count, depth, keep), jnp.bfloat16)],
        vmem=28,
    )


def project_raw_kernel(table, lines, info, *refs):
    count = table.count
    attention, (early, late) = refs[:lines], refs[lines : lines + 2]
    w_ref = refs[lines + 2]
    raw_ref, h_ref = refs[-2:]
    raw = h_ref.shape[1]
    blocks = [
        line_read(table, info, attention, d).astype(jnp.bfloat16) for d in range(count)
    ]
    for slab in range(count):
        place = info[table.place + slab]
        start = pl.multiple_of(place * raw, raw)
        total = jnp.where(
            pl.program_id(0) == 0,
            early[place].astype(jnp.float32),
            late[place].astype(jnp.float32),
        )
        for d in range(count):
            weight = w_ref[info[table.place + d], :, :, pl.ds(start, raw)]
            weight = weight.reshape(blocks[d].shape[1], raw)
            total = total + jnp.dot(blocks[d], weight, preferred_element_type=jnp.float32)
        result = total.astype(jnp.bfloat16)
        raw_ref[:, slab * raw : (slab + 1) * raw] = result
        if slab == 0:
            h_ref[...] = result


def project_raw(table, info, attention, residuals, weights, hidden, raw, rows):
    all_rows, slab = hidden.shape
    count = table.count
    args = [*attention, *residuals, weights, hidden]
    out = jax.ShapeDtypeStruct((all_rows, count * raw), jnp.bfloat16)
    return call(
        functools.partial(project_raw_kernel, table, len(attention)),
        "project_raw",
        info,
        args,
        line_spec(attention, rows, lambda i: i)
        + [
            pl.BlockSpec((count, rows, raw), lambda i, info: (0, 0, 0)),
            pl.BlockSpec((count, rows, raw), lambda i, info: (0, jnp.maximum(i - 1, 0), 0)),
            whole(weights),
            ANYWHERE,
        ],
        [
            pl.BlockSpec((rows, count * raw), lambda i, info: (i, 0)),
            pl.BlockSpec((rows, raw), lambda i, info: (i, slab // raw - 1)),
        ],
        [out, jax.ShapeDtypeStruct(hidden.shape, jnp.bfloat16)],
        grid=(all_rows // rows,),
        aliases={len(args): 1},
        vmem=28,
    )


def norm_kernel(table, lines, keep, slab, info, g_ref, *refs):
    count = table.count
    blocks, out_ref = refs[:lines], refs[-1]
    raw = slab - keep
    values = []
    squares = jnp.zeros((out_ref.shape[0], 1), jnp.float32)

    def read(d):
        found = [(0, keep, line_read(table, info, blocks, d))]
        if raw:
            cols = slice(d * raw, (d + 1) * raw)
            found.append((keep, raw, refs[lines][:, cols].astype(jnp.float32)))
        return found

    for d in range(count):
        for _, _, value in read(d):
            squares = squares + jnp.sum(value * value, axis=1, keepdims=True)
    inverse = lax.rsqrt(squares / (count * slab) + EPS_NORM)
    for d in range(count):
        for offset, width, value in read(d):
            start = pl.multiple_of(info[table.place + d] * slab + offset, HD)
            cols = pl.ds(start, width)
            out_ref[:, cols] = (value * inverse * g_ref[:, cols]).astype(jnp.bfloat16)


def norm_into(table, info, buffer, blocks, raw_hidden, gain, chunk, rows, keep, slab, total_rows):
    width = table.count * slab
    step = min(rows, 32)
    steps = rows // step
    args = [gain.reshape(1, width), *blocks]
    in_specs = [pl.BlockSpec((1, width), lambda i, info: (0, 0))]
    in_specs += line_spec(blocks, step, lambda i: i)
    if raw_hidden is not None:
        args.append(raw_hidden)
        in_specs.append(
            pl.BlockSpec((step, raw_hidden.shape[1]), lambda i, info: (chunk * steps + i, 0))
        )
    aliases = {}
    if buffer is not None:
        args.append(buffer)
        in_specs.append(ANYWHERE)
        aliases = {len(args): 0}
    return call(
        functools.partial(norm_kernel, table, len(blocks), keep, slab),
        "norm",
        info,
        args,
        in_specs,
        pl.BlockSpec((step, width), lambda i, info: (chunk * steps + i, 0)),
        jax.ShapeDtypeStruct((total_rows, width), jnp.bfloat16),
        grid=(steps,),
        aliases=aliases,
    )


def per_device(queries, span_kv, cache, lengths, offset, out_weight, residual, gain):
    rows = queries.shape[0]
    heads = queries.shape[1] // HD
    depth = out_weight.shape[0]
    slab = residual.shape[1]
    contexts = lax.axis_size("context")
    count = lax.axis_size("tensor")
    context_index = lax.axis_index("context")
    tensor_index = lax.axis_index("tensor")
    kv_index = tensor_index * heads // GROUP
    groups = lax.axis_size("groups")
    shares = groups * contexts
    share = lax.axis_index("groups") * contexts + context_index
    raw = slab // 4 if slab % 512 == 0 and rows > CHUNK else 0
    keep = slab - raw
    chunk = min(CHUNK, rows)
    chunks = rows // chunk

    table = Table(contexts, count)
    steering = [context_index, *owners_of(contexts, context_index)]
    steering += [lax.rem(tensor_index + (count - d), count) for d in range(count)]
    steering += [tensor_index == 0, tensor_index == count - 1, share]
    steering += plane_owners(shares, share)
    info = jnp.stack([jnp.asarray(v).astype(jnp.int32) for v in steering])

    cache_local = lax.dynamic_index_in_dim(cache, kv_index, 0, keepdims=False)
    span_local = lax.dynamic_index_in_dim(span_kv, kv_index, 1, keepdims=False)
    positions = offset[0] + context_index * rows + jnp.arange(rows, dtype=jnp.int32)
    both = jnp.concatenate([frequencies(HD)] * 2)
    angles = positions.astype(jnp.float32)[:, None] * both[None, :]
    sign = jnp.where(jnp.arange(HD) < HD // 2, -1.0, 1.0)
    q_turned, payload, *residual_raw = prepare(
        info, queries, span_local, cache_local, jnp.cos(angles),
        jnp.sin(angles) * sign[None, :], lengths, residual, raw, chunk,
    )
    cuts = cut(table, info, out_weight, depth // shares, slab, keep)
    parts = [cuts[0]]
    for shift in range(1, count):
        pairs = [(i, (i + shift) % count) for i in range(count)]
        parts.append(lax.ppermute(cuts[shift], "tensor", pairs))
    own_weights = stack(info, parts, [])
    early, late = [], []
    if raw:
        early = [lax.all_gather(residual_raw[0], "tensor", axis=0, tiled=False)]
        late = [lax.all_gather(residual_raw[1], "tensor", axis=0, tiled=False)]
    pieces = pieces_of(
        payload, "context", contexts, lambda block: gate(info, block, [own_weights, *early])
    )

    mixed = attend(table, info, q_turned, pieces, cache_local.shape[0], chunk)
    weight_pieces = plane_gather(own_weights, groups, contexts)
    attention = line_gather(mixed, count)

    *hidden_parts, hidden = project(table, info, attention, weight_pieces, residual, chunk)
    lines = []
    for number in range(chunks):
        value = hidden_parts[number]
        if number > 1:
            value = gate(info, value, lines[number - 2][1:])
        lines.append(line_gather(value, count))
    raw_hidden = None
    if raw:
        raw_weights = gate(info, cuts[-1], [*late, hidden_parts[0]])
        raw_weights = lax.all_gather(
            raw_weights, ("tensor", "groups", "context"), axis=0, tiled=False
        )
        raw_weights = raw_weights.reshape(count, shares, *cuts[-1].shape)
        raw_hidden, hidden = project_raw(
            table, info, attention, [*early, *late], raw_weights, hidden, raw, chunk
        )
    normed = None
    for number in range(chunks):
        normed = norm_into(
            table, info, normed, lines[number], raw_hidden, gain, number, chunk, keep, slab, rows
        )
    return (hidden, normed)


def solution(mesh):
    in_specs = (
        P(("groups", "context"), "tensor"),
        P(("groups", "context"), None, None),
        P("groups", "context", None),
        P(("groups", "context")),
        P("groups"),
        P("tensor", None),
        P(("groups", "context"), "tensor"),
        P(),
    )
    out_specs = (P(("groups", "context"), "tensor"), P(("groups", "context"), None))
    return jax.shard_map(
        per_device, mesh=mesh, in_specs=in_specs, out_specs=out_specs, check_vma=False
    )
```

```python
import functools
import math

import jax
import jax.numpy as jnp
from jax import lax
from jax.experimental import pallas as pl
from jax.experimental.pallas import tpu as pltpu
from jax.sharding import PartitionSpec as P

GROUP = 8
HD = 128
NEG = -1e30
EPS_NORM = 1e-05
MIB = 1024 * 1024
CHUNK = 128
KEY_BLOCK = 512
ATTEND_FLOPS = 16
TAIL = 16
DIGIT = 32
ANYWHERE = pl.BlockSpec(memory_space=pl.ANY)


def frequencies(head_width):
    counter = jnp.arange(head_width // 2, dtype=jnp.float32)
    base_freq = jnp.exp(-(2.0 * counter / head_width) * math.log(500000.0))
    wavelength = 2.0 * math.pi / base_freq
    smoothing = (8192.0 / wavelength - 1.0) / 3.0
    blended = (1.0 - smoothing) * base_freq / 8.0 + smoothing * base_freq
    return jnp.where(
        wavelength < 2048.0, base_freq, jnp.where(wavelength > 8192.0, base_freq / 8.0, blended)
    )


def pieces_of(value, axis, count, between=lambda block: block):
    if count & (count - 1) == 0:
        held = {0: value}
        bit = count // 2
        while bit:
            pairs = [(i, i ^ bit) for i in range(count)]
            for mask in sorted(held):
                held[mask | bit] = lax.ppermute(held[mask], axis, pairs)
            if bit == count // 2:
                held[bit] = between(held[bit])
            bit //= 2
        return [held[mask] for mask in range(count)]
    blocks = [value]
    for shift in range(1, count):
        pairs = [(i, (i + shift) % count) for i in range(count)]
        blocks.append(lax.ppermute(value, axis, pairs))
    return blocks


def owners_of(count, me):
    if count & (count - 1) == 0:
        return [me ^ mask for mask in range(count)]
    return [(me + count - shift) % count for shift in range(count)]


def plane_gather(value, groups, contexts, between=lambda block: block):
    count = groups * contexts
    if count & (count - 1):
        gathered = lax.all_gather(value, ("groups", "context"), axis=0, tiled=False)
        return [gathered[number] for number in range(count)]
    held = {0: value}
    bits = [1 << b for b in range(contexts.bit_length() - 2, 0, -1)]
    bits += [contexts << b for b in range(groups.bit_length() - 1)]
    bits += [1] if contexts > 1 else []
    for bit in bits:
        axis, flip, size = ("context", bit, contexts)
        if bit >= contexts:
            axis, flip, size = ("groups", bit // contexts, groups)
        pairs = [(i, i ^ flip) for i in range(size)]
        for mask in sorted(held):
            held[mask | bit] = lax.ppermute(held[mask], axis, pairs)
        if bit == bits[0]:
            held[bit] = between(held[bit])
    return [held[mask] for mask in range(count)]


def plane_owners(count, me):
    if count & (count - 1):
        return list(range(count))
    return [me ^ mask for mask in range(count)]


def line_gather(value, count):
    if count != 4:
        return [lax.all_gather(value, "tensor", axis=0, tiled=False)]
    up = lax.ppermute(value, "tensor", [(0, 1), (1, 2), (2, 3)])
    down = lax.ppermute(value, "tensor", [(1, 0), (2, 1), (3, 2)])
    far = lax.ppermute(value, "tensor", [(0, 2), (1, 3), (2, 0), (3, 1)])
    last = lax.ppermute(far, "tensor", [(1, 0), (2, 3)])
    return [value, up, down, far, last]


class Table:
    def __init__(self, contexts, count):
        self.contexts, self.count = contexts, count
        self.owner = 1
        self.place = 1 + contexts
        self.low = self.place + count
        self.high = self.low + 1
        self.share = self.low + 2
        self.rows = self.low + 3


def line_read(table, info, refs, d, cols=slice(None)):
    if len(refs) == 1:
        return refs[0][info[table.place + d], :, cols].astype(jnp.float32)
    if d == 0:
        return refs[0][:, cols].astype(jnp.float32)
    if d == 2:
        return refs[3][:, cols].astype(jnp.float32)
    near = refs[1 if d == 1 else 2][:, cols].astype(jnp.float32)
    other = refs[4][:, cols].astype(jnp.float32)
    at_end = info[table.low if d == 1 else table.high]
    return jnp.where(at_end == 1, other, near)


def line_spec(blocks, rows, index):
    if len(blocks) == 1:
        count, _, width = blocks[0].shape
        return [pl.BlockSpec((count, rows, width), lambda i, info: (0, index(i), 0))]
    width = blocks[0].shape[1]
    return [pl.BlockSpec((rows, width), lambda i, info: (index(i), 0)) for _ in blocks]


def call(kernel, name, info, args, in_specs, out_specs, out_shape, grid=(1,), aliases=None,
         scratch=(), flops=1, vmem=16):
    return pl.pallas_call(
        kernel,
        grid_spec=pltpu.PrefetchScalarGridSpec(
            num_scalar_prefetch=1,
            grid=grid,
            in_specs=in_specs,
            out_specs=out_specs,
            scratch_shapes=list(scratch),
        ),
        out_shape=out_shape,
        input_output_aliases=aliases or {},
        compiler_params=pltpu.CompilerParams(vmem_limit_bytes=vmem * MIB or None),
        cost_estimate=pl.CostEstimate(flops=flops, bytes_accessed=1, transcendentals=0),
        name=name,
    )(info, *args)


def whole(a):
    zeros = (0,) * len(a.shape)
    return pl.BlockSpec(tuple(a.shape), lambda i, info: zeros)


def prepare_kernel(info, q_ref, kv_ref, cache_ref, cos_ref, sin_ref, length_ref, *refs):
    q_out, kv_out = refs[-2:]
    cosine, sine = cos_ref[...], sin_ref[...]
    slots, rows = cache_ref.shape[0], q_ref.shape[0]
    span, tail = slice(slots, slots + rows), slice(slots + rows, slots + rows + TAIL)

    def turn(block):
        block = block.astype(jnp.float32)
        return (block * cosine + pltpu.roll(block, HD // 2, 1) * sine).astype(jnp.bfloat16)

    kv_out[:slots] = cache_ref[...]
    kv_out[span, :HD] = turn(kv_ref[:, :HD])
    kv_out[span, HD:] = kv_ref[:, HD:]
    length = length_ref[0]
    upper = lax.div(length, DIGIT)
    lower = length - upper * DIGIT
    kv_out[tail, :HD] = jnp.full((TAIL, HD), upper.astype(jnp.float32)).astype(jnp.bfloat16)
    kv_out[tail, HD:] = jnp.full((TAIL, HD), lower.astype(jnp.float32)).astype(jnp.bfloat16)
    for head in range(q_ref.shape[1] // HD):
        cols = slice(head * HD, (head + 1) * HD)
        q_out[:, cols] = turn(q_ref[:, cols])


def cut_kernel(table, slab, keep, info, w_ref, r_ref, *refs):
    count, raw = table.count, slab - keep
    outs, rows_ref, sems = refs[:count], refs[-2], refs[-1]
    part = rows_ref.shape[0]
    start = pl.multiple_of(info[table.share] * part, part)
    copies = [pltpu.make_async_copy(w_ref.at[pl.ds(start, part)], rows_ref, sems.at[0])]
    if raw:
        source = r_ref.at[:, pl.ds(keep, raw)]
        copies.append(pltpu.make_async_copy(source, refs[count], sems.at[1]))
    for copy in copies:
        copy.start()
    copies[0].wait()
    for d, out in enumerate(outs):
        target = lax.rem(info[table.place] + d, count)
        out[:, :keep] = rows_ref[:, pl.ds(pl.multiple_of(target * slab, slab), keep)]
        for j in range(count if raw else 0):
            out[:, keep + j * raw : keep + (j + 1) * raw] = rows_ref[
                :, j * slab + keep : (j + 1) * slab
            ]
    if raw:
        copies[1].wait()


def cut(table, info, out_weight, residual, part, keep):
    rows, slab = residual.shape
    raw = slab - keep
    width = keep + table.count * raw
    shapes = [jax.ShapeDtypeStruct((part, width), out_weight.dtype)] * table.count
    if raw:
        shapes.append(jax.ShapeDtypeStruct((rows, raw), residual.dtype))
    return call(
        functools.partial(cut_kernel, table, slab, keep),
        "cut",
        info,
        [out_weight, residual],
        [pl.BlockSpec(memory_space=pltpu.HBM)] * 2,
        [whole(shape) for shape in shapes],
        shapes,
        scratch=[
            pltpu.VMEM((part, out_weight.shape[1]), out_weight.dtype),
            pltpu.SemaphoreType.DMA((2,)),
        ],
        vmem=0,
    )


def prepare(info, queries, span_pairs, cache, cosine, sine, lengths, after):
    rows = queries.shape[0]
    shapes = [
        jax.ShapeDtypeStruct(queries.shape, jnp.bfloat16),
        jax.ShapeDtypeStruct((cache.shape[0] + rows + TAIL, 2 * HD), jnp.bfloat16),
    ]
    args = [queries, span_pairs, cache, cosine, sine, lengths]
    return call(
        prepare_kernel,
        "prepare",
        info,
        [*args, *after],
        [whole(a) for a in args[:-1]]
        + [pl.BlockSpec(memory_space=pltpu.SMEM)]
        + [ANYWHERE] * len(after),
        [whole(shape) for shape in shapes],
        shapes,
        vmem=32,
    )


def stack_kernel(count, begin, info, *refs):
    width = refs[-1].shape[2]
    for number, part in enumerate(refs[:count]):
        refs[-1][number] = part[:, begin : begin + width]


def stack(info, parts, begin, width, after=()):
    shape = jax.ShapeDtypeStruct((len(parts), parts[0].shape[0], width), parts[0].dtype)
    return call(
        functools.partial(stack_kernel, len(parts), begin),
        "stack",
        info,
        [*parts, *after],
        [whole(p) for p in parts] + [ANYWHERE] * len(after),
        whole(shape),
        shape,
    )


def gate_kernel(info, *refs):
    pass


def gate(info, value, after):
    return call(
        gate_kernel,
        "gate",
        info,
        [value, *after],
        [ANYWHERE] * (1 + len(after)),
        ANYWHERE,
        jax.ShapeDtypeStruct(value.shape, value.dtype),
        aliases={1: 0},
    )


def attend_kernel(table, slots, info, q_ref, *refs):
    count = table.contexts
    pieces, out_ref, s_ref = refs[:count], refs[-2], refs[-1]
    rows = q_ref.shape[0]
    heads = q_ref.shape[1] // HD
    chunk = pl.program_id(0)
    mine = info[0]
    q = jnp.concatenate([q_ref[:, h * HD : (h + 1) * HD] for h in range(heads)], axis=0)
    exponent = math.log2(math.e) / math.sqrt(HD)

    blocks = []
    peak = jnp.full((heads * rows, HD), NEG, jnp.float32)
    column = 0
    for kind in ("cache", "span"):
        for number, ref in enumerate(pieces):
            tail = ref.shape[0] - TAIL
            first, last = (0, slots) if kind == "cache" else (slots, tail)
            width = min(KEY_BLOCK, last - first)
            length = ref[tail : tail + 1, :HD].astype(jnp.float32) * DIGIT + ref[
                tail : tail + 1, HD:
            ].astype(jnp.float32)
            length = jnp.concatenate([length] * (width // HD), axis=1)
            for begin in range(first, last, width):
                scores = lax.dot_general(
                    q,
                    ref[begin : begin + width, :HD],
                    (((1,), (1,)), ((), ())),
                    preferred_element_type=jnp.float32,
                )
                if kind == "cache":
                    slot = lax.broadcasted_iota(jnp.int32, (1, width), 1) + begin
                    live = slot.astype(jnp.float32) < length
                    scores = scores + jnp.where(live, 0.0, NEG)
                elif number == 0:
                    key = lax.broadcasted_iota(jnp.int32, (rows, width), 1) + (begin - first)
                    row = lax.broadcasted_iota(jnp.int32, (rows, width), 0) + chunk * rows
                    bias = jnp.where(key <= row, 0.0, NEG)
                    scores = scores + jnp.concatenate([bias] * heads, axis=0)
                else:
                    scores = scores + jnp.where(info[table.owner + number] < mine, 0.0, NEG)
                s_ref[:, column : column + width] = scores
                for lane in range(0, width, HD):
                    peak = jnp.maximum(peak, scores[:, lane : lane + HD])
                blocks.append((ref, begin, column, width))
                column += width
    top = jnp.max(peak, axis=1, keepdims=True)
    total = jnp.zeros((heads * rows, HD), jnp.float32)
    mixed = jnp.zeros((heads * rows, HD), jnp.float32)
    for ref, begin, column, width in blocks:
        weights = jnp.exp2((s_ref[:, column : column + width] - top) * exponent)
        for lane in range(0, width, HD):
            total = total + weights[:, lane : lane + HD]
        mixed = mixed + jnp.dot(
            weights.astype(jnp.bfloat16),
            ref[begin : begin + width, HD:],
            preferred_element_type=jnp.float32,
        )
    result = (mixed / jnp.sum(total, axis=1, keepdims=True)).astype(jnp.bfloat16)
    for h in range(heads):
        out_ref[:, h * HD : (h + 1) * HD] = result[h * rows : (h + 1) * rows]


def attend(table, info, queries, pieces, slots, rows):
    all_rows, width = queries.shape
    heads = width // HD
    keys = sum(a.shape[0] - TAIL for a in pieces)
    chunk_spec = pl.BlockSpec((rows, width), lambda i, info: (i, 0))
    return call(
        functools.partial(attend_kernel, table, slots),
        "attend",
        info,
        [queries, *pieces],
        [chunk_spec] + [whole(a) for a in pieces],
        chunk_spec,
        jax.ShapeDtypeStruct((all_rows, width), jnp.bfloat16),
        grid=(all_rows // rows,),
        scratch=[pltpu.VMEM((heads * rows, keys), jnp.float32)],
        flops=ATTEND_FLOPS * all_rows * heads * keys * HD,
        vmem=28,
    )


def project_kernel(table, lines, shares, keep, chunks, info, *refs):
    count = table.count
    attention, pieces = refs[:lines], refs[lines : lines + shares]
    r_ref = refs[lines + shares]
    parts, h_ref, w_ref = refs[-2 - chunks : -2], refs[-2], refs[-1]
    part_rows = pieces[0].shape[1]

    @pl.when(pl.program_id(0) == 0)
    def _():
        for number, piece in enumerate(pieces):
            start = pl.multiple_of(info[table.rows + number] * part_rows, part_rows)
            for d in range(count):
                w_ref[d, pl.ds(start, part_rows)] = piece[d]

    total = r_ref[:, :keep].astype(jnp.float32)
    for d in range(count):
        block = line_read(table, info, attention, d).astype(jnp.bfloat16)
        total = total + jnp.dot(block, w_ref[d], preferred_element_type=jnp.float32)
    result = total.astype(jnp.bfloat16)
    h_ref[:, :keep] = result
    for number, part in enumerate(parts):

        @pl.when(pl.program_id(0) == number)
        def _():
            part[...] = result


def project(table, info, attention, pieces, residual, rows, after):
    all_rows, slab = residual.shape
    count, part_rows, keep = pieces[0].shape
    depth = len(pieces) * part_rows
    chunks = all_rows // rows
    part = jax.ShapeDtypeStruct((rows, keep), jnp.bfloat16)
    hidden = jax.ShapeDtypeStruct(residual.shape, jnp.bfloat16)
    row_spec = pl.BlockSpec((rows, slab), lambda i, info: (i, 0))
    return call(
        functools.partial(project_kernel, table, len(attention), len(pieces), keep, chunks),
        "project",
        info,
        [*attention, *pieces, residual, *after],
        line_spec(attention, rows, lambda i: i)
        + [whole(p) for p in pieces]
        + [row_spec]
        + [ANYWHERE] * len(after),
        [whole(part)] * chunks + [row_spec],
        [part] * chunks + [hidden],
        grid=(chunks,),
        scratch=[pltpu.VMEM((count, depth, keep), jnp.bfloat16)],
        vmem=28,
    )


def project_raw_kernel(table, lines, info, *refs):
    count = table.count
    attention, r_ref, w_ref = refs[:lines], refs[lines], refs[lines + 1]
    raw_ref, h_ref = refs[-2:]
    raw = h_ref.shape[1]
    blocks = [
        line_read(table, info, attention, d).astype(jnp.bfloat16) for d in range(count)
    ]
    for slab in range(count):
        place = info[table.place + slab]
        start = pl.multiple_of(place * raw, raw)
        total = r_ref[place].astype(jnp.float32)
        for d in range(count):
            weight = w_ref[:, d, :, pl.ds(start, raw)]
            weight = weight.reshape(blocks[d].shape[1], raw)
            total = total + jnp.dot(blocks[d], weight, preferred_element_type=jnp.float32)
        result = total.astype(jnp.bfloat16)
        raw_ref[:, slab * raw : (slab + 1) * raw] = result
        if slab == 0:
            h_ref[...] = result


def project_raw(table, info, attention, residuals, weights, hidden, raw, rows):
    all_rows, slab = hidden.shape
    count = table.count
    args = [*attention, *residuals, weights, hidden]
    out = jax.ShapeDtypeStruct((all_rows, count * raw), jnp.bfloat16)
    return call(
        functools.partial(project_raw_kernel, table, len(attention)),
        "project_raw",
        info,
        args,
        line_spec(attention, rows, lambda i: i)
        + [
            pl.BlockSpec((count, rows, raw), lambda i, info: (0, i, 0)),
            whole(weights),
            ANYWHERE,
        ],
        [
            pl.BlockSpec((rows, count * raw), lambda i, info: (i, 0)),
            pl.BlockSpec((rows, raw), lambda i, info: (i, slab // raw - 1)),
        ],
        [out, jax.ShapeDtypeStruct(hidden.shape, jnp.bfloat16)],
        grid=(all_rows // rows,),
        aliases={len(args): 1},
        vmem=28,
    )


def norm_kernel(table, lines, keep, slab, info, g_ref, *refs):
    count = table.count
    blocks, out_ref = refs[:lines], refs[-1]
    raw = slab - keep
    values = []
    squares = jnp.zeros((out_ref.shape[0], 1), jnp.float32)

    def read(d):
        found = [(0, keep, line_read(table, info, blocks, d))]
        if raw:
            cols = slice(d * raw, (d + 1) * raw)
            found.append((keep, raw, refs[lines][:, cols].astype(jnp.float32)))
        return found

    for d in range(count):
        for _, _, value in read(d):
            squares = squares + jnp.sum(value * value, axis=1, keepdims=True)
    inverse = lax.rsqrt(squares / (count * slab) + EPS_NORM)
    for d in range(count):
        for offset, width, value in read(d):
            start = pl.multiple_of(info[table.place + d] * slab + offset, HD)
            cols = pl.ds(start, width)
            out_ref[:, cols] = (value * inverse * g_ref[:, cols]).astype(jnp.bfloat16)


def norm_into(table, info, buffer, blocks, raw_hidden, gain, chunk, rows, keep, slab, total_rows):
    width = table.count * slab
    step = min(rows, 32)
    steps = rows // step
    args = [gain.reshape(1, width), *blocks]
    in_specs = [pl.BlockSpec((1, width), lambda i, info: (0, 0))]
    in_specs += line_spec(blocks, step, lambda i: i)
    if raw_hidden is not None:
        args.append(raw_hidden)
        in_specs.append(
            pl.BlockSpec((step, raw_hidden.shape[1]), lambda i, info: (chunk * steps + i, 0))
        )
    aliases = {}
    if buffer is not None:
        args.append(buffer)
        in_specs.append(ANYWHERE)
        aliases = {len(args): 0}
    return call(
        functools.partial(norm_kernel, table, len(blocks), keep, slab),
        "norm",
        info,
        args,
        in_specs,
        pl.BlockSpec((step, width), lambda i, info: (chunk * steps + i, 0)),
        jax.ShapeDtypeStruct((total_rows, width), jnp.bfloat16),
        grid=(steps,),
        aliases=aliases,
    )


def per_device(queries, span_kv, cache, lengths, offset, out_weight, residual, gain):
    rows = queries.shape[0]
    heads = queries.shape[1] // HD
    depth = out_weight.shape[0]
    slab = residual.shape[1]
    contexts = lax.axis_size("context")
    count = lax.axis_size("tensor")
    context_index = lax.axis_index("context")
    tensor_index = lax.axis_index("tensor")
    kv_index = tensor_index * heads // GROUP
    groups = lax.axis_size("groups")
    shares = groups * contexts
    share = lax.axis_index("groups") * contexts + context_index
    raw = slab // 4 if slab % 512 == 0 and rows > CHUNK else 0
    keep = slab - raw
    chunk = min(CHUNK, rows)
    chunks = rows // chunk

    table = Table(contexts, count)
    steering = [context_index, *owners_of(contexts, context_index)]
    steering += [lax.rem(tensor_index + (count - d), count) for d in range(count)]
    steering += [tensor_index == 0, tensor_index == count - 1, share]
    steering += plane_owners(shares, share)
    info = jnp.stack([jnp.asarray(v).astype(jnp.int32) for v in steering])

    cache_local = lax.dynamic_index_in_dim(cache, kv_index, 0, keepdims=False)
    span_local = lax.dynamic_index_in_dim(span_kv, kv_index, 1, keepdims=False)
    positions = offset[0] + context_index * rows + jnp.arange(rows, dtype=jnp.int32)
    both = jnp.concatenate([frequencies(HD)] * 2)
    angles = positions.astype(jnp.float32)[:, None] * both[None, :]
    sign = jnp.where(jnp.arange(HD) < HD // 2, -1.0, 1.0)
    cuts = cut(table, info, out_weight, residual, depth // shares, keep)
    parts = [cuts[0]]
    for shift in range(1, count):
        pairs = [(i, (i + shift) % count) for i in range(count)]
        parts.append(lax.ppermute(cuts[shift], "tensor", pairs))
    residuals = []
    if raw:
        residuals = [lax.all_gather(cuts[count], "tensor", axis=0, tiled=False)]
    own_weights = stack(info, parts, 0, keep)

    q_turned, payload = prepare(
        info, queries, span_local, cache_local, jnp.cos(angles),
        jnp.sin(angles) * sign[None, :], lengths, cuts[:1],
    )
    pieces = pieces_of(
        payload, "context", contexts, lambda block: gate(info, block, [own_weights])
    )
    mixed = attend(table, info, q_turned, pieces, cache_local.shape[0], chunk)
    weight_pieces = plane_gather(own_weights, groups, contexts)
    attention = line_gather(mixed, count)

    *hidden_parts, hidden = project(
        table, info, attention, weight_pieces, residual, chunk, residuals
    )
    raw_hidden = None
    if raw:
        raw_weights = stack(info, parts, keep, count * raw, [mixed])
        raw_weights = lax.all_gather(raw_weights, ("groups", "context"), axis=0, tiled=False)
        raw_hidden, hidden = project_raw(
            table, info, attention, residuals, raw_weights, hidden, raw, chunk
        )
    lines = []
    for number in range(chunks):
        value = hidden_parts[number]
        if number > 1:
            made = [raw_hidden] if raw and number == chunks - 1 else []
            value = gate(info, value, [*lines[number - 2][1:], *made])
        lines.append(line_gather(value, count))
    normed = None
    for number in range(chunks):
        normed = norm_into(
            table, info, normed, lines[number], raw_hidden, gain, number, chunk, keep, slab, rows
        )
    return (hidden, normed)


def solution(mesh):
    in_specs = (
        P(("groups", "context"), "tensor"),
        P(("groups", "context"), None, None),
        P("groups", "context", None),
        P(("groups", "context")),
        P("groups"),
        P("tensor", None),
        P(("groups", "context"), "tensor"),
        P(),
    )
    out_specs = (P(("groups", "context"), "tensor"), P(("groups", "context"), None))
    return jax.shard_map(
        per_device, mesh=mesh, in_specs=in_specs, out_specs=out_specs, check_vma=False
    )
```

```python
import functools
import math

import jax
import jax.numpy as jnp
from jax import lax
from jax.experimental import pallas as pl
from jax.experimental.pallas import tpu as pltpu
from jax.sharding import PartitionSpec as P

GROUP = 8
HD = 128
NEG = -1e30
EPS_NORM = 1e-05
MIB = 1024 * 1024
CHUNK = 128
KEY_BLOCK = 512
ATTEND_FLOPS = 16
TAIL = 16
DIGIT = 32
ANYWHERE = pl.BlockSpec(memory_space=pl.ANY)


def frequencies(head_width):
    counter = jnp.arange(head_width // 2, dtype=jnp.float32)
    base_freq = jnp.exp(-(2.0 * counter / head_width) * math.log(500000.0))
    wavelength = 2.0 * math.pi / base_freq
    smoothing = (8192.0 / wavelength - 1.0) / 3.0
    blended = (1.0 - smoothing) * base_freq / 8.0 + smoothing * base_freq
    return jnp.where(
        wavelength < 2048.0, base_freq, jnp.where(wavelength > 8192.0, base_freq / 8.0, blended)
    )


def pieces_of(value, axis, count, between=lambda block: block):
    if count & (count - 1) == 0:
        held = {0: value}
        bit = count // 2
        while bit:
            pairs = [(i, i ^ bit) for i in range(count)]
            for mask in sorted(held):
                held[mask | bit] = lax.ppermute(held[mask], axis, pairs)
            if bit == count // 2:
                held[bit] = between(held[bit])
            bit //= 2
        return [held[mask] for mask in range(count)]
    blocks = [value]
    for shift in range(1, count):
        pairs = [(i, (i + shift) % count) for i in range(count)]
        blocks.append(lax.ppermute(value, axis, pairs))
    blocks[-1] = between(blocks[-1])
    return blocks


def owners_of(count, me):
    if count & (count - 1) == 0:
        return [me ^ mask for mask in range(count)]
    return [(me + count - shift) % count for shift in range(count)]


def line_gather(value, count):
    if count != 4:
        return [lax.all_gather(value, "tensor", axis=0, tiled=False)]
    up = lax.ppermute(value, "tensor", [(0, 1), (1, 2), (2, 3)])
    down = lax.ppermute(value, "tensor", [(1, 0), (2, 1), (3, 2)])
    far = lax.ppermute(value, "tensor", [(0, 2), (1, 3), (2, 0), (3, 1)])
    last = lax.ppermute(far, "tensor", [(1, 0), (2, 3)])
    return [value, up, down, far, last]


class Table:
    def __init__(self, contexts, count):
        self.contexts, self.count = contexts, count
        self.owner = 1
        self.place = 1 + contexts
        self.low = self.place + count
        self.high = self.low + 1
        self.share = self.low + 2


def line_read(table, info, refs, d, cols=slice(None)):
    if len(refs) == 1:
        return refs[0][info[table.place + d], :, cols].astype(jnp.float32)
    if d == 0:
        return refs[0][:, cols].astype(jnp.float32)
    if d == 2:
        return refs[3][:, cols].astype(jnp.float32)
    near = refs[1 if d == 1 else 2][:, cols].astype(jnp.float32)
    other = refs[4][:, cols].astype(jnp.float32)
    at_end = info[table.low if d == 1 else table.high]
    return jnp.where(at_end == 1, other, near)


def line_spec(blocks, rows, index):
    if len(blocks) == 1:
        count, _, width = blocks[0].shape
        return [pl.BlockSpec((count, rows, width), lambda i, info: (0, index(i), 0))]
    width = blocks[0].shape[1]
    return [pl.BlockSpec((rows, width), lambda i, info: (index(i), 0)) for _ in blocks]


def call(kernel, name, info, args, in_specs, out_specs, out_shape, grid=(1,), aliases=None,
         scratch=(), flops=1, vmem=16):
    return pl.pallas_call(
        kernel,
        grid_spec=pltpu.PrefetchScalarGridSpec(
            num_scalar_prefetch=1,
            grid=grid,
            in_specs=in_specs,
            out_specs=out_specs,
            scratch_shapes=list(scratch),
        ),
        out_shape=out_shape,
        input_output_aliases=aliases or {},
        compiler_params=pltpu.CompilerParams(vmem_limit_bytes=vmem * MIB or None),
        cost_estimate=pl.CostEstimate(flops=flops, bytes_accessed=1, transcendentals=0),
        name=name,
    )(info, *args)


def whole(a):
    zeros = (0,) * len(a.shape)
    return pl.BlockSpec(tuple(a.shape), lambda i, info: zeros)


def prepare_kernel(info, q_ref, kv_ref, cache_ref, cos_ref, sin_ref, length_ref, *refs):
    q_out, kv_out = refs[-2:]
    cosine, sine = cos_ref[...], sin_ref[...]
    slots, rows = cache_ref.shape[0], q_ref.shape[0]
    span, tail = slice(slots, slots + rows), slice(slots + rows, slots + rows + TAIL)

    def turn(block):
        block = block.astype(jnp.float32)
        return (block * cosine + pltpu.roll(block, HD // 2, 1) * sine).astype(jnp.bfloat16)

    kv_out[:slots] = cache_ref[...]
    kv_out[span, :HD] = turn(kv_ref[:, :HD])
    kv_out[span, HD:] = kv_ref[:, HD:]
    length = length_ref[0]
    upper = lax.div(length, DIGIT)
    lower = length - upper * DIGIT
    kv_out[tail, :HD] = jnp.full((TAIL, HD), upper.astype(jnp.float32)).astype(jnp.bfloat16)
    kv_out[tail, HD:] = jnp.full((TAIL, HD), lower.astype(jnp.float32)).astype(jnp.bfloat16)
    for head in range(q_ref.shape[1] // HD):
        cols = slice(head * HD, (head + 1) * HD)
        q_out[:, cols] = turn(q_ref[:, cols])


def cut_kernel(table, slab, keep, info, w_ref, *refs):
    count, raw = table.count, slab - keep
    outs, rows_ref, sem = refs[:count], refs[-2], refs[-1]
    part = rows_ref.shape[0]
    start = pl.multiple_of(info[table.share] * part, part)
    copy = pltpu.make_async_copy(w_ref.at[pl.ds(start, part)], rows_ref, sem)
    copy.start()
    copy.wait()
    for d, out in enumerate(outs):
        target = lax.rem(info[table.place] + d, count)
        out[:, :keep] = rows_ref[:, pl.ds(pl.multiple_of(target * slab, slab), keep)]
        for j in range(count if raw else 0):
            out[:, keep + j * raw : keep + (j + 1) * raw] = rows_ref[
                :, j * slab + keep : (j + 1) * slab
            ]


def cut(table, info, out_weight, part, slab, keep):
    shape = jax.ShapeDtypeStruct((part, keep + table.count * (slab - keep)), out_weight.dtype)
    return call(
        functools.partial(cut_kernel, table, slab, keep),
        "cut",
        info,
        [out_weight],
        [ANYWHERE],
        [whole(shape)] * table.count,
        [shape] * table.count,
        scratch=[
            pltpu.VMEM((part, out_weight.shape[1]), out_weight.dtype),
            pltpu.SemaphoreType.DMA(()),
        ],
        vmem=0,
    )


def last_columns_kernel(info, *refs):
    refs[-1][...] = refs[0][...]


def last_columns(info, value, width, after):
    rows, full = value.shape
    shape = jax.ShapeDtypeStruct((rows, width), value.dtype)
    return call(
        last_columns_kernel,
        "last_columns",
        info,
        [value, *after],
        [pl.BlockSpec((rows, width), lambda i, info: (0, full // width - 1))]
        + [ANYWHERE] * len(after),
        whole(shape),
        shape,
    )


def prepare(info, queries, span_pairs, cache, cosine, sine, lengths, after):
    rows = queries.shape[0]
    shapes = [
        jax.ShapeDtypeStruct(queries.shape, jnp.bfloat16),
        jax.ShapeDtypeStruct((cache.shape[0] + rows + TAIL, 2 * HD), jnp.bfloat16),
    ]
    args = [queries, span_pairs, cache, cosine, sine, lengths]
    return call(
        prepare_kernel,
        "prepare",
        info,
        [*args, *after],
        [whole(a) for a in args[:-1]]
        + [pl.BlockSpec(memory_space=pltpu.SMEM)]
        + [ANYWHERE] * len(after),
        [whole(shape) for shape in shapes],
        shapes,
        vmem=32,
    )


def stack_kernel(count, begin, info, *refs):
    width = refs[-1].shape[2]
    for number, part in enumerate(refs[:count]):
        refs[-1][number] = part[:, begin : begin + width]


def stack(info, parts, begin, width, after=()):
    shape = jax.ShapeDtypeStruct((len(parts), parts[0].shape[0], width), parts[0].dtype)
    return call(
        functools.partial(stack_kernel, len(parts), begin),
        "stack",
        info,
        [*parts, *after],
        [whole(p) for p in parts] + [ANYWHERE] * len(after),
        whole(shape),
        shape,
    )


def gate_kernel(info, *refs):
    pass


def gate(info, value, after):
    return call(
        gate_kernel,
        "gate",
        info,
        [value, *after],
        [ANYWHERE] * (1 + len(after)),
        ANYWHERE,
        jax.ShapeDtypeStruct(value.shape, value.dtype),
        aliases={1: 0},
    )


def attend_kernel(table, slots, info, q_ref, *refs):
    count = table.contexts
    pieces, out_ref, s_ref = refs[:count], refs[-2], refs[-1]
    rows = q_ref.shape[0]
    heads = q_ref.shape[1] // HD
    chunk = pl.program_id(0)
    mine = info[0]
    q = jnp.concatenate([q_ref[:, h * HD : (h + 1) * HD] for h in range(heads)], axis=0)
    exponent = math.log2(math.e) / math.sqrt(HD)

    blocks = []
    peak = jnp.full((heads * rows, HD), NEG, jnp.float32)
    column = 0
    for kind in ("cache", "span"):
        for number, ref in enumerate(pieces):
            tail = ref.shape[0] - TAIL
            first, last = (0, slots) if kind == "cache" else (slots, tail)
            width = min(KEY_BLOCK, last - first)
            length = ref[tail : tail + 1, :HD].astype(jnp.float32) * DIGIT + ref[
                tail : tail + 1, HD:
            ].astype(jnp.float32)
            length = jnp.concatenate([length] * (width // HD), axis=1)
            for begin in range(first, last, width):
                scores = lax.dot_general(
                    q,
                    ref[begin : begin + width, :HD],
                    (((1,), (1,)), ((), ())),
                    preferred_element_type=jnp.float32,
                )
                if kind == "cache":
                    slot = lax.broadcasted_iota(jnp.int32, (1, width), 1) + begin
                    live = slot.astype(jnp.float32) < length
                    scores = scores + jnp.where(live, 0.0, NEG)
                elif number == 0:
                    key = lax.broadcasted_iota(jnp.int32, (rows, width), 1) + (begin - first)
                    row = lax.broadcasted_iota(jnp.int32, (rows, width), 0) + chunk * rows
                    bias = jnp.where(key <= row, 0.0, NEG)
                    scores = scores + jnp.concatenate([bias] * heads, axis=0)
                else:
                    scores = scores + jnp.where(info[table.owner + number] < mine, 0.0, NEG)
                s_ref[:, column : column + width] = scores
                for lane in range(0, width, HD):
                    peak = jnp.maximum(peak, scores[:, lane : lane + HD])
                blocks.append((ref, begin, column, width))
                column += width
    top = jnp.max(peak, axis=1, keepdims=True)
    total = jnp.zeros((heads * rows, HD), jnp.float32)
    mixed = jnp.zeros((heads * rows, HD), jnp.float32)
    for ref, begin, column, width in blocks:
        weights = jnp.exp2((s_ref[:, column : column + width] - top) * exponent)
        for lane in range(0, width, HD):
            total = total + weights[:, lane : lane + HD]
        mixed = mixed + jnp.dot(
            weights.astype(jnp.bfloat16),
            ref[begin : begin + width, HD:],
            preferred_element_type=jnp.float32,
        )
    result = (mixed / jnp.sum(total, axis=1, keepdims=True)).astype(jnp.bfloat16)
    for h in range(heads):
        out_ref[:, h * HD : (h + 1) * HD] = result[h * rows : (h + 1) * rows]


def attend(table, info, queries, pieces, slots, rows):
    all_rows, width = queries.shape
    heads = width // HD
    keys = sum(a.shape[0] - TAIL for a in pieces)
    chunk_spec = pl.BlockSpec((rows, width), lambda i, info: (i, 0))
    return call(
        functools.partial(attend_kernel, table, slots),
        "attend",
        info,
        [queries, *pieces],
        [chunk_spec] + [whole(a) for a in pieces],
        chunk_spec,
        jax.ShapeDtypeStruct((all_rows, width), jnp.bfloat16),
        grid=(all_rows // rows,),
        scratch=[pltpu.VMEM((heads * rows, keys), jnp.float32)],
        flops=ATTEND_FLOPS * all_rows * heads * keys * HD,
        vmem=28,
    )


def project_kernel(table, lines, keep, splits, info, *refs):
    count = table.count
    attention, w_ref, r_ref = refs[:lines], refs[lines], refs[lines + 1]
    parts, h_ref = refs[-1 - len(splits) : -1], refs[-1]
    rows = r_ref.shape[0]
    total = r_ref[:, :keep].astype(jnp.float32)
    for d in range(count):
        block = line_read(table, info, attention, d).astype(jnp.bfloat16)
        weight = w_ref[:, d].reshape(block.shape[1], keep)
        total = total + jnp.dot(block, weight, preferred_element_type=jnp.float32)
    result = total.astype(jnp.bfloat16)
    h_ref[:, :keep] = result
    for part, (begin, size) in zip(parts, splits):
        for row in range(begin, begin + size, rows):

            @pl.when(pl.program_id(0) == row // rows)
            def _():
                part[row - begin : row - begin + rows] = result


def project(table, info, attention, weights, residual, rows, splits):
    all_rows, slab = residual.shape
    keep = weights.shape[3]
    parts = [jax.ShapeDtypeStruct((size, keep), jnp.bfloat16) for _, size in splits]
    row_spec = pl.BlockSpec((rows, slab), lambda i, info: (i, 0))
    return call(
        functools.partial(project_kernel, table, len(attention), keep, splits),
        "project",
        info,
        [*attention, weights, residual],
        line_spec(attention, rows, lambda i: i) + [whole(weights), row_spec],
        [whole(part) for part in parts] + [row_spec],
        [*parts, jax.ShapeDtypeStruct(residual.shape, jnp.bfloat16)],
        grid=(all_rows // rows,),
        vmem=28,
    )


def project_raw_kernel(table, lines, raw_lines, info, *refs):
    count = table.count
    attention, residuals = refs[:lines], refs[lines : lines + raw_lines]
    w_ref = refs[lines + raw_lines]
    raw_ref, h_ref = refs[-2:]
    raw = h_ref.shape[1]
    blocks = [
        line_read(table, info, attention, d).astype(jnp.bfloat16) for d in range(count)
    ]
    for slab in range(count):
        start = pl.multiple_of(info[table.place + slab] * raw, raw)
        total = line_read(table, info, residuals, slab)
        for d in range(count):
            weight = w_ref[:, d, :, pl.ds(start, raw)].reshape(blocks[d].shape[1], raw)
            total = total + jnp.dot(blocks[d], weight, preferred_element_type=jnp.float32)
        result = total.astype(jnp.bfloat16)
        raw_ref[:, slab * raw : (slab + 1) * raw] = result
        if slab == 0:
            h_ref[...] = result


def project_raw(table, info, attention, residuals, weights, hidden, raw, rows):
    all_rows, slab = hidden.shape
    args = [*attention, *residuals, weights, hidden]
    out = jax.ShapeDtypeStruct((all_rows, table.count * raw), jnp.bfloat16)
    return call(
        functools.partial(project_raw_kernel, table, len(attention), len(residuals)),
        "project_raw",
        info,
        args,
        line_spec(attention, rows, lambda i: i)
        + line_spec(residuals, rows, lambda i: i)
        + [whole(weights), ANYWHERE],
        [
            pl.BlockSpec((rows, table.count * raw), lambda i, info: (i, 0)),
            pl.BlockSpec((rows, raw), lambda i, info: (i, slab // raw - 1)),
        ],
        [out, jax.ShapeDtypeStruct(hidden.shape, jnp.bfloat16)],
        grid=(all_rows // rows,),
        aliases={len(args): 1},
        vmem=28,
    )


def norm_kernel(table, lines, keep, slab, info, g_ref, *refs):
    count = table.count
    blocks, out_ref = refs[:lines], refs[-1]
    raw = slab - keep
    values = []
    squares = jnp.zeros((out_ref.shape[0], 1), jnp.float32)

    def read(d):
        found = [(0, keep, line_read(table, info, blocks, d))]
        if raw:
            cols = slice(d * raw, (d + 1) * raw)
            found.append((keep, raw, refs[lines][:, cols].astype(jnp.float32)))
        return found

    for d in range(count):
        for _, _, value in read(d):
            squares = squares + jnp.sum(value * value, axis=1, keepdims=True)
    inverse = lax.rsqrt(squares / (count * slab) + EPS_NORM)
    for d in range(count):
        for offset, width, value in read(d):
            start = pl.multiple_of(info[table.place + d] * slab + offset, HD)
            cols = pl.ds(start, width)
            out_ref[:, cols] = (value * inverse * g_ref[:, cols]).astype(jnp.bfloat16)


def norm_into(table, info, buffer, blocks, raw_hidden, gain, begin, rows, keep, slab, total_rows):
    width = table.count * slab
    step = min(rows, 32)
    steps, first = rows // step, begin // step
    args = [gain.reshape(1, width), *blocks]
    in_specs = [pl.BlockSpec((1, width), lambda i, info: (0, 0))]
    in_specs += line_spec(blocks, step, lambda i: i)
    if raw_hidden is not None:
        args.append(raw_hidden)
        in_specs.append(
            pl.BlockSpec((step, raw_hidden.shape[1]), lambda i, info: (first + i, 0))
        )
    aliases = {}
    if buffer is not None:
        args.append(buffer)
        in_specs.append(ANYWHERE)
        aliases = {len(args): 0}
    return call(
        functools.partial(norm_kernel, table, len(blocks), keep, slab),
        "norm",
        info,
        args,
        in_specs,
        pl.BlockSpec((step, width), lambda i, info: (first + i, 0)),
        jax.ShapeDtypeStruct((total_rows, width), jnp.bfloat16),
        grid=(steps,),
        aliases=aliases,
    )


def per_device(queries, span_kv, cache, lengths, offset, out_weight, residual, gain):
    rows = queries.shape[0]
    heads = queries.shape[1] // HD
    depth = out_weight.shape[0]
    slab = residual.shape[1]
    contexts = lax.axis_size("context")
    count = lax.axis_size("tensor")
    context_index = lax.axis_index("context")
    tensor_index = lax.axis_index("tensor")
    kv_index = tensor_index * heads // GROUP
    groups = lax.axis_size("groups")
    shares = groups * contexts
    share = lax.axis_index("groups") * contexts + context_index
    raw = slab // 4 if slab % 512 == 0 and rows > CHUNK else 0
    keep = slab - raw
    chunk = min(CHUNK, rows)
    sizes = [2 * chunk] + [chunk] * (rows // chunk - 2) if rows // chunk > 2 else [rows]
    splits = [(sum(sizes[:n]), size) for n, size in enumerate(sizes)]

    table = Table(contexts, count)
    steering = [context_index, *owners_of(contexts, context_index)]
    steering += [lax.rem(tensor_index + (count - d), count) for d in range(count)]
    steering += [tensor_index == 0, tensor_index == count - 1, share]
    info = jnp.stack([jnp.asarray(v).astype(jnp.int32) for v in steering])

    cache_local = lax.dynamic_index_in_dim(cache, kv_index, 0, keepdims=False)
    span_local = lax.dynamic_index_in_dim(span_kv, kv_index, 1, keepdims=False)
    positions = offset[0] + context_index * rows + jnp.arange(rows, dtype=jnp.int32)
    both = jnp.concatenate([frequencies(HD)] * 2)
    angles = positions.astype(jnp.float32)[:, None] * both[None, :]
    sign = jnp.where(jnp.arange(HD) < HD // 2, -1.0, 1.0)
    plane = ("groups", "context")
    cuts = cut(table, info, out_weight, depth // shares, slab, keep)
    parts = [cuts[0]]
    for shift in range(1, count):
        pairs = [(i, (i + shift) % count) for i in range(count)]
        parts.append(lax.ppermute(cuts[shift], "tensor", pairs))
    q_turned, payload = prepare(
        info, queries, span_local, cache_local, jnp.cos(angles),
        jnp.sin(angles) * sign[None, :], lengths, cuts[:1],
    )
    sent = []

    def between(block):
        sent.append(stack(info, parts, 0, keep, [block]))
        if raw:
            sent.append(last_columns(info, residual, raw, [*parts[1:], block]))
        return gate(info, block, sent)

    pieces = pieces_of(payload, "context", contexts, between)
    own_weights = lax.all_gather(sent[0], plane, axis=0, tiled=False)
    residuals = line_gather(sent[1], count) if raw else []
    mixed = attend(table, info, q_turned, pieces, cache_local.shape[0], chunk)
    if raw:
        mixed = gate(info, mixed, residuals[1:4] or residuals)
    attention = line_gather(mixed, count)

    *hidden_parts, hidden = project(
        table, info, attention, own_weights, residual, chunk, splits
    )
    raw_hidden = None
    if raw:
        raw_weights = stack(info, parts, keep, count * raw, [hidden_parts[0]])
        raw_weights = lax.all_gather(raw_weights, plane, axis=0, tiled=False)
        raw_hidden, hidden = project_raw(
            table, info, attention, residuals, raw_weights, hidden, raw, chunk
        )
    lines = []
    for number in range(len(splits)):
        value = hidden_parts[number]
        if number > 1:
            made = [raw_hidden] if raw and number == len(splits) - 1 else []
            value = gate(info, value, [*lines[number - 2][1:], *made])
        lines.append(line_gather(value, count))
    normed = None
    for (begin, size), blocks in zip(splits, lines):
        normed = norm_into(
            table, info, normed, blocks, raw_hidden, gain, begin, size, keep, slab, rows
        )
    return (hidden, normed)


def solution(mesh):
    in_specs = (
        P(("groups", "context"), "tensor"),
        P(("groups", "context"), None, None),
        P("groups", "context", None),
        P(("groups", "context")),
        P("groups"),
        P("tensor", None),
        P(("groups", "context"), "tensor"),
        P(),
    )
    out_specs = (P(("groups", "context"), "tensor"), P(("groups", "context"), None))
    return jax.shard_map(
        per_device, mesh=mesh, in_specs=in_specs, out_specs=out_specs, check_vma=False
    )
```

```python
import functools
import math

import jax
import jax.numpy as jnp
from jax import lax
from jax.experimental import pallas as pl
from jax.experimental.pallas import tpu as pltpu
from jax.sharding import PartitionSpec as P

GROUP = 8
HD = 128
NEG = -1e30
EPS_NORM = 1e-05
MIB = 1024 * 1024
CHUNK = 128
KEY_BLOCK = 512
ATTEND_FLOPS = 16
TAIL = 16
DIGIT = 32
ANYWHERE = pl.BlockSpec(memory_space=pl.ANY)


def frequencies(head_width):
    counter = jnp.arange(head_width // 2, dtype=jnp.float32)
    base_freq = jnp.exp(-(2.0 * counter / head_width) * math.log(500000.0))
    wavelength = 2.0 * math.pi / base_freq
    smoothing = (8192.0 / wavelength - 1.0) / 3.0
    blended = (1.0 - smoothing) * base_freq / 8.0 + smoothing * base_freq
    return jnp.where(
        wavelength < 2048.0, base_freq, jnp.where(wavelength > 8192.0, base_freq / 8.0, blended)
    )


def pieces_of(value, axis, count, between=lambda block: block):
    if count & (count - 1) == 0:
        held = {0: value}
        bit = count // 2
        while bit:
            pairs = [(i, i ^ bit) for i in range(count)]
            for mask in sorted(held):
                held[mask | bit] = lax.ppermute(held[mask], axis, pairs)
            if bit == count // 2:
                held[bit] = between(held[bit])
            bit //= 2
        return [held[mask] for mask in range(count)]
    blocks = [value]
    for shift in range(1, count):
        pairs = [(i, (i + shift) % count) for i in range(count)]
        blocks.append(lax.ppermute(value, axis, pairs))
    blocks[-1] = between(blocks[-1])
    return blocks


def owners_of(count, me):
    if count & (count - 1) == 0:
        return [me ^ mask for mask in range(count)]
    return [(me + count - shift) % count for shift in range(count)]


def plane_gather(value, groups, contexts, between=lambda block: block):
    count = groups * contexts
    if count & (count - 1):
        gathered = lax.all_gather(value, ("groups", "context"), axis=0, tiled=False)
        return [gathered[number] for number in range(count)]
    held = {0: value}
    bits = [1 << b for b in range(contexts.bit_length() - 2, 0, -1)]
    bits += [contexts << b for b in range(groups.bit_length() - 1)]
    bits += [1] if contexts > 1 else []
    for bit in bits:
        axis, flip, size = ("context", bit, contexts)
        if bit >= contexts:
            axis, flip, size = ("groups", bit // contexts, groups)
        pairs = [(i, i ^ flip) for i in range(size)]
        for mask in sorted(held):
            held[mask | bit] = lax.ppermute(held[mask], axis, pairs)
        if bit == bits[0]:
            held[bit] = between(held[bit])
    return [held[mask] for mask in range(count)]


def plane_owners(count, me):
    if count & (count - 1):
        return list(range(count))
    return [me ^ mask for mask in range(count)]


def line_gather(value, count):
    if count != 4:
        return [lax.all_gather(value, "tensor", axis=0, tiled=False)]
    far, last = line_far(value)
    return [value, *line_near(value), far, last]


def line_near(value):
    up = lax.ppermute(value, "tensor", [(0, 1), (1, 2), (2, 3)])
    return up, lax.ppermute(value, "tensor", [(1, 0), (2, 1), (3, 2)])


def line_far(value):
    far = lax.ppermute(value, "tensor", [(0, 2), (1, 3), (2, 0), (3, 1)])
    return far, lax.ppermute(far, "tensor", [(1, 0), (2, 3)])


def chunk_gathers(info, values, copies, made, count):
    if count != 4:
        return [line_gather(value, count) for value in values]
    fars, lines = [], []
    for number, value in enumerate(values):
        if number > 1:
            value = gate(info, value, [fars[number - 2][0]])
        fars.append(line_far(value))
    for number, value in enumerate(copies):
        before = [fars[number - 1][1] if number else fars[0][0]]
        if number == len(copies) // 2:
            before += made
        value = gate(info, value, before)
        lines.append([value, *line_near(value), *fars[number]])
    return lines


class Table:
    def __init__(self, contexts, count):
        self.contexts, self.count = contexts, count
        self.owner = 1
        self.place = 1 + contexts
        self.low = self.place + count
        self.high = self.low + 1
        self.share = self.low + 2
        self.rows = self.low + 3


def line_read(table, info, refs, d, cols=slice(None)):
    if len(refs) == 1:
        return refs[0][info[table.place + d], :, cols].astype(jnp.float32)
    if d == 0:
        return refs[0][:, cols].astype(jnp.float32)
    if d == 2:
        return refs[3][:, cols].astype(jnp.float32)
    near = refs[1 if d == 1 else 2][:, cols].astype(jnp.float32)
    other = refs[4][:, cols].astype(jnp.float32)
    at_end = info[table.low if d == 1 else table.high]
    return jnp.where(at_end == 1, other, near)


def line_spec(blocks, rows, index):
    if len(blocks) == 1:
        count, _, width = blocks[0].shape
        return [pl.BlockSpec((count, rows, width), lambda i, info: (0, index(i), 0))]
    width = blocks[0].shape[1]
    return [pl.BlockSpec((rows, width), lambda i, info: (index(i), 0)) for _ in blocks]


def call(kernel, name, info, args, in_specs, out_specs, out_shape, grid=(1,), aliases=None,
         scratch=(), flops=1, vmem=16):
    return pl.pallas_call(
        kernel,
        grid_spec=pltpu.PrefetchScalarGridSpec(
            num_scalar_prefetch=1,
            grid=grid,
            in_specs=in_specs,
            out_specs=out_specs,
            scratch_shapes=list(scratch),
        ),
        out_shape=out_shape,
        input_output_aliases=aliases or {},
        compiler_params=pltpu.CompilerParams(vmem_limit_bytes=vmem * MIB or None),
        cost_estimate=pl.CostEstimate(flops=flops, bytes_accessed=1, transcendentals=0),
        name=name,
    )(info, *args)


def whole(a):
    zeros = (0,) * len(a.shape)
    return pl.BlockSpec(tuple(a.shape), lambda i, info: zeros)


def prepare_kernel(info, q_ref, kv_ref, cache_ref, cos_ref, sin_ref, length_ref, *refs):
    q_out, kv_out = refs[-2:]
    cosine, sine = cos_ref[...], sin_ref[...]
    slots, rows = cache_ref.shape[0], q_ref.shape[0]
    span, tail = slice(slots, slots + rows), slice(slots + rows, slots + rows + TAIL)

    def turn(block):
        block = block.astype(jnp.float32)
        return (block * cosine + pltpu.roll(block, HD // 2, 1) * sine).astype(jnp.bfloat16)

    kv_out[:slots] = cache_ref[...]
    kv_out[span, :HD] = turn(kv_ref[:, :HD])
    kv_out[span, HD:] = kv_ref[:, HD:]
    length = length_ref[0]
    upper = lax.div(length, DIGIT)
    lower = length - upper * DIGIT
    kv_out[tail, :HD] = jnp.full((TAIL, HD), upper.astype(jnp.float32)).astype(jnp.bfloat16)
    kv_out[tail, HD:] = jnp.full((TAIL, HD), lower.astype(jnp.float32)).astype(jnp.bfloat16)
    for head in range(q_ref.shape[1] // HD):
        cols = slice(head * HD, (head + 1) * HD)
        q_out[:, cols] = turn(q_ref[:, cols])


def cut_kernel(table, slab, keep, info, w_ref, *refs):
    count, raw = table.count, slab - keep
    outs, rows_ref, sem = refs[:count], refs[-2], refs[-1]
    part = rows_ref.shape[0]
    start = pl.multiple_of(info[table.share] * part, part)
    copy = pltpu.make_async_copy(w_ref.at[pl.ds(start, part)], rows_ref, sem)
    copy.start()
    copy.wait()
    for d, out in enumerate(outs):
        target = lax.rem(info[table.place] + d, count)
        out[:, :keep] = rows_ref[:, pl.ds(pl.multiple_of(target * slab, slab), keep)]
        for j in range(count if raw else 0):
            out[:, keep + j * raw : keep + (j + 1) * raw] = rows_ref[
                :, j * slab + keep : (j + 1) * slab
            ]


def cut(table, info, out_weight, part, slab, keep):
    shape = jax.ShapeDtypeStruct((part, keep + table.count * (slab - keep)), out_weight.dtype)
    return call(
        functools.partial(cut_kernel, table, slab, keep),
        "cut",
        info,
        [out_weight],
        [ANYWHERE],
        [whole(shape)] * table.count,
        [shape] * table.count,
        scratch=[
            pltpu.VMEM((part, out_weight.shape[1]), out_weight.dtype),
            pltpu.SemaphoreType.DMA(()),
        ],
        vmem=0,
    )


def last_columns_kernel(info, *refs):
    refs[-1][...] = refs[0][...]
    refs[-2][...] = refs[0][...]


def cut_kernel(table, slab, keep, info, w_ref, *refs):
    count, raw = table.count, slab - keep
    outs, rows_ref, sem = refs[:count], refs[-2], refs[-1]
    part = rows_ref.shape[0]
    start = pl.multiple_of(info[table.share] * part, part)
    copy = pltpu.make_async_copy(w_ref.at[pl.ds(start, part)], rows_ref, sem)
    copy.start()
    copy.wait()
    for d, out in enumerate(outs):
        target = lax.rem(info[table.place] + d, count)
        out[:, :keep] = rows_ref[:, pl.ds(pl.multiple_of(target * slab, slab), keep)]
        for j in range(count if raw else 0):
            out[:, keep + j * raw : keep + (j + 1) * raw] = rows_ref[
                :, j * slab + keep : (j + 1) * slab
            ]


def cut(table, info, out_weight, part, slab, keep):
    shape = jax.ShapeDtypeStruct((part, keep + table.count * (slab - keep)), out_weight.dtype)
    return call(
        functools.partial(cut_kernel, table, slab, keep),
        "cut",
        info,
        [out_weight],
        [ANYWHERE],
        [whole(shape)] * table.count,
        [shape] * table.count,
        scratch=[
            pltpu.VMEM((part, out_weight.shape[1]), out_weight.dtype),
            pltpu.SemaphoreType.DMA(()),
        ],
        vmem=0,
    )


def last_columns_kernel(info, *refs):
    refs[-1][...] = refs[0][...]
    refs[-2][...] = refs[0][...]


def last_columns(info, value, width, after):
    rows, full = value.shape
    shape = jax.ShapeDtypeStruct((rows, width), value.dtype)
    return call(
        last_columns_kernel,
        "last_columns",
        info,
        [value, *after],
        [pl.BlockSpec((rows, width), lambda i, info: (0, full // width - 1))]
        + [ANYWHERE] * len(after),
        [whole(shape)] * 2,
        [shape] * 2,
    )


def prepare(info, queries, span_pairs, cache, cosine, sine, lengths, after):
    rows = queries.shape[0]
    shapes = [
        jax.ShapeDtypeStruct(queries.shape, jnp.bfloat16),
        jax.ShapeDtypeStruct((cache.shape[0] + rows + TAIL, 2 * HD), jnp.bfloat16),
    ]
    args = [queries, span_pairs, cache, cosine, sine, lengths]
    return call(
        prepare_kernel,
        "prepare",
        info,
        [*args, *after],
        [whole(a) for a in args[:-1]]
        + [pl.BlockSpec(memory_space=pltpu.SMEM)]
        + [ANYWHERE] * len(after),
        [whole(shape) for shape in shapes],
        shapes,
        vmem=32,
    )


def stack_kernel(count, info, *refs):
    for number, part in enumerate(refs[:count]):
        refs[-1][number] = part[...]


def stack(info, parts, after):
    shape = jax.ShapeDtypeStruct((len(parts), *parts[0].shape), parts[0].dtype)
    return call(
        functools.partial(stack_kernel, len(parts)),
        "stack",
        info,
        [*parts, *after],
        [whole(p) for p in parts] + [ANYWHERE] * len(after),
        whole(shape),
        shape,
    )


def gate_kernel(info, *refs):
    pass


def gate(info, value, after):
    return call(
        gate_kernel,
        "gate",
        info,
        [value, *after],
        [ANYWHERE] * (1 + len(after)),
        ANYWHERE,
        jax.ShapeDtypeStruct(value.shape, value.dtype),
        aliases={1: 0},
    )


def attend_kernel(table, slots, info, q_ref, *refs):
    count = table.contexts
    pieces, out_ref, s_ref = refs[:count], refs[-2], refs[-1]
    rows = q_ref.shape[0]
    heads = q_ref.shape[1] // HD
    chunk = pl.program_id(0)
    mine = info[0]
    q = jnp.concatenate([q_ref[:, h * HD : (h + 1) * HD] for h in range(heads)], axis=0)
    exponent = math.log2(math.e) / math.sqrt(HD)

    blocks = []
    peak = jnp.full((heads * rows, HD), NEG, jnp.float32)
    column = 0
    for kind in ("cache", "span"):
        for number, ref in enumerate(pieces):
            tail = ref.shape[0] - TAIL
            first, last = (0, slots) if kind == "cache" else (slots, tail)
            width = min(KEY_BLOCK, last - first)
            length = ref[tail : tail + 1, :HD].astype(jnp.float32) * DIGIT + ref[
                tail : tail + 1, HD:
            ].astype(jnp.float32)
            length = jnp.concatenate([length] * (width // HD), axis=1)
            for begin in range(first, last, width):
                scores = lax.dot_general(
                    q,
                    ref[begin : begin + width, :HD],
                    (((1,), (1,)), ((), ())),
                    preferred_element_type=jnp.float32,
                )
                if kind == "cache":
                    slot = lax.broadcasted_iota(jnp.int32, (1, width), 1) + begin
                    live = slot.astype(jnp.float32) < length
                    scores = scores + jnp.where(live, 0.0, NEG)
                elif number == 0:
                    key = lax.broadcasted_iota(jnp.int32, (rows, width), 1) + (begin - first)
                    row = lax.broadcasted_iota(jnp.int32, (rows, width), 0) + chunk * rows
                    bias = jnp.where(key <= row, 0.0, NEG)
                    scores = scores + jnp.concatenate([bias] * heads, axis=0)
                else:
                    scores = scores + jnp.where(info[table.owner + number] < mine, 0.0, NEG)
                s_ref[:, column : column + width] = scores
                for lane in range(0, width, HD):
                    peak = jnp.maximum(peak, scores[:, lane : lane + HD])
                blocks.append((ref, begin, column, width))
                column += width
    top = jnp.max(peak, axis=1, keepdims=True)
    total = jnp.zeros((heads * rows, HD), jnp.float32)
    mixed = jnp.zeros((heads * rows, HD), jnp.float32)
    for ref, begin, column, width in blocks:
        weights = jnp.exp2((s_ref[:, column : column + width] - top) * exponent)
        for lane in range(0, width, HD):
            total = total + weights[:, lane : lane + HD]
        mixed = mixed + jnp.dot(
            weights.astype(jnp.bfloat16),
            ref[begin : begin + width, HD:],
            preferred_element_type=jnp.float32,
        )
    result = (mixed / jnp.sum(total, axis=1, keepdims=True)).astype(jnp.bfloat16)
    for h in range(heads):
        out_ref[:, h * HD : (h + 1) * HD] = result[h * rows : (h + 1) * rows]


def attend(table, info, queries, pieces, slots, rows):
    all_rows, width = queries.shape
    heads = width // HD
    keys = sum(a.shape[0] - TAIL for a in pieces)
    chunk_spec = pl.BlockSpec((rows, width), lambda i, info: (i, 0))
    return call(
        functools.partial(attend_kernel, table, slots),
        "attend",
        info,
        [queries, *pieces],
        [chunk_spec] + [whole(a) for a in pieces],
        chunk_spec,
        jax.ShapeDtypeStruct((all_rows, width), jnp.bfloat16),
        grid=(all_rows // rows,),
        scratch=[pltpu.VMEM((heads * rows, keys), jnp.float32)],
        flops=ATTEND_FLOPS * all_rows * heads * keys * HD,
        vmem=28,
    )


def place_weights(table, info, pieces, w_ref, begin):
    part, width = pieces[0].shape[1], w_ref.shape[2]
    for number, piece in enumerate(pieces):
        start = pl.multiple_of(info[table.rows + number] * part, part)
        for d in range(table.count):
            w_ref[d, pl.ds(start, part)] = piece[d, :, begin : begin + width]


def project_kernel(table, lines, shares, keep, splits, info, *refs):
    count = table.count
    attention, pieces = refs[:lines], refs[lines : lines + shares]
    r_ref = refs[lines + shares]
    parts, h_ref, w_ref = refs[-2 - 2 * len(splits) : -2], refs[-2], refs[-1]
    rows = r_ref.shape[0]

    @pl.when(pl.program_id(0) == 0)
    def _():
        place_weights(table, info, pieces, w_ref, 0)

    total = r_ref[:, :keep].astype(jnp.float32)
    for d in range(count):
        block = line_read(table, info, attention, d).astype(jnp.bfloat16)
        total = total + jnp.dot(block, w_ref[d], preferred_element_type=jnp.float32)
    result = total.astype(jnp.bfloat16)
    h_ref[:, :keep] = result
    for part, (begin, size) in zip(parts, splits * 2):
        for row in range(begin, begin + size, rows):

            @pl.when(pl.program_id(0) == row // rows)
            def _():
                part[row - begin : row - begin + rows] = result


def project(table, info, attention, pieces, residual, keep, rows, splits, after):
    all_rows, slab = residual.shape
    count, part_rows, _ = pieces[0].shape
    parts = [jax.ShapeDtypeStruct((size, keep), jnp.bfloat16) for _, size in splits * 2]
    row_spec = pl.BlockSpec((rows, slab), lambda i, info: (i, 0))
    return call(
        functools.partial(project_kernel, table, len(attention), len(pieces), keep, splits),
        "project",
        info,
        [*attention, *pieces, residual, *after],
        line_spec(attention, rows, lambda i: i)
        + [whole(p) for p in pieces]
        + [row_spec]
        + [ANYWHERE] * len(after),
        [whole(part) for part in parts] + [row_spec],
        [*parts, jax.ShapeDtypeStruct(residual.shape, jnp.bfloat16)],
        grid=(all_rows // rows,),
        scratch=[pltpu.VMEM((count, len(pieces) * part_rows, keep), jnp.bfloat16)],
        vmem=36,
    )


def project_raw_kernel(table, lines, raw_lines, shares, keep, info, *refs):
    count = table.count
    attention, residuals = refs[:lines], refs[lines : lines + raw_lines]
    pieces = refs[lines + raw_lines : lines + raw_lines + shares]
    raw_ref, h_ref, w_ref = refs[-3:]
    raw = h_ref.shape[1]

    @pl.when(pl.program_id(0) == 0)
    def _():
        place_weights(table, info, pieces, w_ref, keep)

    blocks = [
        line_read(table, info, attention, d).astype(jnp.bfloat16) for d in range(count)
    ]
    for slab in range(count):
        cols = pl.ds(pl.multiple_of(info[table.place + slab] * raw, raw), raw)
        total = line_read(table, info, residuals, slab)
        for d in range(count):
            total = total + jnp.dot(
                blocks[d], w_ref[d, :, cols], preferred_element_type=jnp.float32
            )
        result = total.astype(jnp.bfloat16)
        raw_ref[:, slab * raw : (slab + 1) * raw] = result
        if slab == 0:
            h_ref[...] = result


def project_raw(table, info, attention, residuals, pieces, hidden, keep, raw, rows):
    all_rows, slab = hidden.shape
    count, part_rows, _ = pieces[0].shape
    args = [*attention, *residuals, *pieces, hidden]
    out = jax.ShapeDtypeStruct((all_rows, count * raw), jnp.bfloat16)
    return call(
        functools.partial(
            project_raw_kernel, table, len(attention), len(residuals), len(pieces), keep
        ),
        "project_raw",
        info,
        args,
        line_spec(attention, rows, lambda i: i)
        + line_spec(residuals, rows, lambda i: i)
        + [whole(p) for p in pieces]
        + [ANYWHERE],
        [
            pl.BlockSpec((rows, count * raw), lambda i, info: (i, 0)),
            pl.BlockSpec((rows, raw), lambda i, info: (i, slab // raw - 1)),
        ],
        [out, jax.ShapeDtypeStruct(hidden.shape, jnp.bfloat16)],
        grid=(all_rows // rows,),
        aliases={len(args): 1},
        scratch=[pltpu.VMEM((count, len(pieces) * part_rows, count * raw), jnp.bfloat16)],
        vmem=36,
    )


def norm_kernel(table, lines, keep, slab, info, g_ref, *refs):
    count = table.count
    blocks, out_ref = refs[:lines], refs[-1]
    raw = slab - keep
    values = []
    squares = jnp.zeros((out_ref.shape[0], 1), jnp.float32)

    def read(d):
        found = [(0, keep, line_read(table, info, blocks, d))]
        if raw:
            cols = slice(d * raw, (d + 1) * raw)
            found.append((keep, raw, refs[lines][:, cols].astype(jnp.float32)))
        return found

    for d in range(count):
        for _, _, value in read(d):
            squares = squares + jnp.sum(value * value, axis=1, keepdims=True)
    inverse = lax.rsqrt(squares / (count * slab) + EPS_NORM)
    for d in range(count):
        for offset, width, value in read(d):
            start = pl.multiple_of(info[table.place + d] * slab + offset, HD)
            cols = pl.ds(start, width)
            out_ref[:, cols] = (value * inverse * g_ref[:, cols]).astype(jnp.bfloat16)


def norm_into(table, info, buffer, blocks, raw_hidden, gain, begin, rows, keep, slab, total_rows):
    width = table.count * slab
    step = min(rows, 32)
    steps, first = rows // step, begin // step
    args = [gain.reshape(1, width), *blocks]
    in_specs = [pl.BlockSpec((1, width), lambda i, info: (0, 0))]
    in_specs += line_spec(blocks, step, lambda i: i)
    if raw_hidden is not None:
        args.append(raw_hidden)
        in_specs.append(
            pl.BlockSpec((step, raw_hidden.shape[1]), lambda i, info: (first + i, 0))
        )
    aliases = {}
    if buffer is not None:
        args.append(buffer)
        in_specs.append(ANYWHERE)
        aliases = {len(args): 0}
    return call(
        functools.partial(norm_kernel, table, len(blocks), keep, slab),
        "norm",
        info,
        args,
        in_specs,
        pl.BlockSpec((step, width), lambda i, info: (first + i, 0)),
        jax.ShapeDtypeStruct((total_rows, width), jnp.bfloat16),
        grid=(steps,),
        aliases=aliases,
    )


def per_device(queries, span_kv, cache, lengths, offset, out_weight, residual, gain):
    rows = queries.shape[0]
    heads = queries.shape[1] // HD
    depth = out_weight.shape[0]
    slab = residual.shape[1]
    contexts = lax.axis_size("context")
    count = lax.axis_size("tensor")
    context_index = lax.axis_index("context")
    tensor_index = lax.axis_index("tensor")
    kv_index = tensor_index * heads // GROUP
    groups = lax.axis_size("groups")
    shares = groups * contexts
    share = lax.axis_index("groups") * contexts + context_index
    raw = slab // 4 if slab % 512 == 0 and rows > CHUNK else 0
    keep = slab - raw
    chunk = min(CHUNK, rows)
    sizes = [chunk] * (rows // chunk)
    splits = [(sum(sizes[:n]), size) for n, size in enumerate(sizes)]

    table = Table(contexts, count)
    steering = [context_index, *owners_of(contexts, context_index)]
    steering += [lax.rem(tensor_index + (count - d), count) for d in range(count)]
    steering += [tensor_index == 0, tensor_index == count - 1, share]
    steering += plane_owners(shares, share)
    info = jnp.stack([jnp.asarray(v).astype(jnp.int32) for v in steering])

    cache_local = lax.dynamic_index_in_dim(cache, kv_index, 0, keepdims=False)
    span_local = lax.dynamic_index_in_dim(span_kv, kv_index, 1, keepdims=False)
    positions = offset[0] + context_index * rows + jnp.arange(rows, dtype=jnp.int32)
    both = jnp.concatenate([frequencies(HD)] * 2)
    angles = positions.astype(jnp.float32)[:, None] * both[None, :]
    sign = jnp.where(jnp.arange(HD) < HD // 2, -1.0, 1.0)
    cuts = cut(table, info, out_weight, depth // shares, slab, keep)
    parts = [cuts[0]]
    for shift in range(1, count):
        pairs = [(i, (i + shift) % count) for i in range(count)]
        parts.append(lax.ppermute(cuts[shift], "tensor", pairs))
    q_turned, payload = prepare(
        info, queries, span_local, cache_local, jnp.cos(angles),
        jnp.sin(angles) * sign[None, :], lengths, cuts[:1],
    )
    sent = []

    def between(block):
        sent.append(stack(info, parts, [block]))
        if raw:
            sent.extend(last_columns(info, residual, raw, [*parts[1:], block]))
        return gate(info, block, sent)

    pieces = pieces_of(payload, "context", contexts, between)
    mixed = attend(table, info, q_turned, pieces, cache_local.shape[0], chunk)
    weights = plane_gather(
        sent[0], groups, contexts, lambda block: gate(info, block, [mixed])
    )
    residuals = []
    if raw and count == 4:
        far, last = line_far(sent[1])
        near = gate(info, sent[2], [mixed])
        residuals = [near, *line_near(near), far, last]
        mixed = gate(info, mixed, [far])
    elif raw:
        residuals = line_gather(sent[1], count)
    attention = line_gather(mixed, count)

    *hidden_parts, hidden = project(
        table, info, attention, weights, residual, keep, chunk, splits, residuals[1:]
    )
    raw_hidden = None
    if raw:
        raw_hidden, hidden = project_raw(
            table, info, attention, residuals, weights, hidden, keep, raw, chunk
        )
    lines = chunk_gathers(
        info,
        hidden_parts[: len(splits)],
        hidden_parts[len(splits) :],
        [raw_hidden] if raw else [],
        count,
    )
    normed = None
    for (begin, size), blocks in zip(splits, lines):
        normed = norm_into(
            table, info, normed, blocks, raw_hidden, gain, begin, size, keep, slab, rows
        )
    return (hidden, normed)


def solution(mesh):
    in_specs = (
        P(("groups", "context"), "tensor"),
        P(("groups", "context"), None, None),
        P("groups", "context", None),
        P(("groups", "context")),
        P("groups"),
        P("tensor", None),
        P(("groups", "context"), "tensor"),
        P(),
    )
    out_specs = (P(("groups", "context"), "tensor"), P(("groups", "context"), None))
    return jax.shard_map(
        per_device, mesh=mesh, in_specs=in_specs, out_specs=out_specs, check_vma=False
    )
```

```python
import functools
import math

import jax
import jax.numpy as jnp
from jax import lax
from jax.experimental import pallas as pl
from jax.experimental.pallas import tpu as pltpu
from jax.sharding import PartitionSpec as P

GROUP = 8
HD = 128
NEG = -1e30
EPS_NORM = 1e-05
MIB = 1024 * 1024
CHUNK = 128
KEY_BLOCK = 512
ATTEND_FLOPS = 16
RAW_PART = 8
TAIL = 16
DIGIT = 32
ANYWHERE = pl.BlockSpec(memory_space=pl.ANY)


def frequencies(head_width):
    counter = jnp.arange(head_width // 2, dtype=jnp.float32)
    base_freq = jnp.exp(-(2.0 * counter / head_width) * math.log(500000.0))
    wavelength = 2.0 * math.pi / base_freq
    smoothing = (8192.0 / wavelength - 1.0) / 3.0
    blended = (1.0 - smoothing) * base_freq / 8.0 + smoothing * base_freq
    return jnp.where(
        wavelength < 2048.0, base_freq, jnp.where(wavelength > 8192.0, base_freq / 8.0, blended)
    )


def pieces_of(value, axis, count, between=lambda block: block):
    if count & (count - 1) == 0:
        held = {0: value}
        bit = count // 2
        while bit:
            pairs = [(i, i ^ bit) for i in range(count)]
            for mask in sorted(held):
                held[mask | bit] = lax.ppermute(held[mask], axis, pairs)
            if bit == count // 2:
                held[bit] = between(held[bit])
            bit //= 2
        return [held[mask] for mask in range(count)]
    blocks = [value]
    for shift in range(1, count):
        pairs = [(i, (i + shift) % count) for i in range(count)]
        blocks.append(lax.ppermute(value, axis, pairs))
    blocks[-1] = between(blocks[-1])
    return blocks


def owners_of(count, me):
    if count & (count - 1) == 0:
        return [me ^ mask for mask in range(count)]
    return [(me + count - shift) % count for shift in range(count)]


def plane_gather(value, swapped, groups, contexts, first, then):
    count = groups * contexts
    if count & (count - 1):
        gathered = lax.all_gather(value, ("groups", "context"), axis=0, tiled=False)
        return [gathered[number] for number in range(count)]
    held = {0: value}
    bits = [1 << b for b in range(contexts.bit_length() - 2, 0, -1)]
    bits += [contexts << b for b in range(groups.bit_length() - 1)]
    for bit in bits:
        axis, flip, size = ("context", bit, contexts)
        if bit >= contexts:
            axis, flip, size = ("groups", bit // contexts, groups)
        pairs = [(i, i ^ flip) for i in range(size)]
        for mask in sorted(held):
            held[mask | bit] = lax.ppermute(held[mask], axis, pairs)
        if bit == bits[0]:
            held[bit] = first(held[bit])
    if contexts > 1:
        for mask in sorted(held):
            held[mask] = then(held[mask], mask) if mask else held[mask]
            held[mask | 1] = core_swap(held[mask], contexts) if mask else swapped
    return [held[mask] for mask in range(count)]


def core_swap(value, contexts):
    return lax.ppermute(value, "context", [(i, i ^ 1) for i in range(contexts)])


def plane_owners(count, me):
    if count & (count - 1):
        return list(range(count))
    return [me ^ mask for mask in range(count)]


def line_gather(value, count):
    if count != 4:
        return [lax.all_gather(value, "tensor", axis=0, tiled=False)]
    far, last = line_far(value)
    return [value, *line_near(value), far, last]


def line_near(value):
    up = lax.ppermute(value, "tensor", [(0, 1), (1, 2), (2, 3)])
    return up, lax.ppermute(value, "tensor", [(1, 0), (2, 1), (3, 2)])


def line_far(value):
    far = lax.ppermute(value, "tensor", [(0, 2), (1, 3), (2, 0), (3, 1)])
    return far, lax.ppermute(far, "tensor", [(1, 0), (2, 3)])


def chunk_gathers(info, values, copies, first, made, count):
    if count != 4:
        return [line_gather(value, count) for value in values]
    fars, lines = [], []
    for number, value in enumerate(values):
        after = [fars[number - 1][0]] if number else first
        fars.append(line_far(gate(info, value, after) if after else value))
    for number, value in enumerate(copies):
        after = list(lines[number - 1][1:3]) if number else []
        if number > 1:
            after.append(fars[number - 2][1])
        if number == len(copies) // 2:
            after += made
        value = gate(info, value, after) if after else value
        lines.append([value, *line_near(value), *fars[number]])
    return lines


class Table:
    def __init__(self, contexts, count):
        self.contexts, self.count = contexts, count
        self.owner = 1
        self.place = 1 + contexts
        self.low = self.place + count
        self.high = self.low + 1
        self.share = self.low + 2
        self.rows = self.low + 3


def line_read(table, info, refs, d, cols=slice(None)):
    if len(refs) == 1:
        return refs[0][info[table.place + d], :, cols].astype(jnp.float32)
    if d == 0:
        return refs[0][:, cols].astype(jnp.float32)
    if d == 2:
        return refs[3][:, cols].astype(jnp.float32)
    near = refs[1 if d == 1 else 2][:, cols].astype(jnp.float32)
    other = refs[4][:, cols].astype(jnp.float32)
    at_end = info[table.low if d == 1 else table.high]
    return jnp.where(at_end == 1, other, near)


def line_spec(blocks, rows, index):
    if len(blocks) == 1:
        count, _, width = blocks[0].shape
        return [pl.BlockSpec((count, rows, width), lambda i, info: (0, index(i), 0))]
    width = blocks[0].shape[1]
    return [pl.BlockSpec((rows, width), lambda i, info: (index(i), 0)) for _ in blocks]


def call(kernel, name, info, args, in_specs, out_specs, out_shape, grid=(1,), aliases=None,
         scratch=(), flops=1, vmem=16):
    return pl.pallas_call(
        kernel,
        grid_spec=pltpu.PrefetchScalarGridSpec(
            num_scalar_prefetch=1,
            grid=grid,
            in_specs=in_specs,
            out_specs=out_specs,
            scratch_shapes=list(scratch),
        ),
        out_shape=out_shape,
        input_output_aliases=aliases or {},
        compiler_params=pltpu.CompilerParams(vmem_limit_bytes=vmem * MIB or None),
        cost_estimate=pl.CostEstimate(flops=flops, bytes_accessed=1, transcendentals=0),
        name=name,
    )(info, *args)


def whole(a):
    zeros = (0,) * len(a.shape)
    return pl.BlockSpec(tuple(a.shape), lambda i, info: zeros)


def prepare_kernel(info, q_ref, kv_ref, cache_ref, cos_ref, sin_ref, length_ref, *refs):
    q_out, kv_out = refs[-2:]
    cosine, sine = cos_ref[...], sin_ref[...]
    slots, rows = cache_ref.shape[0], q_ref.shape[0]
    span, tail = slice(slots, slots + rows), slice(slots + rows, slots + rows + TAIL)

    def turn(block):
        block = block.astype(jnp.float32)
        return (block * cosine + pltpu.roll(block, HD // 2, 1) * sine).astype(jnp.bfloat16)

    kv_out[:slots] = cache_ref[...]
    kv_out[span, :HD] = turn(kv_ref[:, :HD])
    kv_out[span, HD:] = kv_ref[:, HD:]
    length = length_ref[0]
    upper = lax.div(length, DIGIT)
    lower = length - upper * DIGIT
    kv_out[tail, :HD] = jnp.full((TAIL, HD), upper.astype(jnp.float32)).astype(jnp.bfloat16)
    kv_out[tail, HD:] = jnp.full((TAIL, HD), lower.astype(jnp.float32)).astype(jnp.bfloat16)
    for head in range(q_ref.shape[1] // HD):
        cols = slice(head * HD, (head + 1) * HD)
        q_out[:, cols] = turn(q_ref[:, cols])


def cut_kernel(table, slab, keep, info, w_ref, *refs):
    count, raw = table.count, slab - keep
    outs, rows_ref, sem = refs[:count], refs[-2], refs[-1]
    part = rows_ref.shape[0]
    start = pl.multiple_of(info[table.share] * part, part)
    copy = pltpu.make_async_copy(w_ref.at[pl.ds(start, part)], rows_ref, sem)
    copy.start()
    copy.wait()
    for d, out in enumerate(outs):
        target = lax.rem(info[table.place] + d, count)
        out[:, :keep] = rows_ref[:, pl.ds(pl.multiple_of(target * slab, slab), keep)]
        for j in range(count if raw else 0):
            out[:, keep + j * raw : keep + (j + 1) * raw] = rows_ref[
                :, j * slab + keep : (j + 1) * slab
            ]


def cut(table, info, out_weight, part, slab, keep):
    shape = jax.ShapeDtypeStruct((part, keep + table.count * (slab - keep)), out_weight.dtype)
    return call(
        functools.partial(cut_kernel, table, slab, keep),
        "cut",
        info,
        [out_weight],
        [ANYWHERE],
        [whole(shape)] * table.count,
        [shape] * table.count,
        scratch=[
            pltpu.VMEM((part, out_weight.shape[1]), out_weight.dtype),
            pltpu.SemaphoreType.DMA(()),
        ],
        vmem=0,
    )


def last_columns_kernel(info, *refs):
    refs[-1][...] = refs[0][...]
    refs[-2][...] = refs[0][...]


def last_columns(info, value, width, after):
    rows, full = value.shape
    shape = jax.ShapeDtypeStruct((rows, width), value.dtype)
    return call(
        last_columns_kernel,
        "last_columns",
        info,
        [value, *after],
        [pl.BlockSpec((rows, width), lambda i, info: (0, full // width - 1))]
        + [ANYWHERE] * len(after),
        [whole(shape)] * 2,
        [shape] * 2,
    )


def prepare(info, queries, span_pairs, cache, cosine, sine, lengths, after):
    rows = queries.shape[0]
    shapes = [
        jax.ShapeDtypeStruct(queries.shape, jnp.bfloat16),
        jax.ShapeDtypeStruct((cache.shape[0] + rows + TAIL, 2 * HD), jnp.bfloat16),
    ]
    args = [queries, span_pairs, cache, cosine, sine, lengths]
    return call(
        prepare_kernel,
        "prepare",
        info,
        [*args, *after],
        [whole(a) for a in args[:-1]]
        + [pl.BlockSpec(memory_space=pltpu.SMEM)]
        + [ANYWHERE] * len(after),
        [whole(shape) for shape in shapes],
        shapes,
        vmem=32,
    )


def stack_kernel(count, info, *refs):
    for number, part in enumerate(refs[:count]):
        refs[-1][number] = part[...]


def stack(info, parts, after):
    shape = jax.ShapeDtypeStruct((len(parts), *parts[0].shape), parts[0].dtype)
    return call(
        functools.partial(stack_kernel, len(parts)),
        "stack",
        info,
        [*parts, *after],
        [whole(p) for p in parts] + [ANYWHERE] * len(after),
        whole(shape),
        shape,
    )


def gate_kernel(info, *refs):
    pass


def gate(info, value, after):
    return call(
        gate_kernel,
        "gate",
        info,
        [value, *after],
        [ANYWHERE] * (1 + len(after)),
        ANYWHERE,
        jax.ShapeDtypeStruct(value.shape, value.dtype),
        aliases={1: 0},
    )


def attend_kernel(table, slots, info, q_ref, *refs):
    count = table.contexts
    pieces, out_ref, s_ref = refs[:count], refs[-2], refs[-1]
    rows = q_ref.shape[0]
    heads = q_ref.shape[1] // HD
    chunk = pl.program_id(0)
    mine = info[0]
    q = jnp.concatenate([q_ref[:, h * HD : (h + 1) * HD] for h in range(heads)], axis=0)
    exponent = math.log2(math.e) / math.sqrt(HD)

    blocks = []
    peak = jnp.full((heads * rows, HD), NEG, jnp.float32)
    column = 0
    for kind in ("cache", "span"):
        for number, ref in enumerate(pieces):
            tail = ref.shape[0] - TAIL
            first, last = (0, slots) if kind == "cache" else (slots, tail)
            width = min(KEY_BLOCK, last - first)
            length = ref[tail : tail + 1, :HD].astype(jnp.float32) * DIGIT + ref[
                tail : tail + 1, HD:
            ].astype(jnp.float32)
            length = jnp.concatenate([length] * (width // HD), axis=1)
            for begin in range(first, last, width):
                scores = lax.dot_general(
                    q,
                    ref[begin : begin + width, :HD],
                    (((1,), (1,)), ((), ())),
                    preferred_element_type=jnp.float32,
                )
                if kind == "cache":
                    slot = lax.broadcasted_iota(jnp.int32, (1, width), 1) + begin
                    live = slot.astype(jnp.float32) < length
                    scores = scores + jnp.where(live, 0.0, NEG)
                elif number == 0:
                    key = lax.broadcasted_iota(jnp.int32, (rows, width), 1) + (begin - first)
                    row = lax.broadcasted_iota(jnp.int32, (rows, width), 0) + chunk * rows
                    bias = jnp.where(key <= row, 0.0, NEG)
                    scores = scores + jnp.concatenate([bias] * heads, axis=0)
                else:
                    scores = scores + jnp.where(info[table.owner + number] < mine, 0.0, NEG)
                s_ref[:, column : column + width] = scores
                for lane in range(0, width, HD):
                    peak = jnp.maximum(peak, scores[:, lane : lane + HD])
                blocks.append((ref, begin, column, width))
                column += width
    top = jnp.max(peak, axis=1, keepdims=True)
    total = jnp.zeros((heads * rows, HD), jnp.float32)
    mixed = jnp.zeros((heads * rows, HD), jnp.float32)
    for ref, begin, column, width in blocks:
        weights = jnp.exp2((s_ref[:, column : column + width] - top) * exponent)
        for lane in range(0, width, HD):
            total = total + weights[:, lane : lane + HD]
        mixed = mixed + jnp.dot(
            weights.astype(jnp.bfloat16),
            ref[begin : begin + width, HD:],
            preferred_element_type=jnp.float32,
        )
    result = (mixed / jnp.sum(total, axis=1, keepdims=True)).astype(jnp.bfloat16)
    for h in range(heads):
        out_ref[:, h * HD : (h + 1) * HD] = result[h * rows : (h + 1) * rows]


def attend(table, info, queries, pieces, slots, rows, after):
    all_rows, width = queries.shape
    heads = width // HD
    keys = sum(a.shape[0] - TAIL for a in pieces)
    chunk_spec = pl.BlockSpec((rows, width), lambda i, info: (i, 0))
    return call(
        functools.partial(attend_kernel, table, slots),
        "attend",
        info,
        [queries, *pieces, *after],
        [chunk_spec] + [whole(a) for a in pieces] + [ANYWHERE] * len(after),
        chunk_spec,
        jax.ShapeDtypeStruct((all_rows, width), jnp.bfloat16),
        grid=(all_rows // rows,),
        scratch=[pltpu.VMEM((heads * rows, keys), jnp.float32)],
        flops=ATTEND_FLOPS * all_rows * heads * keys * HD,
        vmem=28,
    )


def place_weights(table, info, pieces, w_ref, begin):
    part, width = pieces[0].shape[1], w_ref.shape[2]
    for number, piece in enumerate(pieces):
        start = pl.multiple_of(info[table.rows + number] * part, part)
        for d in range(table.count):
            w_ref[d, pl.ds(start, part)] = piece[d, :, begin : begin + width]


def project_kernel(table, lines, shares, keep, splits, info, *refs):
    count = table.count
    attention, pieces = refs[:lines], refs[lines : lines + shares]
    r_ref = refs[lines + shares]
    parts, h_ref, w_ref = refs[-2 - 2 * len(splits) : -2], refs[-2], refs[-1]
    rows = r_ref.shape[0]

    @pl.when(pl.program_id(0) == 0)
    def _():
        place_weights(table, info, pieces, w_ref, 0)

    total = r_ref[:, :keep].astype(jnp.float32)
    for d in range(count):
        block = line_read(table, info, attention, d).astype(jnp.bfloat16)
        total = total + jnp.dot(block, w_ref[d], preferred_element_type=jnp.float32)
    result = total.astype(jnp.bfloat16)
    h_ref[:, :keep] = result
    for part, (begin, size) in zip(parts, splits * 2):
        for row in range(begin, begin + size, rows):

            @pl.when(pl.program_id(0) == row // rows)
            def _():
                part[row - begin : row - begin + rows] = result


def project(table, info, attention, pieces, residual, keep, rows, splits, after):
    all_rows, slab = residual.shape
    count, part_rows, _ = pieces[0].shape
    parts = [jax.ShapeDtypeStruct((size, keep), jnp.bfloat16) for _, size in splits * 2]
    row_spec = pl.BlockSpec((rows, slab), lambda i, info: (i, 0))
    return call(
        functools.partial(project_kernel, table, len(attention), len(pieces), keep, splits),
        "project",
        info,
        [*attention, *pieces, residual, *after],
        line_spec(attention, rows, lambda i: i)
        + [whole(p) for p in pieces]
        + [row_spec]
        + [ANYWHERE] * len(after),
        [whole(part) for part in parts] + [row_spec],
        [*parts, jax.ShapeDtypeStruct(residual.shape, jnp.bfloat16)],
        grid=(all_rows // rows,),
        scratch=[pltpu.VMEM((count, len(pieces) * part_rows, keep), jnp.bfloat16)],
        vmem=36,
    )


def project_raw_kernel(table, lines, raw_lines, shares, keep, info, *refs):
    count = table.count
    attention, residuals = refs[:lines], refs[lines : lines + raw_lines]
    pieces = refs[lines + raw_lines : lines + raw_lines + shares]
    raw_ref, h_ref, w_ref = refs[-3:]
    raw = h_ref.shape[1]

    @pl.when(pl.program_id(0) == 0)
    def _():
        place_weights(table, info, pieces, w_ref, keep)

    blocks = [
        line_read(table, info, attention, d).astype(jnp.bfloat16) for d in range(count)
    ]
    for slab in range(count):
        cols = pl.ds(pl.multiple_of(info[table.place + slab] * raw, raw), raw)
        total = line_read(table, info, residuals, slab)
        for d in range(count):
            total = total + jnp.dot(
                blocks[d], w_ref[d, :, cols], preferred_element_type=jnp.float32
            )
        result = total.astype(jnp.bfloat16)
        raw_ref[:, slab * raw : (slab + 1) * raw] = result
        if slab == 0:
            h_ref[...] = result


def project_raw(table, info, attention, residuals, pieces, hidden, keep, raw, rows):
    all_rows, slab = hidden.shape
    count, part_rows, _ = pieces[0].shape
    args = [*attention, *residuals, *pieces, hidden]
    out = jax.ShapeDtypeStruct((all_rows, count * raw), jnp.bfloat16)
    return call(
        functools.partial(
            project_raw_kernel, table, len(attention), len(residuals), len(pieces), keep
        ),
        "project_raw",
        info,
        args,
        line_spec(attention, rows, lambda i: i)
        + line_spec(residuals, rows, lambda i: i)
        + [whole(p) for p in pieces]
        + [ANYWHERE],
        [
            pl.BlockSpec((rows, count * raw), lambda i, info: (i, 0)),
            pl.BlockSpec((rows, raw), lambda i, info: (i, slab // raw - 1)),
        ],
        [out, jax.ShapeDtypeStruct(hidden.shape, jnp.bfloat16)],
        grid=(all_rows // rows,),
        aliases={len(args): 1},
        scratch=[pltpu.VMEM((count, len(pieces) * part_rows, count * raw), jnp.bfloat16)],
        vmem=36,
    )


def norm_kernel(table, lines, keep, slab, info, g_ref, *refs):
    count = table.count
    blocks, out_ref = refs[:lines], refs[-1]
    raw = slab - keep
    values = []
    squares = jnp.zeros((out_ref.shape[0], 1), jnp.float32)

    def read(d):
        found = [(0, keep, line_read(table, info, blocks, d))]
        if raw:
            cols = slice(d * raw, (d + 1) * raw)
            found.append((keep, raw, refs[lines][:, cols].astype(jnp.float32)))
        return found

    for d in range(count):
        for _, _, value in read(d):
            squares = squares + jnp.sum(value * value, axis=1, keepdims=True)
    inverse = lax.rsqrt(squares / (count * slab) + EPS_NORM)
    for d in range(count):
        for offset, width, value in read(d):
            start = pl.multiple_of(info[table.place + d] * slab + offset, HD)
            cols = pl.ds(start, width)
            out_ref[:, cols] = (value * inverse * g_ref[:, cols]).astype(jnp.bfloat16)


def norm_into(table, info, buffer, blocks, raw_hidden, gain, begin, rows, keep, slab, total_rows):
    width = table.count * slab
    step = min(rows, 32)
    steps, first = rows // step, begin // step
    args = [gain.reshape(1, width), *blocks]
    in_specs = [pl.BlockSpec((1, width), lambda i, info: (0, 0))]
    in_specs += line_spec(blocks, step, lambda i: i)
    if raw_hidden is not None:
        args.append(raw_hidden)
        in_specs.append(
            pl.BlockSpec((step, raw_hidden.shape[1]), lambda i, info: (first + i, 0))
        )
    aliases = {}
    if buffer is not None:
        args.append(buffer)
        in_specs.append(ANYWHERE)
        aliases = {len(args): 0}
    return call(
        functools.partial(norm_kernel, table, len(blocks), keep, slab),
        "norm",
        info,
        args,
        in_specs,
        pl.BlockSpec((step, width), lambda i, info: (first + i, 0)),
        jax.ShapeDtypeStruct((total_rows, width), jnp.bfloat16),
        grid=(steps,),
        aliases=aliases,
    )


def per_device(queries, span_kv, cache, lengths, offset, out_weight, residual, gain):
    rows = queries.shape[0]
    heads = queries.shape[1] // HD
    depth = out_weight.shape[0]
    slab = residual.shape[1]
    contexts = lax.axis_size("context")
    count = lax.axis_size("tensor")
    context_index = lax.axis_index("context")
    tensor_index = lax.axis_index("tensor")
    kv_index = tensor_index * heads // GROUP
    groups = lax.axis_size("groups")
    shares = groups * contexts
    share = lax.axis_index("groups") * contexts + context_index
    raw = slab // RAW_PART if slab % (RAW_PART * HD) == 0 else 0
    keep = slab - raw
    chunk = min(CHUNK, rows)
    sizes = [chunk] * (rows // chunk)
    splits = [(sum(sizes[:n]), size) for n, size in enumerate(sizes)]

    table = Table(contexts, count)
    steering = [context_index, *owners_of(contexts, context_index)]
    steering += [lax.rem(tensor_index + (count - d), count) for d in range(count)]
    steering += [tensor_index == 0, tensor_index == count - 1, share]
    steering += plane_owners(shares, share)
    info = jnp.stack([jnp.asarray(v).astype(jnp.int32) for v in steering])

    cache_local = lax.dynamic_index_in_dim(cache, kv_index, 0, keepdims=False)
    span_local = lax.dynamic_index_in_dim(span_kv, kv_index, 1, keepdims=False)
    positions = offset[0] + context_index * rows + jnp.arange(rows, dtype=jnp.int32)
    both = jnp.concatenate([frequencies(HD)] * 2)
    angles = positions.astype(jnp.float32)[:, None] * both[None, :]
    sign = jnp.where(jnp.arange(HD) < HD // 2, -1.0, 1.0)
    cuts = cut(table, info, out_weight, depth // shares, slab, keep)
    parts = [cuts[0]]
    for shift in range(1, count):
        pairs = [(i, (i + shift) % count) for i in range(count)]
        parts.append(lax.ppermute(cuts[shift], "tensor", pairs))
    q_turned, payload = prepare(
        info, queries, span_local, cache_local, jnp.cos(angles),
        jnp.sin(angles) * sign[None, :], lengths, cuts[:1],
    )
    sent = []

    def between(block):
        sent.append(stack(info, parts, [payload]))
        if raw:
            sent.extend(last_columns(info, residual, raw, [*parts[1:], payload]))
        return gate(info, block, sent)

    pieces = pieces_of(payload, "context", contexts, between)
    early = line_far(sent[1]) if raw and count == 4 else ()
    swapped = core_swap(sent[0], contexts) if contexts % 2 == 0 else sent[0]
    mixed = attend(
        table, info, q_turned, pieces, cache_local.shape[0], chunk, [*early[:1], swapped]
    )
    if count == 4:
        far, last = line_far(mixed)
        attention = [mixed, *line_near(mixed), far, last]
    else:
        attention = line_gather(mixed, count)
        far = mixed
    weights = plane_gather(
        sent[0],
        swapped,
        groups,
        contexts,
        lambda block: gate(info, block, [mixed]),
        lambda block, mask: gate(info, block, attention[1 : 3 if mask & (mask - 1) == 0 else 5]),
    )
    residuals = []
    if early:
        near = gate(info, sent[2], [far])
        residuals = [near, *line_near(near), *early]
    elif raw:
        residuals = line_gather(sent[1], count)

    *hidden_parts, hidden = project(
        table, info, attention, weights, residual, keep, chunk, splits, residuals[4:]
    )
    raw_hidden = None
    if raw:
        raw_hidden, hidden = project_raw(
            table, info, attention, residuals, weights, hidden, keep, raw, chunk
        )
    lines = chunk_gathers(
        info,
        hidden_parts[: len(splits)],
        hidden_parts[len(splits) :],
        residuals[1:3],
        [raw_hidden] if raw else [],
        count,
    )
    normed = None
    for (begin, size), blocks in zip(splits, lines):
        normed = norm_into(
            table, info, normed, blocks, raw_hidden, gain, begin, size, keep, slab, rows
        )
    return (hidden, normed)


def solution(mesh):
    in_specs = (
        P(("groups", "context"), "tensor"),
        P(("groups", "context"), None, None),
        P("groups", "context", None),
        P(("groups", "context")),
        P("groups"),
        P("tensor", None),
        P(("groups", "context"), "tensor"),
        P(),
    )
    out_specs = (P(("groups", "context"), "tensor"), P(("groups", "context"), None))
    return jax.shard_map(
        per_device, mesh=mesh, in_specs=in_specs, out_specs=out_specs, check_vma=False
    )
```

```python
import functools
import math

import jax
import jax.numpy as jnp
from jax import lax
from jax.experimental import pallas as pl
from jax.experimental.pallas import tpu as pltpu
from jax.sharding import PartitionSpec as P

GROUP = 8
HD = 128
NEG = -1e30
EPS_NORM = 1e-05
MIB = 1024 * 1024
CHUNK = 128
KEY_BLOCK = 512
ATTEND_FLOPS = 16
RAW_PART = 4
TAIL = 16
DIGIT = 32
ANYWHERE = pl.BlockSpec(memory_space=pl.ANY)


def frequencies(head_width):
    counter = jnp.arange(head_width // 2, dtype=jnp.float32)
    base_freq = jnp.exp(-(2.0 * counter / head_width) * math.log(500000.0))
    wavelength = 2.0 * math.pi / base_freq
    smoothing = (8192.0 / wavelength - 1.0) / 3.0
    blended = (1.0 - smoothing) * base_freq / 8.0 + smoothing * base_freq
    return jnp.where(
        wavelength < 2048.0, base_freq, jnp.where(wavelength > 8192.0, base_freq / 8.0, blended)
    )


def pieces_of(value, axis, count, between=lambda block: block):
    if count & (count - 1) == 0:
        held = {0: value}
        bit = count // 2
        while bit:
            pairs = [(i, i ^ bit) for i in range(count)]
            for mask in sorted(held):
                held[mask | bit] = lax.ppermute(held[mask], axis, pairs)
            if bit == count // 2:
                held[bit] = between(held[bit])
            bit //= 2
        return [held[mask] for mask in range(count)]
    blocks = [value]
    for shift in range(1, count):
        pairs = [(i, (i + shift) % count) for i in range(count)]
        blocks.append(lax.ppermute(value, axis, pairs))
    blocks[-1] = between(blocks[-1])
    return blocks


def owners_of(count, me):
    if count & (count - 1) == 0:
        return [me ^ mask for mask in range(count)]
    return [(me + count - shift) % count for shift in range(count)]


def plane_gather(value, groups, contexts, first, then):
    count = groups * contexts
    if count & (count - 1):
        gathered = lax.all_gather(value, ("groups", "context"), axis=0, tiled=False)
        return [gathered[number] for number in range(count)]
    held = {0: value}
    bits = [1 << b for b in range(contexts.bit_length() - 2, 0, -1)]
    bits += [contexts << b for b in range(groups.bit_length() - 1)]
    for bit in bits:
        axis, flip, size = ("context", bit, contexts)
        if bit >= contexts:
            axis, flip, size = ("groups", bit // contexts, groups)
        pairs = [(i, i ^ flip) for i in range(size)]
        for mask in sorted(held):
            held[mask | bit] = lax.ppermute(held[mask], axis, pairs)
        if bit == bits[0]:
            held[bit] = first(held[bit])
    if contexts > 1:
        for mask in sorted(held):
            held[mask] = then(held[mask], mask) if mask else held[mask]
            held[mask | 1] = core_swap(held[mask], contexts)
    return [held[mask] for mask in range(count)]


def core_swap(value, contexts):
    return lax.ppermute(value, "context", [(i, i ^ 1) for i in range(contexts)])


def plane_owners(count, me):
    if count & (count - 1):
        return list(range(count))
    return [me ^ mask for mask in range(count)]


def line_gather(value, count):
    if count != 4:
        return [lax.all_gather(value, "tensor", axis=0, tiled=False)]
    far, last = line_far(value)
    return [value, *line_near(value), far, last]


def line_near(value):
    up = lax.ppermute(value, "tensor", [(0, 1), (1, 2), (2, 3)])
    return up, lax.ppermute(value, "tensor", [(1, 0), (2, 1), (3, 2)])


def line_far(value):
    far = lax.ppermute(value, "tensor", [(0, 2), (1, 3), (2, 0), (3, 1)])
    return far, lax.ppermute(far, "tensor", [(1, 0), (2, 3)])


def chunk_gathers(info, values, copies, first, made, count):
    if count != 4:
        return [line_gather(value, count) for value in values]
    fars, lines = [], []
    for number, value in enumerate(values):
        fars.append(line_far(gate(info, value, [fars[-1][0]]) if number else value))
    for number, value in enumerate(copies):
        after = list(lines[number - 1][1:3]) if number else []
        if number > 1:
            after.append(fars[number - 2][1])
        if number == 1:
            after += first
        if number == len(copies) // 2:
            after += made
        value = gate(info, value, after) if after else value
        lines.append([value, *line_near(value), *fars[number]])
    return lines


class Table:
    def __init__(self, contexts, count):
        self.contexts, self.count = contexts, count
        self.owner = 1
        self.place = 1 + contexts
        self.low = self.place + count
        self.high = self.low + 1
        self.share = self.low + 2
        self.rows = self.low + 3


def line_read(table, info, refs, d, cols=slice(None)):
    if len(refs) == 1:
        return refs[0][info[table.place + d], :, cols].astype(jnp.float32)
    if d == 0:
        return refs[0][:, cols].astype(jnp.float32)
    if d == 2:
        return refs[3][:, cols].astype(jnp.float32)
    near = refs[1 if d == 1 else 2][:, cols].astype(jnp.float32)
    other = refs[4][:, cols].astype(jnp.float32)
    at_end = info[table.low if d == 1 else table.high]
    return jnp.where(at_end == 1, other, near)


def line_spec(blocks, rows, index):
    if len(blocks) == 1:
        count, _, width = blocks[0].shape
        return [pl.BlockSpec((count, rows, width), lambda i, info: (0, index(i), 0))]
    width = blocks[0].shape[1]
    return [pl.BlockSpec((rows, width), lambda i, info: (index(i), 0)) for _ in blocks]


def call(kernel, name, info, args, in_specs, out_specs, out_shape, grid=(1,), aliases=None,
         scratch=(), flops=1, vmem=16):
    return pl.pallas_call(
        kernel,
        grid_spec=pltpu.PrefetchScalarGridSpec(
            num_scalar_prefetch=1,
            grid=grid,
            in_specs=in_specs,
            out_specs=out_specs,
            scratch_shapes=list(scratch),
        ),
        out_shape=out_shape,
        input_output_aliases=aliases or {},
        compiler_params=pltpu.CompilerParams(vmem_limit_bytes=vmem * MIB or None),
        cost_estimate=pl.CostEstimate(flops=flops, bytes_accessed=1, transcendentals=0),
        name=name,
    )(info, *args)


def whole(a):
    zeros = (0,) * len(a.shape)
    return pl.BlockSpec(tuple(a.shape), lambda i, info: zeros)


def prepare_kernel(table, slab, keep, info, q_hbm, kv_hbm, cache_hbm, w_hbm, cos_ref, sin_ref,
                   length_ref, *refs):
    count, raw = table.count, slab - keep
    q_out, kv_out, outs = refs[0], refs[1], refs[2 : 2 + count]
    q_ref, kv_ref, w_ref, sems = refs[2 + count :]
    slots, rows, part = cache_hbm.shape[0], q_ref.shape[0], w_ref.shape[0]
    span, tail = slice(slots, slots + rows), slice(slots + rows, slots + rows + TAIL)
    start = pl.multiple_of(info[table.share] * part, part)
    moves = [
        (w_hbm.at[pl.ds(start, part)], w_ref),
        (kv_hbm, kv_ref),
        (q_hbm, q_ref),
        (cache_hbm, kv_out.at[pl.ds(0, slots)]),
    ]
    copies = [pltpu.make_async_copy(*move, sems.at[n]) for n, move in enumerate(moves)]
    for copy in copies:
        copy.start()

    copies[0].wait()
    for d, out in enumerate(outs):
        target = lax.rem(info[table.place] + d, count)
        out[:, :keep] = w_ref[:, pl.ds(pl.multiple_of(target * slab, slab), keep)]
        for j in range(count if raw else 0):
            out[:, keep + j * raw : keep + (j + 1) * raw] = w_ref[
                :, j * slab + keep : (j + 1) * slab
            ]

    cosine, sine = cos_ref[...], sin_ref[...]

    def turn(block):
        block = block.astype(jnp.float32)
        return (block * cosine + pltpu.roll(block, HD // 2, 1) * sine).astype(jnp.bfloat16)

    copies[1].wait()
    kv_out[span, :HD] = turn(kv_ref[:, :HD])
    kv_out[span, HD:] = kv_ref[:, HD:]
    length = length_ref[0]
    upper = lax.div(length, DIGIT)
    lower = length - upper * DIGIT
    kv_out[tail, :HD] = jnp.full((TAIL, HD), upper.astype(jnp.float32)).astype(jnp.bfloat16)
    kv_out[tail, HD:] = jnp.full((TAIL, HD), lower.astype(jnp.float32)).astype(jnp.bfloat16)
    copies[2].wait()
    for head in range(q_ref.shape[1] // HD):
        cols = slice(head * HD, (head + 1) * HD)
        q_out[:, cols] = turn(q_ref[:, cols])
    copies[3].wait()


def prepare(table, info, queries, span_pairs, cache, out_weight, cosine, sine, lengths, part,
            slab, keep):
    rows = queries.shape[0]
    shapes = [
        jax.ShapeDtypeStruct(queries.shape, jnp.bfloat16),
        jax.ShapeDtypeStruct((cache.shape[0] + rows + TAIL, 2 * HD), jnp.bfloat16),
    ]
    width = keep + table.count * (slab - keep)
    shapes += [jax.ShapeDtypeStruct((part, width), out_weight.dtype)] * table.count
    return call(
        functools.partial(prepare_kernel, table, slab, keep),
        "prepare",
        info,
        [queries, span_pairs, cache, out_weight, cosine, sine, lengths],
        [ANYWHERE] * 4
        + [whole(cosine), whole(sine), pl.BlockSpec(memory_space=pltpu.SMEM)],
        [whole(shape) for shape in shapes],
        shapes,
        scratch=[
            pltpu.VMEM(queries.shape, jnp.bfloat16),
            pltpu.VMEM(span_pairs.shape, jnp.bfloat16),
            pltpu.VMEM((part, out_weight.shape[1]), out_weight.dtype),
            pltpu.SemaphoreType.DMA((4,)),
        ],
        vmem=0,
    )


def last_columns_kernel(info, *refs):
    refs[-1][...] = refs[0][...]
    refs[-2][...] = refs[0][...]


def last_columns(info, value, width, after):
    rows, full = value.shape
    shape = jax.ShapeDtypeStruct((rows, width), value.dtype)
    return call(
        last_columns_kernel,
        "last_columns",
        info,
        [value, *after],
        [pl.BlockSpec((rows, width), lambda i, info: (0, full // width - 1))]
        + [ANYWHERE] * len(after),
        [whole(shape)] * 2,
        [shape] * 2,
    )


def stack_kernel(count, info, *refs):
    for number, part in enumerate(refs[:count]):
        refs[-1][number] = part[...]


def stack(info, parts, after):
    shape = jax.ShapeDtypeStruct((len(parts), *parts[0].shape), parts[0].dtype)
    return call(
        functools.partial(stack_kernel, len(parts)),
        "stack",
        info,
        [*parts, *after],
        [whole(p) for p in parts] + [ANYWHERE] * len(after),
        whole(shape),
        shape,
    )


def gate_kernel(info, *refs):
    pass


def gate(info, value, after):
    return call(
        gate_kernel,
        "gate",
        info,
        [value, *after],
        [ANYWHERE] * (1 + len(after)),
        ANYWHERE,
        jax.ShapeDtypeStruct(value.shape, value.dtype),
        aliases={1: 0},
    )


def attend_kernel(table, slots, info, q_ref, *refs):
    count = table.contexts
    pieces, out_ref, s_ref = refs[:count], refs[-2], refs[-1]
    rows = q_ref.shape[0]
    heads = q_ref.shape[1] // HD
    chunk = pl.program_id(0)
    mine = info[0]
    q = jnp.concatenate([q_ref[:, h * HD : (h + 1) * HD] for h in range(heads)], axis=0)
    exponent = math.log2(math.e) / math.sqrt(HD)

    blocks = []
    peak = jnp.full((heads * rows, HD), NEG, jnp.float32)
    column = 0
    for kind in ("cache", "span"):
        for number, ref in enumerate(pieces):
            tail = ref.shape[0] - TAIL
            first, last = (0, slots) if kind == "cache" else (slots, tail)
            width = min(KEY_BLOCK, last - first)
            length = ref[tail : tail + 1, :HD].astype(jnp.float32) * DIGIT + ref[
                tail : tail + 1, HD:
            ].astype(jnp.float32)
            length = jnp.concatenate([length] * (width // HD), axis=1)
            for begin in range(first, last, width):
                scores = lax.dot_general(
                    q,
                    ref[begin : begin + width, :HD],
                    (((1,), (1,)), ((), ())),
                    preferred_element_type=jnp.float32,
                )
                if kind == "cache":
                    slot = lax.broadcasted_iota(jnp.int32, (1, width), 1) + begin
                    live = slot.astype(jnp.float32) < length
                    scores = scores + jnp.where(live, 0.0, NEG)
                elif number == 0:
                    key = lax.broadcasted_iota(jnp.int32, (rows, width), 1) + (begin - first)
                    row = lax.broadcasted_iota(jnp.int32, (rows, width), 0) + chunk * rows
                    bias = jnp.where(key <= row, 0.0, NEG)
                    scores = scores + jnp.concatenate([bias] * heads, axis=0)
                else:
                    scores = scores + jnp.where(info[table.owner + number] < mine, 0.0, NEG)
                s_ref[:, column : column + width] = scores
                for lane in range(0, width, HD):
                    peak = jnp.maximum(peak, scores[:, lane : lane + HD])
                blocks.append((ref, begin, column, width))
                column += width
    top = jnp.max(peak, axis=1, keepdims=True)
    total = jnp.zeros((heads * rows, HD), jnp.float32)
    mixed = jnp.zeros((heads * rows, HD), jnp.float32)
    for ref, begin, column, width in blocks:
        weights = jnp.exp2((s_ref[:, column : column + width] - top) * exponent)
        for lane in range(0, width, HD):
            total = total + weights[:, lane : lane + HD]
        mixed = mixed + jnp.dot(
            weights.astype(jnp.bfloat16),
            ref[begin : begin + width, HD:],
            preferred_element_type=jnp.float32,
        )
    result = (mixed / jnp.sum(total, axis=1, keepdims=True)).astype(jnp.bfloat16)
    for h in range(heads):
        out_ref[:, h * HD : (h + 1) * HD] = result[h * rows : (h + 1) * rows]


def attend(table, info, queries, pieces, slots, rows):
    all_rows, width = queries.shape
    heads = width // HD
    keys = sum(a.shape[0] - TAIL for a in pieces)
    chunk_spec = pl.BlockSpec((rows, width), lambda i, info: (i, 0))
    return call(
        functools.partial(attend_kernel, table, slots),
        "attend",
        info,
        [queries, *pieces],
        [chunk_spec] + [whole(a) for a in pieces],
        chunk_spec,
        jax.ShapeDtypeStruct((all_rows, width), jnp.bfloat16),
        grid=(all_rows // rows,),
        scratch=[pltpu.VMEM((heads * rows, keys), jnp.float32)],
        flops=ATTEND_FLOPS * all_rows * heads * keys * HD,
        vmem=28,
    )


def place_weights(table, info, pieces, w_ref, begin):
    part, width = pieces[0].shape[1], w_ref.shape[2]
    for number, piece in enumerate(pieces):
        start = pl.multiple_of(info[table.rows + number] * part, part)
        for d in range(table.count):
            w_ref[d, pl.ds(start, part)] = piece[d, :, begin : begin + width]


def project_kernel(table, lines, shares, keep, splits, info, *refs):
    count = table.count
    attention, pieces = refs[:lines], refs[lines : lines + shares]
    r_ref = refs[lines + shares]
    parts, h_ref, w_ref = refs[-2 - 2 * len(splits) : -2], refs[-2], refs[-1]
    rows = r_ref.shape[0]

    @pl.when(pl.program_id(0) == 0)
    def _():
        place_weights(table, info, pieces, w_ref, 0)

    total = r_ref[:, :keep].astype(jnp.float32)
    for d in range(count):
        block = line_read(table, info, attention, d).astype(jnp.bfloat16)
        total = total + jnp.dot(block, w_ref[d], preferred_element_type=jnp.float32)
    result = total.astype(jnp.bfloat16)
    h_ref[:, :keep] = result
    for part, (begin, size) in zip(parts, splits * 2):
        for row in range(begin, begin + size, rows):

            @pl.when(pl.program_id(0) == row // rows)
            def _():
                part[row - begin : row - begin + rows] = result


def project(table, info, attention, pieces, residual, keep, rows, splits):
    all_rows, slab = residual.shape
    count, part_rows, _ = pieces[0].shape
    parts = [jax.ShapeDtypeStruct((size, keep), jnp.bfloat16) for _, size in splits * 2]
    row_spec = pl.BlockSpec((rows, slab), lambda i, info: (i, 0))
    return call(
        functools.partial(project_kernel, table, len(attention), len(pieces), keep, splits),
        "project",
        info,
        [*attention, *pieces, residual],
        line_spec(attention, rows, lambda i: i)
        + [whole(p) for p in pieces]
        + [row_spec],
        [whole(part) for part in parts] + [row_spec],
        [*parts, jax.ShapeDtypeStruct(residual.shape, jnp.bfloat16)],
        grid=(all_rows // rows,),
        scratch=[pltpu.VMEM((count, len(pieces) * part_rows, keep), jnp.bfloat16)],
        vmem=36,
    )


def project_raw_kernel(table, lines, raw_lines, shares, keep, info, *refs):
    count = table.count
    attention, residuals = refs[:lines], refs[lines : lines + raw_lines]
    pieces = refs[lines + raw_lines : lines + raw_lines + shares]
    raw_ref, h_ref, w_ref = refs[-3:]
    raw = h_ref.shape[1]

    @pl.when(pl.program_id(0) == 0)
    def _():
        place_weights(table, info, pieces, w_ref, keep)

    blocks = [
        line_read(table, info, attention, d).astype(jnp.bfloat16) for d in range(count)
    ]
    for slab in range(count):
        cols = pl.ds(pl.multiple_of(info[table.place + slab] * raw, raw), raw)
        total = line_read(table, info, residuals, slab)
        for d in range(count):
            total = total + jnp.dot(
                blocks[d], w_ref[d, :, cols], preferred_element_type=jnp.float32
            )
        result = total.astype(jnp.bfloat16)
        raw_ref[:, slab * raw : (slab + 1) * raw] = result
        if slab == 0:
            h_ref[...] = result


def project_raw(table, info, attention, residuals, pieces, hidden, keep, raw, rows):
    all_rows, slab = hidden.shape
    count, part_rows, _ = pieces[0].shape
    args = [*attention, *residuals, *pieces, hidden]
    out = jax.ShapeDtypeStruct((all_rows, count * raw), jnp.bfloat16)
    return call(
        functools.partial(
            project_raw_kernel, table, len(attention), len(residuals), len(pieces), keep
        ),
        "project_raw",
        info,
        args,
        line_spec(attention, rows, lambda i: i)
        + line_spec(residuals, rows, lambda i: i)
        + [whole(p) for p in pieces]
        + [ANYWHERE],
        [
            pl.BlockSpec((rows, count * raw), lambda i, info: (i, 0)),
            pl.BlockSpec((rows, raw), lambda i, info: (i, slab // raw - 1)),
        ],
        [out, jax.ShapeDtypeStruct(hidden.shape, jnp.bfloat16)],
        grid=(all_rows // rows,),
        aliases={len(args): 1},
        scratch=[pltpu.VMEM((count, len(pieces) * part_rows, count * raw), jnp.bfloat16)],
        vmem=36,
    )


def norm_kernel(table, lines, keep, slab, info, g_ref, *refs):
    count = table.count
    blocks, out_ref = refs[:lines], refs[-1]
    raw = slab - keep
    values = []
    squares = jnp.zeros((out_ref.shape[0], 1), jnp.float32)

    def read(d):
        found = [(0, keep, line_read(table, info, blocks, d))]
        if raw:
            cols = slice(d * raw, (d + 1) * raw)
            found.append((keep, raw, refs[lines][:, cols].astype(jnp.float32)))
        return found

    for d in range(count):
        for _, _, value in read(d):
            squares = squares + jnp.sum(value * value, axis=1, keepdims=True)
    inverse = lax.rsqrt(squares / (count * slab) + EPS_NORM)
    for d in range(count):
        for offset, width, value in read(d):
            start = pl.multiple_of(info[table.place + d] * slab + offset, HD)
            cols = pl.ds(start, width)
            out_ref[:, cols] = (value * inverse * g_ref[:, cols]).astype(jnp.bfloat16)


def norm_into(table, info, buffer, blocks, raw_hidden, gain, begin, rows, keep, slab, total_rows):
    width = table.count * slab
    step = min(rows, 32)
    steps, first = rows // step, begin // step
    args = [gain.reshape(1, width), *blocks]
    in_specs = [pl.BlockSpec((1, width), lambda i, info: (0, 0))]
    in_specs += line_spec(blocks, step, lambda i: i)
    if raw_hidden is not None:
        args.append(raw_hidden)
        in_specs.append(
            pl.BlockSpec((step, raw_hidden.shape[1]), lambda i, info: (first + i, 0))
        )
    aliases = {}
    if buffer is not None:
        args.append(buffer)
        in_specs.append(ANYWHERE)
        aliases = {len(args): 0}
    return call(
        functools.partial(norm_kernel, table, len(blocks), keep, slab),
        "norm",
        info,
        args,
        in_specs,
        pl.BlockSpec((step, width), lambda i, info: (first + i, 0)),
        jax.ShapeDtypeStruct((total_rows, width), jnp.bfloat16),
        grid=(steps,),
        aliases=aliases,
    )


def per_device(queries, span_kv, cache, lengths, offset, out_weight, residual, gain):
    rows = queries.shape[0]
    heads = queries.shape[1] // HD
    depth = out_weight.shape[0]
    slab = residual.shape[1]
    contexts = lax.axis_size("context")
    count = lax.axis_size("tensor")
    context_index = lax.axis_index("context")
    tensor_index = lax.axis_index("tensor")
    kv_index = tensor_index * heads // GROUP
    groups = lax.axis_size("groups")
    shares = groups * contexts
    share = lax.axis_index("groups") * contexts + context_index
    raw = slab // RAW_PART if slab % (RAW_PART * HD) == 0 else 0
    keep = slab - raw
    chunk = min(CHUNK, rows)
    sizes = [chunk] * (rows // chunk)
    splits = [(sum(sizes[:n]), size) for n, size in enumerate(sizes)]

    table = Table(contexts, count)
    steering = [context_index, *owners_of(contexts, context_index)]
    steering += [lax.rem(tensor_index + (count - d), count) for d in range(count)]
    steering += [tensor_index == 0, tensor_index == count - 1, share]
    steering += plane_owners(shares, share)
    info = jnp.stack([jnp.asarray(v).astype(jnp.int32) for v in steering])

    cache_local = lax.dynamic_index_in_dim(cache, kv_index, 0, keepdims=False)
    span_local = lax.dynamic_index_in_dim(span_kv, kv_index, 1, keepdims=False)
    positions = offset[0] + context_index * rows + jnp.arange(rows, dtype=jnp.int32)
    both = jnp.concatenate([frequencies(HD)] * 2)
    angles = positions.astype(jnp.float32)[:, None] * both[None, :]
    sign = jnp.where(jnp.arange(HD) < HD // 2, -1.0, 1.0)
    q_turned, payload, *cuts = prepare(
        table, info, queries, span_local, cache_local, out_weight, jnp.cos(angles),
        jnp.sin(angles) * sign[None, :], lengths, depth // shares, slab, keep,
    )
    parts = [cuts[0]]
    for shift in range(1, count):
        pairs = [(i, (i + shift) % count) for i in range(count)]
        parts.append(lax.ppermute(cuts[shift], "tensor", pairs))
    sent = []

    def between(block):
        sent.append(stack(info, parts, []))
        if raw:
            sent.extend(last_columns(info, residual, raw, parts[1:]))
        return gate(info, block, sent)

    pieces = pieces_of(payload, "context", contexts, between)
    mixed = attend(table, info, q_turned, pieces, cache_local.shape[0], chunk)
    residuals = []
    if raw and count == 4:
        residuals = [sent[2], *line_near(sent[2]), *line_far(sent[1])]
    elif raw:
        residuals = line_gather(sent[1], count)
    ready = gate(info, mixed, residuals[1:4]) if raw else mixed
    attention = line_gather(ready, count)
    weights = plane_gather(
        sent[0],
        groups,
        contexts,
        lambda block: gate(info, block, [mixed]),
        lambda block, mask: gate(info, block, attention[1 : 3 if mask & (mask - 1) == 0 else 5]),
    )

    *hidden_parts, hidden = project(
        table, info, attention, weights, residual, keep, chunk, splits
    )
    raw_hidden = None
    if raw:
        raw_hidden, hidden = project_raw(
            table, info, attention, residuals, weights, hidden, keep, raw, chunk
        )
    lines = chunk_gathers(
        info,
        hidden_parts[: len(splits)],
        hidden_parts[len(splits) :],
        residuals[4:],
        [raw_hidden] if raw else [],
        count,
    )
    normed = None
    for (begin, size), blocks in zip(splits, lines):
        normed = norm_into(
            table, info, normed, blocks, raw_hidden, gain, begin, size, keep, slab, rows
        )
    return (hidden, normed)


def solution(mesh):
    in_specs = (
        P(("groups", "context"), "tensor"),
        P(("groups", "context"), None, None),
        P("groups", "context", None),
        P(("groups", "context")),
        P("groups"),
        P("tensor", None),
        P(("groups", "context"), "tensor"),
        P(),
    )
    out_specs = (P(("groups", "context"), "tensor"), P(("groups", "context"), None))
    return jax.shard_map(
        per_device, mesh=mesh, in_specs=in_specs, out_specs=out_specs, check_vma=False
    )
```

```python
import functools
import math

import jax
import jax.numpy as jnp
from jax import lax
from jax.experimental import pallas as pl
from jax.experimental.pallas import tpu as pltpu
from jax.sharding import PartitionSpec as P

GROUP = 8
HD = 128
NEG = -1e30
EPS_NORM = 1e-05
MIB = 1024 * 1024
CHUNK = 128
KEY_BLOCK = 512
ATTEND_FLOPS = 16
RAW_PART = 4
TAIL = 16
DIGIT = 32
ANYWHERE = pl.BlockSpec(memory_space=pl.ANY)


def frequencies(head_width):
    counter = jnp.arange(head_width // 2, dtype=jnp.float32)
    base_freq = jnp.exp(-(2.0 * counter / head_width) * math.log(500000.0))
    wavelength = 2.0 * math.pi / base_freq
    smoothing = (8192.0 / wavelength - 1.0) / 3.0
    blended = (1.0 - smoothing) * base_freq / 8.0 + smoothing * base_freq
    return jnp.where(
        wavelength < 2048.0, base_freq, jnp.where(wavelength > 8192.0, base_freq / 8.0, blended)
    )


def pieces_of(value, axis, count, between=lambda block: block):
    if count & (count - 1) == 0:
        held = {0: value}
        bit = count // 2
        while bit:
            pairs = [(i, i ^ bit) for i in range(count)]
            for mask in sorted(held):
                held[mask | bit] = lax.ppermute(held[mask], axis, pairs)
            if bit == count // 2:
                held[bit] = between(held[bit])
            bit //= 2
        return [held[mask] for mask in range(count)]
    blocks = [value]
    for shift in range(1, count):
        pairs = [(i, (i + shift) % count) for i in range(count)]
        blocks.append(lax.ppermute(value, axis, pairs))
    blocks[-1] = between(blocks[-1])
    return blocks


def owners_of(count, me):
    if count & (count - 1) == 0:
        return [me ^ mask for mask in range(count)]
    return [(me + count - shift) % count for shift in range(count)]


def plane_gather(value, groups, contexts, first, then):
    count = groups * contexts
    if count & (count - 1):
        gathered = lax.all_gather(value, ("groups", "context"), axis=0, tiled=False)
        return [gathered[number] for number in range(count)]
    held = {0: value}
    bits = [1 << b for b in range(contexts.bit_length() - 2, 0, -1)]
    bits += [contexts << b for b in range(groups.bit_length() - 1)]
    for bit in bits:
        axis, flip, size = ("context", bit, contexts)
        if bit >= contexts:
            axis, flip, size = ("groups", bit // contexts, groups)
        pairs = [(i, i ^ flip) for i in range(size)]
        for mask in sorted(held):
            held[mask | bit] = lax.ppermute(held[mask], axis, pairs)
        if bit == bits[0]:
            held[bit] = first(held[bit])
    if contexts > 1:
        for mask in sorted(held):
            held[mask] = then(held[mask], mask) if mask else held[mask]
            held[mask | 1] = core_swap(held[mask], contexts)
    return [held[mask] for mask in range(count)]


def core_swap(value, contexts):
    return lax.ppermute(value, "context", [(i, i ^ 1) for i in range(contexts)])


def plane_owners(count, me):
    if count & (count - 1):
        return list(range(count))
    return [me ^ mask for mask in range(count)]


def line_gather(value, count):
    if count != 4:
        return [lax.all_gather(value, "tensor", axis=0, tiled=False)]
    far, last = line_far(value)
    return [value, *line_near(value), far, last]


def line_near(value):
    up = lax.ppermute(value, "tensor", [(0, 1), (1, 2), (2, 3)])
    return up, lax.ppermute(value, "tensor", [(1, 0), (2, 1), (3, 2)])


def line_far(value):
    far = lax.ppermute(value, "tensor", [(0, 2), (1, 3), (2, 0), (3, 1)])
    return far, lax.ppermute(far, "tensor", [(1, 0), (2, 3)])


def chunk_gathers(info, values, copies, first, made, count):
    if count != 4:
        return [line_gather(value, count) for value in values]
    fars, lines = [], []
    for number, value in enumerate(values):
        after = [fars[-1][0]] if number else first
        fars.append(line_far(gate(info, value, after) if after else value))
    for number, value in enumerate(copies):
        after = list(lines[number - 1][1:3]) if number else []
        if number > 1:
            after.append(fars[number - 2][1])
        if number == len(copies) // 2:
            after += made
        value = gate(info, value, after) if after else value
        lines.append([value, *line_near(value), *fars[number]])
    return lines


class Table:
    def __init__(self, contexts, count):
        self.contexts, self.count = contexts, count
        self.owner = 1
        self.place = 1 + contexts
        self.low = self.place + count
        self.high = self.low + 1
        self.share = self.low + 2
        self.rows = self.low + 3


def line_read(table, info, refs, d, cols=slice(None)):
    if len(refs) == 1:
        return refs[0][info[table.place + d], :, cols].astype(jnp.float32)
    if d == 0:
        return refs[0][:, cols].astype(jnp.float32)
    if d == 2:
        return refs[3][:, cols].astype(jnp.float32)
    near = refs[1 if d == 1 else 2][:, cols].astype(jnp.float32)
    other = refs[4][:, cols].astype(jnp.float32)
    at_end = info[table.low if d == 1 else table.high]
    return jnp.where(at_end == 1, other, near)


def line_spec(blocks, rows, index):
    if len(blocks) == 1:
        count, _, width = blocks[0].shape
        return [pl.BlockSpec((count, rows, width), lambda i, info: (0, index(i), 0))]
    width = blocks[0].shape[1]
    return [pl.BlockSpec((rows, width), lambda i, info: (index(i), 0)) for _ in blocks]


def call(kernel, name, info, args, in_specs, out_specs, out_shape, grid=(1,), aliases=None,
         scratch=(), flops=1, vmem=16):
    return pl.pallas_call(
        kernel,
        grid_spec=pltpu.PrefetchScalarGridSpec(
            num_scalar_prefetch=1,
            grid=grid,
            in_specs=in_specs,
            out_specs=out_specs,
            scratch_shapes=list(scratch),
        ),
        out_shape=out_shape,
        input_output_aliases=aliases or {},
        compiler_params=pltpu.CompilerParams(vmem_limit_bytes=vmem * MIB or None),
        cost_estimate=pl.CostEstimate(flops=flops, bytes_accessed=1, transcendentals=0),
        name=name,
    )(info, *args)


def whole(a):
    zeros = (0,) * len(a.shape)
    return pl.BlockSpec(tuple(a.shape), lambda i, info: zeros)


def prepare_kernel(table, slab, keep, info, q_hbm, kv_hbm, cache_hbm, w_hbm, cos_ref, sin_ref,
                   length_ref, *refs):
    count, raw = table.count, slab - keep
    q_out, kv_out, outs = refs[0], refs[1], refs[2 : 2 + count]
    q_ref, kv_ref, w_ref, sems = refs[2 + count :]
    slots, rows, part = cache_hbm.shape[0], q_ref.shape[0], w_ref.shape[0]
    span, tail = slice(slots, slots + rows), slice(slots + rows, slots + rows + TAIL)
    start = pl.multiple_of(info[table.share] * part, part)
    moves = [
        (w_hbm.at[pl.ds(start, part)], w_ref),
        (kv_hbm, kv_ref),
        (q_hbm, q_ref),
        (cache_hbm, kv_out.at[pl.ds(0, slots)]),
    ]
    copies = [pltpu.make_async_copy(*move, sems.at[n]) for n, move in enumerate(moves)]
    for copy in copies:
        copy.start()

    copies[0].wait()
    for d, out in enumerate(outs):
        target = lax.rem(info[table.place] + d, count)
        out[:, :keep] = w_ref[:, pl.ds(pl.multiple_of(target * slab, slab), keep)]
        for j in range(count if raw else 0):
            out[:, keep + j * raw : keep + (j + 1) * raw] = w_ref[
                :, j * slab + keep : (j + 1) * slab
            ]

    cosine, sine = cos_ref[...], sin_ref[...]

    def turn(block):
        block = block.astype(jnp.float32)
        return (block * cosine + pltpu.roll(block, HD // 2, 1) * sine).astype(jnp.bfloat16)

    copies[1].wait()
    kv_out[span, :HD] = turn(kv_ref[:, :HD])
    kv_out[span, HD:] = kv_ref[:, HD:]
    length = length_ref[0]
    upper = lax.div(length, DIGIT)
    lower = length - upper * DIGIT
    kv_out[tail, :HD] = jnp.full((TAIL, HD), upper.astype(jnp.float32)).astype(jnp.bfloat16)
    kv_out[tail, HD:] = jnp.full((TAIL, HD), lower.astype(jnp.float32)).astype(jnp.bfloat16)
    copies[2].wait()
    for head in range(q_ref.shape[1] // HD):
        cols = slice(head * HD, (head + 1) * HD)
        q_out[:, cols] = turn(q_ref[:, cols])
    copies[3].wait()


def prepare(table, info, queries, span_pairs, cache, out_weight, cosine, sine, lengths, part,
            slab, keep):
    rows = queries.shape[0]
    shapes = [
        jax.ShapeDtypeStruct(queries.shape, jnp.bfloat16),
        jax.ShapeDtypeStruct((cache.shape[0] + rows + TAIL, 2 * HD), jnp.bfloat16),
    ]
    width = keep + table.count * (slab - keep)
    shapes += [jax.ShapeDtypeStruct((part, width), out_weight.dtype)] * table.count
    return call(
        functools.partial(prepare_kernel, table, slab, keep),
        "prepare",
        info,
        [queries, span_pairs, cache, out_weight, cosine, sine, lengths],
        [ANYWHERE] * 4
        + [whole(cosine), whole(sine), pl.BlockSpec(memory_space=pltpu.SMEM)],
        [whole(shape) for shape in shapes],
        shapes,
        scratch=[
            pltpu.VMEM(queries.shape, jnp.bfloat16),
            pltpu.VMEM(span_pairs.shape, jnp.bfloat16),
            pltpu.VMEM((part, out_weight.shape[1]), out_weight.dtype),
            pltpu.SemaphoreType.DMA((4,)),
        ],
        vmem=0,
    )


def last_columns_kernel(info, *refs):
    refs[-1][...] = refs[0][...]
    refs[-2][...] = refs[0][...]


def last_columns(info, value, width, after):
    rows, full = value.shape
    shape = jax.ShapeDtypeStruct((rows, width), value.dtype)
    return call(
        last_columns_kernel,
        "last_columns",
        info,
        [value, *after],
        [pl.BlockSpec((rows, width), lambda i, info: (0, full // width - 1))]
        + [ANYWHERE] * len(after),
        [whole(shape)] * 2,
        [shape] * 2,
    )


def stack_kernel(count, info, *refs):
    for number, part in enumerate(refs[:count]):
        refs[-1][number] = part[...]


def stack(info, parts, after):
    shape = jax.ShapeDtypeStruct((len(parts), *parts[0].shape), parts[0].dtype)
    return call(
        functools.partial(stack_kernel, len(parts)),
        "stack",
        info,
        [*parts, *after],
        [whole(p) for p in parts] + [ANYWHERE] * len(after),
        whole(shape),
        shape,
    )


def gate_kernel(info, *refs):
    pass


def gate(info, value, after):
    return call(
        gate_kernel,
        "gate",
        info,
        [value, *after],
        [ANYWHERE] * (1 + len(after)),
        ANYWHERE,
        jax.ShapeDtypeStruct(value.shape, value.dtype),
        aliases={1: 0},
    )


def attend_kernel(table, slots, info, q_ref, *refs):
    count = table.contexts
    pieces, out_ref, s_ref = refs[:count], refs[-2], refs[-1]
    rows = q_ref.shape[0]
    heads = q_ref.shape[1] // HD
    chunk = pl.program_id(0)
    mine = info[0]
    q = jnp.concatenate([q_ref[:, h * HD : (h + 1) * HD] for h in range(heads)], axis=0)
    exponent = math.log2(math.e) / math.sqrt(HD)

    blocks = []
    peak = jnp.full((heads * rows, HD), NEG, jnp.float32)
    column = 0
    for kind in ("cache", "span"):
        for number, ref in enumerate(pieces):
            tail = ref.shape[0] - TAIL
            first, last = (0, slots) if kind == "cache" else (slots, tail)
            width = min(KEY_BLOCK, last - first)
            length = ref[tail : tail + 1, :HD].astype(jnp.float32) * DIGIT + ref[
                tail : tail + 1, HD:
            ].astype(jnp.float32)
            length = jnp.concatenate([length] * (width // HD), axis=1)
            for begin in range(first, last, width):
                scores = lax.dot_general(
                    q,
                    ref[begin : begin + width, :HD],
                    (((1,), (1,)), ((), ())),
                    preferred_element_type=jnp.float32,
                )
                if kind == "cache":
                    slot = lax.broadcasted_iota(jnp.int32, (1, width), 1) + begin
                    live = slot.astype(jnp.float32) < length
                    scores = scores + jnp.where(live, 0.0, NEG)
                elif number == 0:
                    key = lax.broadcasted_iota(jnp.int32, (rows, width), 1) + (begin - first)
                    row = lax.broadcasted_iota(jnp.int32, (rows, width), 0) + chunk * rows
                    bias = jnp.where(key <= row, 0.0, NEG)
                    scores = scores + jnp.concatenate([bias] * heads, axis=0)
                else:
                    scores = scores + jnp.where(info[table.owner + number] < mine, 0.0, NEG)
                s_ref[:, column : column + width] = scores
                for lane in range(0, width, HD):
                    peak = jnp.maximum(peak, scores[:, lane : lane + HD])
                blocks.append((ref, begin, column, width))
                column += width
    top = jnp.max(peak, axis=1, keepdims=True)
    total = jnp.zeros((heads * rows, HD), jnp.float32)
    mixed = jnp.zeros((heads * rows, HD), jnp.float32)
    for ref, begin, column, width in blocks:
        weights = jnp.exp2((s_ref[:, column : column + width] - top) * exponent)
        for lane in range(0, width, HD):
            total = total + weights[:, lane : lane + HD]
        mixed = mixed + jnp.dot(
            weights.astype(jnp.bfloat16),
            ref[begin : begin + width, HD:],
            preferred_element_type=jnp.float32,
        )
    result = (mixed / jnp.sum(total, axis=1, keepdims=True)).astype(jnp.bfloat16)
    for h in range(heads):
        out_ref[:, h * HD : (h + 1) * HD] = result[h * rows : (h + 1) * rows]


def attend(table, info, queries, pieces, slots, rows):
    all_rows, width = queries.shape
    heads = width // HD
    keys = sum(a.shape[0] - TAIL for a in pieces)
    chunk_spec = pl.BlockSpec((rows, width), lambda i, info: (i, 0))
    return call(
        functools.partial(attend_kernel, table, slots),
        "attend",
        info,
        [queries, *pieces],
        [chunk_spec] + [whole(a) for a in pieces],
        chunk_spec,
        jax.ShapeDtypeStruct((all_rows, width), jnp.bfloat16),
        grid=(all_rows // rows,),
        scratch=[pltpu.VMEM((heads * rows, keys), jnp.float32)],
        flops=ATTEND_FLOPS * all_rows * heads * keys * HD,
        vmem=28,
    )


def place_weights(table, info, pieces, w_ref, begin):
    part, width = pieces[0].shape[1], w_ref.shape[2]
    for number, piece in enumerate(pieces):
        start = pl.multiple_of(info[table.rows + number] * part, part)
        for d in range(table.count):
            w_ref[d, pl.ds(start, part)] = piece[d, :, begin : begin + width]


def project_kernel(table, lines, shares, keep, splits, info, *refs):
    count = table.count
    attention, pieces = refs[:lines], refs[lines : lines + shares]
    r_ref = refs[lines + shares]
    parts, h_ref, w_ref = refs[-2 - 2 * len(splits) : -2], refs[-2], refs[-1]
    rows = r_ref.shape[0]

    @pl.when(pl.program_id(0) == 0)
    def _():
        place_weights(table, info, pieces, w_ref, 0)

    total = r_ref[:, :keep].astype(jnp.float32)
    for d in range(count):
        block = line_read(table, info, attention, d).astype(jnp.bfloat16)
        total = total + jnp.dot(block, w_ref[d], preferred_element_type=jnp.float32)
    result = total.astype(jnp.bfloat16)
    h_ref[:, :keep] = result
    for part, (begin, size) in zip(parts, splits * 2):
        for row in range(begin, begin + size, rows):

            @pl.when(pl.program_id(0) == row // rows)
            def _():
                part[row - begin : row - begin + rows] = result


def project(table, info, attention, pieces, residual, keep, rows, splits):
    all_rows, slab = residual.shape
    count, part_rows, _ = pieces[0].shape
    parts = [jax.ShapeDtypeStruct((size, keep), jnp.bfloat16) for _, size in splits * 2]
    row_spec = pl.BlockSpec((rows, slab), lambda i, info: (i, 0))
    return call(
        functools.partial(project_kernel, table, len(attention), len(pieces), keep, splits),
        "project",
        info,
        [*attention, *pieces, residual],
        line_spec(attention, rows, lambda i: i)
        + [whole(p) for p in pieces]
        + [row_spec],
        [whole(part) for part in parts] + [row_spec],
        [*parts, jax.ShapeDtypeStruct(residual.shape, jnp.bfloat16)],
        grid=(all_rows // rows,),
        scratch=[pltpu.VMEM((count, len(pieces) * part_rows, keep), jnp.bfloat16)],
        vmem=36,
    )


def project_raw_kernel(table, lines, raw_lines, shares, keep, info, *refs):
    count = table.count
    attention, residuals = refs[:lines], refs[lines : lines + raw_lines]
    pieces = refs[lines + raw_lines : lines + raw_lines + shares]
    raw_ref, h_ref, w_ref = refs[-3:]
    raw = h_ref.shape[1]

    @pl.when(pl.program_id(0) == 0)
    def _():
        place_weights(table, info, pieces, w_ref, keep)

    blocks = [
        line_read(table, info, attention, d).astype(jnp.bfloat16) for d in range(count)
    ]
    for slab in range(count):
        cols = pl.ds(pl.multiple_of(info[table.place + slab] * raw, raw), raw)
        total = line_read(table, info, residuals, slab)
        for d in range(count):
            total = total + jnp.dot(
                blocks[d], w_ref[d, :, cols], preferred_element_type=jnp.float32
            )
        result = total.astype(jnp.bfloat16)
        raw_ref[:, slab * raw : (slab + 1) * raw] = result
        if slab == 0:
            h_ref[...] = result


def project_raw(table, info, attention, residuals, pieces, hidden, keep, raw, rows):
    all_rows, slab = hidden.shape
    count, part_rows, _ = pieces[0].shape
    args = [*attention, *residuals, *pieces, hidden]
    out = jax.ShapeDtypeStruct((all_rows, count * raw), jnp.bfloat16)
    return call(
        functools.partial(
            project_raw_kernel, table, len(attention), len(residuals), len(pieces), keep
        ),
        "project_raw",
        info,
        args,
        line_spec(attention, rows, lambda i: i)
        + line_spec(residuals, rows, lambda i: i)
        + [whole(p) for p in pieces]
        + [ANYWHERE],
        [
            pl.BlockSpec((rows, count * raw), lambda i, info: (i, 0)),
            pl.BlockSpec((rows, raw), lambda i, info: (i, slab // raw - 1)),
        ],
        [out, jax.ShapeDtypeStruct(hidden.shape, jnp.bfloat16)],
        grid=(all_rows // rows,),
        aliases={len(args): 1},
        scratch=[pltpu.VMEM((count, len(pieces) * part_rows, count * raw), jnp.bfloat16)],
        vmem=36,
    )


def norm_kernel(table, lines, keep, slab, info, g_ref, *refs):
    count = table.count
    blocks, out_ref = refs[:lines], refs[-1]
    raw = slab - keep
    values = []
    squares = jnp.zeros((out_ref.shape[0], 1), jnp.float32)

    def read(d):
        found = [(0, keep, line_read(table, info, blocks, d))]
        if raw:
            cols = slice(d * raw, (d + 1) * raw)
            found.append((keep, raw, refs[lines][:, cols].astype(jnp.float32)))
        return found

    for d in range(count):
        for _, _, value in read(d):
            squares = squares + jnp.sum(value * value, axis=1, keepdims=True)
    inverse = lax.rsqrt(squares / (count * slab) + EPS_NORM)
    for d in range(count):
        for offset, width, value in read(d):
            start = pl.multiple_of(info[table.place + d] * slab + offset, HD)
            cols = pl.ds(start, width)
            out_ref[:, cols] = (value * inverse * g_ref[:, cols]).astype(jnp.bfloat16)


def norm_into(table, info, buffer, blocks, raw_hidden, gain, begin, rows, keep, slab, total_rows):
    width = table.count * slab
    step = min(rows, 32)
    steps, first = rows // step, begin // step
    args = [gain.reshape(1, width), *blocks]
    in_specs = [pl.BlockSpec((1, width), lambda i, info: (0, 0))]
    in_specs += line_spec(blocks, step, lambda i: i)
    if raw_hidden is not None:
        args.append(raw_hidden)
        in_specs.append(
            pl.BlockSpec((step, raw_hidden.shape[1]), lambda i, info: (first + i, 0))
        )
    aliases = {}
    if buffer is not None:
        args.append(buffer)
        in_specs.append(ANYWHERE)
        aliases = {len(args): 0}
    return call(
        functools.partial(norm_kernel, table, len(blocks), keep, slab),
        "norm",
        info,
        args,
        in_specs,
        pl.BlockSpec((step, width), lambda i, info: (first + i, 0)),
        jax.ShapeDtypeStruct((total_rows, width), jnp.bfloat16),
        grid=(steps,),
        aliases=aliases,
    )


def per_device(queries, span_kv, cache, lengths, offset, out_weight, residual, gain):
    rows = queries.shape[0]
    heads = queries.shape[1] // HD
    depth = out_weight.shape[0]
    slab = residual.shape[1]
    contexts = lax.axis_size("context")
    count = lax.axis_size("tensor")
    context_index = lax.axis_index("context")
    tensor_index = lax.axis_index("tensor")
    kv_index = tensor_index * heads // GROUP
    groups = lax.axis_size("groups")
    shares = groups * contexts
    share = lax.axis_index("groups") * contexts + context_index
    raw = slab // RAW_PART if slab % (RAW_PART * HD) == 0 else 0
    keep = slab - raw
    chunk = min(CHUNK, rows)
    sizes = [chunk] * (rows // chunk)
    splits = [(sum(sizes[:n]), size) for n, size in enumerate(sizes)]

    table = Table(contexts, count)
    steering = [context_index, *owners_of(contexts, context_index)]
    steering += [lax.rem(tensor_index + (count - d), count) for d in range(count)]
    steering += [tensor_index == 0, tensor_index == count - 1, share]
    steering += plane_owners(shares, share)
    info = jnp.stack([jnp.asarray(v).astype(jnp.int32) for v in steering])

    cache_local = lax.dynamic_index_in_dim(cache, kv_index, 0, keepdims=False)
    span_local = lax.dynamic_index_in_dim(span_kv, kv_index, 1, keepdims=False)
    positions = offset[0] + context_index * rows + jnp.arange(rows, dtype=jnp.int32)
    both = jnp.concatenate([frequencies(HD)] * 2)
    angles = positions.astype(jnp.float32)[:, None] * both[None, :]
    sign = jnp.where(jnp.arange(HD) < HD // 2, -1.0, 1.0)
    q_turned, payload, *cuts = prepare(
        table, info, queries, span_local, cache_local, out_weight, jnp.cos(angles),
        jnp.sin(angles) * sign[None, :], lengths, depth // shares, slab, keep,
    )
    parts = [cuts[0]]
    for shift in range(1, count):
        pairs = [(i, (i + shift) % count) for i in range(count)]
        parts.append(lax.ppermute(cuts[shift], "tensor", pairs))
    sent = []

    def between(block):
        sent.append(stack(info, parts, []))
        if raw:
            sent.extend(last_columns(info, residual, raw, parts[1:]))
        return gate(info, block, sent)

    pieces = pieces_of(payload, "context", contexts, between)
    mixed = attend(table, info, q_turned, pieces, cache_local.shape[0], chunk)
    residuals = []
    if raw and count == 4:
        early = line_far(sent[1])
        attention = line_gather(gate(info, mixed, early[:1]), count)
        near = gate(info, sent[2], attention[3:4])
        residuals = [near, *line_near(near), *early]
    else:
        attention = line_gather(mixed, count)
        residuals = line_gather(sent[1], count) if raw else []
    weights = plane_gather(
        sent[0],
        groups,
        contexts,
        lambda block: gate(info, block, [mixed]),
        lambda block, mask: gate(info, block, attention[3:4] if mask in (mask & -mask,) else attention[1:]),
    )

    *hidden_parts, hidden = project(
        table, info, attention, weights, residual, keep, chunk, splits
    )
    raw_hidden = None
    if raw:
        raw_hidden, hidden = project_raw(
            table, info, attention, residuals, weights, hidden, keep, raw, chunk
        )
    lines = chunk_gathers(
        info,
        hidden_parts[: len(splits)],
        hidden_parts[len(splits) :],
        [*residuals[1:3], *residuals[4:]],
        [raw_hidden] if raw else [],
        count,
    )
    normed = None
    for (begin, size), blocks in zip(splits, lines):
        normed = norm_into(
            table, info, normed, blocks, raw_hidden, gain, begin, size, keep, slab, rows
        )
    return (hidden, normed)


def solution(mesh):
    in_specs = (
        P(("groups", "context"), "tensor"),
        P(("groups", "context"), None, None),
        P("groups", "context", None),
        P(("groups", "context")),
        P("groups"),
        P("tensor", None),
        P(("groups", "context"), "tensor"),
        P(),
    )
    out_specs = (P(("groups", "context"), "tensor"), P(("groups", "context"), None))
    return jax.shard_map(
        per_device, mesh=mesh, in_specs=in_specs, out_specs=out_specs, check_vma=False
    )
```

```python
import functools
import math

import jax
import jax.numpy as jnp
from jax import lax
from jax.experimental import pallas as pl
from jax.experimental.pallas import tpu as pltpu
from jax.sharding import PartitionSpec as P

GROUP = 8
HD = 128
NEG = -1e30
EPS_NORM = 1e-05
MIB = 1024 * 1024
CHUNK = 128
KEY_BLOCK = 512
ATTEND_FLOPS = 16
RAW_PART = 8
TAIL = 16
DIGIT = 32
ANYWHERE = pl.BlockSpec(memory_space=pl.ANY)


def frequencies(head_width):
    counter = jnp.arange(head_width // 2, dtype=jnp.float32)
    base_freq = jnp.exp(-(2.0 * counter / head_width) * math.log(500000.0))
    wavelength = 2.0 * math.pi / base_freq
    smoothing = (8192.0 / wavelength - 1.0) / 3.0
    blended = (1.0 - smoothing) * base_freq / 8.0 + smoothing * base_freq
    return jnp.where(
        wavelength < 2048.0, base_freq, jnp.where(wavelength > 8192.0, base_freq / 8.0, blended)
    )


def pieces_of(value, axis, count, between=lambda block: block):
    if count & (count - 1) == 0:
        held = {0: value}
        bit = count // 2
        while bit:
            pairs = [(i, i ^ bit) for i in range(count)]
            for mask in sorted(held):
                held[mask | bit] = lax.ppermute(held[mask], axis, pairs)
            if bit == count // 2:
                held[bit] = between(held[bit])
            bit //= 2
        return [held[mask] for mask in range(count)]
    blocks = [value]
    for shift in range(1, count):
        pairs = [(i, (i + shift) % count) for i in range(count)]
        blocks.append(lax.ppermute(value, axis, pairs))
    blocks[-1] = between(blocks[-1])
    return blocks


def owners_of(count, me):
    if count & (count - 1) == 0:
        return [me ^ mask for mask in range(count)]
    return [(me + count - shift) % count for shift in range(count)]


def plane_gather(value, groups, contexts, first, then):
    count = groups * contexts
    if count & (count - 1):
        gathered = lax.all_gather(value, ("groups", "context"), axis=0, tiled=False)
        return [gathered[number] for number in range(count)]
    held = {0: value}
    bits = [1 << b for b in range(contexts.bit_length() - 2, 0, -1)]
    bits += [contexts << b for b in range(groups.bit_length() - 1)]
    for bit in bits:
        axis, flip, size = ("context", bit, contexts)
        if bit >= contexts:
            axis, flip, size = ("groups", bit // contexts, groups)
        pairs = [(i, i ^ flip) for i in range(size)]
        for mask in sorted(held):
            held[mask | bit] = lax.ppermute(held[mask], axis, pairs)
        if bit == bits[0]:
            held[bit] = first(held[bit])
    if contexts > 1:
        for mask in sorted(held):
            held[mask] = then(held[mask], mask) if mask else held[mask]
            held[mask | 1] = core_swap(held[mask], contexts)
    return [held[mask] for mask in range(count)]


def core_swap(value, contexts):
    return lax.ppermute(value, "context", [(i, i ^ 1) for i in range(contexts)])


def plane_owners(count, me):
    if count & (count - 1):
        return list(range(count))
    return [me ^ mask for mask in range(count)]


def line_gather(value, count):
    if count != 4:
        return [lax.all_gather(value, "tensor", axis=0, tiled=False)]
    far, last = line_far(value)
    return [value, *line_near(value), far, last]


def line_near(value):
    up = lax.ppermute(value, "tensor", [(0, 1), (1, 2), (2, 3)])
    return up, lax.ppermute(value, "tensor", [(1, 0), (2, 1), (3, 2)])


def line_far(value):
    far = lax.ppermute(value, "tensor", [(0, 2), (1, 3), (2, 0), (3, 1)])
    return far, lax.ppermute(far, "tensor", [(1, 0), (2, 3)])


def chunk_gathers(info, values, copies, first, made, count):
    if count != 4:
        return [line_gather(value, count) for value in values]
    fars, lines = [], []
    for number, value in enumerate(values):
        fars.append(line_far(gate(info, value, [fars[-1][0]]) if number else value))
    for number, value in enumerate(copies):
        after = list(lines[number - 1][1:3]) if number else []
        if number > 1:
            after.append(fars[number - 2][1])
        if number == 1:
            after += first
        if number == len(copies) // 2:
            after += made
        value = gate(info, value, after) if after else value
        lines.append([value, *line_near(value), *fars[number]])
    return lines


class Table:
    def __init__(self, contexts, count):
        self.contexts, self.count = contexts, count
        self.owner = 1
        self.place = 1 + contexts
        self.low = self.place + count
        self.high = self.low + 1
        self.share = self.low + 2
        self.rows = self.low + 3


def line_read(table, info, refs, d, cols=slice(None)):
    if len(refs) == 1:
        return refs[0][info[table.place + d], :, cols].astype(jnp.float32)
    if d == 0:
        return refs[0][:, cols].astype(jnp.float32)
    if d == 2:
        return refs[3][:, cols].astype(jnp.float32)
    near = refs[1 if d == 1 else 2][:, cols].astype(jnp.float32)
    other = refs[4][:, cols].astype(jnp.float32)
    at_end = info[table.low if d == 1 else table.high]
    return jnp.where(at_end == 1, other, near)


def line_spec(blocks, rows, index):
    if len(blocks) == 1:
        count, _, width = blocks[0].shape
        return [pl.BlockSpec((count, rows, width), lambda i, info: (0, index(i), 0))]
    width = blocks[0].shape[1]
    return [pl.BlockSpec((rows, width), lambda i, info: (index(i), 0)) for _ in blocks]


def call(kernel, name, info, args, in_specs, out_specs, out_shape, grid=(1,), aliases=None,
         scratch=(), flops=1, vmem=16):
    return pl.pallas_call(
        kernel,
        grid_spec=pltpu.PrefetchScalarGridSpec(
            num_scalar_prefetch=1,
            grid=grid,
            in_specs=in_specs,
            out_specs=out_specs,
            scratch_shapes=list(scratch),
        ),
        out_shape=out_shape,
        input_output_aliases=aliases or {},
        compiler_params=pltpu.CompilerParams(vmem_limit_bytes=vmem * MIB or None),
        cost_estimate=pl.CostEstimate(flops=flops, bytes_accessed=1, transcendentals=0),
        name=name,
    )(info, *args)


def whole(a):
    zeros = (0,) * len(a.shape)
    return pl.BlockSpec(tuple(a.shape), lambda i, info: zeros)


def prepare_kernel(table, slab, keep, info, q_hbm, kv_hbm, cache_hbm, w_hbm, cos_ref, sin_ref,
                   length_ref, *refs):
    count, raw = table.count, slab - keep
    q_out, kv_out, outs = refs[0], refs[1], refs[2 : 2 + count]
    q_ref, kv_ref, w_ref, sems = refs[2 + count :]
    slots, rows, part = cache_hbm.shape[0], q_ref.shape[0], w_ref.shape[0]
    span, tail = slice(slots, slots + rows), slice(slots + rows, slots + rows + TAIL)
    start = pl.multiple_of(info[table.share] * part, part)
    moves = [
        (w_hbm.at[pl.ds(start, part)], w_ref),
        (kv_hbm, kv_ref),
        (q_hbm, q_ref),
        (cache_hbm, kv_out.at[pl.ds(0, slots)]),
    ]
    copies = [pltpu.make_async_copy(*move, sems.at[n]) for n, move in enumerate(moves)]
    for copy in copies:
        copy.start()

    copies[0].wait()
    for d, out in enumerate(outs):
        target = lax.rem(info[table.place] + d, count)
        out[:, :keep] = w_ref[:, pl.ds(pl.multiple_of(target * slab, slab), keep)]
        for j in range(count if raw else 0):
            out[:, keep + j * raw : keep + (j + 1) * raw] = w_ref[
                :, j * slab + keep : (j + 1) * slab
            ]

    cosine, sine = cos_ref[...], sin_ref[...]

    def turn(block):
        block = block.astype(jnp.float32)
        return (block * cosine + pltpu.roll(block, HD // 2, 1) * sine).astype(jnp.bfloat16)

    copies[1].wait()
    kv_out[span, :HD] = turn(kv_ref[:, :HD])
    kv_out[span, HD:] = kv_ref[:, HD:]
    length = length_ref[0]
    upper = lax.div(length, DIGIT)
    lower = length - upper * DIGIT
    kv_out[tail, :HD] = jnp.full((TAIL, HD), upper.astype(jnp.float32)).astype(jnp.bfloat16)
    kv_out[tail, HD:] = jnp.full((TAIL, HD), lower.astype(jnp.float32)).astype(jnp.bfloat16)
    copies[2].wait()
    for head in range(q_ref.shape[1] // HD):
        cols = slice(head * HD, (head + 1) * HD)
        q_out[:, cols] = turn(q_ref[:, cols])
    copies[3].wait()


def prepare(table, info, queries, span_pairs, cache, out_weight, cosine, sine, lengths, part,
            slab, keep):
    rows = queries.shape[0]
    shapes = [
        jax.ShapeDtypeStruct(queries.shape, jnp.bfloat16),
        jax.ShapeDtypeStruct((cache.shape[0] + rows + TAIL, 2 * HD), jnp.bfloat16),
    ]
    width = keep + table.count * (slab - keep)
    shapes += [jax.ShapeDtypeStruct((part, width), out_weight.dtype)] * table.count
    return call(
        functools.partial(prepare_kernel, table, slab, keep),
        "prepare",
        info,
        [queries, span_pairs, cache, out_weight, cosine, sine, lengths],
        [ANYWHERE] * 4
        + [whole(cosine), whole(sine), pl.BlockSpec(memory_space=pltpu.SMEM)],
        [whole(shape) for shape in shapes],
        shapes,
        scratch=[
            pltpu.VMEM(queries.shape, jnp.bfloat16),
            pltpu.VMEM(span_pairs.shape, jnp.bfloat16),
            pltpu.VMEM((part, out_weight.shape[1]), out_weight.dtype),
            pltpu.SemaphoreType.DMA((4,)),
        ],
        vmem=0,
    )


def last_columns_kernel(info, *refs):
    refs[-1][...] = refs[0][...]
    refs[-2][...] = refs[0][...]


def last_columns(info, value, width, after):
    rows, full = value.shape
    shape = jax.ShapeDtypeStruct((rows, width), value.dtype)
    return call(
        last_columns_kernel,
        "last_columns",
        info,
        [value, *after],
        [pl.BlockSpec((rows, width), lambda i, info: (0, full // width - 1))]
        + [ANYWHERE] * len(after),
        [whole(shape)] * 2,
        [shape] * 2,
    )


def stack_kernel(count, info, *refs):
    for number, part in enumerate(refs[:count]):
        refs[-1][number] = part[...]


def stack(info, parts, after):
    shape = jax.ShapeDtypeStruct((len(parts), *parts[0].shape), parts[0].dtype)
    return call(
        functools.partial(stack_kernel, len(parts)),
        "stack",
        info,
        [*parts, *after],
        [whole(p) for p in parts] + [ANYWHERE] * len(after),
        whole(shape),
        shape,
    )


def gate_kernel(info, *refs):
    pass


def gate(info, value, after):
    return call(
        gate_kernel,
        "gate",
        info,
        [value, *after],
        [ANYWHERE] * (1 + len(after)),
        ANYWHERE,
        jax.ShapeDtypeStruct(value.shape, value.dtype),
        aliases={1: 0},
    )


def attend_kernel(table, slots, info, q_ref, *refs):
    count = table.contexts
    pieces, out_ref, s_ref = refs[:count], refs[-2], refs[-1]
    rows = q_ref.shape[0]
    heads = q_ref.shape[1] // HD
    chunk = pl.program_id(0)
    mine = info[0]
    q = jnp.concatenate([q_ref[:, h * HD : (h + 1) * HD] for h in range(heads)], axis=0)
    exponent = math.log2(math.e) / math.sqrt(HD)

    blocks = []
    peak = jnp.full((heads * rows, HD), NEG, jnp.float32)
    column = 0
    for kind in ("cache", "span"):
        for number, ref in enumerate(pieces):
            tail = ref.shape[0] - TAIL
            first, last = (0, slots) if kind == "cache" else (slots, tail)
            width = min(KEY_BLOCK, last - first)
            length = ref[tail : tail + 1, :HD].astype(jnp.float32) * DIGIT + ref[
                tail : tail + 1, HD:
            ].astype(jnp.float32)
            length = jnp.concatenate([length] * (width // HD), axis=1)
            for begin in range(first, last, width):
                scores = lax.dot_general(
                    q,
                    ref[begin : begin + width, :HD],
                    (((1,), (1,)), ((), ())),
                    preferred_element_type=jnp.float32,
                )
                if kind == "cache":
                    slot = lax.broadcasted_iota(jnp.int32, (1, width), 1) + begin
                    live = slot.astype(jnp.float32) < length
                    scores = scores + jnp.where(live, 0.0, NEG)
                elif number == 0:
                    key = lax.broadcasted_iota(jnp.int32, (rows, width), 1) + (begin - first)
                    row = lax.broadcasted_iota(jnp.int32, (rows, width), 0) + chunk * rows
                    bias = jnp.where(key <= row, 0.0, NEG)
                    scores = scores + jnp.concatenate([bias] * heads, axis=0)
                else:
                    scores = scores + jnp.where(info[table.owner + number] < mine, 0.0, NEG)
                s_ref[:, column : column + width] = scores
                for lane in range(0, width, HD):
                    peak = jnp.maximum(peak, scores[:, lane : lane + HD])
                blocks.append((ref, begin, column, width))
                column += width
    top = jnp.max(peak, axis=1, keepdims=True)
    total = jnp.zeros((heads * rows, HD), jnp.float32)
    mixed = jnp.zeros((heads * rows, HD), jnp.float32)
    for ref, begin, column, width in blocks:
        weights = jnp.exp2((s_ref[:, column : column + width] - top) * exponent)
        for lane in range(0, width, HD):
            total = total + weights[:, lane : lane + HD]
        mixed = mixed + jnp.dot(
            weights.astype(jnp.bfloat16),
            ref[begin : begin + width, HD:],
            preferred_element_type=jnp.float32,
        )
    result = (mixed / jnp.sum(total, axis=1, keepdims=True)).astype(jnp.bfloat16)
    for h in range(heads):
        out_ref[:, h * HD : (h + 1) * HD] = result[h * rows : (h + 1) * rows]


def attend(table, info, queries, pieces, slots, rows):
    all_rows, width = queries.shape
    heads = width // HD
    keys = sum(a.shape[0] - TAIL for a in pieces)
    chunk_spec = pl.BlockSpec((rows, width), lambda i, info: (i, 0))
    return call(
        functools.partial(attend_kernel, table, slots),
        "attend",
        info,
        [queries, *pieces],
        [chunk_spec] + [whole(a) for a in pieces],
        chunk_spec,
        jax.ShapeDtypeStruct((all_rows, width), jnp.bfloat16),
        grid=(all_rows // rows,),
        scratch=[pltpu.VMEM((heads * rows, keys), jnp.float32)],
        flops=ATTEND_FLOPS * all_rows * heads * keys * HD,
        vmem=28,
    )


def place_weights(table, info, pieces, w_ref, begin):
    part, width = pieces[0].shape[1], w_ref.shape[2]
    for number, piece in enumerate(pieces):
        start = pl.multiple_of(info[table.rows + number] * part, part)
        for d in range(table.count):
            w_ref[d, pl.ds(start, part)] = piece[d, :, begin : begin + width]


def project_kernel(table, lines, shares, keep, splits, info, *refs):
    count = table.count
    attention, pieces = refs[:lines], refs[lines : lines + shares]
    r_ref = refs[lines + shares]
    parts, h_ref, w_ref = refs[-2 - 2 * len(splits) : -2], refs[-2], refs[-1]
    rows = r_ref.shape[0]

    @pl.when(pl.program_id(0) == 0)
    def _():
        place_weights(table, info, pieces, w_ref, 0)

    total = r_ref[:, :keep].astype(jnp.float32)
    for d in range(count):
        block = line_read(table, info, attention, d).astype(jnp.bfloat16)
        total = total + jnp.dot(block, w_ref[d], preferred_element_type=jnp.float32)
    result = total.astype(jnp.bfloat16)
    h_ref[:, :keep] = result
    for part, (begin, size) in zip(parts, splits * 2):
        for row in range(begin, begin + size, rows):

            @pl.when(pl.program_id(0) == row // rows)
            def _():
                part[row - begin : row - begin + rows] = result


def project(table, info, attention, pieces, residual, keep, rows, splits):
    all_rows, slab = residual.shape
    count, part_rows, _ = pieces[0].shape
    parts = [jax.ShapeDtypeStruct((size, keep), jnp.bfloat16) for _, size in splits * 2]
    row_spec = pl.BlockSpec((rows, slab), lambda i, info: (i, 0))
    return call(
        functools.partial(project_kernel, table, len(attention), len(pieces), keep, splits),
        "project",
        info,
        [*attention, *pieces, residual],
        line_spec(attention, rows, lambda i: i)
        + [whole(p) for p in pieces]
        + [row_spec],
        [whole(part) for part in parts] + [row_spec],
        [*parts, jax.ShapeDtypeStruct(residual.shape, jnp.bfloat16)],
        grid=(all_rows // rows,),
        scratch=[pltpu.VMEM((count, len(pieces) * part_rows, keep), jnp.bfloat16)],
        vmem=36,
    )


def project_raw_kernel(table, lines, raw_lines, shares, keep, info, *refs):
    count = table.count
    attention, residuals = refs[:lines], refs[lines : lines + raw_lines]
    pieces = refs[lines + raw_lines : lines + raw_lines + shares]
    raw_ref, h_ref, w_ref = refs[-3:]
    raw = h_ref.shape[1]

    @pl.when(pl.program_id(0) == 0)
    def _():
        place_weights(table, info, pieces, w_ref, keep)

    blocks = [
        line_read(table, info, attention, d).astype(jnp.bfloat16) for d in range(count)
    ]
    for slab in range(count):
        cols = pl.ds(pl.multiple_of(info[table.place + slab] * raw, raw), raw)
        total = line_read(table, info, residuals, slab)
        for d in range(count):
            total = total + jnp.dot(
                blocks[d], w_ref[d, :, cols], preferred_element_type=jnp.float32
            )
        result = total.astype(jnp.bfloat16)
        raw_ref[:, slab * raw : (slab + 1) * raw] = result
        if slab == 0:
            h_ref[...] = result


def project_raw(table, info, attention, residuals, pieces, hidden, keep, raw, rows):
    all_rows, slab = hidden.shape
    count, part_rows, _ = pieces[0].shape
    args = [*attention, *residuals, *pieces, hidden]
    out = jax.ShapeDtypeStruct((all_rows, count * raw), jnp.bfloat16)
    return call(
        functools.partial(
            project_raw_kernel, table, len(attention), len(residuals), len(pieces), keep
        ),
        "project_raw",
        info,
        args,
        line_spec(attention, rows, lambda i: i)
        + line_spec(residuals, rows, lambda i: i)
        + [whole(p) for p in pieces]
        + [ANYWHERE],
        [
            pl.BlockSpec((rows, count * raw), lambda i, info: (i, 0)),
            pl.BlockSpec((rows, raw), lambda i, info: (i, slab // raw - 1)),
        ],
        [out, jax.ShapeDtypeStruct(hidden.shape, jnp.bfloat16)],
        grid=(all_rows // rows,),
        aliases={len(args): 1},
        scratch=[pltpu.VMEM((count, len(pieces) * part_rows, count * raw), jnp.bfloat16)],
        vmem=36,
    )


def norm_kernel(table, lines, keep, slab, info, g_ref, *refs):
    count = table.count
    blocks, out_ref = refs[:lines], refs[-1]
    raw = slab - keep
    values = []
    squares = jnp.zeros((out_ref.shape[0], 1), jnp.float32)

    def read(d):
        found = [(0, keep, line_read(table, info, blocks, d))]
        if raw:
            cols = slice(d * raw, (d + 1) * raw)
            found.append((keep, raw, refs[lines][:, cols].astype(jnp.float32)))
        return found

    for d in range(count):
        for _, _, value in read(d):
            squares = squares + jnp.sum(value * value, axis=1, keepdims=True)
    inverse = lax.rsqrt(squares / (count * slab) + EPS_NORM)
    for d in range(count):
        for offset, width, value in read(d):
            start = pl.multiple_of(info[table.place + d] * slab + offset, HD)
            cols = pl.ds(start, width)
            out_ref[:, cols] = (value * inverse * g_ref[:, cols]).astype(jnp.bfloat16)


def norm_into(table, info, buffer, blocks, raw_hidden, gain, begin, rows, keep, slab, total_rows):
    width = table.count * slab
    step = min(rows, 32)
    steps, first = rows // step, begin // step
    args = [gain.reshape(1, width), *blocks]
    in_specs = [pl.BlockSpec((1, width), lambda i, info: (0, 0))]
    in_specs += line_spec(blocks, step, lambda i: i)
    if raw_hidden is not None:
        args.append(raw_hidden)
        in_specs.append(
            pl.BlockSpec((step, raw_hidden.shape[1]), lambda i, info: (first + i, 0))
        )
    aliases = {}
    if buffer is not None:
        args.append(buffer)
        in_specs.append(ANYWHERE)
        aliases = {len(args): 0}
    return call(
        functools.partial(norm_kernel, table, len(blocks), keep, slab),
        "norm",
        info,
        args,
        in_specs,
        pl.BlockSpec((step, width), lambda i, info: (first + i, 0)),
        jax.ShapeDtypeStruct((total_rows, width), jnp.bfloat16),
        grid=(steps,),
        aliases=aliases,
    )


def per_device(queries, span_kv, cache, lengths, offset, out_weight, residual, gain):
    rows = queries.shape[0]
    heads = queries.shape[1] // HD
    depth = out_weight.shape[0]
    slab = residual.shape[1]
    contexts = lax.axis_size("context")
    count = lax.axis_size("tensor")
    context_index = lax.axis_index("context")
    tensor_index = lax.axis_index("tensor")
    kv_index = tensor_index * heads // GROUP
    groups = lax.axis_size("groups")
    shares = groups * contexts
    share = lax.axis_index("groups") * contexts + context_index
    raw = slab // RAW_PART if slab % (RAW_PART * HD) == 0 else 0
    keep = slab - raw
    chunk = min(CHUNK, rows)
    sizes = [chunk] * (rows // chunk)
    splits = [(sum(sizes[:n]), size) for n, size in enumerate(sizes)]

    table = Table(contexts, count)
    steering = [context_index, *owners_of(contexts, context_index)]
    steering += [lax.rem(tensor_index + (count - d), count) for d in range(count)]
    steering += [tensor_index == 0, tensor_index == count - 1, share]
    steering += plane_owners(shares, share)
    info = jnp.stack([jnp.asarray(v).astype(jnp.int32) for v in steering])

    cache_local = lax.dynamic_index_in_dim(cache, kv_index, 0, keepdims=False)
    span_local = lax.dynamic_index_in_dim(span_kv, kv_index, 1, keepdims=False)
    positions = offset[0] + context_index * rows + jnp.arange(rows, dtype=jnp.int32)
    both = jnp.concatenate([frequencies(HD)] * 2)
    angles = positions.astype(jnp.float32)[:, None] * both[None, :]
    sign = jnp.where(jnp.arange(HD) < HD // 2, -1.0, 1.0)
    q_turned, payload, *cuts = prepare(
        table, info, queries, span_local, cache_local, out_weight, jnp.cos(angles),
        jnp.sin(angles) * sign[None, :], lengths, depth // shares, slab, keep,
    )
    parts = [cuts[0]]
    for shift in range(1, count):
        pairs = [(i, (i + shift) % count) for i in range(count)]
        parts.append(lax.ppermute(cuts[shift], "tensor", pairs))
    sent = []

    def between(block):
        sent.append(stack(info, parts, []))
        if raw:
            sent.extend(last_columns(info, residual, raw, parts[1:]))
        return gate(info, block, sent)

    pieces = pieces_of(payload, "context", contexts, between)
    mixed = attend(table, info, q_turned, pieces, cache_local.shape[0], chunk)
    residuals = []
    if raw and count == 4:
        residuals = [sent[2], *line_near(sent[2]), *line_far(sent[1])]
    elif raw:
        residuals = line_gather(sent[1], count)
    ready = gate(info, mixed, residuals[1:4]) if raw else mixed
    attention = line_gather(ready, count)
    weights = plane_gather(
        sent[0],
        groups,
        contexts,
        lambda block: gate(info, block, [mixed]),
        lambda block, mask: gate(info, block, attention[1 : 3 if mask & (mask - 1) == 0 else 5]),
    )

    *hidden_parts, hidden = project(
        table, info, attention, weights, residual, keep, chunk, splits
    )
    raw_hidden = None
    if raw:
        raw_hidden, hidden = project_raw(
            table, info, attention, residuals, weights, hidden, keep, raw, chunk
        )
    lines = chunk_gathers(
        info,
        hidden_parts[: len(splits)],
        hidden_parts[len(splits) :],
        residuals[4:],
        [raw_hidden] if raw else [],
        count,
    )
    normed = None
    for (begin, size), blocks in zip(splits, lines):
        normed = norm_into(
            table, info, normed, blocks, raw_hidden, gain, begin, size, keep, slab, rows
        )
    return (hidden, normed)


def solution(mesh):
    in_specs = (
        P(("groups", "context"), "tensor"),
        P(("groups", "context"), None, None),
        P("groups", "context", None),
        P(("groups", "context")),
        P("groups"),
        P("tensor", None),
        P(("groups", "context"), "tensor"),
        P(),
    )
    out_specs = (P(("groups", "context"), "tensor"), P(("groups", "context"), None))
    return jax.shard_map(
        per_device, mesh=mesh, in_specs=in_specs, out_specs=out_specs, check_vma=False
    )
```

```python
import functools
import math

import jax
import jax.numpy as jnp
from jax import lax
from jax.experimental import pallas as pl
from jax.experimental.pallas import tpu as pltpu
from jax.sharding import PartitionSpec as P

GROUP = 8
HD = 128
NEG = -1e30
EPS_NORM = 1e-05
MIB = 1024 * 1024
CHUNK = 128
KEY_BLOCK = 512
ATTEND_FLOPS = 16
TAIL = 16
DIGIT = 32
ANYWHERE = pl.BlockSpec(memory_space=pl.ANY)


def frequencies(head_width):
    counter = jnp.arange(head_width // 2, dtype=jnp.float32)
    base_freq = jnp.exp(-(2.0 * counter / head_width) * math.log(500000.0))
    wavelength = 2.0 * math.pi / base_freq
    smoothing = (8192.0 / wavelength - 1.0) / 3.0
    blended = (1.0 - smoothing) * base_freq / 8.0 + smoothing * base_freq
    return jnp.where(
        wavelength < 2048.0, base_freq, jnp.where(wavelength > 8192.0, base_freq / 8.0, blended)
    )


def pieces_of(value, axis, count, between=lambda block: block):
    if count & (count - 1) == 0:
        held = {0: value}
        bit = count // 2
        while bit:
            pairs = [(i, i ^ bit) for i in range(count)]
            for mask in sorted(held):
                held[mask | bit] = lax.ppermute(held[mask], axis, pairs)
            if bit == count // 2:
                held[bit] = between(held[bit])
            bit //= 2
        return [held[mask] for mask in range(count)]
    blocks = [value]
    for shift in range(1, count):
        pairs = [(i, (i + shift) % count) for i in range(count)]
        blocks.append(lax.ppermute(value, axis, pairs))
    blocks[-1] = between(blocks[-1])
    return blocks


def owners_of(count, me):
    if count & (count - 1) == 0:
        return [me ^ mask for mask in range(count)]
    return [(me + count - shift) % count for shift in range(count)]


def plane_gather(value, groups, contexts, first, then):
    count = groups * contexts
    if count & (count - 1):
        gathered = lax.all_gather(value, ("groups", "context"), axis=0, tiled=False)
        return [gathered[number] for number in range(count)]
    held = {0: value}
    bits = [1 << b for b in range(contexts.bit_length() - 2, 0, -1)]
    bits += [contexts << b for b in range(groups.bit_length() - 1)]
    for bit in bits:
        axis, flip, size = ("context", bit, contexts)
        if bit >= contexts:
            axis, flip, size = ("groups", bit // contexts, groups)
        pairs = [(i, i ^ flip) for i in range(size)]
        for mask in sorted(held):
            if mask:
                held[mask] = first(held[mask], held[bit])
            held[mask | bit] = lax.ppermute(held[mask], axis, pairs)
    if contexts > 1:
        for mask in sorted(held):
            held[mask] = then(held[mask], mask) if mask else held[mask]
            held[mask | 1] = core_swap(held[mask], contexts)
    return [held[mask] for mask in range(count)]


def core_swap(value, contexts):
    return lax.ppermute(value, "context", [(i, i ^ 1) for i in range(contexts)])


def plane_owners(count, me):
    if count & (count - 1):
        return list(range(count))
    return [me ^ mask for mask in range(count)]


def line_gather(value, count):
    if count != 4:
        return [lax.all_gather(value, "tensor", axis=0, tiled=False)]
    far, last = line_far(value)
    return [value, *line_near(value), far, last]


def line_near(value):
    up = lax.ppermute(value, "tensor", [(0, 1), (1, 2), (2, 3)])
    return up, lax.ppermute(value, "tensor", [(1, 0), (2, 1), (3, 2)])


def line_far(value):
    far = lax.ppermute(value, "tensor", [(0, 2), (1, 3), (2, 0), (3, 1)])
    return far, lax.ppermute(far, "tensor", [(1, 0), (2, 3)])


def chunk_gathers(info, values, copies, second, count):
    if count != 4:
        return [line_gather(value, count) for value in values]
    fars, lines = [], []
    for number, value in enumerate(values):
        after = [fars[-1][0]] if number else []
        if number == 1:
            after += second
        fars.append(line_far(gate(info, value, after) if after else value))
    for number, value in enumerate(copies):
        after = list(lines[number - 1][1:3]) if number else []
        if number > 1:
            after.append(fars[number - 2][1])
        value = gate(info, value, after) if after else value
        lines.append([value, *line_near(value), *fars[number]])
    return lines


class Table:
    def __init__(self, contexts, count):
        self.contexts, self.count = contexts, count
        self.owner = 1
        self.place = 1 + contexts
        self.low = self.place + count
        self.high = self.low + 1
        self.share = self.low + 2
        self.rows = self.low + 3


def line_read(table, info, refs, d, cols=slice(None)):
    if len(refs) == 1:
        return refs[0][info[table.place + d], :, cols].astype(jnp.float32)
    if d == 0:
        return refs[0][:, cols].astype(jnp.float32)
    if d == 2:
        return refs[3][:, cols].astype(jnp.float32)
    near = refs[1 if d == 1 else 2][:, cols].astype(jnp.float32)
    other = refs[4][:, cols].astype(jnp.float32)
    at_end = info[table.low if d == 1 else table.high]
    return jnp.where(at_end == 1, other, near)


def line_spec(blocks, rows, index):
    if len(blocks) == 1:
        count, _, width = blocks[0].shape
        return [pl.BlockSpec((count, rows, width), lambda i, info: (0, index(i), 0))]
    width = blocks[0].shape[1]
    return [pl.BlockSpec((rows, width), lambda i, info: (index(i), 0)) for _ in blocks]


def call(kernel, name, info, args, in_specs, out_specs, out_shape, grid=(1,), aliases=None,
         scratch=(), flops=1, vmem=16):
    return pl.pallas_call(
        kernel,
        grid_spec=pltpu.PrefetchScalarGridSpec(
            num_scalar_prefetch=1,
            grid=grid,
            in_specs=in_specs,
            out_specs=out_specs,
            scratch_shapes=list(scratch),
        ),
        out_shape=out_shape,
        input_output_aliases=aliases or {},
        compiler_params=pltpu.CompilerParams(vmem_limit_bytes=vmem * MIB or None),
        cost_estimate=pl.CostEstimate(flops=flops, bytes_accessed=1, transcendentals=0),
        name=name,
    )(info, *args)


def whole(a):
    zeros = (0,) * len(a.shape)
    return pl.BlockSpec(tuple(a.shape), lambda i, info: zeros)


def prepare_kernel(table, slab, info, q_hbm, kv_hbm, cache_hbm, w_hbm, cos_ref, sin_ref,
                   length_ref, *refs):
    count = table.count
    q_out, kv_out, outs = refs[0], refs[1], refs[2 : 2 + count]
    q_ref, kv_ref, w_ref, sems = refs[2 + count :]
    slots, rows, part = cache_hbm.shape[0], q_ref.shape[0], w_ref.shape[0]
    span, tail = slice(slots, slots + rows), slice(slots + rows, slots + rows + TAIL)
    start = pl.multiple_of(info[table.share] * part, part)
    moves = [
        (w_hbm.at[pl.ds(start, part)], w_ref),
        (kv_hbm, kv_ref),
        (q_hbm, q_ref),
        (cache_hbm, kv_out.at[pl.ds(0, slots)]),
    ]
    copies = [pltpu.make_async_copy(*move, sems.at[n]) for n, move in enumerate(moves)]
    for copy in copies:
        copy.start()

    copies[0].wait()
    for d, out in enumerate(outs):
        target = lax.rem(info[table.place] + d, count)
        out[...] = w_ref[:, pl.ds(pl.multiple_of(target * slab, slab), slab)]

    cosine, sine = cos_ref[...], sin_ref[...]

    def turn(block):
        block = block.astype(jnp.float32)
        return (block * cosine + pltpu.roll(block, HD // 2, 1) * sine).astype(jnp.bfloat16)

    copies[1].wait()
    kv_out[span, :HD] = turn(kv_ref[:, :HD])
    kv_out[span, HD:] = kv_ref[:, HD:]
    length = length_ref[0]
    upper = lax.div(length, DIGIT)
    lower = length - upper * DIGIT
    kv_out[tail, :HD] = jnp.full((TAIL, HD), upper.astype(jnp.float32)).astype(jnp.bfloat16)
    kv_out[tail, HD:] = jnp.full((TAIL, HD), lower.astype(jnp.float32)).astype(jnp.bfloat16)
    copies[2].wait()
    for head in range(q_ref.shape[1] // HD):
        cols = slice(head * HD, (head + 1) * HD)
        q_out[:, cols] = turn(q_ref[:, cols])
    copies[3].wait()


def prepare(table, info, queries, span_pairs, cache, out_weight, cosine, sine, lengths, part,
            slab):
    rows = queries.shape[0]
    shapes = [
        jax.ShapeDtypeStruct(queries.shape, jnp.bfloat16),
        jax.ShapeDtypeStruct((cache.shape[0] + rows + TAIL, 2 * HD), jnp.bfloat16),
    ]
    shapes += [jax.ShapeDtypeStruct((part, slab), out_weight.dtype)] * table.count
    return call(
        functools.partial(prepare_kernel, table, slab),
        "prepare",
        info,
        [queries, span_pairs, cache, out_weight, cosine, sine, lengths],
        [ANYWHERE] * 4
        + [whole(cosine), whole(sine), pl.BlockSpec(memory_space=pltpu.SMEM)],
        [whole(shape) for shape in shapes],
        shapes,
        scratch=[
            pltpu.VMEM(queries.shape, jnp.bfloat16),
            pltpu.VMEM(span_pairs.shape, jnp.bfloat16),
            pltpu.VMEM((part, out_weight.shape[1]), out_weight.dtype),
            pltpu.SemaphoreType.DMA((4,)),
        ],
        vmem=0,
    )


def stack_kernel(count, info, *refs):
    for number, part in enumerate(refs[:count]):
        refs[-1][number] = part[...]


def stack(info, parts, after):
    shape = jax.ShapeDtypeStruct((len(parts), *parts[0].shape), parts[0].dtype)
    return call(
        functools.partial(stack_kernel, len(parts)),
        "stack",
        info,
        [*parts, *after],
        [whole(p) for p in parts] + [ANYWHERE] * len(after),
        whole(shape),
        shape,
    )


def gate_kernel(info, *refs):
    pass


def gate(info, value, after):
    return call(
        gate_kernel,
        "gate",
        info,
        [value, *after],
        [ANYWHERE] * (1 + len(after)),
        ANYWHERE,
        jax.ShapeDtypeStruct(value.shape, value.dtype),
        aliases={1: 0},
    )


def attend_kernel(table, slots, first, info, q_ref, *refs):
    count = table.contexts
    pieces, out_ref, s_ref = refs[:count], refs[-2], refs[-1]
    rows = q_ref.shape[0]
    heads = q_ref.shape[1] // HD
    chunk = pl.program_id(0) + first
    mine = info[0]
    q = jnp.concatenate([q_ref[:, h * HD : (h + 1) * HD] for h in range(heads)], axis=0)
    exponent = math.log2(math.e) / math.sqrt(HD)

    blocks = []
    peak = jnp.full((heads * rows, HD), NEG, jnp.float32)
    column = 0
    for kind in ("cache", "span"):
        for number, ref in enumerate(pieces):
            tail = ref.shape[0] - TAIL
            first, last = (0, slots) if kind == "cache" else (slots, tail)
            width = min(KEY_BLOCK, last - first)
            length = ref[tail : tail + 1, :HD].astype(jnp.float32) * DIGIT + ref[
                tail : tail + 1, HD:
            ].astype(jnp.float32)
            length = jnp.concatenate([length] * (width // HD), axis=1)
            for begin in range(first, last, width):
                scores = lax.dot_general(
                    q,
                    ref[begin : begin + width, :HD],
                    (((1,), (1,)), ((), ())),
                    preferred_element_type=jnp.float32,
                )
                if kind == "cache":
                    slot = lax.broadcasted_iota(jnp.int32, (1, width), 1) + begin
                    live = slot.astype(jnp.float32) < length
                    scores = scores + jnp.where(live, 0.0, NEG)
                elif number == 0:
                    key = lax.broadcasted_iota(jnp.int32, (rows, width), 1) + (begin - first)
                    row = lax.broadcasted_iota(jnp.int32, (rows, width), 0) + chunk * rows
                    bias = jnp.where(key <= row, 0.0, NEG)
                    scores = scores + jnp.concatenate([bias] * heads, axis=0)
                else:
                    scores = scores + jnp.where(info[table.owner + number] < mine, 0.0, NEG)
                s_ref[:, column : column + width] = scores
                for lane in range(0, width, HD):
                    peak = jnp.maximum(peak, scores[:, lane : lane + HD])
                blocks.append((ref, begin, column, width))
                column += width
    top = jnp.max(peak, axis=1, keepdims=True)
    total = jnp.zeros((heads * rows, HD), jnp.float32)
    mixed = jnp.zeros((heads * rows, HD), jnp.float32)
    for ref, begin, column, width in blocks:
        weights = jnp.exp2((s_ref[:, column : column + width] - top) * exponent)
        for lane in range(0, width, HD):
            total = total + weights[:, lane : lane + HD]
        mixed = mixed + jnp.dot(
            weights.astype(jnp.bfloat16),
            ref[begin : begin + width, HD:],
            preferred_element_type=jnp.float32,
        )
    result = (mixed / jnp.sum(total, axis=1, keepdims=True)).astype(jnp.bfloat16)
    for h in range(heads):
        out_ref[:, h * HD : (h + 1) * HD] = result[h * rows : (h + 1) * rows]


def attend(table, info, queries, pieces, slots, begin, size, rows):
    width = queries.shape[1]
    heads = width // HD
    keys = sum(a.shape[0] - TAIL for a in pieces)
    first = begin // rows
    return call(
        functools.partial(attend_kernel, table, slots, first),
        "attend",
        info,
        [queries, *pieces],
        [pl.BlockSpec((rows, width), lambda i, info: (first + i, 0))]
        + [whole(a) for a in pieces],
        pl.BlockSpec((rows, width), lambda i, info: (i, 0)),
        jax.ShapeDtypeStruct((size, width), jnp.bfloat16),
        grid=(size // rows,),
        scratch=[pltpu.VMEM((heads * rows, keys), jnp.float32)],
        flops=ATTEND_FLOPS * size * heads * keys * HD,
        vmem=28,
    )


def project_kernel(table, lines, shares, splits, info, *refs):
    count = table.count
    attention, pieces = refs[:lines], refs[lines : lines + shares]
    r_ref = refs[lines + shares]
    parts, h_ref, w_ref = refs[-2 - 2 * len(splits) : -2], refs[-2], refs[-1]
    share_rows = pieces[0].shape[1]
    for number, piece in enumerate(pieces):
        start = pl.multiple_of(info[table.rows + number] * share_rows, share_rows)
        for d in range(count):
            w_ref[d, pl.ds(start, share_rows)] = piece[d]
    blocks = [
        line_read(table, info, attention, d).astype(jnp.bfloat16) for d in range(count)
    ]
    for part, copy, (begin, size) in zip(parts, parts[len(splits) :], splits):
        rows = slice(begin, begin + size)
        total = r_ref[rows].astype(jnp.float32)
        for d in range(count):
            total = total + jnp.dot(
                blocks[d][rows], w_ref[d], preferred_element_type=jnp.float32
            )
        result = total.astype(jnp.bfloat16)
        h_ref[rows] = result
        part[...] = result
        copy[...] = result


def project(table, info, attention, pieces, residual, hidden, half, halves, splits):
    all_rows, slab = residual.shape
    rows = all_rows // halves
    count, share_rows, _ = pieces[0].shape
    parts = [jax.ShapeDtypeStruct((size, slab), jnp.bfloat16) for _, size in splits * 2]
    row_spec = pl.BlockSpec((rows, slab), lambda i, info: (half, 0))
    args = [*attention, *pieces, residual]
    specs = line_spec(attention, rows, lambda i: 0) + [whole(p) for p in pieces] + [row_spec]
    aliases = {}
    if hidden is not None:
        args.append(hidden)
        specs.append(ANYWHERE)
        aliases = {len(args): len(parts)}
    return call(
        functools.partial(project_kernel, table, len(attention), len(pieces), splits),
        "project",
        info,
        args,
        specs,
        [whole(part) for part in parts] + [row_spec],
        [*parts, jax.ShapeDtypeStruct(residual.shape, jnp.bfloat16)],
        aliases=aliases,
        scratch=[pltpu.VMEM((count, len(pieces) * share_rows, slab), jnp.bfloat16)],
        vmem=36,
    )


def norm_kernel(table, lines, info, g_ref, *refs):
    count = table.count
    blocks, out_ref = refs[:lines], refs[-1]
    slab = out_ref.shape[1] // count
    squares = jnp.zeros((out_ref.shape[0], 1), jnp.float32)
    for d in range(count):
        value = line_read(table, info, blocks, d)
        squares = squares + jnp.sum(value * value, axis=1, keepdims=True)
    inverse = lax.rsqrt(squares / (count * slab) + EPS_NORM)
    for d in range(count):
        cols = pl.ds(pl.multiple_of(info[table.place + d] * slab, slab), slab)
        value = line_read(table, info, blocks, d)
        out_ref[:, cols] = (value * inverse * g_ref[:, cols]).astype(jnp.bfloat16)


def norm_into(table, info, buffer, blocks, gain, begin, rows, total_rows):
    width = gain.shape[0]
    step = math.gcd(rows, 32)
    first = begin // step
    args = [gain.reshape(1, width), *blocks]
    in_specs = [pl.BlockSpec((1, width), lambda i, info: (0, 0))]
    in_specs += line_spec(blocks, step, lambda i: i)
    aliases = {}
    if buffer is not None:
        args.append(buffer)
        in_specs.append(ANYWHERE)
        aliases = {len(args): 0}
    return call(
        functools.partial(norm_kernel, table, len(blocks)),
        "norm",
        info,
        args,
        in_specs,
        pl.BlockSpec((step, width), lambda i, info: (first + i, 0)),
        jax.ShapeDtypeStruct((total_rows, width), jnp.bfloat16),
        grid=(rows // step,),
        aliases=aliases,
    )


def per_device(queries, span_kv, cache, lengths, offset, out_weight, residual, gain):
    rows = queries.shape[0]
    heads = queries.shape[1] // HD
    depth = out_weight.shape[0]
    slab = residual.shape[1]
    contexts = lax.axis_size("context")
    count = lax.axis_size("tensor")
    context_index = lax.axis_index("context")
    tensor_index = lax.axis_index("tensor")
    kv_index = tensor_index * heads // GROUP
    groups = lax.axis_size("groups")
    shares = groups * contexts
    share = lax.axis_index("groups") * contexts + context_index
    chunk = min(CHUNK, rows)
    halves = 2 if rows % (2 * chunk) == 0 else 1
    half = rows // halves
    splits = [[(0, chunk), (chunk, half - chunk)] if half > chunk else [(0, half)]] * halves
    if halves == 2 and chunk == 128 and half == 256:
        splits = [splits[0], [(0, 160), (160, 96)]]

    table = Table(contexts, count)
    steering = [context_index, *owners_of(contexts, context_index)]
    steering += [lax.rem(tensor_index + (count - d), count) for d in range(count)]
    steering += [tensor_index == 0, tensor_index == count - 1, share]
    steering += plane_owners(shares, share)
    info = jnp.stack([jnp.asarray(v).astype(jnp.int32) for v in steering])

    cache_local = lax.dynamic_index_in_dim(cache, kv_index, 0, keepdims=False)
    span_local = lax.dynamic_index_in_dim(span_kv, kv_index, 1, keepdims=False)
    positions = offset[0] + context_index * rows + jnp.arange(rows, dtype=jnp.int32)
    both = jnp.concatenate([frequencies(HD)] * 2)
    angles = positions.astype(jnp.float32)[:, None] * both[None, :]
    sign = jnp.where(jnp.arange(HD) < HD // 2, -1.0, 1.0)
    q_turned, payload, *cuts = prepare(
        table, info, queries, span_local, cache_local, out_weight, jnp.cos(angles),
        jnp.sin(angles) * sign[None, :], lengths, depth // shares, slab,
    )
    parts = [cuts[0]]
    for shift in range(1, count):
        pairs = [(i, (i + shift) % count) for i in range(count)]
        parts.append(lax.ppermute(cuts[shift], "tensor", pairs))
    own_weights = stack(info, parts, [])
    pieces = pieces_of(
        payload, "context", contexts, lambda block: gate(info, block, [own_weights])
    )
    slots = cache_local.shape[0]
    mixed = [
        attend(table, info, q_turned, pieces, slots, number * half, half, chunk)
        for number in range(halves)
    ]
    attention = [line_gather(value, count) for value in mixed]
    weights = plane_gather(
        own_weights,
        groups,
        contexts,
        lambda block, other: gate(info, block, [mixed[0], other]),
        lambda block, mask: gate(
            info,
            block,
            attention[0][3:4] if mask in (mask & -mask,) else [*attention[0][1:], *mixed[1:]],
        ),
    )
    values, copies, hidden = [], [], None
    for number in range(halves):
        *made, hidden = project(
            table, info, attention[number], weights, residual, hidden, number, halves,
            splits[number],
        )
        values += made[: len(made) // 2]
        copies += made[len(made) // 2 :]
    lines = chunk_gathers(info, values, copies, attention[-1][1:], count)
    normed, begin = None, 0
    for blocks, value in zip(lines, values):
        normed = norm_into(table, info, normed, blocks, gain, begin, value.shape[0], rows)
        begin += value.shape[0]
    return (hidden, normed)


def solution(mesh):
    in_specs = (
        P(("groups", "context"), "tensor"),
        P(("groups", "context"), None, None),
        P("groups", "context", None),
        P(("groups", "context")),
        P("groups"),
        P("tensor", None),
        P(("groups", "context"), "tensor"),
        P(),
    )
    out_specs = (P(("groups", "context"), "tensor"), P(("groups", "context"), None))
    return jax.shard_map(
        per_device, mesh=mesh, in_specs=in_specs, out_specs=out_specs, check_vma=False
    )
```

```python
import functools
import math

import jax
import jax.numpy as jnp
from jax import lax
from jax.experimental import pallas as pl
from jax.experimental.pallas import tpu as pltpu
from jax.sharding import PartitionSpec as P

GROUP = 8
HD = 128
NEG = -1e30
EPS_NORM = 1e-05
MIB = 1024 * 1024
CHUNK = 128
KEY_BLOCK = 512
ATTEND_FLOPS = 16
RAW_PART = 8
TAIL = 16
DIGIT = 32
ANYWHERE = pl.BlockSpec(memory_space=pl.ANY)


def frequencies(head_width):
    counter = jnp.arange(head_width // 2, dtype=jnp.float32)
    base_freq = jnp.exp(-(2.0 * counter / head_width) * math.log(500000.0))
    wavelength = 2.0 * math.pi / base_freq
    smoothing = (8192.0 / wavelength - 1.0) / 3.0
    blended = (1.0 - smoothing) * base_freq / 8.0 + smoothing * base_freq
    return jnp.where(
        wavelength < 2048.0, base_freq, jnp.where(wavelength > 8192.0, base_freq / 8.0, blended)
    )


def pieces_of(value, axis, count, between=lambda block: block):
    if count & (count - 1) == 0:
        held = {0: value}
        bit = count // 2
        while bit:
            pairs = [(i, i ^ bit) for i in range(count)]
            for mask in sorted(held):
                held[mask | bit] = lax.ppermute(held[mask], axis, pairs)
            if bit == count // 2:
                held[bit] = between(held[bit])
            bit //= 2
        return [held[mask] for mask in range(count)]
    blocks = [value]
    for shift in range(1, count):
        pairs = [(i, (i + shift) % count) for i in range(count)]
        blocks.append(lax.ppermute(value, axis, pairs))
    blocks[-1] = between(blocks[-1])
    return blocks


def owners_of(count, me):
    if count & (count - 1) == 0:
        return [me ^ mask for mask in range(count)]
    return [(me + count - shift) % count for shift in range(count)]


def plane_gather(value, groups, contexts, first, then):
    count = groups * contexts
    if count & (count - 1):
        gathered = lax.all_gather(value, ("groups", "context"), axis=0, tiled=False)
        return [gathered[number] for number in range(count)]
    held = {0: value}
    bits = [1 << b for b in range(contexts.bit_length() - 2, 0, -1)]
    bits += [contexts << b for b in range(groups.bit_length() - 1)]
    for bit in bits:
        axis, flip, size = ("context", bit, contexts)
        if bit >= contexts:
            axis, flip, size = ("groups", bit // contexts, groups)
        pairs = [(i, i ^ flip) for i in range(size)]
        for mask in sorted(held):
            if mask:
                held[mask] = first(held[mask], held[bit])
            held[mask | bit] = lax.ppermute(held[mask], axis, pairs)
    if contexts > 1:
        for mask in sorted(held):
            held[mask] = then(held[mask], mask) if mask else held[mask]
            held[mask | 1] = core_swap(held[mask], contexts)
    return [held[mask] for mask in range(count)]


def core_swap(value, contexts):
    return lax.ppermute(value, "context", [(i, i ^ 1) for i in range(contexts)])


def plane_owners(count, me):
    if count & (count - 1):
        return list(range(count))
    return [me ^ mask for mask in range(count)]


def line_gather(value, count):
    if count != 4:
        return [lax.all_gather(value, "tensor", axis=0, tiled=False)]
    far, last = line_far(value)
    return [value, *line_near(value), far, last]


def line_near(value):
    up = lax.ppermute(value, "tensor", [(0, 1), (1, 2), (2, 3)])
    return up, lax.ppermute(value, "tensor", [(1, 0), (2, 1), (3, 2)])


def line_far(value):
    far = lax.ppermute(value, "tensor", [(0, 2), (1, 3), (2, 0), (3, 1)])
    return far, lax.ppermute(far, "tensor", [(1, 0), (2, 3)])


def chunk_gathers(info, values, copies, second, made, count):
    if count != 4:
        return [line_gather(value, count) for value in values]
    fars, lines = [], []
    for number, value in enumerate(values):
        after = [fars[-1][0]] if number else []
        if number == 1:
            after += second
        fars.append(line_far(gate(info, value, after) if after else value))
    for number, value in enumerate(copies):
        after = [*lines[number - 1][1:3], fars[number - 1][1]] if number else []
        if number == len(copies) // 2:
            after += made
        value = gate(info, value, after) if after else value
        lines.append([value, *line_near(value), *fars[number]])
    return lines


class Table:
    def __init__(self, contexts, count):
        self.contexts, self.count = contexts, count
        self.owner = 1
        self.place = 1 + contexts
        self.low = self.place + count
        self.high = self.low + 1
        self.share = self.low + 2
        self.rows = self.low + 3


def line_read(table, info, refs, d, cols=slice(None)):
    if len(refs) == 1:
        return refs[0][info[table.place + d], :, cols].astype(jnp.float32)
    if d == 0:
        return refs[0][:, cols].astype(jnp.float32)
    if d == 2:
        return refs[3][:, cols].astype(jnp.float32)
    near = refs[1 if d == 1 else 2][:, cols].astype(jnp.float32)
    other = refs[4][:, cols].astype(jnp.float32)
    at_end = info[table.low if d == 1 else table.high]
    return jnp.where(at_end == 1, other, near)


def line_spec(blocks, rows, index):
    if len(blocks) == 1:
        count, _, width = blocks[0].shape
        return [pl.BlockSpec((count, rows, width), lambda i, info: (0, index(i), 0))]
    width = blocks[0].shape[1]
    return [pl.BlockSpec((rows, width), lambda i, info: (index(i), 0)) for _ in blocks]


def call(kernel, name, info, args, in_specs, out_specs, out_shape, grid=(1,), aliases=None,
         scratch=(), flops=1, vmem=16):
    return pl.pallas_call(
        kernel,
        grid_spec=pltpu.PrefetchScalarGridSpec(
            num_scalar_prefetch=1,
            grid=grid,
            in_specs=in_specs,
            out_specs=out_specs,
            scratch_shapes=list(scratch),
        ),
        out_shape=out_shape,
        input_output_aliases=aliases or {},
        compiler_params=pltpu.CompilerParams(vmem_limit_bytes=vmem * MIB or None),
        cost_estimate=pl.CostEstimate(flops=flops, bytes_accessed=1, transcendentals=0),
        name=name,
    )(info, *args)


def whole(a):
    zeros = (0,) * len(a.shape)
    return pl.BlockSpec(tuple(a.shape), lambda i, info: zeros)


def prepare_kernel(table, slab, keep, info, q_hbm, kv_hbm, cache_hbm, w_hbm, cos_ref, sin_ref,
                   length_ref, *refs):
    count, raw = table.count, slab - keep
    q_out, kv_out, outs = refs[0], refs[1], refs[2 : 2 + count]
    q_ref, kv_ref, w_ref, sems = refs[2 + count :]
    slots, rows, part = cache_hbm.shape[0], q_ref.shape[0], w_ref.shape[0]
    span, tail = slice(slots, slots + rows), slice(slots + rows, slots + rows + TAIL)
    start = pl.multiple_of(info[table.share] * part, part)
    moves = [
        (w_hbm.at[pl.ds(start, part)], w_ref),
        (kv_hbm, kv_ref),
        (q_hbm, q_ref),
        (cache_hbm, kv_out.at[pl.ds(0, slots)]),
    ]
    copies = [pltpu.make_async_copy(*move, sems.at[n]) for n, move in enumerate(moves)]
    for copy in copies:
        copy.start()

    copies[0].wait()
    for d, out in enumerate(outs):
        target = lax.rem(info[table.place] + d, count)
        out[:, :keep] = w_ref[:, pl.ds(pl.multiple_of(target * slab, slab), keep)]
        for j in range(count if raw else 0):
            out[:, keep + j * raw : keep + (j + 1) * raw] = w_ref[
                :, j * slab + keep : (j + 1) * slab
            ]

    cosine, sine = cos_ref[...], sin_ref[...]

    def turn(block):
        block = block.astype(jnp.float32)
        return (block * cosine + pltpu.roll(block, HD // 2, 1) * sine).astype(jnp.bfloat16)

    copies[1].wait()
    kv_out[span, :HD] = turn(kv_ref[:, :HD])
    kv_out[span, HD:] = kv_ref[:, HD:]
    length = length_ref[0]
    upper = lax.div(length, DIGIT)
    lower = length - upper * DIGIT
    kv_out[tail, :HD] = jnp.full((TAIL, HD), upper.astype(jnp.float32)).astype(jnp.bfloat16)
    kv_out[tail, HD:] = jnp.full((TAIL, HD), lower.astype(jnp.float32)).astype(jnp.bfloat16)
    copies[2].wait()
    for head in range(q_ref.shape[1] // HD):
        cols = slice(head * HD, (head + 1) * HD)
        q_out[:, cols] = turn(q_ref[:, cols])
    copies[3].wait()


def prepare(table, info, queries, span_pairs, cache, out_weight, cosine, sine, lengths, part,
            slab, keep):
    rows = queries.shape[0]
    shapes = [
        jax.ShapeDtypeStruct(queries.shape, jnp.bfloat16),
        jax.ShapeDtypeStruct((cache.shape[0] + rows + TAIL, 2 * HD), jnp.bfloat16),
    ]
    width = keep + table.count * (slab - keep)
    shapes += [jax.ShapeDtypeStruct((part, width), out_weight.dtype)] * table.count
    return call(
        functools.partial(prepare_kernel, table, slab, keep),
        "prepare",
        info,
        [queries, span_pairs, cache, out_weight, cosine, sine, lengths],
        [ANYWHERE] * 4
        + [whole(cosine), whole(sine), pl.BlockSpec(memory_space=pltpu.SMEM)],
        [whole(shape) for shape in shapes],
        shapes,
        scratch=[
            pltpu.VMEM(queries.shape, jnp.bfloat16),
            pltpu.VMEM(span_pairs.shape, jnp.bfloat16),
            pltpu.VMEM((part, out_weight.shape[1]), out_weight.dtype),
            pltpu.SemaphoreType.DMA((4,)),
        ],
        vmem=0,
    )


def last_columns_kernel(info, *refs):
    refs[-1][...] = refs[0][...]


def last_columns(info, value, width, after):
    rows, full = value.shape
    shape = jax.ShapeDtypeStruct((rows, width), value.dtype)
    return call(
        last_columns_kernel,
        "last_columns",
        info,
        [value, *after],
        [pl.BlockSpec((rows, width), lambda i, info: (0, full // width - 1))]
        + [ANYWHERE] * len(after),
        whole(shape),
        shape,
    )


def stack_kernel(count, info, *refs):
    for number, part in enumerate(refs[:count]):
        refs[-1][number] = part[...]


def stack(info, parts, after):
    shape = jax.ShapeDtypeStruct((len(parts), *parts[0].shape), parts[0].dtype)
    return call(
        functools.partial(stack_kernel, len(parts)),
        "stack",
        info,
        [*parts, *after],
        [whole(p) for p in parts] + [ANYWHERE] * len(after),
        whole(shape),
        shape,
    )


def gate_kernel(info, *refs):
    pass


def gate(info, value, after):
    return call(
        gate_kernel,
        "gate",
        info,
        [value, *after],
        [ANYWHERE] * (1 + len(after)),
        ANYWHERE,
        jax.ShapeDtypeStruct(value.shape, value.dtype),
        aliases={1: 0},
    )


def attend_kernel(table, slots, first, info, q_ref, *refs):
    count = table.contexts
    pieces, out_ref, s_ref = refs[:count], refs[-2], refs[-1]
    rows = q_ref.shape[0]
    heads = q_ref.shape[1] // HD
    chunk = pl.program_id(0) + first
    mine = info[0]
    q = jnp.concatenate([q_ref[:, h * HD : (h + 1) * HD] for h in range(heads)], axis=0)
    exponent = math.log2(math.e) / math.sqrt(HD)

    blocks = []
    peak = jnp.full((heads * rows, HD), NEG, jnp.float32)
    column = 0
    for kind in ("cache", "span"):
        for number, ref in enumerate(pieces):
            tail = ref.shape[0] - TAIL
            first, last = (0, slots) if kind == "cache" else (slots, tail)
            width = min(KEY_BLOCK, last - first)
            length = ref[tail : tail + 1, :HD].astype(jnp.float32) * DIGIT + ref[
                tail : tail + 1, HD:
            ].astype(jnp.float32)
            length = jnp.concatenate([length] * (width // HD), axis=1)
            for begin in range(first, last, width):
                scores = lax.dot_general(
                    q,
                    ref[begin : begin + width, :HD],
                    (((1,), (1,)), ((), ())),
                    preferred_element_type=jnp.float32,
                )
                if kind == "cache":
                    slot = lax.broadcasted_iota(jnp.int32, (1, width), 1) + begin
                    live = slot.astype(jnp.float32) < length
                    scores = scores + jnp.where(live, 0.0, NEG)
                elif number == 0:
                    key = lax.broadcasted_iota(jnp.int32, (rows, width), 1) + (begin - first)
                    row = lax.broadcasted_iota(jnp.int32, (rows, width), 0) + chunk * rows
                    bias = jnp.where(key <= row, 0.0, NEG)
                    scores = scores + jnp.concatenate([bias] * heads, axis=0)
                else:
                    scores = scores + jnp.where(info[table.owner + number] < mine, 0.0, NEG)
                s_ref[:, column : column + width] = scores
                for lane in range(0, width, HD):
                    peak = jnp.maximum(peak, scores[:, lane : lane + HD])
                blocks.append((ref, begin, column, width))
                column += width
    top = jnp.max(peak, axis=1, keepdims=True)
    total = jnp.zeros((heads * rows, HD), jnp.float32)
    mixed = jnp.zeros((heads * rows, HD), jnp.float32)
    for ref, begin, column, width in blocks:
        weights = jnp.exp2((s_ref[:, column : column + width] - top) * exponent)
        for lane in range(0, width, HD):
            total = total + weights[:, lane : lane + HD]
        mixed = mixed + jnp.dot(
            weights.astype(jnp.bfloat16),
            ref[begin : begin + width, HD:],
            preferred_element_type=jnp.float32,
        )
    result = (mixed / jnp.sum(total, axis=1, keepdims=True)).astype(jnp.bfloat16)
    for h in range(heads):
        out_ref[:, h * HD : (h + 1) * HD] = result[h * rows : (h + 1) * rows]


def attend(table, info, queries, pieces, slots, begin, size, rows):
    width = queries.shape[1]
    heads = width // HD
    keys = sum(a.shape[0] - TAIL for a in pieces)
    first = begin // rows
    return call(
        functools.partial(attend_kernel, table, slots, first),
        "attend",
        info,
        [queries, *pieces],
        [pl.BlockSpec((rows, width), lambda i, info: (first + i, 0))]
        + [whole(a) for a in pieces],
        pl.BlockSpec((rows, width), lambda i, info: (i, 0)),
        jax.ShapeDtypeStruct((size, width), jnp.bfloat16),
        grid=(size // rows,),
        scratch=[pltpu.VMEM((heads * rows, keys), jnp.float32)],
        flops=ATTEND_FLOPS * size * heads * keys * HD,
        vmem=28,
    )


def project_kernel(table, lines, shares, splits, info, *refs):
    count = table.count
    attention, pieces = refs[:lines], refs[lines : lines + shares]
    r_ref = refs[lines + shares]
    parts, h_ref, w_ref = refs[-2 - 2 * len(splits) : -2], refs[-2], refs[-1]
    share_rows, keep = pieces[0].shape[1], w_ref.shape[2]
    for number, piece in enumerate(pieces):
        start = pl.multiple_of(info[table.rows + number] * share_rows, share_rows)
        for d in range(count):
            w_ref[d, pl.ds(start, share_rows)] = piece[d, :, :keep]
    blocks = [
        line_read(table, info, attention, d).astype(jnp.bfloat16) for d in range(count)
    ]
    for part, copy, (begin, size) in zip(parts, parts[len(splits) :], splits):
        rows = slice(begin, begin + size)
        total = r_ref[rows, :keep].astype(jnp.float32)
        for d in range(count):
            total = total + jnp.dot(
                blocks[d][rows], w_ref[d], preferred_element_type=jnp.float32
            )
        result = total.astype(jnp.bfloat16)
        h_ref[rows, :keep] = result
        part[...] = result
        copy[...] = result


def project(table, info, attention, pieces, residual, hidden, keep, half, halves, splits):
    all_rows, slab = residual.shape
    rows = all_rows // halves
    count, share_rows, _ = pieces[0].shape
    parts = [jax.ShapeDtypeStruct((size, keep), jnp.bfloat16) for _, size in splits * 2]
    row_spec = pl.BlockSpec((rows, slab), lambda i, info: (half, 0))
    args = [*attention, *pieces, residual]
    specs = line_spec(attention, rows, lambda i: 0) + [whole(p) for p in pieces] + [row_spec]
    aliases = {}
    if hidden is not None:
        args.append(hidden)
        specs.append(ANYWHERE)
        aliases = {len(args): len(parts)}
    return call(
        functools.partial(project_kernel, table, len(attention), len(pieces), splits),
        "project",
        info,
        args,
        specs,
        [whole(part) for part in parts] + [row_spec],
        [*parts, jax.ShapeDtypeStruct(residual.shape, jnp.bfloat16)],
        aliases=aliases,
        scratch=[pltpu.VMEM((count, len(pieces) * share_rows, keep), jnp.bfloat16)],
        vmem=36,
    )


def project_raw_kernel(table, lines, halves, raw_lines, shares, info, *refs):
    count = table.count
    attention, refs = refs[: lines * halves], refs[lines * halves :]
    residuals, pieces = refs[:raw_lines], refs[raw_lines : raw_lines + shares]
    raw_ref, h_ref, w_ref = refs[-3:]
    raw, share_rows = h_ref.shape[1], pieces[0].shape[1]
    keep = pieces[0].shape[2] - w_ref.shape[2]
    step = pl.program_id(0)

    @pl.when(step == 0)
    def _():
        for number, piece in enumerate(pieces):
            start = pl.multiple_of(info[table.rows + number] * share_rows, share_rows)
            for d in range(count):
                w_ref[d, pl.ds(start, share_rows)] = piece[d, :, keep:]

    blocks = []
    for d in range(count):
        block = line_read(table, info, attention[:lines], d)
        if halves == 2:
            other = line_read(table, info, attention[lines:], d)
            block = jnp.where(step < pl.num_programs(0) // 2, block, other)
        blocks.append(block.astype(jnp.bfloat16))
    for slab in range(count):
        cols = pl.ds(pl.multiple_of(info[table.place + slab] * raw, raw), raw)
        total = line_read(table, info, residuals, slab)
        for d in range(count):
            total = total + jnp.dot(
                blocks[d], w_ref[d, :, cols], preferred_element_type=jnp.float32
            )
        result = total.astype(jnp.bfloat16)
        raw_ref[:, slab * raw : (slab + 1) * raw] = result
        if slab == 0:
            h_ref[...] = result


def project_raw(table, info, attention, residuals, pieces, hidden, raw, rows):
    all_rows, slab = hidden.shape
    count, share_rows, _ = pieces[0].shape
    halves, lines = len(attention), len(attention[0])
    steps = all_rows // rows
    args = [*sum(attention, []), *residuals, *pieces, hidden]
    specs = []
    for half, blocks in enumerate(attention):
        first, last = half * (steps // halves), (half + 1) * (steps // halves) - 1
        specs += line_spec(
            blocks, rows, lambda i, a=first, b=last: jnp.clip(i, a, b) - a
        )
    out = jax.ShapeDtypeStruct((all_rows, count * raw), jnp.bfloat16)
    return call(
        functools.partial(
            project_raw_kernel, table, lines, halves, len(residuals), len(pieces)
        ),
        "project_raw",
        info,
        args,
        specs
        + line_spec(residuals, rows, lambda i: i)
        + [whole(p) for p in pieces]
        + [ANYWHERE],
        [
            pl.BlockSpec((rows, count * raw), lambda i, info: (i, 0)),
            pl.BlockSpec((rows, raw), lambda i, info: (i, slab // raw - 1)),
        ],
        [out, jax.ShapeDtypeStruct(hidden.shape, jnp.bfloat16)],
        grid=(steps,),
        aliases={len(args): 1},
        scratch=[pltpu.VMEM((count, len(pieces) * share_rows, count * raw), jnp.bfloat16)],
        vmem=36,
    )


def norm_kernel(table, lines, keep, slab, info, g_ref, *refs):
    count = table.count
    blocks, out_ref = refs[:lines], refs[-1]
    raw = slab - keep
    values = []
    squares = jnp.zeros((out_ref.shape[0], 1), jnp.float32)

    def read(d):
        found = [(0, keep, line_read(table, info, blocks, d))]
        if raw:
            cols = slice(d * raw, (d + 1) * raw)
            found.append((keep, raw, refs[lines][:, cols].astype(jnp.float32)))
        return found

    for d in range(count):
        for _, _, value in read(d):
            squares = squares + jnp.sum(value * value, axis=1, keepdims=True)
    inverse = lax.rsqrt(squares / (count * slab) + EPS_NORM)
    for d in range(count):
        for offset, width, value in read(d):
            start = pl.multiple_of(info[table.place + d] * slab + offset, HD)
            cols = pl.ds(start, width)
            out_ref[:, cols] = (value * inverse * g_ref[:, cols]).astype(jnp.bfloat16)


def norm_into(table, info, buffer, blocks, raw_hidden, gain, begin, rows, keep, slab, total_rows):
    width = table.count * slab
    step = math.gcd(rows, 32)
    steps, first = rows // step, begin // step
    args = [gain.reshape(1, width), *blocks]
    in_specs = [pl.BlockSpec((1, width), lambda i, info: (0, 0))]
    in_specs += line_spec(blocks, step, lambda i: i)
    if raw_hidden is not None:
        args.append(raw_hidden)
        in_specs.append(
            pl.BlockSpec((step, raw_hidden.shape[1]), lambda i, info: (first + i, 0))
        )
    aliases = {}
    if buffer is not None:
        args.append(buffer)
        in_specs.append(ANYWHERE)
        aliases = {len(args): 0}
    return call(
        functools.partial(norm_kernel, table, len(blocks), keep, slab),
        "norm",
        info,
        args,
        in_specs,
        pl.BlockSpec((step, width), lambda i, info: (first + i, 0)),
        jax.ShapeDtypeStruct((total_rows, width), jnp.bfloat16),
        grid=(steps,),
        aliases=aliases,
    )


def per_device(queries, span_kv, cache, lengths, offset, out_weight, residual, gain):
    rows = queries.shape[0]
    heads = queries.shape[1] // HD
    depth = out_weight.shape[0]
    slab = residual.shape[1]
    contexts = lax.axis_size("context")
    count = lax.axis_size("tensor")
    context_index = lax.axis_index("context")
    tensor_index = lax.axis_index("tensor")
    kv_index = tensor_index * heads // GROUP
    groups = lax.axis_size("groups")
    shares = groups * contexts
    share = lax.axis_index("groups") * contexts + context_index
    raw = slab // RAW_PART if slab % (RAW_PART * HD) == 0 else 0
    keep = slab - raw
    chunk = min(CHUNK, rows)
    halves = 2 if rows % (2 * chunk) == 0 else 1
    half = rows // halves
    splits = [[(0, chunk), (chunk, half - chunk)] if half > chunk else [(0, half)]] * halves
    if halves == 2 and chunk == 128 and half == 256:
        splits = [splits[0], [(0, 144), (144, 112)]]

    table = Table(contexts, count)
    steering = [context_index, *owners_of(contexts, context_index)]
    steering += [lax.rem(tensor_index + (count - d), count) for d in range(count)]
    steering += [tensor_index == 0, tensor_index == count - 1, share]
    steering += plane_owners(shares, share)
    info = jnp.stack([jnp.asarray(v).astype(jnp.int32) for v in steering])

    cache_local = lax.dynamic_index_in_dim(cache, kv_index, 0, keepdims=False)
    span_local = lax.dynamic_index_in_dim(span_kv, kv_index, 1, keepdims=False)
    positions = offset[0] + context_index * rows + jnp.arange(rows, dtype=jnp.int32)
    both = jnp.concatenate([frequencies(HD)] * 2)
    angles = positions.astype(jnp.float32)[:, None] * both[None, :]
    sign = jnp.where(jnp.arange(HD) < HD // 2, -1.0, 1.0)
    q_turned, payload, *cuts = prepare(
        table, info, queries, span_local, cache_local, out_weight, jnp.cos(angles),
        jnp.sin(angles) * sign[None, :], lengths, depth // shares, slab, keep,
    )
    parts = [cuts[0]]
    for shift in range(1, count):
        pairs = [(i, (i + shift) % count) for i in range(count)]
        parts.append(lax.ppermute(cuts[shift], "tensor", pairs))
    own_weights = stack(info, parts, [])
    own_raw = [last_columns(info, residual, raw, parts[1:])] if raw else []
    pieces = pieces_of(
        payload, "context", contexts, lambda block: gate(info, block, [own_weights, *own_raw])
    )
    slots = cache_local.shape[0]
    mixed = [
        attend(table, info, q_turned, pieces, slots, number * half, half, chunk)
        for number in range(halves)
    ]
    residuals = line_gather(own_raw[0], count) if raw else []
    ready = [gate(info, mixed[0], residuals[3:4]), *mixed[1:]] if raw else mixed
    attention = [line_gather(value, count) for value in ready]
    before = [*attention[0][1:], *mixed[1:], *residuals[1:3], *residuals[4:]]
    weights = plane_gather(
        own_weights,
        groups,
        contexts,
        lambda block, other: gate(info, block, [mixed[0], other]),
        lambda block, mask: gate(
            info,
            block,
            attention[0][3:4] if mask in (mask & -mask,) else before,
        ),
    )
    values, copies, hidden = [], [], None
    for number in range(halves):
        *made, hidden = project(
            table, info, attention[number], weights, residual, hidden, keep, number,
            halves, splits[number],
        )
        values += made[: len(made) // 2]
        copies += made[len(made) // 2 :]
    raw_hidden = None
    if raw:
        raw_hidden, hidden = project_raw(
            table, info, attention, residuals, weights, hidden, raw, chunk
        )
    lines = chunk_gathers(
        info,
        values,
        copies,
        attention[-1][1:],
        [raw_hidden] if raw else [],
        count,
    )
    normed, begin = None, 0
    for blocks, value in zip(lines, values):
        normed = norm_into(
            table, info, normed, blocks, raw_hidden, gain, begin, value.shape[0], keep, slab, rows
        )
        begin += value.shape[0]
    return (hidden, normed)


def solution(mesh):
    in_specs = (
        P(("groups", "context"), "tensor"),
        P(("groups", "context"), None, None),
        P("groups", "context", None),
        P(("groups", "context")),
        P("groups"),
        P("tensor", None),
        P(("groups", "context"), "tensor"),
        P(),
    )
    out_specs = (P(("groups", "context"), "tensor"), P(("groups", "context"), None))
    return jax.shard_map(
        per_device, mesh=mesh, in_specs=in_specs, out_specs=out_specs, check_vma=False
    )
```

```python
import functools
import math

import jax
import jax.numpy as jnp
from jax import lax
from jax.experimental import pallas as pl
from jax.experimental.pallas import tpu as pltpu
from jax.sharding import PartitionSpec as P

GROUP = 8
HD = 128
NEG = -1e30
EPS_NORM = 1e-05
MIB = 1024 * 1024
CHUNK = 128
KEY_BLOCK = 512
ATTEND_FLOPS = 16
RAW_PART = 8
TAIL = 16
DIGIT = 32
ANYWHERE = pl.BlockSpec(memory_space=pl.ANY)


def frequencies(head_width):
    counter = jnp.arange(head_width // 2, dtype=jnp.float32)
    base_freq = jnp.exp(-(2.0 * counter / head_width) * math.log(500000.0))
    wavelength = 2.0 * math.pi / base_freq
    smoothing = (8192.0 / wavelength - 1.0) / 3.0
    blended = (1.0 - smoothing) * base_freq / 8.0 + smoothing * base_freq
    return jnp.where(
        wavelength < 2048.0, base_freq, jnp.where(wavelength > 8192.0, base_freq / 8.0, blended)
    )


def pieces_of(value, axis, count, between=lambda block: block):
    if count & (count - 1) == 0:
        held = {0: value}
        bit = count // 2
        while bit:
            pairs = [(i, i ^ bit) for i in range(count)]
            for mask in sorted(held):
                held[mask | bit] = lax.ppermute(held[mask], axis, pairs)
            if bit == count // 2:
                held[bit] = between(held[bit])
            bit //= 2
        return [held[mask] for mask in range(count)]
    blocks = [value]
    for shift in range(1, count):
        pairs = [(i, (i + shift) % count) for i in range(count)]
        blocks.append(lax.ppermute(value, axis, pairs))
    blocks[-1] = between(blocks[-1])
    return blocks


def owners_of(count, me):
    if count & (count - 1) == 0:
        return [me ^ mask for mask in range(count)]
    return [(me + count - shift) % count for shift in range(count)]


def plane_gather(value, groups, contexts, first, then):
    count = groups * contexts
    if count & (count - 1):
        gathered = lax.all_gather(value, ("groups", "context"), axis=0, tiled=False)
        return [gathered[number] for number in range(count)]
    held = {0: value}
    bits = [1 << b for b in range(contexts.bit_length() - 2, 0, -1)]
    bits += [contexts << b for b in range(groups.bit_length() - 1)]
    for bit in bits:
        axis, flip, size = ("context", bit, contexts)
        if bit >= contexts:
            axis, flip, size = ("groups", bit // contexts, groups)
        pairs = [(i, i ^ flip) for i in range(size)]
        for mask in sorted(held):
            if mask:
                held[mask] = first(held[mask], held[bit])
            held[mask | bit] = lax.ppermute(held[mask], axis, pairs)
    if contexts > 1:
        for mask in sorted(held):
            held[mask] = then(held[mask], mask) if mask else held[mask]
            held[mask | 1] = core_swap(held[mask], contexts)
    return [held[mask] for mask in range(count)]


def core_swap(value, contexts):
    return lax.ppermute(value, "context", [(i, i ^ 1) for i in range(contexts)])


def plane_owners(count, me):
    if count & (count - 1):
        return list(range(count))
    return [me ^ mask for mask in range(count)]


def line_gather(value, count):
    if count != 4:
        return [lax.all_gather(value, "tensor", axis=0, tiled=False)]
    far, last = line_far(value)
    return [value, *line_near(value), far, last]


def line_near(value):
    up = lax.ppermute(value, "tensor", [(0, 1), (1, 2), (2, 3)])
    return up, lax.ppermute(value, "tensor", [(1, 0), (2, 1), (3, 2)])


def line_far(value):
    far = lax.ppermute(value, "tensor", [(0, 2), (1, 3), (2, 0), (3, 1)])
    return far, lax.ppermute(far, "tensor", [(1, 0), (2, 3)])


def chunk_gathers(info, values, copies, second, made, count):
    if count != 4:
        return [line_gather(value, count) for value in values]
    fars, lines = [], []
    for number, value in enumerate(values):
        after = [fars[-1][0]] if number else []
        if number == 1:
            after += second
        fars.append(line_far(gate(info, value, after) if after else value))
    for number, value in enumerate(copies):
        after = list(lines[number - 1][1:3]) if number else []
        if number > 1:
            after.append(fars[number - 2][1])
        if number == len(copies) // 2:
            after += made
        value = gate(info, value, after) if after else value
        lines.append([value, *line_near(value), *fars[number]])
    return lines


class Table:
    def __init__(self, contexts, count):
        self.contexts, self.count = contexts, count
        self.owner = 1
        self.place = 1 + contexts
        self.low = self.place + count
        self.high = self.low + 1
        self.share = self.low + 2
        self.rows = self.low + 3


def line_read(table, info, refs, d, cols=slice(None)):
    if len(refs) == 1:
        return refs[0][info[table.place + d], :, cols].astype(jnp.float32)
    if d == 0:
        return refs[0][:, cols].astype(jnp.float32)
    if d == 2:
        return refs[3][:, cols].astype(jnp.float32)
    near = refs[1 if d == 1 else 2][:, cols].astype(jnp.float32)
    other = refs[4][:, cols].astype(jnp.float32)
    at_end = info[table.low if d == 1 else table.high]
    return jnp.where(at_end == 1, other, near)


def line_spec(blocks, rows, index):
    if len(blocks) == 1:
        count, _, width = blocks[0].shape
        return [pl.BlockSpec((count, rows, width), lambda i, info: (0, index(i), 0))]
    width = blocks[0].shape[1]
    return [pl.BlockSpec((rows, width), lambda i, info: (index(i), 0)) for _ in blocks]


def call(kernel, name, info, args, in_specs, out_specs, out_shape, grid=(1,), aliases=None,
         scratch=(), flops=1, vmem=16):
    return pl.pallas_call(
        kernel,
        grid_spec=pltpu.PrefetchScalarGridSpec(
            num_scalar_prefetch=1,
            grid=grid,
            in_specs=in_specs,
            out_specs=out_specs,
            scratch_shapes=list(scratch),
        ),
        out_shape=out_shape,
        input_output_aliases=aliases or {},
        compiler_params=pltpu.CompilerParams(vmem_limit_bytes=vmem * MIB or None),
        cost_estimate=pl.CostEstimate(flops=flops, bytes_accessed=1, transcendentals=0),
        name=name,
    )(info, *args)


def whole(a):
    zeros = (0,) * len(a.shape)
    return pl.BlockSpec(tuple(a.shape), lambda i, info: zeros)


def prepare_kernel(table, slab, keep, info, q_hbm, kv_hbm, cache_hbm, w_hbm, cos_ref, sin_ref,
                   length_ref, *refs):
    count, raw = table.count, slab - keep
    q_out, kv_out, outs = refs[0], refs[1], refs[2 : 2 + count]
    q_ref, kv_ref, w_ref, sems = refs[2 + count :]
    slots, rows, part = cache_hbm.shape[0], q_ref.shape[0], w_ref.shape[0]
    span, tail = slice(slots, slots + rows), slice(slots + rows, slots + rows + TAIL)
    start = pl.multiple_of(info[table.share] * part, part)
    moves = [
        (w_hbm.at[pl.ds(start, part)], w_ref),
        (kv_hbm, kv_ref),
        (q_hbm, q_ref),
        (cache_hbm, kv_out.at[pl.ds(0, slots)]),
    ]
    copies = [pltpu.make_async_copy(*move, sems.at[n]) for n, move in enumerate(moves)]
    for copy in copies:
        copy.start()

    copies[0].wait()
    for d, out in enumerate(outs):
        target = lax.rem(info[table.place] + d, count)
        out[:, :keep] = w_ref[:, pl.ds(pl.multiple_of(target * slab, slab), keep)]
        for j in range(count if raw else 0):
            out[:, keep + j * raw : keep + (j + 1) * raw] = w_ref[
                :, j * slab + keep : (j + 1) * slab
            ]

    cosine, sine = cos_ref[...], sin_ref[...]

    def turn(block):
        block = block.astype(jnp.float32)
        return (block * cosine + pltpu.roll(block, HD // 2, 1) * sine).astype(jnp.bfloat16)

    copies[1].wait()
    kv_out[span, :HD] = turn(kv_ref[:, :HD])
    kv_out[span, HD:] = kv_ref[:, HD:]
    length = length_ref[0]
    upper = lax.div(length, DIGIT)
    lower = length - upper * DIGIT
    kv_out[tail, :HD] = jnp.full((TAIL, HD), upper.astype(jnp.float32)).astype(jnp.bfloat16)
    kv_out[tail, HD:] = jnp.full((TAIL, HD), lower.astype(jnp.float32)).astype(jnp.bfloat16)
    copies[2].wait()
    for head in range(q_ref.shape[1] // HD):
        cols = slice(head * HD, (head + 1) * HD)
        q_out[:, cols] = turn(q_ref[:, cols])
    copies[3].wait()


def prepare(table, info, queries, span_pairs, cache, out_weight, cosine, sine, lengths, part,
            slab, keep):
    rows = queries.shape[0]
    shapes = [
        jax.ShapeDtypeStruct(queries.shape, jnp.bfloat16),
        jax.ShapeDtypeStruct((cache.shape[0] + rows + TAIL, 2 * HD), jnp.bfloat16),
    ]
    width = keep + table.count * (slab - keep)
    shapes += [jax.ShapeDtypeStruct((part, width), out_weight.dtype)] * table.count
    return call(
        functools.partial(prepare_kernel, table, slab, keep),
        "prepare",
        info,
        [queries, span_pairs, cache, out_weight, cosine, sine, lengths],
        [ANYWHERE] * 4
        + [whole(cosine), whole(sine), pl.BlockSpec(memory_space=pltpu.SMEM)],
        [whole(shape) for shape in shapes],
        shapes,
        scratch=[
            pltpu.VMEM(queries.shape, jnp.bfloat16),
            pltpu.VMEM(span_pairs.shape, jnp.bfloat16),
            pltpu.VMEM((part, out_weight.shape[1]), out_weight.dtype),
            pltpu.SemaphoreType.DMA((4,)),
        ],
        vmem=0,
    )


def last_columns_kernel(info, *refs):
    refs[-1][...] = refs[0][...]


def last_columns(info, value, width, after):
    rows, full = value.shape
    shape = jax.ShapeDtypeStruct((rows, width), value.dtype)
    return call(
        last_columns_kernel,
        "last_columns",
        info,
        [value, *after],
        [pl.BlockSpec((rows, width), lambda i, info: (0, full // width - 1))]
        + [ANYWHERE] * len(after),
        whole(shape),
        shape,
    )


def stack_kernel(count, info, *refs):
    for number, part in enumerate(refs[:count]):
        refs[-1][number] = part[...]


def stack(info, parts, after):
    shape = jax.ShapeDtypeStruct((len(parts), *parts[0].shape), parts[0].dtype)
    return call(
        functools.partial(stack_kernel, len(parts)),
        "stack",
        info,
        [*parts, *after],
        [whole(p) for p in parts] + [ANYWHERE] * len(after),
        whole(shape),
        shape,
    )


def gate_kernel(info, *refs):
    pass


def gate(info, value, after):
    return call(
        gate_kernel,
        "gate",
        info,
        [value, *after],
        [ANYWHERE] * (1 + len(after)),
        ANYWHERE,
        jax.ShapeDtypeStruct(value.shape, value.dtype),
        aliases={1: 0},
    )


def attend_kernel(table, slots, first, info, q_ref, *refs):
    count = table.contexts
    pieces, out_ref, s_ref = refs[:count], refs[-2], refs[-1]
    rows = q_ref.shape[0]
    heads = q_ref.shape[1] // HD
    chunk = pl.program_id(0) + first
    mine = info[0]
    q = jnp.concatenate([q_ref[:, h * HD : (h + 1) * HD] for h in range(heads)], axis=0)
    exponent = math.log2(math.e) / math.sqrt(HD)

    blocks = []
    peak = jnp.full((heads * rows, HD), NEG, jnp.float32)
    column = 0
    for kind in ("cache", "span"):
        for number, ref in enumerate(pieces):
            tail = ref.shape[0] - TAIL
            first, last = (0, slots) if kind == "cache" else (slots, tail)
            width = min(KEY_BLOCK, last - first)
            length = ref[tail : tail + 1, :HD].astype(jnp.float32) * DIGIT + ref[
                tail : tail + 1, HD:
            ].astype(jnp.float32)
            length = jnp.concatenate([length] * (width // HD), axis=1)
            for begin in range(first, last, width):
                scores = lax.dot_general(
                    q,
                    ref[begin : begin + width, :HD],
                    (((1,), (1,)), ((), ())),
                    preferred_element_type=jnp.float32,
                )
                if kind == "cache":
                    slot = lax.broadcasted_iota(jnp.int32, (1, width), 1) + begin
                    live = slot.astype(jnp.float32) < length
                    scores = scores + jnp.where(live, 0.0, NEG)
                elif number == 0:
                    key = lax.broadcasted_iota(jnp.int32, (rows, width), 1) + (begin - first)
                    row = lax.broadcasted_iota(jnp.int32, (rows, width), 0) + chunk * rows
                    bias = jnp.where(key <= row, 0.0, NEG)
                    scores = scores + jnp.concatenate([bias] * heads, axis=0)
                else:
                    scores = scores + jnp.where(info[table.owner + number] < mine, 0.0, NEG)
                s_ref[:, column : column + width] = scores
                for lane in range(0, width, HD):
                    peak = jnp.maximum(peak, scores[:, lane : lane + HD])
                blocks.append((ref, begin, column, width))
                column += width
    top = jnp.max(peak, axis=1, keepdims=True)
    total = jnp.zeros((heads * rows, HD), jnp.float32)
    mixed = jnp.zeros((heads * rows, HD), jnp.float32)
    for ref, begin, column, width in blocks:
        weights = jnp.exp2((s_ref[:, column : column + width] - top) * exponent)
        for lane in range(0, width, HD):
            total = total + weights[:, lane : lane + HD]
        mixed = mixed + jnp.dot(
            weights.astype(jnp.bfloat16),
            ref[begin : begin + width, HD:],
            preferred_element_type=jnp.float32,
        )
    result = (mixed / jnp.sum(total, axis=1, keepdims=True)).astype(jnp.bfloat16)
    for h in range(heads):
        out_ref[:, h * HD : (h + 1) * HD] = result[h * rows : (h + 1) * rows]


def attend(table, info, queries, pieces, slots, begin, size, rows):
    width = queries.shape[1]
    heads = width // HD
    keys = sum(a.shape[0] - TAIL for a in pieces)
    first = begin // rows
    return call(
        functools.partial(attend_kernel, table, slots, first),
        "attend",
        info,
        [queries, *pieces],
        [pl.BlockSpec((rows, width), lambda i, info: (first + i, 0))]
        + [whole(a) for a in pieces],
        pl.BlockSpec((rows, width), lambda i, info: (i, 0)),
        jax.ShapeDtypeStruct((size, width), jnp.bfloat16),
        grid=(size // rows,),
        scratch=[pltpu.VMEM((heads * rows, keys), jnp.float32)],
        flops=ATTEND_FLOPS * size * heads * keys * HD,
        vmem=28,
    )


def project_kernel(table, lines, shares, splits, info, *refs):
    count = table.count
    attention, pieces = refs[:lines], refs[lines : lines + shares]
    r_ref = refs[lines + shares]
    parts, h_ref, w_ref = refs[-2 - 2 * len(splits) : -2], refs[-2], refs[-1]
    share_rows, keep = pieces[0].shape[1], w_ref.shape[2]
    for number, piece in enumerate(pieces):
        start = pl.multiple_of(info[table.rows + number] * share_rows, share_rows)
        for d in range(count):
            w_ref[d, pl.ds(start, share_rows)] = piece[d, :, :keep]
    blocks = [
        line_read(table, info, attention, d).astype(jnp.bfloat16) for d in range(count)
    ]
    for part, copy, (begin, size) in zip(parts, parts[len(splits) :], splits):
        rows = slice(begin, begin + size)
        total = r_ref[rows, :keep].astype(jnp.float32)
        for d in range(count):
            total = total + jnp.dot(
                blocks[d][rows], w_ref[d], preferred_element_type=jnp.float32
            )
        result = total.astype(jnp.bfloat16)
        h_ref[rows, :keep] = result
        part[...] = result
        copy[...] = result


def project(table, info, attention, pieces, residual, hidden, keep, half, halves, splits):
    all_rows, slab = residual.shape
    rows = all_rows // halves
    count, share_rows, _ = pieces[0].shape
    parts = [jax.ShapeDtypeStruct((size, keep), jnp.bfloat16) for _, size in splits * 2]
    row_spec = pl.BlockSpec((rows, slab), lambda i, info: (half, 0))
    args = [*attention, *pieces, residual]
    specs = line_spec(attention, rows, lambda i: 0) + [whole(p) for p in pieces] + [row_spec]
    aliases = {}
    if hidden is not None:
        args.append(hidden)
        specs.append(ANYWHERE)
        aliases = {len(args): len(parts)}
    return call(
        functools.partial(project_kernel, table, len(attention), len(pieces), splits),
        "project",
        info,
        args,
        specs,
        [whole(part) for part in parts] + [row_spec],
        [*parts, jax.ShapeDtypeStruct(residual.shape, jnp.bfloat16)],
        aliases=aliases,
        scratch=[pltpu.VMEM((count, len(pieces) * share_rows, keep), jnp.bfloat16)],
        vmem=36,
    )


def project_raw_kernel(table, lines, halves, raw_lines, shares, info, *refs):
    count = table.count
    attention, refs = refs[: lines * halves], refs[lines * halves :]
    residuals, pieces = refs[:raw_lines], refs[raw_lines : raw_lines + shares]
    raw_ref, h_ref, w_ref = refs[-3:]
    raw, share_rows = h_ref.shape[1], pieces[0].shape[1]
    keep = pieces[0].shape[2] - w_ref.shape[2]
    step = pl.program_id(0)

    @pl.when(step == 0)
    def _():
        for number, piece in enumerate(pieces):
            start = pl.multiple_of(info[table.rows + number] * share_rows, share_rows)
            for d in range(count):
                w_ref[d, pl.ds(start, share_rows)] = piece[d, :, keep:]

    blocks = []
    for d in range(count):
        block = line_read(table, info, attention[:lines], d)
        if halves == 2:
            other = line_read(table, info, attention[lines:], d)
            block = jnp.where(step < pl.num_programs(0) // 2, block, other)
        blocks.append(block.astype(jnp.bfloat16))
    for slab in range(count):
        cols = pl.ds(pl.multiple_of(info[table.place + slab] * raw, raw), raw)
        total = line_read(table, info, residuals, slab)
        for d in range(count):
            total = total + jnp.dot(
                blocks[d], w_ref[d, :, cols], preferred_element_type=jnp.float32
            )
        result = total.astype(jnp.bfloat16)
        raw_ref[:, slab * raw : (slab + 1) * raw] = result
        if slab == 0:
            h_ref[...] = result


def project_raw(table, info, attention, residuals, pieces, hidden, raw, rows):
    all_rows, slab = hidden.shape
    count, share_rows, _ = pieces[0].shape
    halves, lines = len(attention), len(attention[0])
    steps = all_rows // rows
    args = [*sum(attention, []), *residuals, *pieces, hidden]
    specs = []
    for half, blocks in enumerate(attention):
        first, last = half * (steps // halves), (half + 1) * (steps // halves) - 1
        specs += line_spec(
            blocks, rows, lambda i, a=first, b=last: jnp.clip(i, a, b) - a
        )
    out = jax.ShapeDtypeStruct((all_rows, count * raw), jnp.bfloat16)
    return call(
        functools.partial(
            project_raw_kernel, table, lines, halves, len(residuals), len(pieces)
        ),
        "project_raw",
        info,
        args,
        specs
        + line_spec(residuals, rows, lambda i: i)
        + [whole(p) for p in pieces]
        + [ANYWHERE],
        [
            pl.BlockSpec((rows, count * raw), lambda i, info: (i, 0)),
            pl.BlockSpec((rows, raw), lambda i, info: (i, slab // raw - 1)),
        ],
        [out, jax.ShapeDtypeStruct(hidden.shape, jnp.bfloat16)],
        grid=(steps,),
        aliases={len(args): 1},
        scratch=[pltpu.VMEM((count, len(pieces) * share_rows, count * raw), jnp.bfloat16)],
        vmem=36,
    )


def norm_kernel(table, lines, keep, slab, info, g_ref, *refs):
    count = table.count
    blocks, out_ref = refs[:lines], refs[-1]
    raw = slab - keep
    values = []
    squares = jnp.zeros((out_ref.shape[0], 1), jnp.float32)

    def read(d):
        found = [(0, keep, line_read(table, info, blocks, d))]
        if raw:
            cols = slice(d * raw, (d + 1) * raw)
            found.append((keep, raw, refs[lines][:, cols].astype(jnp.float32)))
        return found

    for d in range(count):
        for _, _, value in read(d):
            squares = squares + jnp.sum(value * value, axis=1, keepdims=True)
    inverse = lax.rsqrt(squares / (count * slab) + EPS_NORM)
    for d in range(count):
        for offset, width, value in read(d):
            start = pl.multiple_of(info[table.place + d] * slab + offset, HD)
            cols = pl.ds(start, width)
            out_ref[:, cols] = (value * inverse * g_ref[:, cols]).astype(jnp.bfloat16)


def norm_into(table, info, buffer, blocks, raw_hidden, gain, begin, rows, keep, slab, total_rows):
    width = table.count * slab
    step = math.gcd(rows, 32)
    steps, first = rows // step, begin // step
    args = [gain.reshape(1, width), *blocks]
    in_specs = [pl.BlockSpec((1, width), lambda i, info: (0, 0))]
    in_specs += line_spec(blocks, step, lambda i: i)
    if raw_hidden is not None:
        args.append(raw_hidden)
        in_specs.append(
            pl.BlockSpec((step, raw_hidden.shape[1]), lambda i, info: (first + i, 0))
        )
    aliases = {}
    if buffer is not None:
        args.append(buffer)
        in_specs.append(ANYWHERE)
        aliases = {len(args): 0}
    return call(
        functools.partial(norm_kernel, table, len(blocks), keep, slab),
        "norm",
        info,
        args,
        in_specs,
        pl.BlockSpec((step, width), lambda i, info: (first + i, 0)),
        jax.ShapeDtypeStruct((total_rows, width), jnp.bfloat16),
        grid=(steps,),
        aliases=aliases,
    )


def per_device(queries, span_kv, cache, lengths, offset, out_weight, residual, gain):
    rows = queries.shape[0]
    heads = queries.shape[1] // HD
    depth = out_weight.shape[0]
    slab = residual.shape[1]
    contexts = lax.axis_size("context")
    count = lax.axis_size("tensor")
    context_index = lax.axis_index("context")
    tensor_index = lax.axis_index("tensor")
    kv_index = tensor_index * heads // GROUP
    groups = lax.axis_size("groups")
    shares = groups * contexts
    share = lax.axis_index("groups") * contexts + context_index
    raw = slab // RAW_PART if slab % (RAW_PART * HD) == 0 else 0
    keep = slab - raw
    chunk = min(CHUNK, rows)
    halves = 1
    half = rows // halves
    splits = [[(begin, chunk) for begin in range(0, half, chunk)]] * halves

    table = Table(contexts, count)
    steering = [context_index, *owners_of(contexts, context_index)]
    steering += [lax.rem(tensor_index + (count - d), count) for d in range(count)]
    steering += [tensor_index == 0, tensor_index == count - 1, share]
    steering += plane_owners(shares, share)
    info = jnp.stack([jnp.asarray(v).astype(jnp.int32) for v in steering])

    cache_local = lax.dynamic_index_in_dim(cache, kv_index, 0, keepdims=False)
    span_local = lax.dynamic_index_in_dim(span_kv, kv_index, 1, keepdims=False)
    positions = offset[0] + context_index * rows + jnp.arange(rows, dtype=jnp.int32)
    both = jnp.concatenate([frequencies(HD)] * 2)
    angles = positions.astype(jnp.float32)[:, None] * both[None, :]
    sign = jnp.where(jnp.arange(HD) < HD // 2, -1.0, 1.0)
    q_turned, payload, *cuts = prepare(
        table, info, queries, span_local, cache_local, out_weight, jnp.cos(angles),
        jnp.sin(angles) * sign[None, :], lengths, depth // shares, slab, keep,
    )
    parts = [cuts[0]]
    for shift in range(1, count):
        pairs = [(i, (i + shift) % count) for i in range(count)]
        parts.append(lax.ppermute(cuts[shift], "tensor", pairs))
    own_weights = stack(info, parts, [])
    own_raw = [last_columns(info, residual, raw, parts[1:])] if raw else []
    pieces = pieces_of(
        payload, "context", contexts, lambda block: gate(info, block, [own_weights, *own_raw])
    )
    slots = cache_local.shape[0]
    mixed = [
        attend(table, info, q_turned, pieces, slots, number * half, half, chunk)
        for number in range(halves)
    ]
    residuals = line_gather(own_raw[0], count) if raw else []
    ready = [gate(info, mixed[0], residuals[3:4]), *mixed[1:]] if raw else mixed
    attention = [line_gather(value, count) for value in ready]
    before = [*attention[0][1:], *mixed[1:], *residuals[1:3], *residuals[4:]]
    weights = plane_gather(
        own_weights,
        groups,
        contexts,
        lambda block, other: gate(info, block, [mixed[0], other]),
        lambda block, mask: gate(
            info,
            block,
            attention[0][3:4] if mask in (mask & -mask,) else before,
        ),
    )
    values, copies, hidden = [], [], None
    for number in range(halves):
        *made, hidden = project(
            table, info, attention[number], weights, residual, hidden, keep, number,
            halves, splits[number],
        )
        values += made[: len(made) // 2]
        copies += made[len(made) // 2 :]
    raw_hidden = None
    if raw:
        raw_hidden, hidden = project_raw(
            table, info, attention, residuals, weights, hidden, raw, chunk
        )
    lines = chunk_gathers(
        info,
        values,
        copies,
        attention[-1][1:] if halves > 1 else [],
        [raw_hidden] if raw else [],
        count,
    )
    normed, begin = None, 0
    for blocks, value in zip(lines, values):
        normed = norm_into(
            table, info, normed, blocks, raw_hidden, gain, begin, value.shape[0], keep, slab, rows
        )
        begin += value.shape[0]
    return (hidden, normed)


def solution(mesh):
    in_specs = (
        P(("groups", "context"), "tensor"),
        P(("groups", "context"), None, None),
        P("groups", "context", None),
        P(("groups", "context")),
        P("groups"),
        P("tensor", None),
        P(("groups", "context"), "tensor"),
        P(),
    )
    out_specs = (P(("groups", "context"), "tensor"), P(("groups", "context"), None))
    return jax.shard_map(
        per_device, mesh=mesh, in_specs=in_specs, out_specs=out_specs, check_vma=False
    )
```

```python
import functools
import math

import jax
import jax.numpy as jnp
from jax import lax
from jax.experimental import pallas as pl
from jax.experimental.pallas import tpu as pltpu
from jax.sharding import PartitionSpec as P

GROUP = 8
HD = 128
NEG = -1e30
EPS_NORM = 1e-05
MIB = 1024 * 1024
CHUNK = 128
KEY_BLOCK = 512
ATTEND_FLOPS = 16
RAW_PART = 8
TAIL = 16
DIGIT = 32
ANYWHERE = pl.BlockSpec(memory_space=pl.ANY)


def frequencies(head_width):
    counter = jnp.arange(head_width // 2, dtype=jnp.float32)
    base_freq = jnp.exp(-(2.0 * counter / head_width) * math.log(500000.0))
    wavelength = 2.0 * math.pi / base_freq
    smoothing = (8192.0 / wavelength - 1.0) / 3.0
    blended = (1.0 - smoothing) * base_freq / 8.0 + smoothing * base_freq
    return jnp.where(
        wavelength < 2048.0, base_freq, jnp.where(wavelength > 8192.0, base_freq / 8.0, blended)
    )


def pieces_of(value, axis, count, between=lambda block: block):
    if count & (count - 1) == 0:
        held = {0: value}
        bit = count // 2
        while bit:
            pairs = [(i, i ^ bit) for i in range(count)]
            for mask in sorted(held):
                held[mask | bit] = lax.ppermute(held[mask], axis, pairs)
            if bit == count // 2:
                held[bit] = between(held[bit])
            bit //= 2
        return [held[mask] for mask in range(count)]
    blocks = [value]
    for shift in range(1, count):
        pairs = [(i, (i + shift) % count) for i in range(count)]
        blocks.append(lax.ppermute(value, axis, pairs))
    blocks[-1] = between(blocks[-1])
    return blocks


def owners_of(count, me):
    if count & (count - 1) == 0:
        return [me ^ mask for mask in range(count)]
    return [(me + count - shift) % count for shift in range(count)]


def plane_gather(value, groups, contexts, first, then):
    count = groups * contexts
    if count & (count - 1):
        gathered = lax.all_gather(value, ("groups", "context"), axis=0, tiled=False)
        return [gathered[number] for number in range(count)]
    held = {0: value}
    bits = [1 << b for b in range(contexts.bit_length() - 2, 0, -1)]
    bits += [contexts << b for b in range(groups.bit_length() - 1)]
    for bit in bits:
        axis, flip, size = ("context", bit, contexts)
        if bit >= contexts:
            axis, flip, size = ("groups", bit // contexts, groups)
        pairs = [(i, i ^ flip) for i in range(size)]
        for mask in sorted(held):
            if mask:
                held[mask] = first(held[mask], held[bit])
            held[mask | bit] = lax.ppermute(held[mask], axis, pairs)
    if contexts > 1:
        for mask in sorted(held):
            held[mask] = then(held[mask], mask) if mask else held[mask]
            held[mask | 1] = core_swap(held[mask], contexts)
    return [held[mask] for mask in range(count)]


def core_swap(value, contexts):
    return lax.ppermute(value, "context", [(i, i ^ 1) for i in range(contexts)])


def plane_owners(count, me):
    if count & (count - 1):
        return list(range(count))
    return [me ^ mask for mask in range(count)]


def line_gather(value, count):
    if count != 4:
        return [lax.all_gather(value, "tensor", axis=0, tiled=False)]
    far, last = line_far(value)
    return [value, *line_near(value), far, last]


def line_near(value):
    up = lax.ppermute(value, "tensor", [(0, 1), (1, 2), (2, 3)])
    return up, lax.ppermute(value, "tensor", [(1, 0), (2, 1), (3, 2)])


def line_far(value):
    far = lax.ppermute(value, "tensor", [(0, 2), (1, 3), (2, 0), (3, 1)])
    return far, lax.ppermute(far, "tensor", [(1, 0), (2, 3)])


def chunk_gathers(info, values, copies, second, made, count):
    if count != 4:
        return [line_gather(value, count) for value in values]
    fars, lines = [], []
    for number, value in enumerate(values):
        after = [fars[-1][0]] if number else []
        if number == 1:
            after += second
        fars.append(line_far(gate(info, value, after) if after else value))
    for number, value in enumerate(copies):
        after = list(lines[number - 1][1:3]) if number else []
        if number > 1:
            after.append(fars[number - 2][1])
        if number == len(copies) // 2:
            after += made
        value = gate(info, value, after) if after else value
        lines.append([value, *line_near(value), *fars[number]])
    return lines


class Table:
    def __init__(self, contexts, count):
        self.contexts, self.count = contexts, count
        self.owner = 1
        self.place = 1 + contexts
        self.low = self.place + count
        self.high = self.low + 1
        self.share = self.low + 2
        self.rows = self.low + 3


def line_read(table, info, refs, d, cols=slice(None)):
    if len(refs) == 1:
        return refs[0][info[table.place + d], :, cols].astype(jnp.float32)
    if d == 0:
        return refs[0][:, cols].astype(jnp.float32)
    if d == 2:
        return refs[3][:, cols].astype(jnp.float32)
    near = refs[1 if d == 1 else 2][:, cols].astype(jnp.float32)
    other = refs[4][:, cols].astype(jnp.float32)
    at_end = info[table.low if d == 1 else table.high]
    return jnp.where(at_end == 1, other, near)


def line_spec(blocks, rows, index):
    if len(blocks) == 1:
        count, _, width = blocks[0].shape
        return [pl.BlockSpec((count, rows, width), lambda i, info: (0, index(i), 0))]
    width = blocks[0].shape[1]
    return [pl.BlockSpec((rows, width), lambda i, info: (index(i), 0)) for _ in blocks]


def call(kernel, name, info, args, in_specs, out_specs, out_shape, grid=(1,), aliases=None,
         scratch=(), flops=1, vmem=16):
    return pl.pallas_call(
        kernel,
        grid_spec=pltpu.PrefetchScalarGridSpec(
            num_scalar_prefetch=1,
            grid=grid,
            in_specs=in_specs,
            out_specs=out_specs,
            scratch_shapes=list(scratch),
        ),
        out_shape=out_shape,
        input_output_aliases=aliases or {},
        compiler_params=pltpu.CompilerParams(vmem_limit_bytes=vmem * MIB or None),
        cost_estimate=pl.CostEstimate(flops=flops, bytes_accessed=1, transcendentals=0),
        name=name,
    )(info, *args)


def whole(a):
    zeros = (0,) * len(a.shape)
    return pl.BlockSpec(tuple(a.shape), lambda i, info: zeros)


def prepare_kernel(table, slab, keep, info, q_hbm, kv_hbm, cache_hbm, w_hbm, r_hbm, cos_ref,
                   sin_ref, length_ref, *refs):
    count, raw = table.count, slab - keep
    q_out, kv_out, outs = refs[0], refs[1], refs[2 : 2 + count]
    q_ref, kv_ref, w_ref, sems = refs[-4:]
    slots, rows, part = cache_hbm.shape[0], q_ref.shape[0], w_ref.shape[0]
    span, tail = slice(slots, slots + rows), slice(slots + rows, slots + rows + TAIL)
    start = pl.multiple_of(info[table.share] * part, part)
    moves = [
        (w_hbm.at[pl.ds(start, part)], w_ref),
        (kv_hbm, kv_ref),
        (q_hbm, q_ref),
        (cache_hbm, kv_out.at[pl.ds(0, slots)]),
    ]
    if raw:
        moves.append((r_hbm.at[:, pl.ds(keep, raw)], refs[2 + count]))
    copies = [pltpu.make_async_copy(*move, sems.at[n]) for n, move in enumerate(moves)]
    for copy in copies:
        copy.start()

    copies[0].wait()
    for d, out in enumerate(outs):
        target = lax.rem(info[table.place] + d, count)
        out[:, :keep] = w_ref[:, pl.ds(pl.multiple_of(target * slab, slab), keep)]
        for j in range(count if raw else 0):
            out[:, keep + j * raw : keep + (j + 1) * raw] = w_ref[
                :, j * slab + keep : (j + 1) * slab
            ]

    cosine, sine = cos_ref[...], sin_ref[...]

    def turn(block):
        block = block.astype(jnp.float32)
        return (block * cosine + pltpu.roll(block, HD // 2, 1) * sine).astype(jnp.bfloat16)

    copies[1].wait()
    kv_out[span, :HD] = turn(kv_ref[:, :HD])
    kv_out[span, HD:] = kv_ref[:, HD:]
    length = length_ref[0]
    upper = lax.div(length, DIGIT)
    lower = length - upper * DIGIT
    kv_out[tail, :HD] = jnp.full((TAIL, HD), upper.astype(jnp.float32)).astype(jnp.bfloat16)
    kv_out[tail, HD:] = jnp.full((TAIL, HD), lower.astype(jnp.float32)).astype(jnp.bfloat16)
    copies[2].wait()
    for head in range(q_ref.shape[1] // HD):
        cols = slice(head * HD, (head + 1) * HD)
        q_out[:, cols] = turn(q_ref[:, cols])
    for copy in copies[3:]:
        copy.wait()


def prepare(table, info, queries, span_pairs, cache, out_weight, residual, cosine, sine, lengths,
            part, keep):
    rows, slab = residual.shape
    shapes = [
        jax.ShapeDtypeStruct(queries.shape, jnp.bfloat16),
        jax.ShapeDtypeStruct((cache.shape[0] + rows + TAIL, 2 * HD), jnp.bfloat16),
    ]
    width = keep + table.count * (slab - keep)
    shapes += [jax.ShapeDtypeStruct((part, width), out_weight.dtype)] * table.count
    if keep < slab:
        shapes.append(jax.ShapeDtypeStruct((rows, slab - keep), residual.dtype))
    return call(
        functools.partial(prepare_kernel, table, slab, keep),
        "prepare",
        info,
        [queries, span_pairs, cache, out_weight, residual, cosine, sine, lengths],
        [ANYWHERE] * 5
        + [whole(cosine), whole(sine), pl.BlockSpec(memory_space=pltpu.SMEM)],
        [whole(shape) for shape in shapes],
        shapes,
        scratch=[
            pltpu.VMEM(queries.shape, jnp.bfloat16),
            pltpu.VMEM(span_pairs.shape, jnp.bfloat16),
            pltpu.VMEM((part, out_weight.shape[1]), out_weight.dtype),
            pltpu.SemaphoreType.DMA((5,)),
        ],
        vmem=0,
    )


def stack_kernel(count, info, *refs):
    for number, part in enumerate(refs[:count]):
        refs[-1][number] = part[...]


def stack(info, parts, after):
    shape = jax.ShapeDtypeStruct((len(parts), *parts[0].shape), parts[0].dtype)
    return call(
        functools.partial(stack_kernel, len(parts)),
        "stack",
        info,
        [*parts, *after],
        [whole(p) for p in parts] + [ANYWHERE] * len(after),
        whole(shape),
        shape,
    )


def gate_kernel(info, *refs):
    pass


def gate(info, value, after):
    return call(
        gate_kernel,
        "gate",
        info,
        [value, *after],
        [ANYWHERE] * (1 + len(after)),
        ANYWHERE,
        jax.ShapeDtypeStruct(value.shape, value.dtype),
        aliases={1: 0},
    )


def attend_kernel(table, slots, first, info, q_ref, *refs):
    count = table.contexts
    pieces, out_ref, s_ref = refs[:count], refs[-2], refs[-1]
    rows = q_ref.shape[0]
    heads = q_ref.shape[1] // HD
    chunk = pl.program_id(0) + first
    mine = info[0]
    q = jnp.concatenate([q_ref[:, h * HD : (h + 1) * HD] for h in range(heads)], axis=0)
    exponent = math.log2(math.e) / math.sqrt(HD)

    blocks = []
    peak = jnp.full((heads * rows, HD), NEG, jnp.float32)
    column = 0
    for kind in ("cache", "span"):
        for number, ref in enumerate(pieces):
            tail = ref.shape[0] - TAIL
            first, last = (0, slots) if kind == "cache" else (slots, tail)
            width = min(KEY_BLOCK, last - first)
            length = ref[tail : tail + 1, :HD].astype(jnp.float32) * DIGIT + ref[
                tail : tail + 1, HD:
            ].astype(jnp.float32)
            length = jnp.concatenate([length] * (width // HD), axis=1)
            for begin in range(first, last, width):
                scores = lax.dot_general(
                    q,
                    ref[begin : begin + width, :HD],
                    (((1,), (1,)), ((), ())),
                    preferred_element_type=jnp.float32,
                )
                if kind == "cache":
                    slot = lax.broadcasted_iota(jnp.int32, (1, width), 1) + begin
                    live = slot.astype(jnp.float32) < length
                    scores = scores + jnp.where(live, 0.0, NEG)
                elif number == 0:
                    key = lax.broadcasted_iota(jnp.int32, (rows, width), 1) + (begin - first)
                    row = lax.broadcasted_iota(jnp.int32, (rows, width), 0) + chunk * rows
                    bias = jnp.where(key <= row, 0.0, NEG)
                    scores = scores + jnp.concatenate([bias] * heads, axis=0)
                else:
                    scores = scores + jnp.where(info[table.owner + number] < mine, 0.0, NEG)
                s_ref[:, column : column + width] = scores
                for lane in range(0, width, HD):
                    peak = jnp.maximum(peak, scores[:, lane : lane + HD])
                blocks.append((ref, begin, column, width))
                column += width
    top = jnp.max(peak, axis=1, keepdims=True)
    total = jnp.zeros((heads * rows, HD), jnp.float32)
    mixed = jnp.zeros((heads * rows, HD), jnp.float32)
    for ref, begin, column, width in blocks:
        weights = jnp.exp2((s_ref[:, column : column + width] - top) * exponent)
        for lane in range(0, width, HD):
            total = total + weights[:, lane : lane + HD]
        mixed = mixed + jnp.dot(
            weights.astype(jnp.bfloat16),
            ref[begin : begin + width, HD:],
            preferred_element_type=jnp.float32,
        )
    result = (mixed / jnp.sum(total, axis=1, keepdims=True)).astype(jnp.bfloat16)
    for h in range(heads):
        out_ref[:, h * HD : (h + 1) * HD] = result[h * rows : (h + 1) * rows]


def attend(table, info, queries, pieces, slots, begin, size, rows):
    width = queries.shape[1]
    heads = width // HD
    keys = sum(a.shape[0] - TAIL for a in pieces)
    first = begin // rows
    return call(
        functools.partial(attend_kernel, table, slots, first),
        "attend",
        info,
        [queries, *pieces],
        [pl.BlockSpec((rows, width), lambda i, info: (first + i, 0))]
        + [whole(a) for a in pieces],
        pl.BlockSpec((rows, width), lambda i, info: (i, 0)),
        jax.ShapeDtypeStruct((size, width), jnp.bfloat16),
        grid=(size // rows,),
        scratch=[pltpu.VMEM((heads * rows, keys), jnp.float32)],
        flops=ATTEND_FLOPS * size * heads * keys * HD,
        vmem=28,
    )


def project_kernel(table, lines, shares, splits, info, *refs):
    count = table.count
    attention, pieces = refs[:lines], refs[lines : lines + shares]
    r_ref = refs[lines + shares]
    parts, h_ref, w_ref = refs[-2 - 2 * len(splits) : -2], refs[-2], refs[-1]
    share_rows, keep = pieces[0].shape[1], w_ref.shape[2]
    for number, piece in enumerate(pieces):
        start = pl.multiple_of(info[table.rows + number] * share_rows, share_rows)
        for d in range(count):
            w_ref[d, pl.ds(start, share_rows)] = piece[d, :, :keep]
    blocks = [
        line_read(table, info, attention, d).astype(jnp.bfloat16) for d in range(count)
    ]
    for part, copy, (begin, size) in zip(parts, parts[len(splits) :], splits):
        rows = slice(begin, begin + size)
        total = r_ref[rows, :keep].astype(jnp.float32)
        for d in range(count):
            total = total + jnp.dot(
                blocks[d][rows], w_ref[d], preferred_element_type=jnp.float32
            )
        result = total.astype(jnp.bfloat16)
        h_ref[rows, :keep] = result
        part[...] = result
        copy[...] = result


def project(table, info, attention, pieces, residual, hidden, keep, half, halves, splits):
    all_rows, slab = residual.shape
    rows = all_rows // halves
    count, share_rows, _ = pieces[0].shape
    parts = [jax.ShapeDtypeStruct((size, keep), jnp.bfloat16) for _, size in splits * 2]
    row_spec = pl.BlockSpec((rows, slab), lambda i, info: (half, 0))
    args = [*attention, *pieces, residual]
    specs = line_spec(attention, rows, lambda i: 0) + [whole(p) for p in pieces] + [row_spec]
    aliases = {}
    if hidden is not None:
        args.append(hidden)
        specs.append(ANYWHERE)
        aliases = {len(args): len(parts)}
    return call(
        functools.partial(project_kernel, table, len(attention), len(pieces), splits),
        "project",
        info,
        args,
        specs,
        [whole(part) for part in parts] + [row_spec],
        [*parts, jax.ShapeDtypeStruct(residual.shape, jnp.bfloat16)],
        aliases=aliases,
        scratch=[pltpu.VMEM((count, len(pieces) * share_rows, keep), jnp.bfloat16)],
        vmem=36,
    )


def project_raw_kernel(table, lines, halves, raw_lines, shares, info, *refs):
    count = table.count
    attention, refs = refs[: lines * halves], refs[lines * halves :]
    residuals, pieces = refs[:raw_lines], refs[raw_lines : raw_lines + shares]
    raw_ref, h_ref, w_ref = refs[-3:]
    raw, share_rows = h_ref.shape[1], pieces[0].shape[1]
    keep = pieces[0].shape[2] - w_ref.shape[2]
    step = pl.program_id(0)

    @pl.when(step == 0)
    def _():
        for number, piece in enumerate(pieces):
            start = pl.multiple_of(info[table.rows + number] * share_rows, share_rows)
            for d in range(count):
                w_ref[d, pl.ds(start, share_rows)] = piece[d, :, keep:]

    blocks = []
    for d in range(count):
        block = line_read(table, info, attention[:lines], d)
        if halves == 2:
            other = line_read(table, info, attention[lines:], d)
            block = jnp.where(step < pl.num_programs(0) // 2, block, other)
        blocks.append(block.astype(jnp.bfloat16))
    for slab in range(count):
        cols = pl.ds(pl.multiple_of(info[table.place + slab] * raw, raw), raw)
        total = line_read(table, info, residuals, slab)
        for d in range(count):
            total = total + jnp.dot(
                blocks[d], w_ref[d, :, cols], preferred_element_type=jnp.float32
            )
        result = total.astype(jnp.bfloat16)
        raw_ref[:, slab * raw : (slab + 1) * raw] = result
        if slab == 0:
            h_ref[...] = result


def project_raw(table, info, attention, residuals, pieces, hidden, raw, rows):
    all_rows, slab = hidden.shape
    count, share_rows, _ = pieces[0].shape
    halves, lines = len(attention), len(attention[0])
    steps = all_rows // rows
    args = [*sum(attention, []), *residuals, *pieces, hidden]
    specs = []
    for half, blocks in enumerate(attention):
        first, last = half * (steps // halves), (half + 1) * (steps // halves) - 1
        specs += line_spec(
            blocks, rows, lambda i, a=first, b=last: jnp.clip(i, a, b) - a
        )
    out = jax.ShapeDtypeStruct((all_rows, count * raw), jnp.bfloat16)
    return call(
        functools.partial(
            project_raw_kernel, table, lines, halves, len(residuals), len(pieces)
        ),
        "project_raw",
        info,
        args,
        specs
        + line_spec(residuals, rows, lambda i: i)
        + [whole(p) for p in pieces]
        + [ANYWHERE],
        [
            pl.BlockSpec((rows, count * raw), lambda i, info: (i, 0)),
            pl.BlockSpec((rows, raw), lambda i, info: (i, slab // raw - 1)),
        ],
        [out, jax.ShapeDtypeStruct(hidden.shape, jnp.bfloat16)],
        grid=(steps,),
        aliases={len(args): 1},
        scratch=[pltpu.VMEM((count, len(pieces) * share_rows, count * raw), jnp.bfloat16)],
        vmem=36,
    )


def norm_kernel(table, lines, keep, slab, info, g_ref, *refs):
    count = table.count
    blocks, out_ref = refs[:lines], refs[-1]
    raw = slab - keep
    values = []
    squares = jnp.zeros((out_ref.shape[0], 1), jnp.float32)

    def read(d):
        found = [(0, keep, line_read(table, info, blocks, d))]
        if raw:
            cols = slice(d * raw, (d + 1) * raw)
            found.append((keep, raw, refs[lines][:, cols].astype(jnp.float32)))
        return found

    for d in range(count):
        for _, _, value in read(d):
            squares = squares + jnp.sum(value * value, axis=1, keepdims=True)
    inverse = lax.rsqrt(squares / (count * slab) + EPS_NORM)
    for d in range(count):
        for offset, width, value in read(d):
            start = pl.multiple_of(info[table.place + d] * slab + offset, HD)
            cols = pl.ds(start, width)
            out_ref[:, cols] = (value * inverse * g_ref[:, cols]).astype(jnp.bfloat16)


def norm_into(table, info, buffer, blocks, raw_hidden, gain, begin, rows, keep, slab, total_rows):
    width = table.count * slab
    step = math.gcd(rows, 32)
    steps, first = rows // step, begin // step
    args = [gain.reshape(1, width), *blocks]
    in_specs = [pl.BlockSpec((1, width), lambda i, info: (0, 0))]
    in_specs += line_spec(blocks, step, lambda i: i)
    if raw_hidden is not None:
        args.append(raw_hidden)
        in_specs.append(
            pl.BlockSpec((step, raw_hidden.shape[1]), lambda i, info: (first + i, 0))
        )
    aliases = {}
    if buffer is not None:
        args.append(buffer)
        in_specs.append(ANYWHERE)
        aliases = {len(args): 0}
    return call(
        functools.partial(norm_kernel, table, len(blocks), keep, slab),
        "norm",
        info,
        args,
        in_specs,
        pl.BlockSpec((step, width), lambda i, info: (first + i, 0)),
        jax.ShapeDtypeStruct((total_rows, width), jnp.bfloat16),
        grid=(steps,),
        aliases=aliases,
    )


def per_device(queries, span_kv, cache, lengths, offset, out_weight, residual, gain):
    rows = queries.shape[0]
    heads = queries.shape[1] // HD
    depth = out_weight.shape[0]
    slab = residual.shape[1]
    contexts = lax.axis_size("context")
    count = lax.axis_size("tensor")
    context_index = lax.axis_index("context")
    tensor_index = lax.axis_index("tensor")
    kv_index = tensor_index * heads // GROUP
    groups = lax.axis_size("groups")
    shares = groups * contexts
    share = lax.axis_index("groups") * contexts + context_index
    raw = slab // RAW_PART if slab % (RAW_PART * HD) == 0 else 0
    keep = slab - raw
    chunk = min(CHUNK, rows)
    halves = 1
    half = rows // halves
    splits = [[(begin, chunk) for begin in range(0, half, chunk)]] * halves

    table = Table(contexts, count)
    steering = [context_index, *owners_of(contexts, context_index)]
    steering += [lax.rem(tensor_index + (count - d), count) for d in range(count)]
    steering += [tensor_index == 0, tensor_index == count - 1, share]
    steering += plane_owners(shares, share)
    info = jnp.stack([jnp.asarray(v).astype(jnp.int32) for v in steering])

    cache_local = lax.dynamic_index_in_dim(cache, kv_index, 0, keepdims=False)
    span_local = lax.dynamic_index_in_dim(span_kv, kv_index, 1, keepdims=False)
    positions = offset[0] + context_index * rows + jnp.arange(rows, dtype=jnp.int32)
    both = jnp.concatenate([frequencies(HD)] * 2)
    angles = positions.astype(jnp.float32)[:, None] * both[None, :]
    sign = jnp.where(jnp.arange(HD) < HD // 2, -1.0, 1.0)
    q_turned, payload, *cuts = prepare(
        table, info, queries, span_local, cache_local, out_weight, residual, jnp.cos(angles),
        jnp.sin(angles) * sign[None, :], lengths, depth // shares, keep,
    )
    parts = [cuts[0]]
    for shift in range(1, count):
        pairs = [(i, (i + shift) % count) for i in range(count)]
        parts.append(lax.ppermute(cuts[shift], "tensor", pairs))
    own_weights = stack(info, parts, [])
    own_raw = [gate(info, cuts[count], parts[1:])] if raw else []
    pieces = pieces_of(
        payload, "context", contexts, lambda block: gate(info, block, [own_weights, *own_raw])
    )
    slots = cache_local.shape[0]
    mixed = [
        attend(table, info, q_turned, pieces, slots, number * half, half, chunk)
        for number in range(halves)
    ]
    residuals = line_gather(own_raw[0], count) if raw else []
    ready = [gate(info, mixed[0], residuals[1:4] or residuals), *mixed[1:]] if raw else mixed
    attention = [line_gather(value, count) for value in ready]
    before = [*attention[0][1:], *mixed[1:], *residuals[4:]]
    weights = plane_gather(
        own_weights,
        groups,
        contexts,
        lambda block, other: gate(info, block, mixed[:1]),
        lambda block, mask: gate(
            info,
            block,
            attention[0][1:3] if mask in (mask & -mask,) else before,
        ),
    )
    values, copies, hidden = [], [], None
    for number in range(halves):
        *made, hidden = project(
            table, info, attention[number], weights, residual, hidden, keep, number,
            halves, splits[number],
        )
        values += made[: len(made) // 2]
        copies += made[len(made) // 2 :]
    raw_hidden = None
    if raw:
        raw_hidden, hidden = project_raw(
            table, info, attention, residuals, weights, hidden, raw, chunk
        )
    lines = chunk_gathers(
        info,
        values,
        copies,
        attention[-1][1:] if halves > 1 else [],
        [raw_hidden] if raw else [],
        count,
    )
    normed, begin = None, 0
    for blocks, value in zip(lines, values):
        normed = norm_into(
            table, info, normed, blocks, raw_hidden, gain, begin, value.shape[0], keep, slab, rows
        )
        begin += value.shape[0]
    return (hidden, normed)


def solution(mesh):
    in_specs = (
        P(("groups", "context"), "tensor"),
        P(("groups", "context"), None, None),
        P("groups", "context", None),
        P(("groups", "context")),
        P("groups"),
        P("tensor", None),
        P(("groups", "context"), "tensor"),
        P(),
    )
    out_specs = (P(("groups", "context"), "tensor"), P(("groups", "context"), None))
    return jax.shard_map(
        per_device, mesh=mesh, in_specs=in_specs, out_specs=out_specs, check_vma=False
    )
```

```python
import functools
import math

import jax
import jax.numpy as jnp
from jax import lax
from jax.experimental import pallas as pl
from jax.experimental.pallas import tpu as pltpu
from jax.sharding import PartitionSpec as P

GROUP = 8
HD = 128
NEG = -1e30
EPS_NORM = 1e-05
MIB = 1024 * 1024
CHUNK = 128
KEY_BLOCK = 512
ATTEND_FLOPS = 16
RAW_PART = 4
TAIL = 16
DIGIT = 32
ANYWHERE = pl.BlockSpec(memory_space=pl.ANY)


def frequencies(head_width):
    counter = jnp.arange(head_width // 2, dtype=jnp.float32)
    base_freq = jnp.exp(-(2.0 * counter / head_width) * math.log(500000.0))
    wavelength = 2.0 * math.pi / base_freq
    smoothing = (8192.0 / wavelength - 1.0) / 3.0
    blended = (1.0 - smoothing) * base_freq / 8.0 + smoothing * base_freq
    return jnp.where(
        wavelength < 2048.0, base_freq, jnp.where(wavelength > 8192.0, base_freq / 8.0, blended)
    )


def pieces_of(value, axis, count, between=lambda block: block):
    if count & (count - 1) == 0:
        held = {0: value}
        bit = count // 2
        while bit:
            pairs = [(i, i ^ bit) for i in range(count)]
            for mask in sorted(held):
                held[mask | bit] = lax.ppermute(held[mask], axis, pairs)
            if bit == count // 2:
                held[bit] = between(held[bit])
            bit //= 2
        return [held[mask] for mask in range(count)]
    blocks = [value]
    for shift in range(1, count):
        pairs = [(i, (i + shift) % count) for i in range(count)]
        blocks.append(lax.ppermute(value, axis, pairs))
    blocks[-1] = between(blocks[-1])
    return blocks


def owners_of(count, me):
    if count & (count - 1) == 0:
        return [me ^ mask for mask in range(count)]
    return [(me + count - shift) % count for shift in range(count)]


def plane_gather(value, groups, contexts, first, then):
    count = groups * contexts
    if count & (count - 1):
        gathered = lax.all_gather(value, ("groups", "context"), axis=0, tiled=False)
        return [gathered[number] for number in range(count)]
    held = {0: value}
    bits = [1 << b for b in range(contexts.bit_length() - 2, 0, -1)]
    bits += [contexts << b for b in range(groups.bit_length() - 1)]
    for bit in bits:
        axis, flip, size = ("context", bit, contexts)
        if bit >= contexts:
            axis, flip, size = ("groups", bit // contexts, groups)
        pairs = [(i, i ^ flip) for i in range(size)]
        for mask in sorted(held):
            if mask:
                held[mask] = first(held[mask], held[bit])
            held[mask | bit] = lax.ppermute(held[mask], axis, pairs)
    if contexts > 1:
        for mask in sorted(held):
            held[mask] = then(held[mask], mask) if mask else held[mask]
            held[mask | 1] = core_swap(held[mask], contexts)
    return [held[mask] for mask in range(count)]


def core_swap(value, contexts):
    return lax.ppermute(value, "context", [(i, i ^ 1) for i in range(contexts)])


def plane_owners(count, me):
    if count & (count - 1):
        return list(range(count))
    return [me ^ mask for mask in range(count)]


def line_gather(value, count):
    if count != 4:
        return [lax.all_gather(value, "tensor", axis=0, tiled=False)]
    far, last = line_far(value)
    return [value, *line_near(value), far, last]


def line_near(value):
    up = lax.ppermute(value, "tensor", [(0, 1), (1, 2), (2, 3)])
    return up, lax.ppermute(value, "tensor", [(1, 0), (2, 1), (3, 2)])


def line_far(value):
    far = lax.ppermute(value, "tensor", [(0, 2), (1, 3), (2, 0), (3, 1)])
    return far, lax.ppermute(far, "tensor", [(1, 0), (2, 3)])


def chunk_gathers(info, values, copies, second, made, count):
    if count != 4:
        return [line_gather(value, count) for value in values]
    fars, lines = [], []
    for number, value in enumerate(values):
        after = [fars[-1][0]] if number else []
        if number == 1:
            after += second
        fars.append(line_far(gate(info, value, after) if after else value))
    for number, value in enumerate(copies):
        after = list(lines[number - 1][1:3]) if number else []
        if number > 1:
            after.append(fars[number - 2][1])
        if number == len(copies) // 2:
            after += made
        value = gate(info, value, after) if after else value
        lines.append([value, *line_near(value), *fars[number]])
    return lines


class Table:
    def __init__(self, contexts, count):
        self.contexts, self.count = contexts, count
        self.owner = 1
        self.place = 1 + contexts
        self.low = self.place + count
        self.high = self.low + 1
        self.share = self.low + 2
        self.rows = self.low + 3


def line_read(table, info, refs, d, cols=slice(None)):
    if len(refs) == 1:
        return refs[0][info[table.place + d], :, cols].astype(jnp.float32)
    if d == 0:
        return refs[0][:, cols].astype(jnp.float32)
    if d == 2:
        return refs[3][:, cols].astype(jnp.float32)
    near = refs[1 if d == 1 else 2][:, cols].astype(jnp.float32)
    other = refs[4][:, cols].astype(jnp.float32)
    at_end = info[table.low if d == 1 else table.high]
    return jnp.where(at_end == 1, other, near)


def line_spec(blocks, rows, index):
    if len(blocks) == 1:
        count, _, width = blocks[0].shape
        return [pl.BlockSpec((count, rows, width), lambda i, info: (0, index(i), 0))]
    width = blocks[0].shape[1]
    return [pl.BlockSpec((rows, width), lambda i, info: (index(i), 0)) for _ in blocks]


def call(kernel, name, info, args, in_specs, out_specs, out_shape, grid=(1,), aliases=None,
         scratch=(), flops=1, vmem=16):
    return pl.pallas_call(
        kernel,
        grid_spec=pltpu.PrefetchScalarGridSpec(
            num_scalar_prefetch=1,
            grid=grid,
            in_specs=in_specs,
            out_specs=out_specs,
            scratch_shapes=list(scratch),
        ),
        out_shape=out_shape,
        input_output_aliases=aliases or {},
        compiler_params=pltpu.CompilerParams(vmem_limit_bytes=vmem * MIB or None),
        cost_estimate=pl.CostEstimate(flops=flops, bytes_accessed=1, transcendentals=0),
        name=name,
    )(info, *args)


def whole(a):
    zeros = (0,) * len(a.shape)
    return pl.BlockSpec(tuple(a.shape), lambda i, info: zeros)


def prepare_kernel(table, slab, keep, info, q_hbm, kv_hbm, cache_hbm, w_hbm, r_hbm, cos_ref,
                   sin_ref, length_ref, *refs):
    count, raw = table.count, slab - keep
    q_out, kv_out, outs = refs[0], refs[1], refs[2 : 2 + count]
    q_ref, kv_ref, w_ref, sems = refs[-4:]
    slots, rows, part = cache_hbm.shape[0], q_ref.shape[0], w_ref.shape[0]
    span, tail = slice(slots, slots + rows), slice(slots + rows, slots + rows + TAIL)
    start = pl.multiple_of(info[table.share] * part, part)
    moves = [
        (w_hbm.at[pl.ds(start, part)], w_ref),
        (kv_hbm, kv_ref),
        (q_hbm, q_ref),
        (cache_hbm, kv_out.at[pl.ds(0, slots)]),
    ]
    if raw:
        moves.append((r_hbm.at[:, pl.ds(keep, raw)], refs[2 + count]))
        moves.append((r_hbm.at[:, pl.ds(keep, raw)], refs[3 + count]))
    copies = [pltpu.make_async_copy(*move, sems.at[n]) for n, move in enumerate(moves)]
    for copy in copies:
        copy.start()

    copies[0].wait()
    for d, out in enumerate(outs):
        target = lax.rem(info[table.place] + d, count)
        out[:, :keep] = w_ref[:, pl.ds(pl.multiple_of(target * slab, slab), keep)]
        for j in range(count if raw else 0):
            out[:, keep + j * raw : keep + (j + 1) * raw] = w_ref[
                :, j * slab + keep : (j + 1) * slab
            ]

    cosine, sine = cos_ref[...], sin_ref[...]

    def turn(block):
        block = block.astype(jnp.float32)
        return (block * cosine + pltpu.roll(block, HD // 2, 1) * sine).astype(jnp.bfloat16)

    copies[1].wait()
    kv_out[span, :HD] = turn(kv_ref[:, :HD])
    kv_out[span, HD:] = kv_ref[:, HD:]
    length = length_ref[0]
    upper = lax.div(length, DIGIT)
    lower = length - upper * DIGIT
    kv_out[tail, :HD] = jnp.full((TAIL, HD), upper.astype(jnp.float32)).astype(jnp.bfloat16)
    kv_out[tail, HD:] = jnp.full((TAIL, HD), lower.astype(jnp.float32)).astype(jnp.bfloat16)
    copies[2].wait()
    for head in range(q_ref.shape[1] // HD):
        cols = slice(head * HD, (head + 1) * HD)
        q_out[:, cols] = turn(q_ref[:, cols])
    for copy in copies[3:]:
        copy.wait()


def prepare(table, info, queries, span_pairs, cache, out_weight, residual, cosine, sine, lengths,
            part, keep):
    rows, slab = residual.shape
    shapes = [
        jax.ShapeDtypeStruct(queries.shape, jnp.bfloat16),
        jax.ShapeDtypeStruct((cache.shape[0] + rows + TAIL, 2 * HD), jnp.bfloat16),
    ]
    width = keep + table.count * (slab - keep)
    shapes += [jax.ShapeDtypeStruct((part, width), out_weight.dtype)] * table.count
    if keep < slab:
        shapes += [jax.ShapeDtypeStruct((rows, slab - keep), residual.dtype)] * 2
    return call(
        functools.partial(prepare_kernel, table, slab, keep),
        "prepare",
        info,
        [queries, span_pairs, cache, out_weight, residual, cosine, sine, lengths],
        [ANYWHERE] * 5
        + [whole(cosine), whole(sine), pl.BlockSpec(memory_space=pltpu.SMEM)],
        [whole(shape) for shape in shapes],
        shapes,
        scratch=[
            pltpu.VMEM(queries.shape, jnp.bfloat16),
            pltpu.VMEM(span_pairs.shape, jnp.bfloat16),
            pltpu.VMEM((part, out_weight.shape[1]), out_weight.dtype),
            pltpu.SemaphoreType.DMA((6,)),
        ],
        vmem=0,
    )


def stack_kernel(count, info, *refs):
    for number, part in enumerate(refs[:count]):
        refs[-1][number] = part[...]


def stack(info, parts, after):
    shape = jax.ShapeDtypeStruct((len(parts), *parts[0].shape), parts[0].dtype)
    return call(
        functools.partial(stack_kernel, len(parts)),
        "stack",
        info,
        [*parts, *after],
        [whole(p) for p in parts] + [ANYWHERE] * len(after),
        whole(shape),
        shape,
    )


def gate_kernel(info, *refs):
    pass


def gate(info, value, after):
    return call(
        gate_kernel,
        "gate",
        info,
        [value, *after],
        [ANYWHERE] * (1 + len(after)),
        ANYWHERE,
        jax.ShapeDtypeStruct(value.shape, value.dtype),
        aliases={1: 0},
    )


def attend_kernel(table, slots, first, info, q_ref, *refs):
    count = table.contexts
    pieces, out_ref, s_ref = refs[:count], refs[-2], refs[-1]
    rows = q_ref.shape[0]
    heads = q_ref.shape[1] // HD
    chunk = pl.program_id(0) + first
    mine = info[0]
    q = jnp.concatenate([q_ref[:, h * HD : (h + 1) * HD] for h in range(heads)], axis=0)
    exponent = math.log2(math.e) / math.sqrt(HD)

    blocks = []
    peak = jnp.full((heads * rows, HD), NEG, jnp.float32)
    column = 0
    for kind in ("cache", "span"):
        for number, ref in enumerate(pieces):
            tail = ref.shape[0] - TAIL
            first, last = (0, slots) if kind == "cache" else (slots, tail)
            width = min(KEY_BLOCK, last - first)
            length = ref[tail : tail + 1, :HD].astype(jnp.float32) * DIGIT + ref[
                tail : tail + 1, HD:
            ].astype(jnp.float32)
            length = jnp.concatenate([length] * (width // HD), axis=1)
            for begin in range(first, last, width):
                scores = lax.dot_general(
                    q,
                    ref[begin : begin + width, :HD],
                    (((1,), (1,)), ((), ())),
                    preferred_element_type=jnp.float32,
                )
                if kind == "cache":
                    slot = lax.broadcasted_iota(jnp.int32, (1, width), 1) + begin
                    live = slot.astype(jnp.float32) < length
                    scores = scores + jnp.where(live, 0.0, NEG)
                elif number == 0:
                    key = lax.broadcasted_iota(jnp.int32, (rows, width), 1) + (begin - first)
                    row = lax.broadcasted_iota(jnp.int32, (rows, width), 0) + chunk * rows
                    bias = jnp.where(key <= row, 0.0, NEG)
                    scores = scores + jnp.concatenate([bias] * heads, axis=0)
                else:
                    scores = scores + jnp.where(info[table.owner + number] < mine, 0.0, NEG)
                s_ref[:, column : column + width] = scores
                for lane in range(0, width, HD):
                    peak = jnp.maximum(peak, scores[:, lane : lane + HD])
                blocks.append((ref, begin, column, width))
                column += width
    top = jnp.max(peak, axis=1, keepdims=True)
    total = jnp.zeros((heads * rows, HD), jnp.float32)
    mixed = jnp.zeros((heads * rows, HD), jnp.float32)
    for ref, begin, column, width in blocks:
        weights = jnp.exp2((s_ref[:, column : column + width] - top) * exponent)
        for lane in range(0, width, HD):
            total = total + weights[:, lane : lane + HD]
        mixed = mixed + jnp.dot(
            weights.astype(jnp.bfloat16),
            ref[begin : begin + width, HD:],
            preferred_element_type=jnp.float32,
        )
    result = (mixed / jnp.sum(total, axis=1, keepdims=True)).astype(jnp.bfloat16)
    for h in range(heads):
        out_ref[:, h * HD : (h + 1) * HD] = result[h * rows : (h + 1) * rows]


def attend(table, info, queries, pieces, slots, begin, size, rows):
    width = queries.shape[1]
    heads = width // HD
    keys = sum(a.shape[0] - TAIL for a in pieces)
    first = begin // rows
    return call(
        functools.partial(attend_kernel, table, slots, first),
        "attend",
        info,
        [queries, *pieces],
        [pl.BlockSpec((rows, width), lambda i, info: (first + i, 0))]
        + [whole(a) for a in pieces],
        pl.BlockSpec((rows, width), lambda i, info: (i, 0)),
        jax.ShapeDtypeStruct((size, width), jnp.bfloat16),
        grid=(size // rows,),
        scratch=[pltpu.VMEM((heads * rows, keys), jnp.float32)],
        flops=ATTEND_FLOPS * size * heads * keys * HD,
        vmem=28,
    )


def project_kernel(table, lines, shares, splits, info, *refs):
    count = table.count
    attention, pieces = refs[:lines], refs[lines : lines + shares]
    r_ref = refs[lines + shares]
    parts, h_ref, w_ref = refs[-2 - 2 * len(splits) : -2], refs[-2], refs[-1]
    share_rows, keep = pieces[0].shape[1], w_ref.shape[2]
    for number, piece in enumerate(pieces):
        start = pl.multiple_of(info[table.rows + number] * share_rows, share_rows)
        for d in range(count):
            w_ref[d, pl.ds(start, share_rows)] = piece[d, :, :keep]
    blocks = [
        line_read(table, info, attention, d).astype(jnp.bfloat16) for d in range(count)
    ]
    for part, copy, (begin, size) in zip(parts, parts[len(splits) :], splits):
        rows = slice(begin, begin + size)
        total = r_ref[rows, :keep].astype(jnp.float32)
        for d in range(count):
            total = total + jnp.dot(
                blocks[d][rows], w_ref[d], preferred_element_type=jnp.float32
            )
        result = total.astype(jnp.bfloat16)
        h_ref[rows, :keep] = result
        part[...] = result
        copy[...] = result


def project(table, info, attention, pieces, residual, hidden, keep, half, halves, splits):
    all_rows, slab = residual.shape
    rows = all_rows // halves
    count, share_rows, _ = pieces[0].shape
    parts = [jax.ShapeDtypeStruct((size, keep), jnp.bfloat16) for _, size in splits * 2]
    row_spec = pl.BlockSpec((rows, slab), lambda i, info: (half, 0))
    args = [*attention, *pieces, residual]
    specs = line_spec(attention, rows, lambda i: 0) + [whole(p) for p in pieces] + [row_spec]
    aliases = {}
    if hidden is not None:
        args.append(hidden)
        specs.append(ANYWHERE)
        aliases = {len(args): len(parts)}
    return call(
        functools.partial(project_kernel, table, len(attention), len(pieces), splits),
        "project",
        info,
        args,
        specs,
        [whole(part) for part in parts] + [row_spec],
        [*parts, jax.ShapeDtypeStruct(residual.shape, jnp.bfloat16)],
        aliases=aliases,
        scratch=[pltpu.VMEM((count, len(pieces) * share_rows, keep), jnp.bfloat16)],
        vmem=36,
    )


def project_raw_kernel(table, lines, halves, raw_lines, shares, info, *refs):
    count = table.count
    attention, refs = refs[: lines * halves], refs[lines * halves :]
    residuals, pieces = refs[:raw_lines], refs[raw_lines : raw_lines + shares]
    raw_ref, h_ref, w_ref = refs[-3:]
    raw, share_rows = h_ref.shape[1], pieces[0].shape[1]
    keep = pieces[0].shape[2] - w_ref.shape[2]
    step = pl.program_id(0)

    @pl.when(step == 0)
    def _():
        for number, piece in enumerate(pieces):
            start = pl.multiple_of(info[table.rows + number] * share_rows, share_rows)
            for d in range(count):
                w_ref[d, pl.ds(start, share_rows)] = piece[d, :, keep:]

    blocks = []
    for d in range(count):
        block = line_read(table, info, attention[:lines], d)
        if halves == 2:
            other = line_read(table, info, attention[lines:], d)
            block = jnp.where(step < pl.num_programs(0) // 2, block, other)
        blocks.append(block.astype(jnp.bfloat16))
    for slab in range(count):
        cols = pl.ds(pl.multiple_of(info[table.place + slab] * raw, raw), raw)
        total = line_read(table, info, residuals, slab)
        for d in range(count):
            total = total + jnp.dot(
                blocks[d], w_ref[d, :, cols], preferred_element_type=jnp.float32
            )
        result = total.astype(jnp.bfloat16)
        raw_ref[:, slab * raw : (slab + 1) * raw] = result
        if slab == 0:
            h_ref[...] = result


def project_raw(table, info, attention, residuals, pieces, hidden, raw, rows):
    all_rows, slab = hidden.shape
    count, share_rows, _ = pieces[0].shape
    halves, lines = len(attention), len(attention[0])
    steps = all_rows // rows
    args = [*sum(attention, []), *residuals, *pieces, hidden]
    specs = []
    for half, blocks in enumerate(attention):
        first, last = half * (steps // halves), (half + 1) * (steps // halves) - 1
        specs += line_spec(
            blocks, rows, lambda i, a=first, b=last: jnp.clip(i, a, b) - a
        )
    out = jax.ShapeDtypeStruct((all_rows, count * raw), jnp.bfloat16)
    return call(
        functools.partial(
            project_raw_kernel, table, lines, halves, len(residuals), len(pieces)
        ),
        "project_raw",
        info,
        args,
        specs
        + line_spec(residuals, rows, lambda i: i)
        + [whole(p) for p in pieces]
        + [ANYWHERE],
        [
            pl.BlockSpec((rows, count * raw), lambda i, info: (i, 0)),
            pl.BlockSpec((rows, raw), lambda i, info: (i, slab // raw - 1)),
        ],
        [out, jax.ShapeDtypeStruct(hidden.shape, jnp.bfloat16)],
        grid=(steps,),
        aliases={len(args): 1},
        scratch=[pltpu.VMEM((count, len(pieces) * share_rows, count * raw), jnp.bfloat16)],
        vmem=36,
    )


def norm_kernel(table, lines, keep, slab, info, g_ref, *refs):
    count = table.count
    blocks, out_ref = refs[:lines], refs[-1]
    raw = slab - keep
    values = []
    squares = jnp.zeros((out_ref.shape[0], 1), jnp.float32)

    def read(d):
        found = [(0, keep, line_read(table, info, blocks, d))]
        if raw:
            cols = slice(d * raw, (d + 1) * raw)
            found.append((keep, raw, refs[lines][:, cols].astype(jnp.float32)))
        return found

    for d in range(count):
        for _, _, value in read(d):
            squares = squares + jnp.sum(value * value, axis=1, keepdims=True)
    inverse = lax.rsqrt(squares / (count * slab) + EPS_NORM)
    for d in range(count):
        for offset, width, value in read(d):
            start = pl.multiple_of(info[table.place + d] * slab + offset, HD)
            cols = pl.ds(start, width)
            out_ref[:, cols] = (value * inverse * g_ref[:, cols]).astype(jnp.bfloat16)


def norm_into(table, info, buffer, blocks, raw_hidden, gain, begin, rows, keep, slab, total_rows):
    width = table.count * slab
    step = math.gcd(rows, 32)
    steps, first = rows // step, begin // step
    args = [gain.reshape(1, width), *blocks]
    in_specs = [pl.BlockSpec((1, width), lambda i, info: (0, 0))]
    in_specs += line_spec(blocks, step, lambda i: i)
    if raw_hidden is not None:
        args.append(raw_hidden)
        in_specs.append(
            pl.BlockSpec((step, raw_hidden.shape[1]), lambda i, info: (first + i, 0))
        )
    aliases = {}
    if buffer is not None:
        args.append(buffer)
        in_specs.append(ANYWHERE)
        aliases = {len(args): 0}
    return call(
        functools.partial(norm_kernel, table, len(blocks), keep, slab),
        "norm",
        info,
        args,
        in_specs,
        pl.BlockSpec((step, width), lambda i, info: (first + i, 0)),
        jax.ShapeDtypeStruct((total_rows, width), jnp.bfloat16),
        grid=(steps,),
        aliases=aliases,
    )


def per_device(queries, span_kv, cache, lengths, offset, out_weight, residual, gain):
    rows = queries.shape[0]
    heads = queries.shape[1] // HD
    depth = out_weight.shape[0]
    slab = residual.shape[1]
    contexts = lax.axis_size("context")
    count = lax.axis_size("tensor")
    context_index = lax.axis_index("context")
    tensor_index = lax.axis_index("tensor")
    kv_index = tensor_index * heads // GROUP
    groups = lax.axis_size("groups")
    shares = groups * contexts
    share = lax.axis_index("groups") * contexts + context_index
    raw = slab // RAW_PART if slab % (RAW_PART * HD) == 0 else 0
    keep = slab - raw
    chunk = min(CHUNK, rows)
    halves = 1
    half = rows // halves
    splits = [[(begin, chunk) for begin in range(0, half, chunk)]] * halves

    table = Table(contexts, count)
    steering = [context_index, *owners_of(contexts, context_index)]
    steering += [lax.rem(tensor_index + (count - d), count) for d in range(count)]
    steering += [tensor_index == 0, tensor_index == count - 1, share]
    steering += plane_owners(shares, share)
    info = jnp.stack([jnp.asarray(v).astype(jnp.int32) for v in steering])

    cache_local = lax.dynamic_index_in_dim(cache, kv_index, 0, keepdims=False)
    span_local = lax.dynamic_index_in_dim(span_kv, kv_index, 1, keepdims=False)
    positions = offset[0] + context_index * rows + jnp.arange(rows, dtype=jnp.int32)
    both = jnp.concatenate([frequencies(HD)] * 2)
    angles = positions.astype(jnp.float32)[:, None] * both[None, :]
    sign = jnp.where(jnp.arange(HD) < HD // 2, -1.0, 1.0)
    q_turned, payload, *cuts = prepare(
        table, info, queries, span_local, cache_local, out_weight, residual, jnp.cos(angles),
        jnp.sin(angles) * sign[None, :], lengths, depth // shares, keep,
    )
    parts = [cuts[0]]
    for shift in range(1, count):
        pairs = [(i, (i + shift) % count) for i in range(count)]
        parts.append(lax.ppermute(cuts[shift], "tensor", pairs))
    own_weights = stack(info, parts, [])
    own_raw = [gate(info, cuts[count], parts[1:])] if raw else []
    pieces = pieces_of(
        payload, "context", contexts, lambda block: gate(info, block, [own_weights, *own_raw])
    )
    slots = cache_local.shape[0]
    mixed = [
        attend(table, info, q_turned, pieces, slots, number * half, half, chunk)
        for number in range(halves)
    ]
    residuals, early = [], ()
    if raw and count == 4:
        early = line_far(own_raw[0])
    attention = [
        line_gather(gate(info, value, early[:1]) if early else value, count) for value in mixed
    ]
    if early:
        near = gate(info, cuts[count + 1], attention[0][3:4])
        residuals = [near, *line_near(near), *early]
    elif raw:
        residuals = line_gather(own_raw[0], count)
    before = [*attention[0][1:], *mixed[1:], *residuals[1:3], *residuals[4:]]
    weights = plane_gather(
        own_weights,
        groups,
        contexts,
        lambda block, other: gate(info, block, mixed[:1]),
        lambda block, mask: gate(
            info,
            block,
            attention[0][1:3] if mask in (mask & -mask,) else before,
        ),
    )
    values, copies, hidden = [], [], None
    for number in range(halves):
        *made, hidden = project(
            table, info, attention[number], weights, residual, hidden, keep, number,
            halves, splits[number],
        )
        values += made[: len(made) // 2]
        copies += made[len(made) // 2 :]
    raw_hidden = None
    if raw:
        raw_hidden, hidden = project_raw(
            table, info, attention, residuals, weights, hidden, raw, chunk
        )
    lines = chunk_gathers(
        info,
        values,
        copies,
        attention[-1][1:] if halves > 1 else [],
        [raw_hidden] if raw else [],
        count,
    )
    normed, begin = None, 0
    for blocks, value in zip(lines, values):
        normed = norm_into(
            table, info, normed, blocks, raw_hidden, gain, begin, value.shape[0], keep, slab, rows
        )
        begin += value.shape[0]
    return (hidden, normed)


def solution(mesh):
    in_specs = (
        P(("groups", "context"), "tensor"),
        P(("groups", "context"), None, None),
        P("groups", "context", None),
        P(("groups", "context")),
        P("groups"),
        P("tensor", None),
        P(("groups", "context"), "tensor"),
        P(),
    )
    out_specs = (P(("groups", "context"), "tensor"), P(("groups", "context"), None))
    return jax.shard_map(
        per_device, mesh=mesh, in_specs=in_specs, out_specs=out_specs, check_vma=False
    )
```

```python
import functools
import math

import jax
import jax.numpy as jnp
from jax import lax
from jax.experimental import pallas as pl
from jax.experimental.pallas import tpu as pltpu
from jax.sharding import PartitionSpec as P

GROUP = 8
HD = 128
NEG = -1e30
EPS_NORM = 1e-05
MIB = 1024 * 1024
CHUNK = 128
KEY_BLOCK = 512
ATTEND_FLOPS = 16
RAW_PART = 4
TAIL = 16
DIGIT = 32
ANYWHERE = pl.BlockSpec(memory_space=pl.ANY)


def frequencies(head_width):
    counter = jnp.arange(head_width // 2, dtype=jnp.float32)
    base_freq = jnp.exp(-(2.0 * counter / head_width) * math.log(500000.0))
    wavelength = 2.0 * math.pi / base_freq
    smoothing = (8192.0 / wavelength - 1.0) / 3.0
    blended = (1.0 - smoothing) * base_freq / 8.0 + smoothing * base_freq
    return jnp.where(
        wavelength < 2048.0, base_freq, jnp.where(wavelength > 8192.0, base_freq / 8.0, blended)
    )


def pieces_of(value, axis, count, between=lambda block: block):
    if count & (count - 1) == 0:
        held = {0: value}
        bit = count // 2
        while bit:
            pairs = [(i, i ^ bit) for i in range(count)]
            for mask in sorted(held):
                held[mask | bit] = lax.ppermute(held[mask], axis, pairs)
            if bit == count // 2:
                held[bit] = between(held[bit])
            bit //= 2
        return [held[mask] for mask in range(count)]
    blocks = [value]
    for shift in range(1, count):
        pairs = [(i, (i + shift) % count) for i in range(count)]
        blocks.append(lax.ppermute(value, axis, pairs))
    blocks[-1] = between(blocks[-1])
    return blocks


def owners_of(count, me):
    if count & (count - 1) == 0:
        return [me ^ mask for mask in range(count)]
    return [(me + count - shift) % count for shift in range(count)]


def plane_gather(value, groups, contexts, first, then):
    count = groups * contexts
    if count & (count - 1):
        gathered = lax.all_gather(value, ("groups", "context"), axis=0, tiled=False)
        return [gathered[number] for number in range(count)]
    held = {0: value}
    bits = [1 << b for b in range(contexts.bit_length() - 2, 0, -1)]
    bits += [contexts << b for b in range(groups.bit_length() - 1)]
    for bit in bits:
        axis, flip, size = ("context", bit, contexts)
        if bit >= contexts:
            axis, flip, size = ("groups", bit // contexts, groups)
        pairs = [(i, i ^ flip) for i in range(size)]
        for mask in sorted(held):
            if mask:
                held[mask] = first(held[mask], held[bit])
            held[mask | bit] = lax.ppermute(held[mask], axis, pairs)
    if contexts > 1:
        for mask in sorted(held):
            held[mask] = then(held[mask], mask) if mask else held[mask]
            held[mask | 1] = core_swap(held[mask], contexts)
    return [held[mask] for mask in range(count)]


def core_swap(value, contexts):
    return lax.ppermute(value, "context", [(i, i ^ 1) for i in range(contexts)])


def plane_owners(count, me):
    if count & (count - 1):
        return list(range(count))
    return [me ^ mask for mask in range(count)]


def line_gather(value, count):
    if count != 4:
        return [lax.all_gather(value, "tensor", axis=0, tiled=False)]
    far, last = line_far(value)
    return [value, *line_near(value), far, last]


def line_near(value):
    up = lax.ppermute(value, "tensor", [(0, 1), (1, 2), (2, 3)])
    return up, lax.ppermute(value, "tensor", [(1, 0), (2, 1), (3, 2)])


def line_far(value):
    far = lax.ppermute(value, "tensor", [(0, 2), (1, 3), (2, 0), (3, 1)])
    return far, lax.ppermute(far, "tensor", [(1, 0), (2, 3)])


def chunk_gathers(info, values, copies, second, made, count):
    if count != 4:
        return [line_gather(value, count) for value in values]
    fars, lines = [], []
    for number, value in enumerate(values):
        after = [fars[-1][0]] if number else []
        if number == 1:
            after += second
        fars.append(line_far(gate(info, value, after) if after else value))
    for number, value in enumerate(copies):
        after = list(lines[number - 1][1:3]) if number else []
        if number > 1:
            after.append(fars[number - 2][1])
        if number == len(copies) // 2:
            after += made
        value = gate(info, value, after) if after else value
        lines.append([value, *line_near(value), *fars[number]])
    return lines


class Table:
    def __init__(self, contexts, count):
        self.contexts, self.count = contexts, count
        self.owner = 1
        self.place = 1 + contexts
        self.low = self.place + count
        self.high = self.low + 1
        self.share = self.low + 2
        self.rows = self.low + 3


def line_read(table, info, refs, d, cols=slice(None)):
    if len(refs) == 1:
        return refs[0][info[table.place + d], :, cols].astype(jnp.float32)
    if d == 0:
        return refs[0][:, cols].astype(jnp.float32)
    if d == 2:
        return refs[3][:, cols].astype(jnp.float32)
    near = refs[1 if d == 1 else 2][:, cols].astype(jnp.float32)
    other = refs[4][:, cols].astype(jnp.float32)
    at_end = info[table.low if d == 1 else table.high]
    return jnp.where(at_end == 1, other, near)


def line_spec(blocks, rows, index):
    if len(blocks) == 1:
        count, _, width = blocks[0].shape
        return [pl.BlockSpec((count, rows, width), lambda i, info: (0, index(i), 0))]
    width = blocks[0].shape[1]
    return [pl.BlockSpec((rows, width), lambda i, info: (index(i), 0)) for _ in blocks]


def call(kernel, name, info, args, in_specs, out_specs, out_shape, grid=(1,), aliases=None,
         scratch=(), flops=1, vmem=16):
    return pl.pallas_call(
        kernel,
        grid_spec=pltpu.PrefetchScalarGridSpec(
            num_scalar_prefetch=1,
            grid=grid,
            in_specs=in_specs,
            out_specs=out_specs,
            scratch_shapes=list(scratch),
        ),
        out_shape=out_shape,
        input_output_aliases=aliases or {},
        compiler_params=pltpu.CompilerParams(vmem_limit_bytes=vmem * MIB or None),
        cost_estimate=pl.CostEstimate(flops=flops, bytes_accessed=1, transcendentals=0),
        name=name,
    )(info, *args)


def whole(a):
    zeros = (0,) * len(a.shape)
    return pl.BlockSpec(tuple(a.shape), lambda i, info: zeros)


def prepare_kernel(table, slab, keep, info, q_hbm, kv_hbm, cache_hbm, w_hbm, r_hbm, cos_ref,
                   sin_ref, length_ref, *refs):
    count, raw = table.count, slab - keep
    q_out, kv_out, outs = refs[0], refs[1], refs[2 : 2 + count]
    q_ref, kv_ref, w_ref, sems = refs[-4:]
    slots, rows, part = cache_hbm.shape[0], q_ref.shape[0], w_ref.shape[0]
    span, tail = slice(slots, slots + rows), slice(slots + rows, slots + rows + TAIL)
    start = pl.multiple_of(info[table.share] * part, part)
    moves = [
        (w_hbm.at[pl.ds(start, part)], w_ref),
        (kv_hbm, kv_ref),
        (q_hbm, q_ref),
        (cache_hbm, kv_out.at[pl.ds(0, slots)]),
    ]
    if raw:
        moves.append((r_hbm.at[:, pl.ds(keep, raw)], refs[2 + count]))
        moves.append((r_hbm.at[:, pl.ds(keep, raw)], refs[3 + count]))
    copies = [pltpu.make_async_copy(*move, sems.at[n]) for n, move in enumerate(moves)]
    for copy in copies:
        copy.start()

    copies[0].wait()
    for d, out in enumerate(outs):
        target = lax.rem(info[table.place] + d, count)
        out[:, :keep] = w_ref[:, pl.ds(pl.multiple_of(target * slab, slab), keep)]
        for j in range(count if raw else 0):
            out[:, keep + j * raw : keep + (j + 1) * raw] = w_ref[
                :, j * slab + keep : (j + 1) * slab
            ]

    cosine, sine = cos_ref[...], sin_ref[...]

    def turn(block):
        block = block.astype(jnp.float32)
        return (block * cosine + pltpu.roll(block, HD // 2, 1) * sine).astype(jnp.bfloat16)

    copies[1].wait()
    kv_out[span, :HD] = turn(kv_ref[:, :HD])
    kv_out[span, HD:] = kv_ref[:, HD:]
    length = length_ref[0]
    upper = lax.div(length, DIGIT)
    lower = length - upper * DIGIT
    kv_out[tail, :HD] = jnp.full((TAIL, HD), upper.astype(jnp.float32)).astype(jnp.bfloat16)
    kv_out[tail, HD:] = jnp.full((TAIL, HD), lower.astype(jnp.float32)).astype(jnp.bfloat16)
    copies[2].wait()
    for head in range(q_ref.shape[1] // HD):
        cols = slice(head * HD, (head + 1) * HD)
        q_out[:, cols] = turn(q_ref[:, cols])
    for copy in copies[3:]:
        copy.wait()


def prepare(table, info, queries, span_pairs, cache, out_weight, residual, cosine, sine, lengths,
            part, keep):
    rows, slab = residual.shape
    shapes = [
        jax.ShapeDtypeStruct(queries.shape, jnp.bfloat16),
        jax.ShapeDtypeStruct((cache.shape[0] + rows + TAIL, 2 * HD), jnp.bfloat16),
    ]
    width = keep + table.count * (slab - keep)
    shapes += [jax.ShapeDtypeStruct((part, width), out_weight.dtype)] * table.count
    if keep < slab:
        shapes += [jax.ShapeDtypeStruct((rows, slab - keep), residual.dtype)] * 2
    return call(
        functools.partial(prepare_kernel, table, slab, keep),
        "prepare",
        info,
        [queries, span_pairs, cache, out_weight, residual, cosine, sine, lengths],
        [ANYWHERE] * 5
        + [whole(cosine), whole(sine), pl.BlockSpec(memory_space=pltpu.SMEM)],
        [whole(shape) for shape in shapes],
        shapes,
        scratch=[
            pltpu.VMEM(queries.shape, jnp.bfloat16),
            pltpu.VMEM(span_pairs.shape, jnp.bfloat16),
            pltpu.VMEM((part, out_weight.shape[1]), out_weight.dtype),
            pltpu.SemaphoreType.DMA((6,)),
        ],
        vmem=0,
    )


def stack_kernel(count, info, *refs):
    for number, part in enumerate(refs[:count]):
        refs[-1][number] = part[...]


def stack(info, parts, after):
    shape = jax.ShapeDtypeStruct((len(parts), *parts[0].shape), parts[0].dtype)
    return call(
        functools.partial(stack_kernel, len(parts)),
        "stack",
        info,
        [*parts, *after],
        [whole(p) for p in parts] + [ANYWHERE] * len(after),
        whole(shape),
        shape,
    )


def gate_kernel(info, *refs):
    pass


def gate(info, value, after):
    return call(
        gate_kernel,
        "gate",
        info,
        [value, *after],
        [ANYWHERE] * (1 + len(after)),
        ANYWHERE,
        jax.ShapeDtypeStruct(value.shape, value.dtype),
        aliases={1: 0},
    )


def attend_kernel(table, slots, first, info, q_ref, *refs):
    count = table.contexts
    pieces, out_ref, s_ref = refs[:count], refs[-2], refs[-1]
    rows = q_ref.shape[0]
    heads = q_ref.shape[1] // HD
    chunk = pl.program_id(0) + first
    mine = info[0]
    q = jnp.concatenate([q_ref[:, h * HD : (h + 1) * HD] for h in range(heads)], axis=0)
    exponent = math.log2(math.e) / math.sqrt(HD)

    blocks = []
    peak = jnp.full((heads * rows, HD), NEG, jnp.float32)
    column = 0
    for kind in ("cache", "span"):
        for number, ref in enumerate(pieces):
            tail = ref.shape[0] - TAIL
            first, last = (0, slots) if kind == "cache" else (slots, tail)
            width = min(KEY_BLOCK, last - first)
            length = ref[tail : tail + 1, :HD].astype(jnp.float32) * DIGIT + ref[
                tail : tail + 1, HD:
            ].astype(jnp.float32)
            length = jnp.concatenate([length] * (width // HD), axis=1)
            for begin in range(first, last, width):
                scores = lax.dot_general(
                    q,
                    ref[begin : begin + width, :HD],
                    (((1,), (1,)), ((), ())),
                    preferred_element_type=jnp.float32,
                )
                if kind == "cache":
                    slot = lax.broadcasted_iota(jnp.int32, (1, width), 1) + begin
                    live = slot.astype(jnp.float32) < length
                    scores = scores + jnp.where(live, 0.0, NEG)
                elif number == 0:
                    key = lax.broadcasted_iota(jnp.int32, (rows, width), 1) + (begin - first)
                    row = lax.broadcasted_iota(jnp.int32, (rows, width), 0) + chunk * rows
                    bias = jnp.where(key <= row, 0.0, NEG)
                    scores = scores + jnp.concatenate([bias] * heads, axis=0)
                else:
                    scores = scores + jnp.where(info[table.owner + number] < mine, 0.0, NEG)
                s_ref[:, column : column + width] = scores
                for lane in range(0, width, HD):
                    peak = jnp.maximum(peak, scores[:, lane : lane + HD])
                blocks.append((ref, begin, column, width))
                column += width
    top = jnp.max(peak, axis=1, keepdims=True)
    total = jnp.zeros((heads * rows, HD), jnp.float32)
    mixed = jnp.zeros((heads * rows, HD), jnp.float32)
    for ref, begin, column, width in blocks:
        weights = jnp.exp2((s_ref[:, column : column + width] - top) * exponent)
        for lane in range(0, width, HD):
            total = total + weights[:, lane : lane + HD]
        mixed = mixed + jnp.dot(
            weights.astype(jnp.bfloat16),
            ref[begin : begin + width, HD:],
            preferred_element_type=jnp.float32,
        )
    result = (mixed / jnp.sum(total, axis=1, keepdims=True)).astype(jnp.bfloat16)
    for h in range(heads):
        out_ref[:, h * HD : (h + 1) * HD] = result[h * rows : (h + 1) * rows]


def attend(table, info, queries, pieces, slots, begin, size, rows):
    width = queries.shape[1]
    heads = width // HD
    keys = sum(a.shape[0] - TAIL for a in pieces)
    first = begin // rows
    return call(
        functools.partial(attend_kernel, table, slots, first),
        "attend",
        info,
        [queries, *pieces],
        [pl.BlockSpec((rows, width), lambda i, info: (first + i, 0))]
        + [whole(a) for a in pieces],
        pl.BlockSpec((rows, width), lambda i, info: (i, 0)),
        jax.ShapeDtypeStruct((size, width), jnp.bfloat16),
        grid=(size // rows,),
        scratch=[pltpu.VMEM((heads * rows, keys), jnp.float32)],
        flops=ATTEND_FLOPS * size * heads * keys * HD,
        vmem=28,
    )


def project_kernel(table, lines, shares, splits, info, *refs):
    count = table.count
    attention, pieces = refs[:lines], refs[lines : lines + shares]
    r_ref = refs[lines + shares]
    parts, h_ref, w_ref = refs[-2 - 2 * len(splits) : -2], refs[-2], refs[-1]
    share_rows, keep = pieces[0].shape[1], w_ref.shape[2]
    for number, piece in enumerate(pieces):
        start = pl.multiple_of(info[table.rows + number] * share_rows, share_rows)
        for d in range(count):
            w_ref[d, pl.ds(start, share_rows)] = piece[d, :, :keep]
    blocks = [
        line_read(table, info, attention, d).astype(jnp.bfloat16) for d in range(count)
    ]
    for part, copy, (begin, size) in zip(parts, parts[len(splits) :], splits):
        rows = slice(begin, begin + size)
        total = r_ref[rows, :keep].astype(jnp.float32)
        for d in range(count):
            total = total + jnp.dot(
                blocks[d][rows], w_ref[d], preferred_element_type=jnp.float32
            )
        result = total.astype(jnp.bfloat16)
        h_ref[rows, :keep] = result
        part[...] = result
        copy[...] = result


def project(table, info, attention, pieces, residual, hidden, keep, half, halves, splits):
    all_rows, slab = residual.shape
    rows = all_rows // halves
    count, share_rows, _ = pieces[0].shape
    parts = [jax.ShapeDtypeStruct((size, keep), jnp.bfloat16) for _, size in splits * 2]
    row_spec = pl.BlockSpec((rows, slab), lambda i, info: (half, 0))
    args = [*attention, *pieces, residual]
    specs = line_spec(attention, rows, lambda i: 0) + [whole(p) for p in pieces] + [row_spec]
    aliases = {}
    if hidden is not None:
        args.append(hidden)
        specs.append(ANYWHERE)
        aliases = {len(args): len(parts)}
    return call(
        functools.partial(project_kernel, table, len(attention), len(pieces), splits),
        "project",
        info,
        args,
        specs,
        [whole(part) for part in parts] + [row_spec],
        [*parts, jax.ShapeDtypeStruct(residual.shape, jnp.bfloat16)],
        aliases=aliases,
        scratch=[pltpu.VMEM((count, len(pieces) * share_rows, keep), jnp.bfloat16)],
        vmem=36,
    )


def project_raw_kernel(table, lines, halves, raw_lines, shares, info, *refs):
    count = table.count
    attention, refs = refs[: lines * halves], refs[lines * halves :]
    residuals, pieces = refs[:raw_lines], refs[raw_lines : raw_lines + shares]
    raw_ref, h_ref, w_ref = refs[-3:]
    raw, share_rows = h_ref.shape[1], pieces[0].shape[1]
    keep = pieces[0].shape[2] - w_ref.shape[2]
    step = pl.program_id(0)

    @pl.when(step == 0)
    def _():
        for number, piece in enumerate(pieces):
            start = pl.multiple_of(info[table.rows + number] * share_rows, share_rows)
            for d in range(count):
                w_ref[d, pl.ds(start, share_rows)] = piece[d, :, keep:]

    blocks = []
    for d in range(count):
        block = line_read(table, info, attention[:lines], d)
        if halves == 2:
            other = line_read(table, info, attention[lines:], d)
            block = jnp.where(step < pl.num_programs(0) // 2, block, other)
        blocks.append(block.astype(jnp.bfloat16))
    for slab in range(count):
        cols = pl.ds(pl.multiple_of(info[table.place + slab] * raw, raw), raw)
        total = line_read(table, info, residuals, slab)
        for d in range(count):
            total = total + jnp.dot(
                blocks[d], w_ref[d, :, cols], preferred_element_type=jnp.float32
            )
        result = total.astype(jnp.bfloat16)
        raw_ref[:, slab * raw : (slab + 1) * raw] = result
        if slab == 0:
            h_ref[...] = result


def project_raw(table, info, attention, residuals, pieces, hidden, raw, rows):
    all_rows, slab = hidden.shape
    count, share_rows, _ = pieces[0].shape
    halves, lines = len(attention), len(attention[0])
    steps = all_rows // rows
    args = [*sum(attention, []), *residuals, *pieces, hidden]
    specs = []
    for half, blocks in enumerate(attention):
        first, last = half * (steps // halves), (half + 1) * (steps // halves) - 1
        specs += line_spec(
            blocks, rows, lambda i, a=first, b=last: jnp.clip(i, a, b) - a
        )
    out = jax.ShapeDtypeStruct((all_rows, count * raw), jnp.bfloat16)
    return call(
        functools.partial(
            project_raw_kernel, table, lines, halves, len(residuals), len(pieces)
        ),
        "project_raw",
        info,
        args,
        specs
        + line_spec(residuals, rows, lambda i: i)
        + [whole(p) for p in pieces]
        + [ANYWHERE],
        [
            pl.BlockSpec((rows, count * raw), lambda i, info: (i, 0)),
            pl.BlockSpec((rows, raw), lambda i, info: (i, slab // raw - 1)),
        ],
        [out, jax.ShapeDtypeStruct(hidden.shape, jnp.bfloat16)],
        grid=(steps,),
        aliases={len(args): 1},
        scratch=[pltpu.VMEM((count, len(pieces) * share_rows, count * raw), jnp.bfloat16)],
        vmem=36,
    )


def norm_kernel(table, lines, keep, slab, info, g_ref, *refs):
    count = table.count
    blocks, out_ref = refs[:lines], refs[-1]
    raw = slab - keep
    values = []
    squares = jnp.zeros((out_ref.shape[0], 1), jnp.float32)

    def read(d):
        found = [(0, keep, line_read(table, info, blocks, d))]
        if raw:
            cols = slice(d * raw, (d + 1) * raw)
            found.append((keep, raw, refs[lines][:, cols].astype(jnp.float32)))
        return found

    for d in range(count):
        for _, _, value in read(d):
            squares = squares + jnp.sum(value * value, axis=1, keepdims=True)
    inverse = lax.rsqrt(squares / (count * slab) + EPS_NORM)
    for d in range(count):
        for offset, width, value in read(d):
            start = pl.multiple_of(info[table.place + d] * slab + offset, HD)
            cols = pl.ds(start, width)
            out_ref[:, cols] = (value * inverse * g_ref[:, cols]).astype(jnp.bfloat16)


def norm_into(table, info, buffer, blocks, raw_hidden, gain, begin, rows, keep, slab, total_rows):
    width = table.count * slab
    step = math.gcd(rows, 32)
    steps, first = rows // step, begin // step
    args = [gain.reshape(1, width), *blocks]
    in_specs = [pl.BlockSpec((1, width), lambda i, info: (0, 0))]
    in_specs += line_spec(blocks, step, lambda i: i)
    if raw_hidden is not None:
        args.append(raw_hidden)
        in_specs.append(
            pl.BlockSpec((step, raw_hidden.shape[1]), lambda i, info: (first + i, 0))
        )
    aliases = {}
    if buffer is not None:
        args.append(buffer)
        in_specs.append(ANYWHERE)
        aliases = {len(args): 0}
    return call(
        functools.partial(norm_kernel, table, len(blocks), keep, slab),
        "norm",
        info,
        args,
        in_specs,
        pl.BlockSpec((step, width), lambda i, info: (first + i, 0)),
        jax.ShapeDtypeStruct((total_rows, width), jnp.bfloat16),
        grid=(steps,),
        aliases=aliases,
    )


def per_device(queries, span_kv, cache, lengths, offset, out_weight, residual, gain):
    rows = queries.shape[0]
    heads = queries.shape[1] // HD
    depth = out_weight.shape[0]
    slab = residual.shape[1]
    contexts = lax.axis_size("context")
    count = lax.axis_size("tensor")
    context_index = lax.axis_index("context")
    tensor_index = lax.axis_index("tensor")
    kv_index = tensor_index * heads // GROUP
    groups = lax.axis_size("groups")
    shares = groups * contexts
    share = lax.axis_index("groups") * contexts + context_index
    raw = slab // RAW_PART if slab % (RAW_PART * HD) == 0 else 0
    keep = slab - raw
    chunk = min(CHUNK, rows)
    halves = 1
    half = rows // halves
    splits = [[(begin, chunk) for begin in range(0, half, chunk)]] * halves

    table = Table(contexts, count)
    steering = [context_index, *owners_of(contexts, context_index)]
    steering += [lax.rem(tensor_index + (count - d), count) for d in range(count)]
    steering += [tensor_index == 0, tensor_index == count - 1, share]
    steering += plane_owners(shares, share)
    info = jnp.stack([jnp.asarray(v).astype(jnp.int32) for v in steering])

    cache_local = lax.dynamic_index_in_dim(cache, kv_index, 0, keepdims=False)
    span_local = lax.dynamic_index_in_dim(span_kv, kv_index, 1, keepdims=False)
    positions = offset[0] + context_index * rows + jnp.arange(rows, dtype=jnp.int32)
    both = jnp.concatenate([frequencies(HD)] * 2)
    angles = positions.astype(jnp.float32)[:, None] * both[None, :]
    sign = jnp.where(jnp.arange(HD) < HD // 2, -1.0, 1.0)
    q_turned, payload, *cuts = prepare(
        table, info, queries, span_local, cache_local, out_weight, residual, jnp.cos(angles),
        jnp.sin(angles) * sign[None, :], lengths, depth // shares, keep,
    )
    parts = [cuts[0]]
    for shift in range(1, count):
        pairs = [(i, (i + shift) % count) for i in range(count)]
        parts.append(lax.ppermute(cuts[shift], "tensor", pairs))
    own_weights = stack(info, parts, [])
    own_raw = [gate(info, cuts[count], parts[1:])] if raw else []
    pieces = pieces_of(
        payload, "context", contexts, lambda block: gate(info, block, [own_weights, *own_raw])
    )
    slots = cache_local.shape[0]
    mixed = [
        attend(table, info, q_turned, pieces, slots, number * half, half, chunk)
        for number in range(halves)
    ]
    residuals, early = [], ()
    if raw and count == 4:
        early = [lax.ppermute(own_raw[0], "tensor", [(0, 2), (1, 3), (2, 0), (3, 1)])]
    attention = [
        line_gather(gate(info, value, early[:1]) if early else value, count) for value in mixed
    ]
    if early:
        near = gate(info, cuts[count + 1], attention[0][1:])
        far = gate(info, early[0], attention[0][1:])
        residuals = [near, *line_near(near), far, lax.ppermute(far, "tensor", [(1, 0), (2, 3)])]
    elif raw:
        residuals = line_gather(own_raw[0], count)
    before = [*attention[0][1:], *mixed[1:], *residuals[1:3], *residuals[4:]]
    weights = plane_gather(
        own_weights,
        groups,
        contexts,
        lambda block, other: gate(info, block, mixed[:1]),
        lambda block, mask: gate(
            info,
            block,
            attention[0][1:3] if mask in (mask & -mask,) else before,
        ),
    )
    values, copies, hidden = [], [], None
    for number in range(halves):
        *made, hidden = project(
            table, info, attention[number], weights, residual, hidden, keep, number,
            halves, splits[number],
        )
        values += made[: len(made) // 2]
        copies += made[len(made) // 2 :]
    raw_hidden = None
    if raw:
        raw_hidden, hidden = project_raw(
            table, info, attention, residuals, weights, hidden, raw, chunk
        )
    lines = chunk_gathers(
        info,
        values,
        copies,
        attention[-1][1:] if halves > 1 else [],
        [raw_hidden] if raw else [],
        count,
    )
    normed, begin = None, 0
    for blocks, value in zip(lines, values):
        normed = norm_into(
            table, info, normed, blocks, raw_hidden, gain, begin, value.shape[0], keep, slab, rows
        )
        begin += value.shape[0]
    return (hidden, normed)


def solution(mesh):
    in_specs = (
        P(("groups", "context"), "tensor"),
        P(("groups", "context"), None, None),
        P("groups", "context", None),
        P(("groups", "context")),
        P("groups"),
        P("tensor", None),
        P(("groups", "context"), "tensor"),
        P(),
    )
    out_specs = (P(("groups", "context"), "tensor"), P(("groups", "context"), None))
    return jax.shard_map(
        per_device, mesh=mesh, in_specs=in_specs, out_specs=out_specs, check_vma=False
    )
```

```python
import functools
import math

import jax
import jax.numpy as jnp
from jax import lax
from jax.experimental import pallas as pl
from jax.experimental.pallas import tpu as pltpu
from jax.sharding import PartitionSpec as P

GROUP = 8
HD = 128
NEG = -1e30
EPS_NORM = 1e-05
MIB = 1024 * 1024
CHUNK = 128
KEY_BLOCK = 512
ATTEND_FLOPS = 16
RAW_PART = 8
TAIL = 16
DIGIT = 32
ANYWHERE = pl.BlockSpec(memory_space=pl.ANY)


def frequencies(head_width):
    counter = jnp.arange(head_width // 2, dtype=jnp.float32)
    base_freq = jnp.exp(-(2.0 * counter / head_width) * math.log(500000.0))
    wavelength = 2.0 * math.pi / base_freq
    smoothing = (8192.0 / wavelength - 1.0) / 3.0
    blended = (1.0 - smoothing) * base_freq / 8.0 + smoothing * base_freq
    return jnp.where(
        wavelength < 2048.0, base_freq, jnp.where(wavelength > 8192.0, base_freq / 8.0, blended)
    )


def pieces_of(value, axis, count, between=lambda block: block):
    if count & (count - 1) == 0:
        held = {0: value}
        bit = count // 2
        while bit:
            pairs = [(i, i ^ bit) for i in range(count)]
            for mask in sorted(held):
                held[mask | bit] = lax.ppermute(held[mask], axis, pairs)
            if bit == count // 2:
                held[bit] = between(held[bit])
            bit //= 2
        return [held[mask] for mask in range(count)]
    blocks = [value]
    for shift in range(1, count):
        pairs = [(i, (i + shift) % count) for i in range(count)]
        blocks.append(lax.ppermute(value, axis, pairs))
    blocks[-1] = between(blocks[-1])
    return blocks


def owners_of(count, me):
    if count & (count - 1) == 0:
        return [me ^ mask for mask in range(count)]
    return [(me + count - shift) % count for shift in range(count)]


def plane_gather(value, groups, contexts, first, then):
    count = groups * contexts
    if count & (count - 1):
        gathered = lax.all_gather(value, ("groups", "context"), axis=0, tiled=False)
        return [gathered[number] for number in range(count)]
    held = {0: value}
    bits = [1 << b for b in range(contexts.bit_length() - 2, 0, -1)]
    bits += [contexts << b for b in range(groups.bit_length() - 1)]
    for bit in bits:
        axis, flip, size = ("context", bit, contexts)
        if bit >= contexts:
            axis, flip, size = ("groups", bit // contexts, groups)
        pairs = [(i, i ^ flip) for i in range(size)]
        for mask in sorted(held):
            if mask:
                held[mask] = first(held[mask], held[bit])
            held[mask | bit] = lax.ppermute(held[mask], axis, pairs)
    if contexts > 1:
        for mask in sorted(held):
            held[mask] = then(held[mask], mask) if mask else held[mask]
            held[mask | 1] = core_swap(held[mask], contexts)
    return [held[mask] for mask in range(count)]


def core_swap(value, contexts):
    return lax.ppermute(value, "context", [(i, i ^ 1) for i in range(contexts)])


def plane_owners(count, me):
    if count & (count - 1):
        return list(range(count))
    return [me ^ mask for mask in range(count)]


def line_gather(value, count):
    if count != 4:
        return [lax.all_gather(value, "tensor", axis=0, tiled=False)]
    far, last = line_far(value)
    return [value, *line_near(value), far, last]


def line_near(value):
    up = lax.ppermute(value, "tensor", [(0, 1), (1, 2), (2, 3)])
    return up, lax.ppermute(value, "tensor", [(1, 0), (2, 1), (3, 2)])


def line_far(value):
    far = lax.ppermute(value, "tensor", [(0, 2), (1, 3), (2, 0), (3, 1)])
    return far, lax.ppermute(far, "tensor", [(1, 0), (2, 3)])


def chunk_gathers(info, values, copies, second, made, count):
    if count != 4:
        return [line_gather(value, count) for value in values]
    fars, lines = [], []
    for number, value in enumerate(values):
        after = [fars[-1][0]] if number else []
        if number == 1:
            after += second + made
        fars.append(line_far(gate(info, value, after) if after else value))
    for number, value in enumerate(copies):
        after = list(lines[number - 1][1:3]) if number else []
        if number > 1:
            after.append(fars[number - 2][1])
        value = gate(info, value, after) if after else value
        lines.append([value, *line_near(value), *fars[number]])
    return lines


class Table:
    def __init__(self, contexts, count):
        self.contexts, self.count = contexts, count
        self.owner = 1
        self.place = 1 + contexts
        self.low = self.place + count
        self.high = self.low + 1
        self.share = self.low + 2
        self.rows = self.low + 3


def line_read(table, info, refs, d, cols=slice(None)):
    if len(refs) == 1:
        return refs[0][info[table.place + d], :, cols].astype(jnp.float32)
    if d == 0:
        return refs[0][:, cols].astype(jnp.float32)
    if d == 2:
        return refs[3][:, cols].astype(jnp.float32)
    near = refs[1 if d == 1 else 2][:, cols].astype(jnp.float32)
    other = refs[4][:, cols].astype(jnp.float32)
    at_end = info[table.low if d == 1 else table.high]
    return jnp.where(at_end == 1, other, near)


def line_spec(blocks, rows, index):
    if len(blocks) == 1:
        count, _, width = blocks[0].shape
        return [pl.BlockSpec((count, rows, width), lambda i, info: (0, index(i), 0))]
    width = blocks[0].shape[1]
    return [pl.BlockSpec((rows, width), lambda i, info: (index(i), 0)) for _ in blocks]


def call(kernel, name, info, args, in_specs, out_specs, out_shape, grid=(1,), aliases=None,
         scratch=(), flops=1, vmem=16):
    return pl.pallas_call(
        kernel,
        grid_spec=pltpu.PrefetchScalarGridSpec(
            num_scalar_prefetch=1,
            grid=grid,
            in_specs=in_specs,
            out_specs=out_specs,
            scratch_shapes=list(scratch),
        ),
        out_shape=out_shape,
        input_output_aliases=aliases or {},
        compiler_params=pltpu.CompilerParams(vmem_limit_bytes=vmem * MIB or None),
        cost_estimate=pl.CostEstimate(flops=flops, bytes_accessed=1, transcendentals=0),
        name=name,
    )(info, *args)


def whole(a):
    zeros = (0,) * len(a.shape)
    return pl.BlockSpec(tuple(a.shape), lambda i, info: zeros)


def prepare_kernel(table, slab, keep, info, q_hbm, kv_hbm, cache_hbm, w_hbm, r_hbm, cos_ref,
                   sin_ref, length_ref, *refs):
    count, raw = table.count, slab - keep
    q_out, kv_out, outs = refs[0], refs[1], refs[2 : 2 + count]
    q_ref, kv_ref, w_ref, sems = refs[-4:]
    slots, rows, part = cache_hbm.shape[0], q_ref.shape[0], w_ref.shape[0]
    span, tail = slice(slots, slots + rows), slice(slots + rows, slots + rows + TAIL)
    start = pl.multiple_of(info[table.share] * part, part)
    moves = [
        (w_hbm.at[pl.ds(start, part)], w_ref),
        (kv_hbm, kv_ref),
        (q_hbm, q_ref),
        (cache_hbm, kv_out.at[pl.ds(0, slots)]),
    ]
    if raw:
        moves.append((r_hbm.at[:, pl.ds(keep, raw)], refs[2 + count]))
    copies = [pltpu.make_async_copy(*move, sems.at[n]) for n, move in enumerate(moves)]
    for copy in copies:
        copy.start()

    copies[0].wait()
    for d, out in enumerate(outs):
        target = lax.rem(info[table.place] + d, count)
        out[:, :keep] = w_ref[:, pl.ds(pl.multiple_of(target * slab, slab), keep)]
        for j in range(count if raw else 0):
            out[:, keep + j * raw : keep + (j + 1) * raw] = w_ref[
                :, j * slab + keep : (j + 1) * slab
            ]

    cosine, sine = cos_ref[...], sin_ref[...]

    def turn(block):
        block = block.astype(jnp.float32)
        return (block * cosine + pltpu.roll(block, HD // 2, 1) * sine).astype(jnp.bfloat16)

    copies[1].wait()
    kv_out[span, :HD] = turn(kv_ref[:, :HD])
    kv_out[span, HD:] = kv_ref[:, HD:]
    length = length_ref[0]
    upper = lax.div(length, DIGIT)
    lower = length - upper * DIGIT
    kv_out[tail, :HD] = jnp.full((TAIL, HD), upper.astype(jnp.float32)).astype(jnp.bfloat16)
    kv_out[tail, HD:] = jnp.full((TAIL, HD), lower.astype(jnp.float32)).astype(jnp.bfloat16)
    copies[2].wait()
    for head in range(q_ref.shape[1] // HD):
        cols = slice(head * HD, (head + 1) * HD)
        q_out[:, cols] = turn(q_ref[:, cols])
    for copy in copies[3:]:
        copy.wait()


def prepare(table, info, queries, span_pairs, cache, out_weight, residual, cosine, sine, lengths,
            part, keep):
    rows, slab = residual.shape
    shapes = [
        jax.ShapeDtypeStruct(queries.shape, jnp.bfloat16),
        jax.ShapeDtypeStruct((cache.shape[0] + rows + TAIL, 2 * HD), jnp.bfloat16),
    ]
    width = keep + table.count * (slab - keep)
    shapes += [jax.ShapeDtypeStruct((part, width), out_weight.dtype)] * table.count
    if keep < slab:
        shapes.append(jax.ShapeDtypeStruct((rows, slab - keep), residual.dtype))
    return call(
        functools.partial(prepare_kernel, table, slab, keep),
        "prepare",
        info,
        [queries, span_pairs, cache, out_weight, residual, cosine, sine, lengths],
        [ANYWHERE] * 5
        + [whole(cosine), whole(sine), pl.BlockSpec(memory_space=pltpu.SMEM)],
        [whole(shape) for shape in shapes],
        shapes,
        scratch=[
            pltpu.VMEM(queries.shape, jnp.bfloat16),
            pltpu.VMEM(span_pairs.shape, jnp.bfloat16),
            pltpu.VMEM((part, out_weight.shape[1]), out_weight.dtype),
            pltpu.SemaphoreType.DMA((5,)),
        ],
        vmem=0,
    )


def stack_kernel(count, info, *refs):
    for number, part in enumerate(refs[:count]):
        refs[-1][number] = part[...]


def stack(info, parts, after):
    shape = jax.ShapeDtypeStruct((len(parts), *parts[0].shape), parts[0].dtype)
    return call(
        functools.partial(stack_kernel, len(parts)),
        "stack",
        info,
        [*parts, *after],
        [whole(p) for p in parts] + [ANYWHERE] * len(after),
        whole(shape),
        shape,
    )


def gate_kernel(info, *refs):
    pass


def gate(info, value, after):
    return call(
        gate_kernel,
        "gate",
        info,
        [value, *after],
        [ANYWHERE] * (1 + len(after)),
        ANYWHERE,
        jax.ShapeDtypeStruct(value.shape, value.dtype),
        aliases={1: 0},
    )


def attend_kernel(table, slots, first, info, q_ref, *refs):
    count = table.contexts
    pieces, out_ref, s_ref = refs[:count], refs[-2], refs[-1]
    rows = q_ref.shape[0]
    heads = q_ref.shape[1] // HD
    chunk = pl.program_id(0) + first
    mine = info[0]
    q = jnp.concatenate([q_ref[:, h * HD : (h + 1) * HD] for h in range(heads)], axis=0)
    exponent = math.log2(math.e) / math.sqrt(HD)

    blocks = []
    peak = jnp.full((heads * rows, HD), NEG, jnp.float32)
    column = 0
    for kind in ("cache", "span"):
        for number, ref in enumerate(pieces):
            tail = ref.shape[0] - TAIL
            first, last = (0, slots) if kind == "cache" else (slots, tail)
            width = min(KEY_BLOCK, last - first)
            length = ref[tail : tail + 1, :HD].astype(jnp.float32) * DIGIT + ref[
                tail : tail + 1, HD:
            ].astype(jnp.float32)
            length = jnp.concatenate([length] * (width // HD), axis=1)
            for begin in range(first, last, width):
                scores = lax.dot_general(
                    q,
                    ref[begin : begin + width, :HD],
                    (((1,), (1,)), ((), ())),
                    preferred_element_type=jnp.float32,
                )
                if kind == "cache":
                    slot = lax.broadcasted_iota(jnp.int32, (1, width), 1) + begin
                    live = slot.astype(jnp.float32) < length
                    scores = scores + jnp.where(live, 0.0, NEG)
                elif number == 0:
                    key = lax.broadcasted_iota(jnp.int32, (rows, width), 1) + (begin - first)
                    row = lax.broadcasted_iota(jnp.int32, (rows, width), 0) + chunk * rows
                    bias = jnp.where(key <= row, 0.0, NEG)
                    scores = scores + jnp.concatenate([bias] * heads, axis=0)
                else:
                    scores = scores + jnp.where(info[table.owner + number] < mine, 0.0, NEG)
                s_ref[:, column : column + width] = scores
                for lane in range(0, width, HD):
                    peak = jnp.maximum(peak, scores[:, lane : lane + HD])
                blocks.append((ref, begin, column, width))
                column += width
    top = jnp.max(peak, axis=1, keepdims=True)
    total = jnp.zeros((heads * rows, HD), jnp.float32)
    mixed = jnp.zeros((heads * rows, HD), jnp.float32)
    for ref, begin, column, width in blocks:
        weights = jnp.exp2((s_ref[:, column : column + width] - top) * exponent)
        for lane in range(0, width, HD):
            total = total + weights[:, lane : lane + HD]
        mixed = mixed + jnp.dot(
            weights.astype(jnp.bfloat16),
            ref[begin : begin + width, HD:],
            preferred_element_type=jnp.float32,
        )
    result = (mixed / jnp.sum(total, axis=1, keepdims=True)).astype(jnp.bfloat16)
    for h in range(heads):
        out_ref[:, h * HD : (h + 1) * HD] = result[h * rows : (h + 1) * rows]


def attend(table, info, queries, pieces, slots, begin, size, rows):
    width = queries.shape[1]
    heads = width // HD
    keys = sum(a.shape[0] - TAIL for a in pieces)
    first = begin // rows
    return call(
        functools.partial(attend_kernel, table, slots, first),
        "attend",
        info,
        [queries, *pieces],
        [pl.BlockSpec((rows, width), lambda i, info: (first + i, 0))]
        + [whole(a) for a in pieces],
        pl.BlockSpec((rows, width), lambda i, info: (i, 0)),
        jax.ShapeDtypeStruct((size, width), jnp.bfloat16),
        grid=(size // rows,),
        scratch=[pltpu.VMEM((heads * rows, keys), jnp.float32)],
        flops=ATTEND_FLOPS * size * heads * keys * HD,
        vmem=28,
    )


def project_kernel(table, lines, shares, splits, info, *refs):
    count = table.count
    attention, pieces = refs[:lines], refs[lines : lines + shares]
    r_ref = refs[lines + shares]
    parts, h_ref, w_ref = refs[-2 - 2 * len(splits) : -2], refs[-2], refs[-1]
    share_rows, keep = pieces[0].shape[1], w_ref.shape[2]
    for number, piece in enumerate(pieces):
        start = pl.multiple_of(info[table.rows + number] * share_rows, share_rows)
        for d in range(count):
            w_ref[d, pl.ds(start, share_rows)] = piece[d, :, :keep]
    blocks = [
        line_read(table, info, attention, d).astype(jnp.bfloat16) for d in range(count)
    ]
    for part, copy, (begin, size) in zip(parts, parts[len(splits) :], splits):
        rows = slice(begin, begin + size)
        total = r_ref[rows, :keep].astype(jnp.float32)
        for d in range(count):
            total = total + jnp.dot(
                blocks[d][rows], w_ref[d], preferred_element_type=jnp.float32
            )
        result = total.astype(jnp.bfloat16)
        h_ref[rows, :keep] = result
        part[...] = result
        copy[...] = result


def project(table, info, attention, pieces, residual, hidden, keep, half, halves, splits):
    all_rows, slab = residual.shape
    rows = all_rows // halves
    count, share_rows, _ = pieces[0].shape
    parts = [jax.ShapeDtypeStruct((size, keep), jnp.bfloat16) for _, size in splits * 2]
    row_spec = pl.BlockSpec((rows, slab), lambda i, info: (half, 0))
    args = [*attention, *pieces, residual]
    specs = line_spec(attention, rows, lambda i: 0) + [whole(p) for p in pieces] + [row_spec]
    aliases = {}
    if hidden is not None:
        args.append(hidden)
        specs.append(ANYWHERE)
        aliases = {len(args): len(parts)}
    return call(
        functools.partial(project_kernel, table, len(attention), len(pieces), splits),
        "project",
        info,
        args,
        specs,
        [whole(part) for part in parts] + [row_spec],
        [*parts, jax.ShapeDtypeStruct(residual.shape, jnp.bfloat16)],
        aliases=aliases,
        scratch=[pltpu.VMEM((count, len(pieces) * share_rows, keep), jnp.bfloat16)],
        vmem=36,
    )


def project_raw_kernel(table, lines, halves, raw_lines, shares, info, *refs):
    count = table.count
    attention, refs = refs[: lines * halves], refs[lines * halves :]
    residuals, pieces = refs[:raw_lines], refs[raw_lines : raw_lines + shares]
    raw_ref, h_ref, w_ref = refs[-3:]
    raw, share_rows = h_ref.shape[1], pieces[0].shape[1]
    keep = pieces[0].shape[2] - w_ref.shape[2]
    step = pl.program_id(0)

    @pl.when(step == 0)
    def _():
        for number, piece in enumerate(pieces):
            start = pl.multiple_of(info[table.rows + number] * share_rows, share_rows)
            for d in range(count):
                w_ref[d, pl.ds(start, share_rows)] = piece[d, :, keep:]

    blocks = []
    for d in range(count):
        block = line_read(table, info, attention[:lines], d)
        if halves == 2:
            other = line_read(table, info, attention[lines:], d)
            block = jnp.where(step < pl.num_programs(0) // 2, block, other)
        blocks.append(block.astype(jnp.bfloat16))
    for slab in range(count):
        cols = pl.ds(pl.multiple_of(info[table.place + slab] * raw, raw), raw)
        total = line_read(table, info, residuals, slab)
        for d in range(count):
            total = total + jnp.dot(
                blocks[d], w_ref[d, :, cols], preferred_element_type=jnp.float32
            )
        result = total.astype(jnp.bfloat16)
        raw_ref[:, slab * raw : (slab + 1) * raw] = result
        if slab == 0:
            h_ref[...] = result


def project_raw(table, info, attention, residuals, pieces, hidden, raw, rows):
    all_rows, slab = hidden.shape
    count, share_rows, _ = pieces[0].shape
    halves, lines = len(attention), len(attention[0])
    steps = all_rows // rows
    args = [*sum(attention, []), *residuals, *pieces, hidden]
    specs = []
    for half, blocks in enumerate(attention):
        first, last = half * (steps // halves), (half + 1) * (steps // halves) - 1
        specs += line_spec(
            blocks, rows, lambda i, a=first, b=last: jnp.clip(i, a, b) - a
        )
    out = jax.ShapeDtypeStruct((all_rows, count * raw), jnp.bfloat16)
    return call(
        functools.partial(
            project_raw_kernel, table, lines, halves, len(residuals), len(pieces)
        ),
        "project_raw",
        info,
        args,
        specs
        + line_spec(residuals, rows, lambda i: i)
        + [whole(p) for p in pieces]
        + [ANYWHERE],
        [
            pl.BlockSpec((rows, count * raw), lambda i, info: (i, 0)),
            pl.BlockSpec((rows, raw), lambda i, info: (i, slab // raw - 1)),
        ],
        [out, jax.ShapeDtypeStruct(hidden.shape, jnp.bfloat16)],
        grid=(steps,),
        aliases={len(args): 1},
        scratch=[pltpu.VMEM((count, len(pieces) * share_rows, count * raw), jnp.bfloat16)],
        vmem=36,
    )


def norm_kernel(table, lines, keep, slab, info, g_ref, *refs):
    count = table.count
    blocks, out_ref = refs[:lines], refs[-1]
    raw = slab - keep
    values = []
    squares = jnp.zeros((out_ref.shape[0], 1), jnp.float32)

    def read(d):
        found = [(0, keep, line_read(table, info, blocks, d))]
        if raw:
            cols = slice(d * raw, (d + 1) * raw)
            found.append((keep, raw, refs[lines][:, cols].astype(jnp.float32)))
        return found

    for d in range(count):
        for _, _, value in read(d):
            squares = squares + jnp.sum(value * value, axis=1, keepdims=True)
    inverse = lax.rsqrt(squares / (count * slab) + EPS_NORM)
    for d in range(count):
        for offset, width, value in read(d):
            start = pl.multiple_of(info[table.place + d] * slab + offset, HD)
            cols = pl.ds(start, width)
            out_ref[:, cols] = (value * inverse * g_ref[:, cols]).astype(jnp.bfloat16)


def norm_into(table, info, buffer, blocks, raw_hidden, gain, begin, rows, keep, slab, total_rows):
    width = table.count * slab
    step = math.gcd(rows, 32)
    steps, first = rows // step, begin // step
    args = [gain.reshape(1, width), *blocks]
    in_specs = [pl.BlockSpec((1, width), lambda i, info: (0, 0))]
    in_specs += line_spec(blocks, step, lambda i: i)
    if raw_hidden is not None:
        args.append(raw_hidden)
        in_specs.append(
            pl.BlockSpec((step, raw_hidden.shape[1]), lambda i, info: (first + i, 0))
        )
    aliases = {}
    if buffer is not None:
        args.append(buffer)
        in_specs.append(ANYWHERE)
        aliases = {len(args): 0}
    return call(
        functools.partial(norm_kernel, table, len(blocks), keep, slab),
        "norm",
        info,
        args,
        in_specs,
        pl.BlockSpec((step, width), lambda i, info: (first + i, 0)),
        jax.ShapeDtypeStruct((total_rows, width), jnp.bfloat16),
        grid=(steps,),
        aliases=aliases,
    )


def per_device(queries, span_kv, cache, lengths, offset, out_weight, residual, gain):
    rows = queries.shape[0]
    heads = queries.shape[1] // HD
    depth = out_weight.shape[0]
    slab = residual.shape[1]
    contexts = lax.axis_size("context")
    count = lax.axis_size("tensor")
    context_index = lax.axis_index("context")
    tensor_index = lax.axis_index("tensor")
    kv_index = tensor_index * heads // GROUP
    groups = lax.axis_size("groups")
    shares = groups * contexts
    share = lax.axis_index("groups") * contexts + context_index
    raw = slab // RAW_PART if slab % (RAW_PART * HD) == 0 else 0
    keep = slab - raw
    chunk = min(CHUNK, rows)
    halves = 1
    half = rows // halves
    sizes = [chunk] * (half // chunk)
    if len(sizes) > 1 and chunk % 128 == 0:
        sizes[0] += 32
        sizes[-1] -= 32
    splits = [[(sum(sizes[:n]), size) for n, size in enumerate(sizes)]] * halves

    table = Table(contexts, count)
    steering = [context_index, *owners_of(contexts, context_index)]
    steering += [lax.rem(tensor_index + (count - d), count) for d in range(count)]
    steering += [tensor_index == 0, tensor_index == count - 1, share]
    steering += plane_owners(shares, share)
    info = jnp.stack([jnp.asarray(v).astype(jnp.int32) for v in steering])

    cache_local = lax.dynamic_index_in_dim(cache, kv_index, 0, keepdims=False)
    span_local = lax.dynamic_index_in_dim(span_kv, kv_index, 1, keepdims=False)
    positions = offset[0] + context_index * rows + jnp.arange(rows, dtype=jnp.int32)
    both = jnp.concatenate([frequencies(HD)] * 2)
    angles = positions.astype(jnp.float32)[:, None] * both[None, :]
    sign = jnp.where(jnp.arange(HD) < HD // 2, -1.0, 1.0)
    q_turned, payload, *cuts = prepare(
        table, info, queries, span_local, cache_local, out_weight, residual, jnp.cos(angles),
        jnp.sin(angles) * sign[None, :], lengths, depth // shares, keep,
    )
    parts = [cuts[0]]
    for shift in range(1, count):
        pairs = [(i, (i + shift) % count) for i in range(count)]
        parts.append(lax.ppermute(cuts[shift], "tensor", pairs))
    own_weights = stack(info, parts, [])
    own_raw = [gate(info, cuts[count], parts[1:])] if raw else []
    pieces = pieces_of(
        payload, "context", contexts, lambda block: gate(info, block, [own_weights, *own_raw])
    )
    slots = cache_local.shape[0]
    mixed = [
        attend(table, info, q_turned, pieces, slots, number * half, half, chunk)
        for number in range(halves)
    ]
    residuals = line_gather(own_raw[0], count) if raw else []
    ready = [gate(info, mixed[0], residuals[1:4] or residuals), *mixed[1:]] if raw else mixed
    attention = [line_gather(value, count) for value in ready]
    before = [*attention[0][1:], *mixed[1:], *residuals[4:]]
    weights = plane_gather(
        own_weights,
        groups,
        contexts,
        lambda block, other: gate(info, block, mixed[:1]),
        lambda block, mask: gate(
            info,
            block,
            attention[0][1:3] if mask in (mask & -mask,) else before,
        ),
    )
    values, copies, hidden = [], [], None
    for number in range(halves):
        *made, hidden = project(
            table, info, attention[number], weights, residual, hidden, keep, number,
            halves, splits[number],
        )
        values += made[: len(made) // 2]
        copies += made[len(made) // 2 :]
    raw_hidden = None
    if raw:
        raw_hidden, hidden = project_raw(
            table, info, attention, residuals, weights, hidden, raw, chunk
        )
    lines = chunk_gathers(
        info,
        values,
        copies,
        attention[-1][1:] if halves > 1 else [],
        [raw_hidden] if raw else [],
        count,
    )
    normed, begin = None, 0
    for blocks, value in zip(lines, values):
        normed = norm_into(
            table, info, normed, blocks, raw_hidden, gain, begin, value.shape[0], keep, slab, rows
        )
        begin += value.shape[0]
    return (hidden, normed)


def solution(mesh):
    in_specs = (
        P(("groups", "context"), "tensor"),
        P(("groups", "context"), None, None),
        P("groups", "context", None),
        P(("groups", "context")),
        P("groups"),
        P("tensor", None),
        P(("groups", "context"), "tensor"),
        P(),
    )
    out_specs = (P(("groups", "context"), "tensor"), P(("groups", "context"), None))
    return jax.shard_map(
        per_device, mesh=mesh, in_specs=in_specs, out_specs=out_specs, check_vma=False
    )
```

```python
import functools
import math

import jax
import jax.numpy as jnp
from jax import lax
from jax.experimental import pallas as pl
from jax.experimental.pallas import tpu as pltpu
from jax.sharding import PartitionSpec as P

GROUP = 8
HD = 128
NEG = -1e30
EPS_NORM = 1e-05
MIB = 1024 * 1024
CHUNK = 128
KEY_BLOCK = 512
ATTEND_FLOPS = 16
RAW_PART = 8
TAIL = 16
DIGIT = 32
ANYWHERE = pl.BlockSpec(memory_space=pl.ANY)


def frequencies(head_width):
    counter = jnp.arange(head_width // 2, dtype=jnp.float32)
    base_freq = jnp.exp(-(2.0 * counter / head_width) * math.log(500000.0))
    wavelength = 2.0 * math.pi / base_freq
    smoothing = (8192.0 / wavelength - 1.0) / 3.0
    blended = (1.0 - smoothing) * base_freq / 8.0 + smoothing * base_freq
    return jnp.where(
        wavelength < 2048.0, base_freq, jnp.where(wavelength > 8192.0, base_freq / 8.0, blended)
    )


def pieces_of(value, axis, count, between=lambda block: block):
    if count & (count - 1) == 0:
        held = {0: value}
        bit = count // 2
        while bit:
            pairs = [(i, i ^ bit) for i in range(count)]
            for mask in sorted(held):
                held[mask | bit] = lax.ppermute(held[mask], axis, pairs)
            if bit == count // 2:
                held[bit] = between(held[bit])
            bit //= 2
        return [held[mask] for mask in range(count)]
    blocks = [value]
    for shift in range(1, count):
        pairs = [(i, (i + shift) % count) for i in range(count)]
        blocks.append(lax.ppermute(value, axis, pairs))
    blocks[-1] = between(blocks[-1])
    return blocks


def owners_of(count, me):
    if count & (count - 1) == 0:
        return [me ^ mask for mask in range(count)]
    return [(me + count - shift) % count for shift in range(count)]


def plane_gather(value, groups, contexts, first, then):
    count = groups * contexts
    if count & (count - 1):
        gathered = lax.all_gather(value, ("groups", "context"), axis=0, tiled=False)
        return [gathered[number] for number in range(count)]
    held = {0: value}
    bits = [1 << b for b in range(contexts.bit_length() - 2, 0, -1)]
    bits += [contexts << b for b in range(groups.bit_length() - 1)]
    for bit in bits:
        axis, flip, size = ("context", bit, contexts)
        if bit >= contexts:
            axis, flip, size = ("groups", bit // contexts, groups)
        pairs = [(i, i ^ flip) for i in range(size)]
        for mask in sorted(held):
            if mask:
                held[mask] = first(held[mask], held[bit])
            held[mask | bit] = lax.ppermute(held[mask], axis, pairs)
    if contexts > 1:
        for mask in sorted(held):
            held[mask] = then(held[mask], mask) if mask else held[mask]
            held[mask | 1] = core_swap(held[mask], contexts)
    return [held[mask] for mask in range(count)]


def core_swap(value, contexts):
    return lax.ppermute(value, "context", [(i, i ^ 1) for i in range(contexts)])


def plane_owners(count, me):
    if count & (count - 1):
        return list(range(count))
    return [me ^ mask for mask in range(count)]


def line_gather(value, count):
    if count != 4:
        return [lax.all_gather(value, "tensor", axis=0, tiled=False)]
    far, last = line_far(value)
    return [value, *line_near(value), far, last]


def line_near(value):
    up = lax.ppermute(value, "tensor", [(0, 1), (1, 2), (2, 3)])
    return up, lax.ppermute(value, "tensor", [(1, 0), (2, 1), (3, 2)])


def line_far(value):
    far = lax.ppermute(value, "tensor", [(0, 2), (1, 3), (2, 0), (3, 1)])
    return far, lax.ppermute(far, "tensor", [(1, 0), (2, 3)])


def chunk_gathers(info, values, copies, second, made, count):
    if count != 4:
        return [line_gather(value, count) for value in values]
    fars, lines = [], []
    for number, value in enumerate(values):
        after = [fars[-1][0]] if number else []
        if number == 1:
            after += second + made
        fars.append(line_far(gate(info, value, after) if after else value))
    for number, value in enumerate(copies):
        after = list(lines[number - 1][1:3]) if number else []
        if number > 1:
            after.append(fars[number - 2][1])
        value = gate(info, value, after) if after else value
        lines.append([value, *line_near(value), *fars[number]])
    return lines


class Table:
    def __init__(self, contexts, count):
        self.contexts, self.count = contexts, count
        self.owner = 1
        self.place = 1 + contexts
        self.low = self.place + count
        self.high = self.low + 1
        self.share = self.low + 2
        self.rows = self.low + 3


def line_read(table, info, refs, d, cols=slice(None)):
    if len(refs) == 1:
        return refs[0][info[table.place + d], :, cols].astype(jnp.float32)
    if d == 0:
        return refs[0][:, cols].astype(jnp.float32)
    if d == 2:
        return refs[3][:, cols].astype(jnp.float32)
    near = refs[1 if d == 1 else 2][:, cols].astype(jnp.float32)
    other = refs[4][:, cols].astype(jnp.float32)
    at_end = info[table.low if d == 1 else table.high]
    return jnp.where(at_end == 1, other, near)


def line_spec(blocks, rows, index):
    if len(blocks) == 1:
        count, _, width = blocks[0].shape
        return [pl.BlockSpec((count, rows, width), lambda i, info: (0, index(i), 0))]
    width = blocks[0].shape[1]
    return [pl.BlockSpec((rows, width), lambda i, info: (index(i), 0)) for _ in blocks]


def call(kernel, name, info, args, in_specs, out_specs, out_shape, grid=(1,), aliases=None,
         scratch=(), flops=1, vmem=16):
    return pl.pallas_call(
        kernel,
        grid_spec=pltpu.PrefetchScalarGridSpec(
            num_scalar_prefetch=1,
            grid=grid,
            in_specs=in_specs,
            out_specs=out_specs,
            scratch_shapes=list(scratch),
        ),
        out_shape=out_shape,
        input_output_aliases=aliases or {},
        compiler_params=pltpu.CompilerParams(vmem_limit_bytes=vmem * MIB or None),
        cost_estimate=pl.CostEstimate(flops=flops, bytes_accessed=1, transcendentals=0),
        name=name,
    )(info, *args)


def whole(a):
    zeros = (0,) * len(a.shape)
    return pl.BlockSpec(tuple(a.shape), lambda i, info: zeros)


def prepare_kernel(table, slab, keep, info, q_hbm, kv_hbm, cache_hbm, w_hbm, r_hbm, cos_ref,
                   sin_ref, length_ref, *refs):
    count, raw = table.count, slab - keep
    q_out, kv_out, outs = refs[0], refs[1], refs[2 : 2 + count]
    q_ref, kv_ref, w_ref, sems = refs[-4:]
    slots, rows, part = cache_hbm.shape[0], q_ref.shape[0], w_ref.shape[0]
    span, tail = slice(slots, slots + rows), slice(slots + rows, slots + rows + TAIL)
    start = pl.multiple_of(info[table.share] * part, part)
    moves = [
        (w_hbm.at[pl.ds(start, part)], w_ref),
        (kv_hbm, kv_ref),
        (q_hbm, q_ref),
        (cache_hbm, kv_out.at[pl.ds(0, slots)]),
    ]
    if raw:
        moves.append((r_hbm.at[:, pl.ds(keep, raw)], refs[2 + count]))
    copies = [pltpu.make_async_copy(*move, sems.at[n]) for n, move in enumerate(moves)]
    for copy in copies:
        copy.start()

    copies[0].wait()
    for d, out in enumerate(outs):
        target = lax.rem(info[table.place] + d, count)
        out[:, :keep] = w_ref[:, pl.ds(pl.multiple_of(target * slab, slab), keep)]
        for j in range(count if raw else 0):
            out[:, keep + j * raw : keep + (j + 1) * raw] = w_ref[
                :, j * slab + keep : (j + 1) * slab
            ]

    cosine, sine = cos_ref[...], sin_ref[...]

    def turn(block):
        block = block.astype(jnp.float32)
        return (block * cosine + pltpu.roll(block, HD // 2, 1) * sine).astype(jnp.bfloat16)

    copies[1].wait()
    kv_out[span, :HD] = turn(kv_ref[:, :HD])
    kv_out[span, HD:] = kv_ref[:, HD:]
    length = length_ref[0]
    upper = lax.div(length, DIGIT)
    lower = length - upper * DIGIT
    kv_out[tail, :HD] = jnp.full((TAIL, HD), upper.astype(jnp.float32)).astype(jnp.bfloat16)
    kv_out[tail, HD:] = jnp.full((TAIL, HD), lower.astype(jnp.float32)).astype(jnp.bfloat16)
    copies[2].wait()
    for head in range(q_ref.shape[1] // HD):
        cols = slice(head * HD, (head + 1) * HD)
        q_out[:, cols] = turn(q_ref[:, cols])
    for copy in copies[3:]:
        copy.wait()


def prepare(table, info, queries, span_pairs, cache, out_weight, residual, cosine, sine, lengths,
            part, keep):
    rows, slab = residual.shape
    shapes = [
        jax.ShapeDtypeStruct(queries.shape, jnp.bfloat16),
        jax.ShapeDtypeStruct((cache.shape[0] + rows + TAIL, 2 * HD), jnp.bfloat16),
    ]
    width = keep + table.count * (slab - keep)
    shapes += [jax.ShapeDtypeStruct((part, width), out_weight.dtype)] * table.count
    if keep < slab:
        shapes.append(jax.ShapeDtypeStruct((rows, slab - keep), residual.dtype))
    return call(
        functools.partial(prepare_kernel, table, slab, keep),
        "prepare",
        info,
        [queries, span_pairs, cache, out_weight, residual, cosine, sine, lengths],
        [ANYWHERE] * 5
        + [whole(cosine), whole(sine), pl.BlockSpec(memory_space=pltpu.SMEM)],
        [whole(shape) for shape in shapes],
        shapes,
        scratch=[
            pltpu.VMEM(queries.shape, jnp.bfloat16),
            pltpu.VMEM(span_pairs.shape, jnp.bfloat16),
            pltpu.VMEM((part, out_weight.shape[1]), out_weight.dtype),
            pltpu.SemaphoreType.DMA((5,)),
        ],
        vmem=0,
    )


def stack_kernel(count, info, *refs):
    for number, part in enumerate(refs[:count]):
        refs[-1][number] = part[...]


def stack(info, parts, after):
    shape = jax.ShapeDtypeStruct((len(parts), *parts[0].shape), parts[0].dtype)
    return call(
        functools.partial(stack_kernel, len(parts)),
        "stack",
        info,
        [*parts, *after],
        [whole(p) for p in parts] + [ANYWHERE] * len(after),
        whole(shape),
        shape,
    )


def gate_kernel(info, *refs):
    pass


def gate(info, value, after):
    return call(
        gate_kernel,
        "gate",
        info,
        [value, *after],
        [ANYWHERE] * (1 + len(after)),
        ANYWHERE,
        jax.ShapeDtypeStruct(value.shape, value.dtype),
        aliases={1: 0},
    )


def attend_kernel(table, slots, first, info, q_ref, *refs):
    count = table.contexts
    pieces, out_ref, s_ref = refs[:count], refs[-2], refs[-1]
    rows = q_ref.shape[0]
    heads = q_ref.shape[1] // HD
    chunk = pl.program_id(0) + first
    mine = info[0]
    q = jnp.concatenate([q_ref[:, h * HD : (h + 1) * HD] for h in range(heads)], axis=0)
    exponent = math.log2(math.e) / math.sqrt(HD)

    blocks = []
    peak = jnp.full((heads * rows, HD), NEG, jnp.float32)
    column = 0
    for kind in ("cache", "span"):
        for number, ref in enumerate(pieces):
            tail = ref.shape[0] - TAIL
            first, last = (0, slots) if kind == "cache" else (slots, tail)
            width = min(KEY_BLOCK, last - first)
            length = ref[tail : tail + 1, :HD].astype(jnp.float32) * DIGIT + ref[
                tail : tail + 1, HD:
            ].astype(jnp.float32)
            length = jnp.concatenate([length] * (width // HD), axis=1)
            for begin in range(first, last, width):
                scores = lax.dot_general(
                    q,
                    ref[begin : begin + width, :HD],
                    (((1,), (1,)), ((), ())),
                    preferred_element_type=jnp.float32,
                )
                if kind == "cache":
                    slot = lax.broadcasted_iota(jnp.int32, (1, width), 1) + begin
                    live = slot.astype(jnp.float32) < length
                    scores = scores + jnp.where(live, 0.0, NEG)
                elif number == 0:
                    key = lax.broadcasted_iota(jnp.int32, (rows, width), 1) + (begin - first)
                    row = lax.broadcasted_iota(jnp.int32, (rows, width), 0) + chunk * rows
                    bias = jnp.where(key <= row, 0.0, NEG)
                    scores = scores + jnp.concatenate([bias] * heads, axis=0)
                else:
                    scores = scores + jnp.where(info[table.owner + number] < mine, 0.0, NEG)
                s_ref[:, column : column + width] = scores
                for lane in range(0, width, HD):
                    peak = jnp.maximum(peak, scores[:, lane : lane + HD])
                blocks.append((ref, begin, column, width))
                column += width
    top = jnp.max(peak, axis=1, keepdims=True)
    total = jnp.zeros((heads * rows, HD), jnp.float32)
    mixed = jnp.zeros((heads * rows, HD), jnp.float32)
    for ref, begin, column, width in blocks:
        weights = jnp.exp2((s_ref[:, column : column + width] - top) * exponent)
        for lane in range(0, width, HD):
            total = total + weights[:, lane : lane + HD]
        mixed = mixed + jnp.dot(
            weights.astype(jnp.bfloat16),
            ref[begin : begin + width, HD:],
            preferred_element_type=jnp.float32,
        )
    result = (mixed / jnp.sum(total, axis=1, keepdims=True)).astype(jnp.bfloat16)
    for h in range(heads):
        out_ref[:, h * HD : (h + 1) * HD] = result[h * rows : (h + 1) * rows]


def attend(table, info, queries, pieces, slots, begin, size, rows):
    width = queries.shape[1]
    heads = width // HD
    keys = sum(a.shape[0] - TAIL for a in pieces)
    first = begin // rows
    return call(
        functools.partial(attend_kernel, table, slots, first),
        "attend",
        info,
        [queries, *pieces],
        [pl.BlockSpec((rows, width), lambda i, info: (first + i, 0))]
        + [whole(a) for a in pieces],
        pl.BlockSpec((rows, width), lambda i, info: (i, 0)),
        jax.ShapeDtypeStruct((size, width), jnp.bfloat16),
        grid=(size // rows,),
        scratch=[pltpu.VMEM((heads * rows, keys), jnp.float32)],
        flops=ATTEND_FLOPS * size * heads * keys * HD,
        vmem=28,
    )


def project_kernel(table, lines, shares, splits, info, *refs):
    count = table.count
    attention, pieces = refs[:lines], refs[lines : lines + shares]
    r_ref = refs[lines + shares]
    parts, h_ref, w_ref = refs[-2 - 2 * len(splits) : -2], refs[-2], refs[-1]
    share_rows, keep = pieces[0].shape[1], w_ref.shape[2]
    for number, piece in enumerate(pieces):
        start = pl.multiple_of(info[table.rows + number] * share_rows, share_rows)
        for d in range(count):
            w_ref[d, pl.ds(start, share_rows)] = piece[d, :, :keep]
    blocks = [
        line_read(table, info, attention, d).astype(jnp.bfloat16) for d in range(count)
    ]
    for part, copy, (begin, size) in zip(parts, parts[len(splits) :], splits):
        rows = slice(begin, begin + size)
        total = r_ref[rows, :keep].astype(jnp.float32)
        for d in range(count):
            total = total + jnp.dot(
                blocks[d][rows], w_ref[d], preferred_element_type=jnp.float32
            )
        result = total.astype(jnp.bfloat16)
        h_ref[rows, :keep] = result
        part[...] = result
        copy[...] = result


def project(table, info, attention, pieces, residual, hidden, keep, half, halves, splits):
    all_rows, slab = residual.shape
    rows = all_rows // halves
    count, share_rows, _ = pieces[0].shape
    parts = [jax.ShapeDtypeStruct((size, keep), jnp.bfloat16) for _, size in splits * 2]
    row_spec = pl.BlockSpec((rows, slab), lambda i, info: (half, 0))
    args = [*attention, *pieces, residual]
    specs = line_spec(attention, rows, lambda i: 0) + [whole(p) for p in pieces] + [row_spec]
    aliases = {}
    if hidden is not None:
        args.append(hidden)
        specs.append(ANYWHERE)
        aliases = {len(args): len(parts)}
    return call(
        functools.partial(project_kernel, table, len(attention), len(pieces), splits),
        "project",
        info,
        args,
        specs,
        [whole(part) for part in parts] + [row_spec],
        [*parts, jax.ShapeDtypeStruct(residual.shape, jnp.bfloat16)],
        aliases=aliases,
        scratch=[pltpu.VMEM((count, len(pieces) * share_rows, keep), jnp.bfloat16)],
        vmem=36,
    )


def project_raw_kernel(table, lines, halves, raw_lines, shares, info, *refs):
    count = table.count
    attention, refs = refs[: lines * halves], refs[lines * halves :]
    residuals, pieces = refs[:raw_lines], refs[raw_lines : raw_lines + shares]
    raw_ref, h_ref, w_ref = refs[-3:]
    raw, share_rows = h_ref.shape[1], pieces[0].shape[1]
    keep = pieces[0].shape[2] - w_ref.shape[2]
    step = pl.program_id(0)

    @pl.when(step == 0)
    def _():
        for number, piece in enumerate(pieces):
            start = pl.multiple_of(info[table.rows + number] * share_rows, share_rows)
            for d in range(count):
                w_ref[d, pl.ds(start, share_rows)] = piece[d, :, keep:]

    blocks = []
    for d in range(count):
        block = line_read(table, info, attention[:lines], d)
        if halves == 2:
            other = line_read(table, info, attention[lines:], d)
            block = jnp.where(step < pl.num_programs(0) // 2, block, other)
        blocks.append(block.astype(jnp.bfloat16))
    for slab in range(count):
        cols = pl.ds(pl.multiple_of(info[table.place + slab] * raw, raw), raw)
        total = line_read(table, info, residuals, slab)
        for d in range(count):
            total = total + jnp.dot(
                blocks[d], w_ref[d, :, cols], preferred_element_type=jnp.float32
            )
        result = total.astype(jnp.bfloat16)
        raw_ref[:, slab * raw : (slab + 1) * raw] = result
        if slab == 0:
            h_ref[...] = result


def project_raw(table, info, attention, residuals, pieces, hidden, raw, rows):
    all_rows, slab = hidden.shape
    count, share_rows, _ = pieces[0].shape
    halves, lines = len(attention), len(attention[0])
    steps = all_rows // rows
    args = [*sum(attention, []), *residuals, *pieces, hidden]
    specs = []
    for half, blocks in enumerate(attention):
        first, last = half * (steps // halves), (half + 1) * (steps // halves) - 1
        specs += line_spec(
            blocks, rows, lambda i, a=first, b=last: jnp.clip(i, a, b) - a
        )
    out = jax.ShapeDtypeStruct((all_rows, count * raw), jnp.bfloat16)
    return call(
        functools.partial(
            project_raw_kernel, table, lines, halves, len(residuals), len(pieces)
        ),
        "project_raw",
        info,
        args,
        specs
        + line_spec(residuals, rows, lambda i: i)
        + [whole(p) for p in pieces]
        + [ANYWHERE],
        [
            pl.BlockSpec((rows, count * raw), lambda i, info: (i, 0)),
            pl.BlockSpec((rows, raw), lambda i, info: (i, slab // raw - 1)),
        ],
        [out, jax.ShapeDtypeStruct(hidden.shape, jnp.bfloat16)],
        grid=(steps,),
        aliases={len(args): 1},
        scratch=[pltpu.VMEM((count, len(pieces) * share_rows, count * raw), jnp.bfloat16)],
        vmem=36,
    )


def norm_kernel(table, lines, keep, slab, info, g_ref, *refs):
    count = table.count
    blocks, out_ref = refs[:lines], refs[-1]
    raw = slab - keep
    values = []
    squares = jnp.zeros((out_ref.shape[0], 1), jnp.float32)

    def read(d):
        found = [(0, keep, line_read(table, info, blocks, d))]
        if raw:
            cols = slice(d * raw, (d + 1) * raw)
            found.append((keep, raw, refs[lines][:, cols].astype(jnp.float32)))
        return found

    for d in range(count):
        for _, _, value in read(d):
            squares = squares + jnp.sum(value * value, axis=1, keepdims=True)
    inverse = lax.rsqrt(squares / (count * slab) + EPS_NORM)
    for d in range(count):
        for offset, width, value in read(d):
            start = pl.multiple_of(info[table.place + d] * slab + offset, HD)
            cols = pl.ds(start, width)
            out_ref[:, cols] = (value * inverse * g_ref[:, cols]).astype(jnp.bfloat16)


def norm_into(table, info, buffer, blocks, raw_hidden, gain, begin, rows, keep, slab, total_rows):
    width = table.count * slab
    step = math.gcd(rows, 32)
    steps, first = rows // step, begin // step
    args = [gain.reshape(1, width), *blocks]
    in_specs = [pl.BlockSpec((1, width), lambda i, info: (0, 0))]
    in_specs += line_spec(blocks, step, lambda i: i)
    if raw_hidden is not None:
        args.append(raw_hidden)
        in_specs.append(
            pl.BlockSpec((step, raw_hidden.shape[1]), lambda i, info: (first + i, 0))
        )
    aliases = {}
    if buffer is not None:
        args.append(buffer)
        in_specs.append(ANYWHERE)
        aliases = {len(args): 0}
    return call(
        functools.partial(norm_kernel, table, len(blocks), keep, slab),
        "norm",
        info,
        args,
        in_specs,
        pl.BlockSpec((step, width), lambda i, info: (first + i, 0)),
        jax.ShapeDtypeStruct((total_rows, width), jnp.bfloat16),
        grid=(steps,),
        aliases=aliases,
    )


def per_device(queries, span_kv, cache, lengths, offset, out_weight, residual, gain):
    rows = queries.shape[0]
    heads = queries.shape[1] // HD
    depth = out_weight.shape[0]
    slab = residual.shape[1]
    contexts = lax.axis_size("context")
    count = lax.axis_size("tensor")
    context_index = lax.axis_index("context")
    tensor_index = lax.axis_index("tensor")
    kv_index = tensor_index * heads // GROUP
    groups = lax.axis_size("groups")
    shares = groups * contexts
    share = lax.axis_index("groups") * contexts + context_index
    raw = slab // RAW_PART if slab % (RAW_PART * HD) == 0 else 0
    keep = slab - raw
    chunk = min(CHUNK, rows)
    halves = 1
    half = rows // halves
    sizes = [chunk] * (half // chunk)
    splits = [[(sum(sizes[:n]), size) for n, size in enumerate(sizes)]] * halves

    table = Table(contexts, count)
    steering = [context_index, *owners_of(contexts, context_index)]
    steering += [lax.rem(tensor_index + (count - d), count) for d in range(count)]
    steering += [tensor_index == 0, tensor_index == count - 1, share]
    steering += plane_owners(shares, share)
    info = jnp.stack([jnp.asarray(v).astype(jnp.int32) for v in steering])

    cache_local = lax.dynamic_index_in_dim(cache, kv_index, 0, keepdims=False)
    span_local = lax.dynamic_index_in_dim(span_kv, kv_index, 1, keepdims=False)
    positions = offset[0] + context_index * rows + jnp.arange(rows, dtype=jnp.int32)
    both = jnp.concatenate([frequencies(HD)] * 2)
    angles = positions.astype(jnp.float32)[:, None] * both[None, :]
    sign = jnp.where(jnp.arange(HD) < HD // 2, -1.0, 1.0)
    q_turned, payload, *cuts = prepare(
        table, info, queries, span_local, cache_local, out_weight, residual, jnp.cos(angles),
        jnp.sin(angles) * sign[None, :], lengths, depth // shares, keep,
    )
    parts = [cuts[0]]
    for shift in range(1, count):
        pairs = [(i, (i + shift) % count) for i in range(count)]
        parts.append(lax.ppermute(cuts[shift], "tensor", pairs))
    own_weights = stack(info, parts, [])
    own_raw = [gate(info, cuts[count], parts[1:])] if raw else []
    pieces = pieces_of(
        payload, "context", contexts, lambda block: gate(info, block, [own_weights, *own_raw])
    )
    slots = cache_local.shape[0]
    mixed = [
        attend(table, info, q_turned, pieces, slots, number * half, half, chunk)
        for number in range(halves)
    ]
    residuals = line_gather(own_raw[0], count) if raw else []
    ready = [gate(info, mixed[0], residuals[1:4] or residuals), *mixed[1:]] if raw else mixed
    attention = [line_gather(value, count) for value in ready]
    before = [*attention[0][1:], *mixed[1:], *residuals[4:]]
    weights = plane_gather(
        own_weights,
        groups,
        contexts,
        lambda block, other: gate(info, block, mixed[:1]),
        lambda block, mask: gate(
            info,
            block,
            attention[0][1:3] if mask in (mask & -mask,) else before,
        ),
    )
    values, copies, hidden = [], [], None
    for number in range(halves):
        *made, hidden = project(
            table, info, attention[number], weights, residual, hidden, keep, number,
            halves, splits[number],
        )
        values += made[: len(made) // 2]
        copies += made[len(made) // 2 :]
    raw_hidden = None
    if raw:
        raw_hidden, hidden = project_raw(
            table, info, attention, residuals, weights, hidden, raw, chunk
        )
    lines = chunk_gathers(
        info,
        values,
        copies,
        attention[-1][1:] if halves > 1 else [],
        [raw_hidden] if raw else [],
        count,
    )
    normed, begin = None, 0
    for blocks, value in zip(lines, values):
        normed = norm_into(
            table, info, normed, blocks, raw_hidden, gain, begin, value.shape[0], keep, slab, rows
        )
        begin += value.shape[0]
    return (hidden, normed)


def solution(mesh):
    in_specs = (
        P(("groups", "context"), "tensor"),
        P(("groups", "context"), None, None),
        P("groups", "context", None),
        P(("groups", "context")),
        P("groups"),
        P("tensor", None),
        P(("groups", "context"), "tensor"),
        P(),
    )
    out_specs = (P(("groups", "context"), "tensor"), P(("groups", "context"), None))
    return jax.shard_map(
        per_device, mesh=mesh, in_specs=in_specs, out_specs=out_specs, check_vma=False
    )
```
